32 devices in a mesh: dp: 16 (over z, x, core), tensor: 2 (over y).
Axes of the slice: x: 2, y: 2, z: 4, core: 2. Of those that a mesh axis runs over, the one named last changes fastest.
Arguments:
- tokens: bfloat16 [32, 256, 1024], P('dp', 'tensor'), may hold values from -6 to 6
- encoder: bfloat16 [32, 128, 1024], P('dp', 'tensor'), may hold values from -6 to 6
- target_doc: int32 [32, 256], P('dp'), may hold values from 0 to 1, as said below
- source_doc: int32 [32, 128], P('dp'), may hold values from 0 to 1, as said below
- self_proj: bfloat16 [1024, 3, 1024], P('dp', None, 'tensor'), may hold values from -0.1875 to 0.1875
- self_out: bfloat16 [1024, 1024], P('tensor', 'dp'), may hold values from -1 to 1
- cross_query: bfloat16 [1024, 1024], P('dp', 'tensor'), may hold values from -0.1875 to 0.1875
- cross_pairs: bfloat16 [1024, 2, 1024], P('dp', None, 'tensor'), may hold values from -0.1875 to 0.1875
- cross_out: bfloat16 [1024, 1024], P('tensor', 'dp'), may hold values from -1 to 1
- hidden_in: bfloat16 [1024, 8192], P(None, ('dp', 'tensor')), may hold values from -0.1875 to 0.1875
- hidden_in_bias: bfloat16 [8192], P(('dp', 'tensor')), may hold values from -3 to 3
- hidden_out: bfloat16 [8192, 1024], P(('dp', 'tensor')), may hold values from -0.09375 to 0.09375
- hidden_out_bias: float32 [1024], P(('dp', 'tensor')), may hold values from -5 to 5
- self_gain: float32 [1024], P(('dp', 'tensor')), may hold values from 0.5 to 1.5
- self_shift: float32 [1024], P(('dp', 'tensor')), may hold values from -1.75 to 1.75
- cross_gain: float32 [1024], P(('dp', 'tensor')), may hold values from 0.5 to 1.5
- cross_shift: float32 [1024], P(('dp', 'tensor')), may hold values from -1.75 to 1.75
- hidden_gain: float32 [1024], P(('dp', 'tensor')), may hold values from 0.5 to 1.5
- hidden_shift: float32 [1024], P(('dp', 'tensor')), may hold values from -1.75 to 1.75
- cotangent: bfloat16 [32, 256, 1024], P('dp', 'tensor'), may hold values from -8 to 8
Outputs:
- result: float32 [32, 256, 1024], P('dp', 'tensor')
- token_grad: float32 [32, 256, 1024], P('dp', 'tensor')
- encoder_grad: float32 [32, 128, 1024], P('dp', 'tensor')
- grad_self_proj: float32 [1024, 3, 1024], P('dp', None, 'tensor')
- grad_self_out: float32 [1024, 1024], P('tensor', 'dp')
- grad_cross_query: float32 [1024, 1024], P('dp', 'tensor')
- grad_cross_pairs: float32 [1024, 2, 1024], P('dp', None, 'tensor')
- grad_cross_out: float32 [1024, 1024], P('tensor', 'dp')
- grad_hidden_in: float32 [1024, 8192], P(None, ('dp', 'tensor'))
- grad_hidden_in_bias: float32 [8192], P(('dp', 'tensor'))
- grad_hidden_out: float32 [8192, 1024], P(('dp', 'tensor'))
- grad_hidden_out_bias: float32 [1024], P(('dp', 'tensor'))
- grad_self_gain: float32 [1024], P(('dp', 'tensor'))
- grad_self_shift: float32 [1024], P(('dp', 'tensor'))
- grad_cross_gain: float32 [1024], P(('dp', 'tensor'))
- grad_cross_shift: float32 [1024], P(('dp', 'tensor'))
- grad_hidden_gain: float32 [1024], P(('dp', 'tensor'))
- grad_hidden_shift: float32 [1024], P(('dp', 'tensor'))
The draws below stay inside these ranges and needn't reach their ends.
Inputs may be any that keep to these rules, and one draw needn't show every extreme that they name: `target_doc`: in each row the numbers are 0 on a first run of 64 to 256 positions, the target sequence, and 1 on the padding after it; some row has no padding. `source_doc`: in each row the numbers are 0 on a first run of 32 to 96 positions, the source sentence, and 1 on the padding after it; some row has a run of exactly 32.
All inputs are finite; a program needn't handle non-finite values.
Results may differ from the reference program's by a relative error of at most 0.024.
Values may be sent and summed in bfloat16 or wider, within the bound.
A program may use at most 120 MiB of HBM per device.

```python
import jax
import jax.numpy as jnp
from jax import lax

D = 1024
HEADS = 16
HEAD = 64
FF = 8192
TOK_MB = 256
ENC_MB = 128
ROWS = 32


def split_rows(seed_key, row_count, length, high_end, leading_end):
    low_end = length // 4
    boundary = jax.random.randint(seed_key, (row_count, 1), low_end, high_end + 1)
    leading = jnp.arange(row_count)[:, None] == 0
    boundary = jnp.where(leading, leading_end, boundary)
    return (jnp.arange(length)[None, :] >= boundary).astype(jnp.int32)


def draw_target_doc(key, part):
    return split_rows(jax.random.fold_in(key, 11), ROWS, TOK_MB, TOK_MB, TOK_MB)


def draw_source_doc(key, part):
    return split_rows(jax.random.fold_in(key, 12), ROWS, ENC_MB, ENC_MB - ENC_MB // 4, ENC_MB // 4)


def raised(drawn, own_key, source, target, blocks, factor):
    owner, partner = [(jnp.arange(drawn.shape[position]) // (drawn.shape[position] // blocks)).reshape([-1 if axis == position else 1 for axis in range(drawn.ndim)]) for position in (source, target)]
    chosen = jax.random.permutation(own_key, blocks)[partner]
    strong = (owner == chosen) | (owner == (partner + blocks // 2) % blocks)
    return jnp.where(strong, factor * drawn, drawn)


def levels(own_key, dims, pieces, smallest, high):
    level = 1.0
    for dim, parts in pieces:
        steps = jax.random.uniform(jax.random.fold_in(jax.random.fold_in(own_key, 6), dim), (parts,), jnp.float32, smallest / len(pieces), high / len(pieces))
        level = level * jnp.repeat(jnp.exp(steps), dims[dim] // parts).reshape((-1,) + (1,) * (len(dims) - 1 - dim))
    return level


def noise(stream_key, dims, scale, bound, shards=(), kind=jnp.bfloat16):
    values = scale * jax.random.normal(stream_key, dims, jnp.float32)
    if shards:
        values = values * levels(stream_key, dims, shards, -0.22, 0.18)
    return jnp.clip(values, -bound, bound).astype(kind)


def gaussian_with(own_key, shape, scale, bound, cuts, heavy, dtype=jnp.bfloat16):
    array = scale * jax.random.normal(own_key, shape, jnp.float32)
    if cuts:
        array = array * levels(own_key, shape, cuts, -0.22, 0.18)
    return jnp.clip(raised(array, jax.random.fold_in(own_key, 3), *heavy), -bound, bound).astype(dtype)


def setup_inputs(seed: int = 0) -> dict:
    arg_keys = jax.random.split(jax.random.key(seed), 21)
    return {
        "tokens": noise(arg_keys[0], (ROWS, TOK_MB, D), 1.0, 6.0, ((0, 16), (1, 2))),
        "encoder": noise(arg_keys[1], (ROWS, ENC_MB, D), 1.0, 6.0, ((0, 16), (1, 2))),
        "target_doc": draw_target_doc(jax.random.fold_in(arg_keys[20], 71), 0),
        "source_doc": draw_source_doc(jax.random.fold_in(arg_keys[20], 71), 0),
        "self_proj": noise(arg_keys[4], (D, 3, D), D ** -0.5, 0.1875, ((0, 16), (2, 2))),
        "self_out": noise(arg_keys[5], (D, D), (D // 32) ** -0.5, 1.0, ((0, 2), (1, 16))),
        "cross_query": noise(arg_keys[6], (D, D), D ** -0.5, 0.1875, ((0, 16), (1, 2))),
        "cross_pairs": noise(arg_keys[7], (D, 2, D), D ** -0.5, 0.1875, ((0, 16), (2, 2))),
        "cross_out": noise(arg_keys[8], (D, D), (D // 32) ** -0.5, 1.0, ((0, 2), (1, 16))),
        "hidden_in": noise(arg_keys[9], (D, FF), D ** -0.5, 0.1875, ((1, 32),)),
        "hidden_in_bias": noise(arg_keys[10], (FF,), 0.5, 3.0, ((0, 32),)),
        "hidden_out": noise(arg_keys[11], (FF, D), (FF // 2) ** -0.5, 0.09375, ((0, 32),)),
        "hidden_out_bias": noise(arg_keys[12], (D,), 0.8, 5.0, ((0, 32),), jnp.float32),
        "self_gain": jnp.clip(1.0 + 0.1 * jax.random.normal(arg_keys[13], (D,), jnp.float32), 0.5, 1.5),
        "self_shift": noise(arg_keys[14], (D,), 0.3, 1.75, ((0, 32),), jnp.float32),
        "cross_gain": jnp.clip(1.0 + 0.1 * jax.random.normal(arg_keys[15], (D,), jnp.float32), 0.5, 1.5),
        "cross_shift": noise(arg_keys[16], (D,), 0.3, 1.75, ((0, 32),), jnp.float32),
        "hidden_gain": jnp.clip(1.0 + 0.1 * jax.random.normal(arg_keys[17], (D,), jnp.float32), 0.5, 1.5),
        "hidden_shift": noise(arg_keys[18], (D,), 0.3, 1.75, ((0, 32),), jnp.float32),
        "cotangent": gaussian_with(arg_keys[19], (ROWS, TOK_MB, D), 1.0, 8.0, ((0, 16), (1, 2)), (0, 2, 16, 2.0)),
    }


EPS = 1e-05
NEGATIVE = -1e+30

@jax.custom_vjp
def low(v):
    return lax.optimization_barrier(v.astype(jnp.bfloat16)).astype(jnp.float32)

@jax.custom_vjp
def low_back(v):
    return v

def low_keep(v):
    return (low(v), None)

def low_pass(kept, grad):
    return (grad,)

def back_keep(v):
    return (v, None)

def back_low(kept, grad):
    return (low(grad),)
low.defvjp(low_keep, low_pass)
low_back.defvjp(back_keep, back_low)

def smooth_gate(values):
    return jax.nn.gelu(values, approximate=True)

def layer_norm(hidden, norm_gain, norm_shift):
    center = hidden - lax.optimization_barrier(jnp.mean(hidden, axis=-1, keepdims=True))
    spread = lax.optimization_barrier(jnp.mean(center * center, axis=-1, keepdims=True))
    return center * lax.rsqrt(spread + EPS) * norm_gain + norm_shift

def project(left, right, form):
    return jnp.einsum(form, left, right, precision=lax.Precision.HIGHEST)

def attention(queries, key_rows, values, allowed):
    length = queries.shape[0]
    source = key_rows.shape[0]
    query_heads = queries.reshape(length, HEADS, HEAD)
    key_heads = key_rows.reshape(source, HEADS, HEAD)
    value_heads = values.reshape(source, HEADS, HEAD)
    scores = project(query_heads, key_heads, 'thd,shd->hts') * HEAD ** (-0.5)
    scores = low_back(scores)
    scores = jnp.where(allowed[None], scores, NEGATIVE)
    softmaxed = low(jax.nn.softmax(scores, axis=-1))
    mixture = project(softmaxed, value_heads, 'hts,shd->thd').reshape(length, HEADS * HEAD)
    return low_back(low(mixture))

def decoder_row(inputs, weights):
    tokens_row, encoder_row, target_row, source_row = inputs
    self_proj, self_out, cross_query, cross_pairs, cross_out, hidden_in, hidden_in_bias, hidden_out, hidden_out_bias, self_gain, self_shift, cross_gain, cross_shift, hidden_gain, hidden_shift = weights
    positions = jnp.arange(target_row.shape[0]).astype(jnp.int32)
    self_allowed = (target_row[:, None] == target_row[None, :]) & (positions[None, :] <= positions[:, None])
    cross_allowed = target_row[:, None] == source_row[None, :]
    normed = low(layer_norm(tokens_row, self_gain, self_shift))
    triple = low_back(low(project(normed, self_proj, 'td,dcj->tcj')))
    head_out = attention(triple[:, 0], triple[:, 1], triple[:, 2], self_allowed)
    hidden = tokens_row + low_back(project(head_out, self_out, 'tj,jd->td'))
    normed = low(layer_norm(hidden, cross_gain, cross_shift))
    queries = low_back(low(project(normed, cross_query, 'td,dj->tj')))
    key_value = low_back(low(project(encoder_row, cross_pairs, 'sd,dcj->scj')))
    head_out = attention(queries, key_value[:, 0], key_value[:, 1], cross_allowed)
    hidden = hidden + low_back(project(head_out, cross_out, 'tj,jd->td'))
    normed = low(layer_norm(hidden, hidden_gain, hidden_shift))
    before = low_back(project(normed, hidden_in, 'td,df->tf') + hidden_in_bias)
    active = low(smooth_gate(before))
    return hidden + low_back(project(active, hidden_out, 'tf,fd->td')) + hidden_out_bias

def reference(tokens, encoder, target_doc, source_doc, self_proj, self_out, cross_query, cross_pairs, cross_out, hidden_in, hidden_in_bias, hidden_out, hidden_out_bias, self_gain, self_shift, cross_gain, cross_shift, hidden_gain, hidden_shift, cotangent):
    weights = (self_proj.astype(jnp.float32), self_out.astype(jnp.float32), cross_query.astype(jnp.float32), cross_pairs.astype(jnp.float32), cross_out.astype(jnp.float32), hidden_in.astype(jnp.float32), hidden_in_bias.astype(jnp.float32), hidden_out.astype(jnp.float32), hidden_out_bias.astype(jnp.float32), self_gain.astype(jnp.float32), self_shift.astype(jnp.float32), cross_gain.astype(jnp.float32), cross_shift.astype(jnp.float32), hidden_gain.astype(jnp.float32), hidden_shift.astype(jnp.float32))

    def whole(tokens_float, encoder_float, weight_set):

        def per_row(inputs):
            return decoder_row(inputs, weight_set)
        return lax.map(jax.checkpoint(per_row), (tokens_float, encoder_float, target_doc, source_doc))
    result, pullback = jax.vjp(whole, tokens.astype(jnp.float32), encoder.astype(jnp.float32), weights)
    token_grad, encoder_grad, weight_grads = pullback(cotangent.astype(jnp.float32))
    return (result, token_grad, encoder_grad, weight_grads[0], weight_grads[1], weight_grads[2], weight_grads[3], weight_grads[4], weight_grads[5], weight_grads[6], weight_grads[7], weight_grads[8], weight_grads[9], weight_grads[10], weight_grads[11], weight_grads[12], weight_grads[13], weight_grads[14])
```

```python
import functools

import jax
import jax.numpy as jnp
from jax import lax
from jax.experimental import pallas as pl
from jax.experimental.pallas import tpu as pltpu
from jax.sharding import PartitionSpec as P

HEAD = 64
EPS = 1e-05
NEGATIVE = -1e30
MESH = pl.DeviceIdType.MESH
HBM = pltpu.HBM
VMEM = pltpu.VMEM
PIECES = 8
FF_PIECES = 16


class Place:
    def __init__(self):
        self.dp = lax.axis_index("dp")
        self.y = lax.axis_index("tensor")
        self.c = lax.rem(self.dp, 2)
        self.x = lax.rem(self.dp // 2, 2)
        self.z = self.dp // 4

    def at(self, z=None, x=None, c=None, y=None):
        z = self.z if z is None else z
        x = self.x if x is None else x
        c = self.c if c is None else c
        y = self.y if y is None else y
        return ((z * 2 + x) * 2 + c, y)

    def core(self):
        return self.at(c=1 - self.c)

    def xn(self):
        return self.at(x=1 - self.x)

    def yn(self):
        return self.at(y=1 - self.y)

    def up(self):
        return self.at(z=self.z + 1)

    def down(self):
        return self.at(z=self.z - 1)


def remote(src, dst, send, recv, device):
    return pltpu.make_async_remote_copy(
        src_ref=src, dst_ref=dst, send_sem=send, recv_sem=recv, device_id=device, device_id_type=MESH
    )


def signal(sem, device):
    pl.semaphore_signal(sem, inc=1, device_id=device, device_id_type=MESH)


class LineGather:
    def __init__(self, place, depth, slot, send, recv):
        self.p, self.n, self.slot, self.send, self.recv = place, depth, slot, send, recv

    def _copy_up(self, k):
        b = self.p.z - k
        return remote(self.slot(b), self.slot(b), self.send.at[0, k], self.recv.at[0, k], self.p.up())

    def _copy_down(self, k):
        b = self.p.z + k
        return remote(self.slot(b), self.slot(b), self.send.at[1, k], self.recv.at[1, k], self.p.down())

    def _from_below(self, k):
        b = self.p.z - k
        return remote(self.slot(b), self.slot(b), self.send.at[0, k - 1], self.recv.at[0, k - 1], self.p.up())

    def _from_above(self, k):
        b = self.p.z + k
        return remote(self.slot(b), self.slot(b), self.send.at[1, k - 1], self.recv.at[1, k - 1], self.p.down())

    def arrive(self, k):
        z = self.p.z

        @pl.when(z - k >= 0)
        def _():
            self._from_below(k).wait_recv()

        @pl.when(z + k <= self.n - 1)
        def _():
            self._from_above(k).wait_recv()

    def step(self, k):
        z = self.p.z
        if k > 0:
            self.arrive(k)
        if k < self.n - 1:

            @pl.when((z - k >= 0) & (z < self.n - 1))
            def _():
                self._copy_up(k).start()

            @pl.when((z + k <= self.n - 1) & (z > 0))
            def _():
                self._copy_down(k).start()

    def sent(self):
        z = self.p.z
        for k in range(self.n - 1):

            @pl.when((z - k >= 0) & (z < self.n - 1))
            def _():
                self._copy_up(k).wait_send()

            @pl.when((z + k <= self.n - 1) & (z > 0))
            def _():
                self._copy_down(k).wait_send()


class PlaneGather:
    def __init__(self, place, slot, send, recv):
        self.p, self.slot, self.send, self.recv = place, slot, send, recv
        p = place
        x, y, c = p.x, p.y, p.c
        ox, oy = 1 - x, 1 - y
        self.moves = [
            ((x, c, y, None), p.xn(), 0),
            ((x, c, y, None), p.yn(), 1),
            ((ox, c, y, 0), p.yn(), 2),
            ((x, c, oy, 1), p.xn(), 3),
            ((x, c, y, None), p.core(), 4),
            ((ox, c, y, None), p.core(), 5),
            ((x, c, oy, None), p.core(), 6),
            ((ox, c, oy, None), p.core(), 7),
        ]
        oc = 1 - c
        self.arrivals = [
            (ox, c, y, None),
            (x, c, oy, None),
            (ox, c, oy, 0),
            (ox, c, oy, 1),
            (x, oc, y, None),
            (ox, oc, y, None),
            (x, oc, oy, None),
            (ox, oc, oy, None),
        ]

    def _move(self, i):
        where, device, s = self.moves[i]
        return remote(self.slot(*where), self.slot(*where), self.send.at[s], self.recv.at[s], device)

    def _arrival(self, i):
        view = self.slot(*self.arrivals[i])
        return remote(view, view, self.send.at[i], self.recv.at[i], self.moves[i][1])

    def begin(self):
        self._move(0).start()
        self._move(1).start()
        self._move(4).start()

    def forward(self):
        self._arrival(0).wait_recv()
        self._move(2).start()
        self._move(5).start()
        self._arrival(1).wait_recv()
        self._move(3).start()
        self._move(6).start()

    def finish(self):
        self._arrival(2).wait_recv()
        self._arrival(3).wait_recv()
        self._move(7).start()

    def end(self):
        for i in range(4, 8):
            self._arrival(i).wait_recv()

    def sent(self):
        for i in range(8):
            self._move(i).wait_send()


def all_barrier(place, count):
    sem = pltpu.get_barrier_semaphore()
    me = place.dp * 2 + place.y

    @pl.loop(1, count)
    def _(j):
        other = lax.rem(me + j, count)
        signal(sem, (other // 2, lax.rem(other, 2)))

    pl.semaphore_wait(sem, count - 1)


def gather_kernel(
    depth,
    attn_ref, win_ref, wout_ref, vec_ref, tok_ref, enc_ref, cot_ref,
    G, Win, Wout, vec_all, tok_row, enc_row, g3,
    lsem, zs, zr, fs, fr, ps, pr, vs, vr, ss, sr,
):
    p = Place()
    count = 8 * depth
    local = []

    def keep(src, dst):
        copy = pltpu.make_async_copy(src, dst, lsem.at[len(local)])
        copy.start()
        local.append(copy)

    me = p.dp * 2 + p.y
    keep(attn_ref, G.at[:, p.y, p.z, p.x, p.c])
    keep(win_ref, Win.at[p.z])
    keep(wout_ref, Wout.at[p.z])
    keep(vec_ref, vec_all.at[me])
    keep(tok_ref.at[p.y], tok_row.at[p.y])
    keep(enc_ref.at[p.y], enc_row.at[p.y])
    keep(cot_ref, g3.at[p.x, p.c, :, p.y])
    all_barrier(p, count)
    for copy in local:
        copy.wait()

    lines = []
    for i in range(PIECES):
        lines.append(LineGather(p, depth, lambda b, i=i: G.at[i, p.y, b, p.x, p.c], zs.at[i], zr.at[i]))
    wr = Win.shape[1] // (FF_PIECES // 2)
    orow = Wout.shape[1] // (FF_PIECES // 2)
    ff = []
    for i in range(FF_PIECES):
        if i < FF_PIECES // 2:
            slot = lambda b, i=i: Win.at[b, pl.ds(i * wr, wr)]
        else:
            slot = lambda b, i=i: Wout.at[b, pl.ds((i - FF_PIECES // 2) * orow, orow)]
        ff.append(LineGather(p, depth, slot, fs.at[i], fr.at[i]))

    def plane_slot(i):
        half = G.shape[5] // 2

        def slot(x, c, y, h):
            if h is None:
                return G.at[i, y, :, x, c]
            return G.at[i, y, :, x, c, pl.ds(h * half, half)]

        return slot

    def g3_slot(x, c, y, h):
        if h is None:
            return g3.at[x, c, :, y]
        return g3.at[x, c, h, y]

    planes = [PlaneGather(p, plane_slot(i), ps.at[i], pr.at[i]) for i in range(PIECES)]
    planes.append(PlaneGather(p, g3_slot, ps.at[PIECES], pr.at[PIECES]))
    swaps = [
        remote(tok_ref.at[1 - p.y], tok_row.at[p.y], ss.at[0], sr.at[0], p.yn()),
        remote(enc_ref.at[1 - p.y], enc_row.at[p.y], ss.at[1], sr.at[1], p.yn()),
    ]
    swaps[0].start()

    @pl.loop(1, count)
    def _(j):
        other = lax.rem(me + j, count)
        remote(vec_ref, vec_all.at[me], vs.at[j], vr.at[j], (other // 2, lax.rem(other, 2))).start()

    swaps[1].start()
    total = max(PIECES + 1 + depth + 3, FF_PIECES + depth)
    for it in range(total):
        for k in range(depth):
            if 0 <= it - k < PIECES:
                lines[it - k].step(k)
        for k in range(depth):
            if 0 <= it - k < FF_PIECES:
                ff[it - k].step(k)
        j = it - (depth - 1)
        if 0 <= j < PIECES + 1:
            planes[j].begin()
        if 0 <= j - 1 < PIECES + 1:
            planes[j - 1].forward()
        if 0 <= j - 2 < PIECES + 1:
            planes[j - 2].finish()
        if 0 <= j - 3 < PIECES + 1:
            planes[j - 3].end()
    for line in lines + ff:
        line.sent()
    for plane in planes:
        plane.sent()
    for copy in swaps:
        copy.wait()

    @pl.loop(1, count)
    def _(j):
        other = lax.rem(me + j, count)
        source = lax.rem(me + count - j, count)
        copy = remote(vec_ref, vec_all.at[source], vs.at[j], vr.at[j], (other // 2, lax.rem(other, 2)))
        copy.wait()


def gather_all(attn, win, wout, vec, tok, enc, cot):
    depth = lax.axis_size("dp") // 4
    rows, cols = attn.shape[1:]
    bf = jnp.bfloat16
    count = 8 * depth
    d = tok.shape[2]
    out_shape = [
        jax.ShapeDtypeStruct((PIECES, 2, depth, 2, 2, rows, cols), bf),
        jax.ShapeDtypeStruct((depth,) + win.shape, bf),
        jax.ShapeDtypeStruct((depth,) + wout.shape, bf),
        jax.ShapeDtypeStruct((count,) + vec.shape, jnp.float32),
        jax.ShapeDtypeStruct(tok.shape, bf),
        jax.ShapeDtypeStruct(enc.shape, bf),
        jax.ShapeDtypeStruct((2, 2, 2, 2) + cot.shape[1:], bf),
    ]
    dma = pltpu.SemaphoreType.DMA
    return pl.pallas_call(
        functools.partial(gather_kernel, depth),
        out_shape=out_shape,
        in_specs=[pl.BlockSpec(memory_space=VMEM)] * 7,
        out_specs=[pl.BlockSpec(memory_space=HBM)] * 7,
        scratch_shapes=[
            dma((7,)),
            dma((PIECES, 2, depth - 1)), dma((PIECES, 2, depth - 1)),
            dma((FF_PIECES, 2, depth - 1)), dma((FF_PIECES, 2, depth - 1)),
            dma((PIECES + 1, 8)), dma((PIECES + 1, 8)),
            dma((count,)), dma((count,)),
            dma((2,)), dma((2,)),
        ],
        compiler_params=pltpu.CompilerParams(
            collective_id=1, has_side_effects=True, vmem_limit_bytes=24 << 20
        ),
        name="gather_all",
    )(attn, win, wout, vec, tok, enc, cot)


def far_first(z, s, depth):
    b = 0
    for place in range(depth):
        order = sorted(range(depth), key=lambda k: (-abs(k - place), k))
        b = jnp.where(z == place, order[s], b)
    return b


class LineReduce:
    def __init__(self, place, depth, part, slots, send, recv):
        self.p, self.n, self.part, self.slots, self.send, self.recv = place, depth, part, slots, send, recv

    def _up(self, b):
        slot = b - (self.p.z + 1)
        return remote(self.part(b), self.slots(slot), self.send.at[b], self.recv.at[slot], self.p.up())

    def _down(self, b):
        slot = self.n - b
        return remote(self.part(b), self.slots(slot), self.send.at[b], self.recv.at[slot], self.p.down())

    def below(self, b):
        slot = b - self.p.z
        return remote(self.slots(slot), self.slots(slot), self.send.at[b], self.recv.at[slot], self.p.up())

    def above(self, b):
        slot = self.n - b
        return remote(self.slots(slot), self.slots(slot), self.send.at[b], self.recv.at[slot], self.p.down())

    def first(self, b):
        z = self.p.z

        @pl.when((z == 0) & (b > z))
        def _():
            self._up(b).start()

        @pl.when((z == self.n - 1) & (b < z))
        def _():
            self._down(b).start()

    def middle(self, b, add):
        z = self.p.z

        @pl.when((z > 0) & (b > z))
        def _():
            self.below(b).wait_recv()
            add(self.part(b), self.slots(b - z))
            self._up(b).start()

        @pl.when((z < self.n - 1) & (b < z))
        def _():
            self.above(b).wait_recv()
            add(self.part(b), self.slots(self.n - b))
            self._down(b).start()

    def last(self, take):
        z = self.p.z

        @pl.when(z > 0)
        def _():
            self.below(z).wait_recv()
            take(self.slots(0))

        @pl.when(z < self.n - 1)
        def _():
            self.above(z).wait_recv()
            take(self.slots(self.n - z))

    def sent(self):
        z = self.p.z

        @pl.loop(0, self.n)
        def _(b):
            @pl.when(b > z)
            def _():
                self._up(b).wait_send()

            @pl.when(b < z)
            def _():
                self._down(b).wait_send()


def add_low(part, other):
    part[...] = (part[...].astype(jnp.float32) + other[...].astype(jnp.float32)).astype(part.dtype)


def gelu_pair(x):
    a, b = 0.7978845608028654, 0.044715
    square = x * x
    t = jnp.tanh(a * x * (1.0 + b * square))
    half = 0.5 * (1.0 + t)
    return x * half, half + 0.5 * x * (1.0 - t * t) * (a * (1.0 + 3.0 * b * square))


NN = (((1,), (0,)), ((), ()))
NT = (((1,), (1,)), ((), ()))
TN = (((0,), (0,)), ((), ()))


def mm(left, right, form=NN):
    return lax.dot_general(left, right, form, preferred_element_type=jnp.float32)


def neighbour_barrier(p, depth):
    sem = pltpu.get_barrier_semaphore()
    for dx in range(2):
        for dc in range(2):
            for dy in range(2):
                if dx + dc + dy:
                    signal(sem, p.at(x=lax.rem(p.x + dx, 2), c=lax.rem(p.c + dc, 2), y=lax.rem(p.y + dy, 2)))

    @pl.loop(1, depth)
    def _(k):
        signal(sem, p.at(z=lax.rem(p.z + k, depth)))

    pl.semaphore_wait(sem, 7 + depth - 1)


def hidden_kernel(
    depth,
    hn_ref, bias_ref, Win, Wout, g3,
    y_out, d_out, gin_out, gout_out, gbias_out,
    HN, G3, WI, WO, Y, D, S, R, acc_in, acc_out, BS, BR, CS, CR, PS, PR,
    lsem, ps, pr, zs, zr, bs, br, cs, cr, xs, xr,
):
    p = Place()
    rows = HN.shape[3]
    width = HN.shape[4]
    loads = [
        pltpu.make_async_copy(Win, WI, lsem.at[0]),
        pltpu.make_async_copy(Wout, WO, lsem.at[1]),
        pltpu.make_async_copy(g3, G3, lsem.at[2]),
    ]
    for load in loads:
        load.start()
    neighbour_barrier(p, depth)
    HN[p.x, p.c, p.y] = hn_ref[...]
    half = rows // 2

    def hn_slot(x, c, y, h):
        if h is None:
            return HN.at[x, c, y]
        return HN.at[x, c, y, pl.ds(h * half, half)]

    gather = PlaneGather(p, hn_slot, ps, pr)
    gather.begin()
    Y[...] = jnp.zeros_like(Y)
    D[...] = jnp.zeros_like(D)
    BS[...] = jnp.zeros_like(BS)
    for load in loads:
        load.wait()
    gather.forward()
    gather.finish()
    gather.end()

    def where(i):
        dc = 1 - i // 4
        dx = 1 - lax.rem(i, 4) // 2
        dy = 1 - lax.rem(i, 2)
        return lax.rem(p.x + dx, 2), lax.rem(p.c + dc, 2), lax.rem(p.y + dy, 2)

    def one_row(b, i, first):
        at = where(i)
        h = HN[at]
        g = G3[at].reshape(rows, width)
        win, wout = WI[b], WO[b]
        before = mm(h, win) + bias_ref[b]
        active, slope = gelu_pair(before)
        active = active.astype(jnp.bfloat16)
        slope = (mm(g, wout, NT) * slope).astype(jnp.bfloat16)
        Y[at] += mm(active, wout)
        D[at] += mm(slope, win, NT)
        acc_out[...] += mm(active, g, TN)
        acc_in[...] += mm(slope, h, TN)
        BS[b, 0:1] += jnp.sum(slope.astype(jnp.float32), axis=0, keepdims=True)

    reduce = LineReduce(p, depth, lambda b: S.at[b], lambda i: R.at[i], zs, zr)

    def open_block():
        acc_in[...] = jnp.zeros_like(acc_in)
        acc_out[...] = jnp.zeros_like(acc_out)

    def close_block(b):
        S[b, 0] = acc_in[...].astype(jnp.bfloat16)
        S[b, 1] = acc_out[...].astype(jnp.bfloat16)

    for s in range(depth - 1):
        b = far_first(p.z, s, depth)
        open_block()

        @pl.loop(0, 8)
        def _(i):
            one_row(b, i, False)

        close_block(b)
        reduce.first(b)
        remote(BS.at[b], BR.at[p.z], bs.at[b], br.at[p.z], p.at(z=b)).start()

    b = p.z
    open_block()

    def to_core(j):
        return remote(CS.at[j], CR.at[j], cs.at[j], cr.at[j], p.core())

    def to_chip(j):
        dx, dy = 1 - j // 2, 1 - lax.rem(j, 2)
        return remote(
            PS.at[j], PR.at[j], xs.at[j], xr.at[j], p.at(x=lax.rem(p.x + dx, 2), y=lax.rem(p.y + dy, 2))
        )

    @pl.loop(0, 4)
    def _(i):
        one_row(b, i, False)
        at = where(i)
        CS[i, 0] = D[at].astype(jnp.bfloat16)
        CS[i, 1] = Y[at].astype(jnp.bfloat16)
        to_core(i).start()

    @pl.loop(4, 8)
    def _(i):
        one_row(b, i, False)
        at = where(i)
        j = i - 4
        to_core(j).wait_recv()
        dsum = D[at] + CR[j, 0].astype(jnp.float32)
        ysum = Y[at] + CR[j, 1].astype(jnp.float32)

        @pl.when(i < 7)
        def _():
            PS[j, 0] = dsum.astype(jnp.bfloat16)
            PS[j, 1] = ysum.astype(jnp.bfloat16)
            to_chip(j).start()

        @pl.when(i == 7)
        def _():
            d_out[...] = dsum
            y_out[...] = ysum

    gin_out[...] = acc_in[...]
    gout_out[...] = acc_out[...]

    @pl.loop(0, 3)
    def _(j):
        to_chip(j).wait_recv()
        d_out[...] += PR[j, 0].astype(jnp.float32)
        y_out[...] += PR[j, 1].astype(jnp.float32)

    for s in range(depth - 1):
        reduce.middle(far_first(p.z, s, depth), add_low)

    def take(slot):
        gin_out[...] += slot[0].astype(jnp.float32)
        gout_out[...] += slot[1].astype(jnp.float32)

    reduce.last(take)
    gbias_out[...] = BS[p.z]

    @pl.loop(1, depth)
    def _(k):
        source = lax.rem(p.z + k, depth)
        remote(BS.at[source], BR.at[source], bs.at[source], br.at[source], p.at(z=source)).wait()
        gbias_out[...] += BR[source]

    reduce.sent()
    gather.sent()

    @pl.loop(0, 4)
    def _(j):
        to_core(j).wait_send()

    @pl.loop(0, 3)
    def _(j):
        to_chip(j).wait_send()


def hidden_block(hn, bias, win, wout, g3):
    depth, width, units = win.shape
    rows = hn.shape[0]
    bf, f32 = jnp.bfloat16, jnp.float32
    dma = pltpu.SemaphoreType.DMA
    vm = pl.BlockSpec(memory_space=VMEM)
    hb = pl.BlockSpec(memory_space=HBM)
    return pl.pallas_call(
        functools.partial(hidden_kernel, depth),
        out_shape=[
            jax.ShapeDtypeStruct((rows, width), f32),
            jax.ShapeDtypeStruct((rows, width), f32),
            jax.ShapeDtypeStruct((units, width), f32),
            jax.ShapeDtypeStruct((units, width), f32),
            jax.ShapeDtypeStruct((8, units), f32),
        ],
        in_specs=[vm, vm, hb, hb, hb],
        out_specs=[vm] * 5,
        scratch_shapes=[
            pltpu.VMEM((2, 2, 2, rows, width), bf),
            pltpu.VMEM(g3.shape, bf),
            pltpu.VMEM(win.shape, bf),
            pltpu.VMEM(wout.shape, bf),
            pltpu.VMEM((2, 2, 2, rows, width), f32),
            pltpu.VMEM((2, 2, 2, rows, width), f32),
            pltpu.VMEM((depth, 2, units, width), bf),
            pltpu.VMEM((depth + 1, 2, units, width), bf),
            pltpu.VMEM((units, width), f32),
            pltpu.VMEM((units, width), f32),
            pltpu.VMEM((depth, 8, units), f32),
            pltpu.VMEM((depth, 8, units), f32),
            pltpu.VMEM((4, 2, rows, width), bf),
            pltpu.VMEM((4, 2, rows, width), bf),
            pltpu.VMEM((3, 2, rows, width), bf),
            pltpu.VMEM((3, 2, rows, width), bf),
            dma((3,)),
            dma((8,)), dma((8,)),
            dma((depth,)), dma((depth + 1,)),
            dma((depth,)), dma((depth,)),
            dma((4,)), dma((4,)),
            dma((3,)), dma((3,)),
        ],
        compiler_params=pltpu.CompilerParams(
            collective_id=2, has_side_effects=True, vmem_limit_bytes=62 << 20
        ),
        name="hidden_block",
    )(hn, bias, win, wout, g3)


def reduce_kernel(
    depth,
    part, vec_ref, res_ref, tg_ref, eg_ref,
    gw_out, vec_out, res_out, tg_out, eg_out,
    MY, CR, PD, PR, R, VR, XS, XR, ES, ER,
    lsem, cs, cr, ds, dr, ps, pr, zs, zr, vs, vr, ss, sr,
):
    p = Place()
    count = 8 * depth
    me = p.dp * 2 + p.y
    ox, oy, oc = 1 - p.x, 1 - p.y, 1 - p.c
    half = MY.shape[4] // 2
    all_barrier(p, count)

    @pl.loop(1, count)
    def _(j):
        other = lax.rem(me + j, count)
        remote(vec_ref.at[other], VR.at[j], vs.at[j], vr.at[j], (other // 2, lax.rem(other, 2))).start()

    rows = res_out.shape[1]
    short = eg_out.shape[1]
    XS[0] = res_ref[pl.ds(oy * rows, rows)].astype(jnp.bfloat16)
    XS[1] = tg_ref[pl.ds(oy * rows, rows)].astype(jnp.bfloat16)
    ES[...] = eg_ref[pl.ds(oy * short, short)].astype(jnp.bfloat16)
    swaps = [
        remote(XS, XR, ss.at[0], sr.at[0], p.yn()),
        remote(ES, ER, ss.at[1], sr.at[1], p.yn()),
    ]

    def load(i):
        return pltpu.make_async_copy(part.at[i, :, :, :, p.c], MY.at[i], lsem.at[i])

    def core(i):
        return remote(part.at[i, :, :, :, oc], CR.at[i], cs.at[i], cr.at[i], p.core())

    def diagonal(i, h):
        return remote(
            MY.at[i, oy, :, ox, pl.ds(h * half, half)], PD.at[i, h], ds.at[i, h], dr.at[i, h],
            p.yn() if h else p.xn(),
        )

    def column(i, h):
        view = MY.at[i, oy, :, p.x] if h else MY.at[i, p.y, :, ox]
        return remote(view, PR.at[i, h], ps.at[i, h], pr.at[i, h], p.yn() if h else p.xn())

    lines = [
        LineReduce(
            p, depth, lambda b, i=i: MY.at[i, p.y, b, p.x], lambda k, i=i: R.at[i, k], zs.at[i], zr.at[i]
        )
        for i in range(PIECES)
    ]

    def stage(i, s):
        if s == 0:
            load(i).start()
            core(i).start()
        elif s == 1:
            load(i).wait()
            core(i).wait_recv()
            add_low(MY.at[i], CR.at[i])
            diagonal(i, 0).start()
            diagonal(i, 1).start()
        elif s == 2:
            diagonal(i, 0).wait_recv()
            add_low(MY.at[i, oy, :, p.x, pl.ds(0, half)], PD.at[i, 0])
            column(i, 1).start()
            diagonal(i, 1).wait_recv()
            add_low(MY.at[i, p.y, :, ox, pl.ds(half, half)], PD.at[i, 1])
            column(i, 0).start()
        elif s == 3:
            column(i, 0).wait_recv()
            column(i, 1).wait_recv()
            view = MY.at[i, p.y, :, p.x]
            view[...] = (
                view[...].astype(jnp.float32)
                + PR[i, 0].astype(jnp.float32)
                + PR[i, 1].astype(jnp.float32)
            ).astype(jnp.bfloat16)
            for k in range(depth - 1):
                lines[i].first(far_first(p.z, k, depth))
        elif s < 3 + depth:
            lines[i].middle(far_first(p.z, s - 4, depth), add_low)
        elif s == 3 + depth:
            gw_out[i] = MY[i, p.y, p.z, p.x].astype(jnp.float32)

            def take(slot):
                gw_out[i] += slot[...].astype(jnp.float32)

            lines[i].last(take)

    for it in range(PIECES + 3 + depth):
        for s in range(4 + depth):
            if 0 <= it - s < PIECES:
                stage(it - s, s)
    swaps[0].start()
    swaps[1].start()
    vec_out[...] = vec_ref[me]

    @pl.loop(1, count)
    def _(j):
        other = lax.rem(me + j, count)
        remote(vec_ref.at[other], VR.at[j], vs.at[j], vr.at[j], (other // 2, lax.rem(other, 2))).wait()
        vec_out[...] += VR[j]

    res_out[p.y] = res_ref[pl.ds(p.y * rows, rows)]
    tg_out[p.y] = tg_ref[pl.ds(p.y * rows, rows)]
    eg_out[p.y] = eg_ref[pl.ds(p.y * short, short)]
    for copy in swaps:
        copy.wait()
    res_out[oy] = XR[0].astype(jnp.float32)
    tg_out[oy] = XR[1].astype(jnp.float32)
    eg_out[oy] = ER[...].astype(jnp.float32)
    for i in range(PIECES):
        core(i).wait_send()
        for h in range(2):
            diagonal(i, h).wait_send()
            column(i, h).wait_send()
        lines[i].sent()


def reduce_all(part, vec, res, tg, eg):
    depth = part.shape[2]
    count = 8 * depth
    rows, cols = part.shape[5:]
    length, width = res.shape
    short = eg.shape[0]
    bf, f32 = jnp.bfloat16, jnp.float32
    dma = pltpu.SemaphoreType.DMA
    vm = pl.BlockSpec(memory_space=VMEM)
    hb = pl.BlockSpec(memory_space=HBM)
    return pl.pallas_call(
        functools.partial(reduce_kernel, depth),
        out_shape=[
            jax.ShapeDtypeStruct((PIECES, rows, cols), f32),
            jax.ShapeDtypeStruct(vec.shape[1:], f32),
            jax.ShapeDtypeStruct((2, length // 2, width), f32),
            jax.ShapeDtypeStruct((2, length // 2, width), f32),
            jax.ShapeDtypeStruct((2, short // 2, width), f32),
        ],
        in_specs=[hb, vm, vm, vm, vm],
        out_specs=[vm] * 5,
        scratch_shapes=[
            pltpu.VMEM((PIECES, 2, depth, 2, rows, cols), bf),
            pltpu.VMEM((PIECES, 2, depth, 2, rows, cols), bf),
            pltpu.VMEM((PIECES, 2, depth, rows // 2, cols), bf),
            pltpu.VMEM((PIECES, 2, depth, rows, cols), bf),
            pltpu.VMEM((PIECES, depth + 1, rows, cols), bf),
            pltpu.VMEM(vec.shape, f32),
            pltpu.VMEM((2, length // 2, width), bf),
            pltpu.VMEM((2, length // 2, width), bf),
            pltpu.VMEM((short // 2, width), bf),
            pltpu.VMEM((short // 2, width), bf),
            dma((PIECES,)),
            dma((PIECES,)), dma((PIECES,)),
            dma((PIECES, 2)), dma((PIECES, 2)),
            dma((PIECES, 2)), dma((PIECES, 2)),
            dma((PIECES, depth)), dma((PIECES, depth + 1)),
            dma((count,)), dma((count,)),
            dma((2,)), dma((2,)),
        ],
        compiler_params=pltpu.CompilerParams(
            collective_id=3, has_side_effects=True, vmem_limit_bytes=56 << 20
        ),
        name="reduce_all",
    )(part, vec, res, tg, eg)


def norm_forward(hidden, gain, shift):
    center = hidden - jnp.mean(hidden, axis=-1, keepdims=True)
    inverse = lax.rsqrt(jnp.mean(center * center, axis=-1, keepdims=True) + EPS)
    normal = center * inverse
    return normal * gain + shift, normal, inverse


def norm_backward(upward, normal, inverse, gain):
    scaled = upward * gain
    centred = (
        scaled
        - jnp.mean(scaled, axis=-1, keepdims=True)
        - normal * jnp.mean(scaled * normal, axis=-1, keepdims=True)
    )
    return centred * inverse, jnp.sum(upward * normal, axis=0), jnp.sum(upward, axis=0)


def split_heads(a):
    return a.reshape(a.shape[0], -1, HEAD)


def ein(form, *operands):
    return jnp.einsum(form, *operands, preferred_element_type=jnp.float32)


def attend(q, k, v, allowed):
    scores = ein("qhd,khd->hqk", split_heads(q), split_heads(k)) * HEAD**-0.5
    scores = jnp.where(allowed[None], scores, NEGATIVE)
    highest = jnp.max(scores, axis=-1, keepdims=True)
    exponent = jnp.exp(scores - highest)
    totals = jnp.sum(exponent, axis=-1, keepdims=True)
    probs = exponent / totals
    mixture = ein("hqk,khd->qhd", probs.astype(jnp.bfloat16), split_heads(v))
    return mixture.reshape(q.shape).astype(jnp.bfloat16), highest + jnp.log(totals)


def attend_backward(q, k, v, allowed, lse, slope):
    scores = ein("qhd,khd->hqk", split_heads(q), split_heads(k)) * HEAD**-0.5
    scores = jnp.where(allowed[None], scores, NEGATIVE)
    probs = jnp.exp(scores - lse)
    up = split_heads(slope)
    dprobs = ein("qhd,khd->hqk", up, split_heads(v))
    dscores = (probs * (dprobs - jnp.sum(probs * dprobs, axis=-1, keepdims=True))).astype(jnp.bfloat16)
    dq = (ein("hqk,khd->qhd", dscores, split_heads(k)) * HEAD**-0.5).astype(jnp.bfloat16)
    dk = (ein("hqk,qhd->khd", dscores, split_heads(q)) * HEAD**-0.5).astype(jnp.bfloat16)
    dv = ein("hqk,qhd->khd", probs.astype(jnp.bfloat16), up).astype(jnp.bfloat16)
    return dq.reshape(q.shape), dk.reshape(k.shape), dv.reshape(v.shape)


def fast_local(
    tokens, encoder, target_doc, source_doc, self_proj, self_out, cross_query, cross_pairs, cross_out,
    hidden_in, hidden_in_bias, hidden_out, hidden_out_bias, self_gain, self_shift, cross_gain, cross_shift,
    hidden_gain, hidden_shift, cotangent,
):
    depth = lax.axis_size("dp") // 4
    count = 8 * depth
    place = Place()
    me = place.dp * 2 + place.y
    bf, f32 = jnp.bfloat16, jnp.float32
    attn = jnp.stack([
        self_proj[:, 0], self_proj[:, 1], self_proj[:, 2], self_out.T,
        cross_pairs[:, 0], cross_pairs[:, 1], cross_query, cross_out.T,
    ])
    vectors = jnp.stack(
        [self_gain, self_shift, cross_gain, cross_shift, hidden_gain, hidden_shift, hidden_out_bias]
    )
    span = vectors.shape[1]
    group = 128 // span
    lane = lax.broadcasted_iota(jnp.int32, (1, 128), 1)
    mine = lane // span == lax.rem(me, group)
    vec = jnp.concatenate([
        jnp.where(mine, jnp.tile(vectors, (1, group)), 0.0),
        jnp.zeros((1, 128), f32),
        hidden_in_bias.astype(f32).reshape(-1, 128),
    ])
    vec = jnp.pad(vec, ((0, -vec.shape[0] % 8), (0, 0)))
    G, win, wout, vec_all, tok_row, enc_row, g3 = gather_all(
        attn, hidden_in, hidden_out, vec, tokens, encoder, cotangent
    )
    full = vec_all[:, :7].reshape(count // group, group, 7, 128).sum(1).transpose(1, 0, 2).reshape(7, -1)
    sg, ss, cg, cs, hg, hs, ob = [full[i] for i in range(7)]
    units = hidden_in.shape[1]
    bias = vec_all[:, 8 : 8 + units // 128].reshape(depth, 8, 1, units)
    bias = lax.dynamic_index_in_dim(bias, (place.x * 2 + place.c) * 2 + place.y, 1, keepdims=False)
    width = tokens.shape[2]
    W = G.reshape(PIECES, 2, width, -1)
    length = tokens.shape[1] * 2
    short = encoder.shape[1] * 2
    tok = tok_row.reshape(length, width).astype(f32)
    enc = enc_row.reshape(short, width)
    up = lax.dynamic_index_in_dim(
        g3.reshape(2, 2, 2, length, width)[place.x, place.c], place.y, 0, keepdims=False
    )
    target = lax.dynamic_index_in_dim(target_doc, place.y, 0, keepdims=False)
    source = lax.dynamic_index_in_dim(source_doc, place.y, 0, keepdims=False)
    positions = jnp.arange(length)
    self_allowed = (target[:, None] == target[None, :]) & (positions[None, :] <= positions[:, None])
    cross_allowed = target[:, None] == source[None, :]

    def project(a, i):
        return ein("td,ydj->tyj", a, W[i]).reshape(a.shape[0], width)

    def project_back(a, i):
        return ein("tyj,ydj->td", a.reshape(a.shape[0], 2, -1), W[i])

    def weight_grad(a, b):
        return ein("td,tyj->ydj", a, b.reshape(b.shape[0], 2, -1)).astype(bf)

    n1, normal1, inverse1 = norm_forward(tok, sg, ss)
    n1 = n1.astype(bf)
    q, k, v = [project(n1, i).astype(bf) for i in range(3)]
    heads1, lse1 = attend(q, k, v, self_allowed)
    middle = tok + project_back(heads1, 3)
    n2, normal2, inverse2 = norm_forward(middle, cg, cs)
    n2 = n2.astype(bf)
    cq = project(n2, 6).astype(bf)
    ck, cv = project(enc, 4).astype(bf), project(enc, 5).astype(bf)
    heads2, lse2 = attend(cq, ck, cv, cross_allowed)
    latter = middle + project_back(heads2, 7)
    n3, normal3, inverse3 = norm_forward(latter, hg, hs)
    y, slope, gin, gout, gbias = hidden_block(n3.astype(bf), bias, win, wout, g3)
    result = latter + y + ob
    up = up.astype(f32)
    g_ob = jnp.sum(up, axis=0)
    slope, g_hg, g_hs = norm_backward(slope, normal3, inverse3, hg)
    up = up + slope
    low = up.astype(bf)
    slope = project(low, 7).astype(bf)
    dcq, dck, dcv = attend_backward(cq, ck, cv, cross_allowed, lse2, slope)
    part_co = weight_grad(low, heads2)
    part_cq = weight_grad(n2, dcq)
    part_ck = weight_grad(enc, dck)
    part_cv = weight_grad(enc, dcv)
    enc_grad = project_back(dck, 4) + project_back(dcv, 5)
    slope, g_cg, g_cs = norm_backward(project_back(dcq, 6), normal2, inverse2, cg)
    up = up + slope
    low = up.astype(bf)
    slope = project(low, 3).astype(bf)
    dq, dk, dv = attend_backward(q, k, v, self_allowed, lse1, slope)
    part_so = weight_grad(low, heads1)
    parts = [weight_grad(n1, d) for d in (dq, dk, dv)]
    slope = project_back(dq, 0) + project_back(dk, 1) + project_back(dv, 2)
    slope, g_sg, g_ss = norm_backward(slope, normal1, inverse1, sg)
    tok_grad = up + slope
    part = jnp.stack([part_co, part_cq, part_ck, part_cv, part_so] + parts).reshape(G.shape)
    vg = jnp.stack([g_sg, g_ss, g_cg, g_cs, g_hg, g_hs, g_ob]).reshape(7, count, span).transpose(1, 0, 2)
    vg = jnp.pad(vg, ((0, 0), (0, 1), (0, 128 - span)))
    gw, vout, res, tg, eg = reduce_all(part, vg, result, tok_grad, enc_grad)
    return (
        res, tg, eg,
        jnp.stack([gw[5], gw[6], gw[7]], axis=1),
        gw[4].T, gw[1], jnp.stack([gw[2], gw[3]], axis=1), gw[0].T,
        gin.T, gbias[0], gout,
        vout[6, :span], vout[0, :span], vout[1, :span], vout[2, :span], vout[3, :span], vout[4, :span], vout[5, :span],
    )


BLOCK_ROWS = 512


def smooth_gate(values):
    return jax.nn.gelu(values, approximate=True)


def plain_norm_forward(hidden, norm_gain, norm_shift):
    center = hidden - jnp.mean(hidden, axis=-1, keepdims=True)
    inverse = lax.rsqrt(jnp.mean(center * center, axis=-1, keepdims=True) + EPS)
    normal = center * inverse
    return (normal * norm_gain + norm_shift, normal, inverse)


def plain_norm_backward(upward, normal, inverse, norm_gain):
    scaled = upward * norm_gain
    centred = (
        scaled
        - jnp.mean(scaled, axis=-1, keepdims=True)
        - normal * jnp.mean(scaled * normal, axis=-1, keepdims=True)
    )
    return (centred * inverse, jnp.sum(upward * normal, axis=0), jnp.sum(upward, axis=0))


def split_blocks(array):
    row_count = array.shape[0]
    block_size = min(BLOCK_ROWS, row_count)
    return array.reshape((row_count // block_size, block_size) + array.shape[1:])


def block_scores(query_block, key_rows, allow_block):
    query_heads = query_block.reshape(query_block.shape[0], -1, HEAD)
    key_heads = key_rows.reshape(key_rows.shape[0], -1, HEAD)
    scores = jnp.einsum(
        "qhd,khd->hqk", query_heads, key_heads, preferred_element_type=jnp.float32
    ) * HEAD ** (-0.5)
    return jnp.where(allow_block[None], scores, NEGATIVE)


def plain_attend(queries, key_rows, values, allowed):
    columns = queries.shape[1]
    value_heads = values.reshape(values.shape[0], -1, HEAD)

    def one_block(pieces):
        query_block, allow_block = pieces
        scores = block_scores(query_block, key_rows, allow_block)
        highest = jnp.max(scores, axis=-1, keepdims=True)
        exponent = jnp.exp(scores - highest)
        totals = jnp.sum(exponent, axis=-1, keepdims=True)
        softmaxed = (exponent / totals).astype(jnp.bfloat16)
        mixture = jnp.einsum(
            "hqk,khd->qhd", softmaxed, value_heads, preferred_element_type=jnp.float32
        )
        return (
            mixture.reshape(query_block.shape[0], columns).astype(jnp.bfloat16),
            (highest + jnp.log(totals))[..., 0],
        )

    mixture, logsum = lax.map(one_block, (split_blocks(queries), split_blocks(allowed)))
    return (mixture.reshape(queries.shape), logsum)


def plain_attend_backward(queries, key_rows, values, allowed, logsum, slope_heads):
    scaling = HEAD ** (-0.5)
    key_heads = key_rows.reshape(key_rows.shape[0], -1, HEAD)
    value_heads = values.reshape(values.shape[0], -1, HEAD)

    def one_block(running, pieces):
        key_total, value_total = running
        query_block, allow_block, logsum_block, slope_block = pieces
        scores = block_scores(query_block, key_rows, allow_block)
        softmaxed = jnp.exp(scores - logsum_block[..., None])
        query_heads = query_block.reshape(query_block.shape[0], -1, HEAD)
        slope_out = slope_block.reshape(slope_block.shape[0], -1, HEAD)
        slope_probs = jnp.einsum(
            "qhd,khd->hqk", slope_out, value_heads, preferred_element_type=jnp.float32
        )
        centred = jnp.sum(softmaxed * slope_probs, axis=-1, keepdims=True)
        slope_scores = (softmaxed * (slope_probs - centred)).astype(jnp.bfloat16)
        slope_query = (
            jnp.einsum("hqk,khd->qhd", slope_scores, key_heads, preferred_element_type=jnp.float32)
            * scaling
        )
        key_total = (
            key_total
            + jnp.einsum(
                "hqk,qhd->khd", slope_scores, query_heads, preferred_element_type=jnp.float32
            )
            * scaling
        )
        value_total = value_total + jnp.einsum(
            "hqk,qhd->khd",
            softmaxed.astype(jnp.bfloat16),
            slope_out,
            preferred_element_type=jnp.float32,
        )
        return (
            (key_total, value_total),
            slope_query.reshape(query_block.shape[0], -1).astype(jnp.bfloat16),
        )

    empty_heads = jnp.zeros(key_heads.shape, jnp.float32)
    (key_total, value_total), slope_query = lax.scan(
        one_block,
        (empty_heads, empty_heads),
        (split_blocks(queries), split_blocks(allowed), logsum, split_blocks(slope_heads)),
    )
    return (
        slope_query.reshape(queries.shape),
        key_total.reshape(key_rows.shape).astype(jnp.bfloat16),
        value_total.reshape(values.shape).astype(jnp.bfloat16),
    )


def gather_rows(local_rows):
    return lax.all_gather(local_rows, "tensor", axis=0, tiled=True)


def sum_rows(partial_sum):
    return lax.psum_scatter(
        partial_sum.astype(jnp.bfloat16), "tensor", scatter_dimension=0, tiled=True
    ).astype(jnp.float32)


def gather_slopes(local_slopes):
    return lax.all_gather(local_slopes, "tensor", axis=0, tiled=True)


def sum_slopes(partial_sum):
    return lax.psum_scatter(
        partial_sum.astype(jnp.bfloat16), "tensor", scatter_dimension=0, tiled=True
    ).astype(jnp.float32)


def reduce_weights(weight_terms):
    return (
        lax.psum_scatter(weight_terms[0], "dp", scatter_dimension=0, tiled=True),
        lax.psum_scatter(weight_terms[1], "dp", scatter_dimension=1, tiled=True),
        lax.psum_scatter(weight_terms[2], "dp", scatter_dimension=0, tiled=True),
        lax.psum_scatter(weight_terms[3], "dp", scatter_dimension=0, tiled=True),
        lax.psum_scatter(weight_terms[4], "dp", scatter_dimension=1, tiled=True),
        lax.psum_scatter(weight_terms[5], "dp", scatter_dimension=1, tiled=True),
        lax.psum_scatter(weight_terms[6], "dp", scatter_dimension=0, tiled=True),
        lax.psum_scatter(weight_terms[7], "dp", scatter_dimension=0, tiled=True),
    )


def plain_local(
    tokens,
    encoder,
    target_doc,
    source_doc,
    self_proj,
    self_out,
    cross_query,
    cross_pairs,
    cross_out,
    hidden_in,
    hidden_in_bias,
    hidden_out,
    hidden_out_bias,
    self_gain,
    self_shift,
    cross_gain,
    cross_shift,
    hidden_gain,
    hidden_shift,
    cotangent,
):
    (
        full_self_gain,
        full_self_shift,
        full_cross_gain,
        full_cross_shift,
        full_hidden_gain,
        full_hidden_shift,
        full_out_bias,
    ) = (
        lax.all_gather(self_gain, ("dp", "tensor"), axis=0, tiled=True),
        lax.all_gather(self_shift, ("dp", "tensor"), axis=0, tiled=True),
        lax.all_gather(cross_gain, ("dp", "tensor"), axis=0, tiled=True),
        lax.all_gather(cross_shift, ("dp", "tensor"), axis=0, tiled=True),
        lax.all_gather(hidden_gain, ("dp", "tensor"), axis=0, tiled=True),
        lax.all_gather(hidden_shift, ("dp", "tensor"), axis=0, tiled=True),
        lax.all_gather(hidden_out_bias, ("dp", "tensor"), axis=0, tiled=True),
    )
    micro_count = tokens.shape[0]
    row_count = tokens.shape[1] * lax.axis_size("tensor")
    positions = jnp.arange(row_count)
    results = []
    token_grads = []
    encoder_grads = []
    vector_total = None
    weight_total = None
    for step_index in range(micro_count):
        forward_weights = (
            lax.all_gather(self_proj, "dp", axis=0, tiled=True),
            lax.all_gather(self_out, "dp", axis=1, tiled=True),
            lax.all_gather(cross_query, "dp", axis=0, tiled=True),
            lax.all_gather(cross_pairs, "dp", axis=0, tiled=True),
            lax.all_gather(cross_out, "dp", axis=1, tiled=True),
            lax.all_gather(hidden_in, "dp", axis=1, tiled=True),
            lax.all_gather(hidden_in_bias, "dp", axis=0, tiled=True),
            lax.all_gather(hidden_out, "dp", axis=0, tiled=True),
        )
        (
            full_proj,
            full_self_out,
            full_query,
            full_pairs,
            full_cross_out,
            full_in,
            full_in_bias,
            full_out,
        ) = forward_weights
        target_row = target_doc[step_index]
        source_row = source_doc[step_index]
        self_allowed = (target_row[:, None] == target_row[None, :]) & (
            positions[None, :] <= positions[:, None]
        )
        cross_allowed = target_row[:, None] == source_row[None, :]
        start_hidden = tokens[step_index].astype(jnp.float32)
        normed_first, normal_first, inverse_first = plain_norm_forward(
            start_hidden, full_self_gain, full_self_shift
        )
        self_rows = gather_rows(normed_first.astype(jnp.bfloat16))
        triple = jnp.einsum(
            "td,dcj->tcj", self_rows, full_proj, preferred_element_type=jnp.float32
        ).astype(jnp.bfloat16)
        self_heads, self_logsum = plain_attend(triple[:, 0], triple[:, 1], triple[:, 2], self_allowed)
        middle = start_hidden + sum_rows(
            jnp.dot(self_heads, full_self_out, preferred_element_type=jnp.float32)
        )
        normed_second, normal_second, inverse_second = plain_norm_forward(
            middle, full_cross_gain, full_cross_shift
        )
        cross_rows, source_rows = (
            lax.all_gather(normed_second.astype(jnp.bfloat16), "tensor", axis=0, tiled=True),
            lax.all_gather(encoder[step_index], "tensor", axis=0, tiled=True),
        )
        cross_queries = jnp.dot(cross_rows, full_query, preferred_element_type=jnp.float32).astype(
            jnp.bfloat16
        )
        key_value = jnp.einsum(
            "sd,dcj->scj", source_rows, full_pairs, preferred_element_type=jnp.float32
        ).astype(jnp.bfloat16)
        cross_heads, cross_logsum = plain_attend(
            cross_queries, key_value[:, 0], key_value[:, 1], cross_allowed
        )
        latter = middle + sum_rows(
            jnp.dot(cross_heads, full_cross_out, preferred_element_type=jnp.float32)
        )
        normed_third, normal_third, inverse_third = plain_norm_forward(
            latter, full_hidden_gain, full_hidden_shift
        )
        hidden_rows = gather_rows(normed_third.astype(jnp.bfloat16))
        before = jnp.dot(
            hidden_rows, full_in, preferred_element_type=jnp.float32
        ) + full_in_bias.astype(jnp.float32)
        gated, gate_pullback = jax.vjp(smooth_gate, before)
        active = gated.astype(jnp.bfloat16)
        results.append(
            latter
            + sum_rows(jnp.dot(active, full_out, preferred_element_type=jnp.float32))
            + full_out_bias
        )
        back_weights = (
            lax.all_gather(self_proj, "dp", axis=0, tiled=True),
            lax.all_gather(self_out, "dp", axis=1, tiled=True),
            lax.all_gather(cross_query, "dp", axis=0, tiled=True),
            lax.all_gather(cross_pairs, "dp", axis=0, tiled=True),
            lax.all_gather(cross_out, "dp", axis=1, tiled=True),
            lax.all_gather(hidden_in, "dp", axis=1, tiled=True),
            lax.all_gather(hidden_in_bias, "dp", axis=0, tiled=True),
            lax.all_gather(hidden_out, "dp", axis=0, tiled=True),
        )
        (
            back_proj,
            back_self_out,
            back_query,
            back_pairs,
            back_cross_out,
            back_in,
            back_in_bias,
            back_out,
        ) = back_weights
        upward = cotangent[step_index].astype(jnp.float32)
        grad_out_bias = jnp.sum(upward, axis=0)
        slope_rows = gather_slopes(upward.astype(jnp.bfloat16))
        grad_out = jnp.einsum("tf,td->fd", active, slope_rows, preferred_element_type=jnp.float32)
        slope_active = jnp.einsum(
            "td,fd->tf", slope_rows, back_out, preferred_element_type=jnp.float32
        )
        slope_before = gate_pullback(slope_active)[0].astype(jnp.bfloat16)
        grad_in_bias = jnp.sum(slope_before.astype(jnp.float32), axis=0)
        grad_in = jnp.einsum(
            "td,tf->df", hidden_rows, slope_before, preferred_element_type=jnp.float32
        )
        slope_normed = sum_slopes(
            jnp.einsum("tf,df->td", slope_before, back_in, preferred_element_type=jnp.float32)
        )
        slope_hidden, grad_hidden_gain, grad_hidden_shift = plain_norm_backward(
            slope_normed, normal_third, inverse_third, full_hidden_gain
        )
        upward = upward + slope_hidden
        slope_rows = gather_slopes(upward.astype(jnp.bfloat16))
        grad_cross_out = jnp.einsum(
            "tj,td->jd", cross_heads, slope_rows, preferred_element_type=jnp.float32
        )
        slope_heads = jnp.einsum(
            "td,jd->tj", slope_rows, back_cross_out, preferred_element_type=jnp.float32
        ).astype(jnp.bfloat16)
        slope_query, slope_keys, slope_values = plain_attend_backward(
            cross_queries,
            key_value[:, 0],
            key_value[:, 1],
            cross_allowed,
            cross_logsum,
            slope_heads,
        )
        slope_pairs = jnp.stack([slope_keys, slope_values], axis=1)
        grad_query = jnp.einsum(
            "td,tj->dj", cross_rows, slope_query, preferred_element_type=jnp.float32
        )
        grad_pairs = jnp.einsum(
            "sd,scj->dcj", source_rows, slope_pairs, preferred_element_type=jnp.float32
        )
        slope_cross, slope_source = (
            lax.psum_scatter(
                jnp.einsum(
                    "tj,dj->td", slope_query, back_query, preferred_element_type=jnp.float32
                ).astype(jnp.bfloat16),
                "tensor",
                scatter_dimension=0,
                tiled=True,
            ).astype(jnp.float32),
            lax.psum_scatter(
                jnp.einsum(
                    "scj,dcj->sd", slope_pairs, back_pairs, preferred_element_type=jnp.float32
                ).astype(jnp.bfloat16),
                "tensor",
                scatter_dimension=0,
                tiled=True,
            ).astype(jnp.float32),
        )
        slope_hidden, grad_cross_gain, grad_cross_shift = plain_norm_backward(
            slope_cross, normal_second, inverse_second, full_cross_gain
        )
        upward = upward + slope_hidden
        slope_rows = gather_slopes(upward.astype(jnp.bfloat16))
        grad_self_out = jnp.einsum(
            "tj,td->jd", self_heads, slope_rows, preferred_element_type=jnp.float32
        )
        slope_heads = jnp.einsum(
            "td,jd->tj", slope_rows, back_self_out, preferred_element_type=jnp.float32
        ).astype(jnp.bfloat16)
        slope_query, slope_keys, slope_values = plain_attend_backward(
            triple[:, 0], triple[:, 1], triple[:, 2], self_allowed, self_logsum, slope_heads
        )
        slope_triple = jnp.stack([slope_query, slope_keys, slope_values], axis=1)
        grad_proj = jnp.einsum(
            "td,tcj->dcj", self_rows, slope_triple, preferred_element_type=jnp.float32
        )
        slope_self = sum_slopes(
            jnp.einsum("tcj,dcj->td", slope_triple, back_proj, preferred_element_type=jnp.float32)
        )
        slope_hidden, grad_self_gain, grad_self_shift = plain_norm_backward(
            slope_self, normal_first, inverse_first, full_self_gain
        )
        token_grads.append(upward + slope_hidden)
        encoder_grads.append(slope_source)
        vector_terms = (
            grad_self_gain,
            grad_self_shift,
            grad_cross_gain,
            grad_cross_shift,
            grad_hidden_gain,
            grad_hidden_shift,
            grad_out_bias,
        )
        vector_total = (
            vector_terms if step_index == 0 else jax.tree.map(jnp.add, vector_total, vector_terms)
        )
        weight_terms = (
            grad_proj,
            grad_self_out,
            grad_query,
            grad_pairs,
            grad_cross_out,
            grad_in,
            grad_in_bias,
            grad_out,
        )
        shard_terms = reduce_weights(weight_terms)
        weight_total = (
            shard_terms if step_index == 0 else jax.tree.map(jnp.add, weight_total, shard_terms)
        )
    vector_shards = (
        lax.psum_scatter(vector_total[0], ("dp", "tensor"), scatter_dimension=0, tiled=True),
        lax.psum_scatter(vector_total[1], ("dp", "tensor"), scatter_dimension=0, tiled=True),
        lax.psum_scatter(vector_total[2], ("dp", "tensor"), scatter_dimension=0, tiled=True),
        lax.psum_scatter(vector_total[3], ("dp", "tensor"), scatter_dimension=0, tiled=True),
        lax.psum_scatter(vector_total[4], ("dp", "tensor"), scatter_dimension=0, tiled=True),
        lax.psum_scatter(vector_total[5], ("dp", "tensor"), scatter_dimension=0, tiled=True),
        lax.psum_scatter(vector_total[6], ("dp", "tensor"), scatter_dimension=0, tiled=True),
    )
    return (
        jnp.stack(results),
        jnp.stack(token_grads),
        jnp.stack(encoder_grads),
        weight_total[0],
        weight_total[1],
        weight_total[2],
        weight_total[3],
        weight_total[4],
        weight_total[5],
        weight_total[6],
        weight_total[7],
        vector_shards[6],
        vector_shards[0],
        vector_shards[1],
        vector_shards[2],
        vector_shards[3],
        vector_shards[4],
        vector_shards[5],
    )


def solution(mesh):
    in_specs = (
        P("dp", "tensor", None),
        P("dp", "tensor", None),
        P("dp", None),
        P("dp", None),
        P("dp", None, "tensor"),
        P("tensor", "dp"),
        P("dp", "tensor"),
        P("dp", None, "tensor"),
        P("tensor", "dp"),
        P(None, ("dp", "tensor")),
        P(("dp", "tensor")),
        P(("dp", "tensor"), None),
        P(("dp", "tensor")),
        P(("dp", "tensor")),
        P(("dp", "tensor")),
        P(("dp", "tensor")),
        P(("dp", "tensor")),
        P(("dp", "tensor")),
        P(("dp", "tensor")),
        P("dp", "tensor", None),
    )
    out_specs = (
        P("dp", "tensor", None),
        P("dp", "tensor", None),
        P("dp", "tensor", None),
        P("dp", None, "tensor"),
        P("tensor", "dp"),
        P("dp", "tensor"),
        P("dp", None, "tensor"),
        P("tensor", "dp"),
        P(None, ("dp", "tensor")),
        P(("dp", "tensor")),
        P(("dp", "tensor"), None),
        P(("dp", "tensor")),
        P(("dp", "tensor")),
        P(("dp", "tensor")),
        P(("dp", "tensor")),
        P(("dp", "tensor")),
        P(("dp", "tensor")),
        P(("dp", "tensor")),
    )

    def run(*arrays):
        width = arrays[0].shape[2]
        aligned = width // mesh.shape["dp"] % 16 == 0 and mesh.shape["dp"] % 4 == 0
        inner = fast_local if aligned and mesh.shape["tensor"] == 2 else plain_local
        return jax.shard_map(inner, mesh=mesh, in_specs=in_specs, out_specs=out_specs, check_vma=False)(*arrays)

    return run
```

```python
import functools

import jax
import jax.numpy as jnp
from jax import lax
from jax.experimental import pallas as pl
from jax.experimental.pallas import tpu as pltpu
from jax.sharding import PartitionSpec as P

HEAD = 64
EPS = 1e-05
NEGATIVE = -1e30
MESH = pl.DeviceIdType.MESH
HBM = pltpu.HBM
VMEM = pltpu.VMEM
PIECES = 8
FF_PIECES = 16


class Place:
    def __init__(self):
        self.dp = lax.axis_index("dp")
        self.y = lax.axis_index("tensor")
        self.c = lax.rem(self.dp, 2)
        self.x = lax.rem(self.dp // 2, 2)
        self.z = self.dp // 4

    def at(self, z=None, x=None, c=None, y=None):
        z = self.z if z is None else z
        x = self.x if x is None else x
        c = self.c if c is None else c
        y = self.y if y is None else y
        return ((z * 2 + x) * 2 + c, y)

    def core(self):
        return self.at(c=1 - self.c)

    def xn(self):
        return self.at(x=1 - self.x)

    def yn(self):
        return self.at(y=1 - self.y)

    def up(self):
        return self.at(z=self.z + 1)

    def down(self):
        return self.at(z=self.z - 1)


def remote(src, dst, send, recv, device):
    return pltpu.make_async_remote_copy(
        src_ref=src, dst_ref=dst, send_sem=send, recv_sem=recv, device_id=device, device_id_type=MESH
    )


def signal(sem, device):
    pl.semaphore_signal(sem, inc=1, device_id=device, device_id_type=MESH)


class LineGather:
    def __init__(self, place, depth, slot, send, recv):
        self.p, self.n, self.slot, self.send, self.recv = place, depth, slot, send, recv

    def _copy_up(self, k):
        b = self.p.z - k
        return remote(self.slot(b), self.slot(b), self.send.at[0, k], self.recv.at[0, k], self.p.up())

    def _copy_down(self, k):
        b = self.p.z + k
        return remote(self.slot(b), self.slot(b), self.send.at[1, k], self.recv.at[1, k], self.p.down())

    def _from_below(self, k):
        b = self.p.z - k
        return remote(self.slot(b), self.slot(b), self.send.at[0, k - 1], self.recv.at[0, k - 1], self.p.up())

    def _from_above(self, k):
        b = self.p.z + k
        return remote(self.slot(b), self.slot(b), self.send.at[1, k - 1], self.recv.at[1, k - 1], self.p.down())

    def arrive(self, k):
        z = self.p.z

        @pl.when(z - k >= 0)
        def _():
            self._from_below(k).wait_recv()

        @pl.when(z + k <= self.n - 1)
        def _():
            self._from_above(k).wait_recv()

    def step(self, k):
        z = self.p.z
        if k > 0:
            self.arrive(k)
        if k < self.n - 1:

            @pl.when((z - k >= 0) & (z < self.n - 1))
            def _():
                self._copy_up(k).start()

            @pl.when((z + k <= self.n - 1) & (z > 0))
            def _():
                self._copy_down(k).start()

    def sent(self):
        z = self.p.z
        for k in range(self.n - 1):

            @pl.when((z - k >= 0) & (z < self.n - 1))
            def _():
                self._copy_up(k).wait_send()

            @pl.when((z + k <= self.n - 1) & (z > 0))
            def _():
                self._copy_down(k).wait_send()


class PlaneGather:
    def __init__(self, place, slot, send, recv):
        self.p, self.slot, self.send, self.recv = place, slot, send, recv
        p = place
        x, y, c = p.x, p.y, p.c
        ox, oy = 1 - x, 1 - y
        self.moves = [
            ((x, c, y, None), p.xn(), 0),
            ((x, c, y, None), p.yn(), 1),
            ((ox, c, y, 0), p.yn(), 2),
            ((x, c, oy, 1), p.xn(), 3),
            ((x, c, y, None), p.core(), 4),
            ((ox, c, y, None), p.core(), 5),
            ((x, c, oy, None), p.core(), 6),
            ((ox, c, oy, None), p.core(), 7),
        ]
        oc = 1 - c
        self.arrivals = [
            (ox, c, y, None),
            (x, c, oy, None),
            (ox, c, oy, 0),
            (ox, c, oy, 1),
            (x, oc, y, None),
            (ox, oc, y, None),
            (x, oc, oy, None),
            (ox, oc, oy, None),
        ]

    def _move(self, i):
        where, device, s = self.moves[i]
        return remote(self.slot(*where), self.slot(*where), self.send.at[s], self.recv.at[s], device)

    def _arrival(self, i):
        view = self.slot(*self.arrivals[i])
        return remote(view, view, self.send.at[i], self.recv.at[i], self.moves[i][1])

    def begin(self):
        self._move(0).start()
        self._move(1).start()
        self._move(4).start()

    def forward(self):
        self._arrival(0).wait_recv()
        self._move(2).start()
        self._move(5).start()
        self._arrival(1).wait_recv()
        self._move(3).start()
        self._move(6).start()

    def finish(self):
        self._arrival(2).wait_recv()
        self._arrival(3).wait_recv()
        self._move(7).start()

    def end(self):
        for i in range(4, 8):
            self._arrival(i).wait_recv()

    def sent(self):
        for i in range(8):
            self._move(i).wait_send()


def all_barrier(place, count):
    sem = pltpu.get_barrier_semaphore()
    me = place.dp * 2 + place.y

    @pl.loop(1, count)
    def _(j):
        other = lax.rem(me + j, count)
        signal(sem, (other // 2, lax.rem(other, 2)))

    pl.semaphore_wait(sem, count - 1)


def far_first(z, s, depth):
    b = 0
    for place in range(depth):
        order = sorted(range(depth), key=lambda k: (-abs(k - place), k))
        b = jnp.where(z == place, order[s], b)
    return b


class LineReduce:
    def __init__(self, place, depth, part, slots, send, recv):
        self.p, self.n, self.part, self.slots, self.send, self.recv = place, depth, part, slots, send, recv

    def _up(self, b):
        slot = b - (self.p.z + 1)
        return remote(self.part(b), self.slots(slot), self.send.at[b], self.recv.at[slot], self.p.up())

    def _down(self, b):
        slot = self.n - b
        return remote(self.part(b), self.slots(slot), self.send.at[b], self.recv.at[slot], self.p.down())

    def below(self, b):
        slot = b - self.p.z
        return remote(self.slots(slot), self.slots(slot), self.send.at[b], self.recv.at[slot], self.p.up())

    def above(self, b):
        slot = self.n - b
        return remote(self.slots(slot), self.slots(slot), self.send.at[b], self.recv.at[slot], self.p.down())

    def first(self, b):
        z = self.p.z

        @pl.when((z == 0) & (b > z))
        def _():
            self._up(b).start()

        @pl.when((z == self.n - 1) & (b < z))
        def _():
            self._down(b).start()

    def middle(self, b, add):
        z = self.p.z

        @pl.when((z > 0) & (b > z))
        def _():
            self.below(b).wait_recv()
            add(self.part(b), self.slots(b - z))
            self._up(b).start()

        @pl.when((z < self.n - 1) & (b < z))
        def _():
            self.above(b).wait_recv()
            add(self.part(b), self.slots(self.n - b))
            self._down(b).start()

    def last(self, take):
        z = self.p.z

        @pl.when(z > 0)
        def _():
            self.below(z).wait_recv()
            take(self.slots(0))

        @pl.when(z < self.n - 1)
        def _():
            self.above(z).wait_recv()
            take(self.slots(self.n - z))

    def sent(self):
        z = self.p.z

        @pl.loop(0, self.n)
        def _(b):
            @pl.when(b > z)
            def _():
                self._up(b).wait_send()

            @pl.when(b < z)
            def _():
                self._down(b).wait_send()


def add_low(part, other):
    part[...] = (part[...].astype(jnp.float32) + other[...].astype(jnp.float32)).astype(part.dtype)


def gelu_pair(x):
    a, b = 0.7978845608028654, 0.044715
    square = x * x
    t = jnp.tanh(a * x * (1.0 + b * square))
    half = 0.5 * (1.0 + t)
    return x * half, half + 0.5 * x * (1.0 - t * t) * (a * (1.0 + 3.0 * b * square))


NN = (((1,), (0,)), ((), ()))
NT = (((1,), (1,)), ((), ()))
TN = (((0,), (0,)), ((), ()))


def mm(left, right, form=NN):
    return lax.dot_general(left, right, form, preferred_element_type=jnp.float32)


def neighbour_barrier(p, depth):
    sem = pltpu.get_barrier_semaphore()
    for dx in range(2):
        for dc in range(2):
            for dy in range(2):
                if dx + dc + dy:
                    signal(sem, p.at(x=lax.rem(p.x + dx, 2), c=lax.rem(p.c + dc, 2), y=lax.rem(p.y + dy, 2)))

    @pl.loop(1, depth)
    def _(k):
        signal(sem, p.at(z=lax.rem(p.z + k, depth)))

    pl.semaphore_wait(sem, 7 + depth - 1)


def layer_norm(x, gain, shift):
    center = x - jnp.mean(x, axis=-1, keepdims=True)
    inverse = lax.rsqrt(jnp.mean(center * center, axis=-1, keepdims=True) + EPS)
    return center * inverse * gain + shift


def attend_pairs(q_ref, k_ref, v_ref, allowed, probs_ref, heads_ref):
    rows = q_ref.shape[0]
    first = lax.broadcasted_iota(jnp.int32, (rows, 128), 1) < HEAD
    both = jnp.concatenate([allowed, allowed], axis=0)

    @pl.loop(0, q_ref.shape[1] // 128)
    def _(h):
        at = (slice(None), pl.ds(pl.multiple_of(h * 128, 128), 128))
        q, k, v = q_ref[at], k_ref[at], v_ref[at]
        zero = jnp.zeros_like(q)
        pair = jnp.concatenate([jnp.where(first, q, zero), jnp.where(first, zero, q)], axis=0)
        scores = jnp.where(both, mm(pair, k, NT) * HEAD**-0.5, NEGATIVE)
        weights = jnp.exp(scores - jnp.max(scores, axis=-1, keepdims=True))
        probs = (weights * (1.0 / jnp.sum(weights, axis=-1, keepdims=True))).astype(jnp.bfloat16)
        probs_ref[h] = probs
        mix = mm(probs, v)
        heads_ref[at] = jnp.where(first, mix[:rows], mix[rows:]).astype(jnp.bfloat16)


Q, K, V, CQ, H1, H2, N1, N2, N3 = range(9)
CK, CV, ENC = range(3)


def forward_kernel(
    depth, ff_now,
    attn_ref, win_ref, wout_ref, vec_ref, tok_ref, enc_ref, cot_ref, tcol_ref, trow_ref, srow_ref,
    G, Win, Wout, g3, act_out, ctx_out, mid_out, p1_out, p2_out, full_out, bias_out,
    W, TOK, VEC, FULL, ACT, CTX, MID, P1, P2,
    lsem, wsem, osem, zs, zr, fs, fr, ps, pr, vs, vr, ss, sr,
):
    p = Place()
    count = 8 * depth
    me = p.dp * 2 + p.y
    rows, width = ACT.shape[1:]
    short = CTX.shape[1]
    local = []

    def keep(src, dst):
        copy = pltpu.make_async_copy(src, dst, lsem.at[len(local)])
        copy.start()
        local.append(copy)

    keep(attn_ref, G.at[:, p.y, p.z, p.x, p.c])
    keep(win_ref, Win.at[p.z])
    keep(wout_ref, Wout.at[p.z])
    keep(cot_ref, g3.at[p.x, p.c, :, p.y])
    half, few = rows // 2, short // 2
    TOK[p.y] = tok_ref[p.y]
    CTX[ENC, pl.ds(pl.multiple_of(p.y * few, few), few)] = enc_ref[p.y]
    VEC[me] = vec_ref[...]
    all_barrier(p, count)
    for copy in local:
        copy.wait()

    lines = []
    for i in range(PIECES):
        lines.append(LineGather(p, depth, lambda b, i=i: G.at[i, p.y, b, p.x, p.c], zs.at[i], zr.at[i]))
    wr = Win.shape[1] // (FF_PIECES // 2)
    orow = Wout.shape[1] // (FF_PIECES // 2)
    ff = []
    for i in range(ff_now):
        if i < FF_PIECES // 2:
            slot = lambda b, i=i: Win.at[b, pl.ds(i * wr, wr)]
        else:
            slot = lambda b, i=i: Wout.at[b, pl.ds((i - FF_PIECES // 2) * orow, orow)]
        ff.append(LineGather(p, depth, slot, fs.at[i], fr.at[i]))

    def plane_slot(i):
        part = G.shape[5] // 2

        def slot(x, c, y, h):
            if h is None:
                return G.at[i, y, :, x, c]
            return G.at[i, y, :, x, c, pl.ds(h * part, part)]

        return slot

    def g3_slot(x, c, y, h):
        if h is None:
            return g3.at[x, c, :, y]
        return g3.at[x, c, h, y]

    planes = [PlaneGather(p, plane_slot(i), ps.at[i], pr.at[i]) for i in range(PIECES)]
    planes.append(PlaneGather(p, g3_slot, ps.at[PIECES], pr.at[PIECES]))
    few_at = pl.ds(pl.multiple_of(p.y * few, few), few)
    swaps = [
        remote(tok_ref.at[1 - p.y], TOK.at[p.y], ss.at[0], sr.at[0], p.yn()),
        remote(enc_ref.at[1 - p.y], CTX.at[ENC, few_at], ss.at[1], sr.at[1], p.yn()),
    ]

    def swapped(i):
        if i == 0:
            view = TOK.at[1 - p.y]
        else:
            view = CTX.at[ENC, pl.ds(pl.multiple_of((1 - p.y) * few, few), few)]
        remote(view, view, ss.at[i], sr.at[i], p.yn()).wait_recv()

    @pl.loop(1, count)
    def _(j):
        other = lax.rem(me + j, count)
        remote(vec_ref, VEC.at[me], vs.at[j], vr.at[j], (other // 2, lax.rem(other, 2))).start()

    swaps[0].start()
    swaps[1].start()

    saved = []

    def save(src, dst):
        copy = pltpu.make_async_copy(src, dst, osem.at[len(saved)])
        copy.start()
        saved.append(copy)

    def vector(i):
        return FULL[i : i + 1]

    def weight(i):
        copy = pltpu.make_async_copy(G.at[i], W, wsem.at[0])
        copy.start()
        copy.wait()

    def project(a, store):
        for y in range(2):
            store(y * (width // 2), mm(a, W[y].reshape(width, width // 2)))

    def project_back(a_ref):
        total = None
        for y in range(2):
            term = mm(a_ref[:, y * (width // 2) : (y + 1) * (width // 2)], W[y].reshape(width, width // 2), NT)
            total = term if total is None else total + term
        return total

    def into(ref, i):
        def store(at, value):
            ref[i, :, at : at + width // 2] = value.astype(jnp.bfloat16)

        return store

    def first_norm():
        @pl.loop(1, count)
        def _(j):
            source = lax.rem(me + count - j, count)
            remote(VEC.at[source], VEC.at[source], vs.at[j], vr.at[j], p.yn()).wait_recv()

        group = count * 128 // width
        for k in range(width // 128):
            piece = VEC[group * k, 0:8]
            for j in range(1, group):
                piece += VEC[group * k + j, 0:8]
            FULL[:, k * 128 : (k + 1) * 128] = piece
        save(FULL, full_out)

        @pl.loop(0, depth)
        def _(b):
            source = VEC[((b * 2 + p.x) * 2 + p.c) * 2 + p.y]
            for k in range(bias_out.shape[2] // 128):
                bias_out[b, :, k * 128 : (k + 1) * 128] = jnp.broadcast_to(source[8 + k : 9 + k], (8, 128))

        swapped(0)
        tok = TOK[...].reshape(rows, width).astype(jnp.float32)
        MID[0] = tok
        ACT[N1] = layer_norm(tok, vector(0), vector(1)).astype(jnp.bfloat16)
        save(ACT.at[N1], act_out.at[N1])

    def qkv(i):
        weight(i)
        project(ACT[N1], into(ACT, (Q, K, V)[i]))
        save(ACT.at[(Q, K, V)[i]], act_out.at[(Q, K, V)[i]])

    def self_attention():
        same = tcol_ref[:, 0:1] == trow_ref[0:1, :]
        back = lax.broadcasted_iota(jnp.int32, (rows, rows), 1) <= lax.broadcasted_iota(jnp.int32, (rows, rows), 0)
        attend_pairs(ACT.at[Q], ACT.at[K], ACT.at[V], same & back, P1, ACT.at[H1])
        save(P1, p1_out)
        save(ACT.at[H1], act_out.at[H1])

    def self_project():
        weight(3)
        middle = MID[0] + project_back(ACT.at[H1])
        MID[1] = middle
        ACT[N2] = layer_norm(middle, vector(2), vector(3)).astype(jnp.bfloat16)
        save(MID.at[0:2], mid_out.at[0:2])
        save(ACT.at[N2], act_out.at[N2])

    def pairs(i):
        if i == 0:
            swapped(1)
        weight(4 + i)
        project(CTX[ENC], into(CTX, (CK, CV)[i]))

    def cross_attention():
        save(CTX, ctx_out)
        weight(6)
        project(ACT[N2], into(ACT, CQ))
        save(ACT.at[CQ], act_out.at[CQ])
        attend_pairs(ACT.at[CQ], CTX.at[CK], CTX.at[CV], tcol_ref[:, 0:1] == srow_ref[0:1, :], P2, ACT.at[H2])
        save(P2, p2_out)
        save(ACT.at[H2], act_out.at[H2])

    def cross_project():
        weight(7)
        latter = MID[1] + project_back(ACT.at[H2])
        MID[2] = latter
        ACT[N3] = layer_norm(latter, vector(4), vector(5)).astype(jnp.bfloat16)
        save(ACT.at[N3], act_out.at[N3])
        save(MID.at[2], mid_out.at[2])

    work = {
        0: [functools.partial(qkv, 0)],
        1: [functools.partial(qkv, 1)],
        2: [functools.partial(qkv, 2), self_attention],
        3: [self_project],
        4: [functools.partial(pairs, 0)],
        5: [functools.partial(pairs, 1)],
        6: [cross_attention],
        7: [cross_project],
    }
    total = max(PIECES + 1 + depth + 3, ff_now + depth)
    for it in range(total):
        for k in range(depth):
            if 0 <= it - k < PIECES:
                lines[it - k].step(k)
        for k in range(depth):
            if 0 <= it - k < ff_now:
                ff[it - k].step(k)
        if it == depth - 1:
            first_norm()
        j = it - (depth - 1)
        if 0 <= j < PIECES + 1:
            planes[j].begin()
        if 0 <= j - 1 < PIECES + 1:
            planes[j - 1].forward()
        if 0 <= j - 2 < PIECES + 1:
            planes[j - 2].finish()
        if 0 <= j - 3 < PIECES + 1:
            planes[j - 3].end()
            for task in work.get(j - 3, []):
                task()
    for line in lines + ff:
        line.sent()
    for plane in planes:
        plane.sent()
    for copy in swaps:
        copy.wait_send()
    for copy in saved:
        copy.wait()

    @pl.loop(1, count)
    def _(j):
        other = lax.rem(me + j, count)
        remote(vec_ref, VEC.at[me], vs.at[j], vr.at[j], (other // 2, lax.rem(other, 2))).wait_send()


FF_NOW = 16


def forward_all(attn, win, wout, vec, tok, enc, cot, tcol, trow, srow):
    depth = lax.axis_size("dp") // 4
    rows, cols = attn.shape[1:]
    bf, f32 = jnp.bfloat16, jnp.float32
    count = 8 * depth
    length, short, d = 2 * tok.shape[1], 2 * enc.shape[1], tok.shape[2]
    pairs = d // 128
    saves = [
        jax.ShapeDtypeStruct((9, length, d), bf),
        jax.ShapeDtypeStruct((3, short, d), bf),
        jax.ShapeDtypeStruct((3, length, d), f32),
        jax.ShapeDtypeStruct((pairs, 2 * length, length), bf),
        jax.ShapeDtypeStruct((pairs, 2 * length, short), bf),
        jax.ShapeDtypeStruct((8, d), f32),
    ]
    whole = (2, depth, 2, 2, rows, cols)
    out_shape = [
        jax.ShapeDtypeStruct((PIECES,) + whole, bf),
        jax.ShapeDtypeStruct((depth,) + win.shape, bf),
        jax.ShapeDtypeStruct((depth,) + wout.shape, bf),
        jax.ShapeDtypeStruct((2, 2, 2, 2) + cot.shape[1:], bf),
    ] + saves + [jax.ShapeDtypeStruct((depth, 8, wout.shape[0]), f32)]
    dma = pltpu.SemaphoreType.DMA
    hb, vm = pl.BlockSpec(memory_space=HBM), pl.BlockSpec(memory_space=VMEM)
    return pl.pallas_call(
        functools.partial(forward_kernel, depth, FF_NOW),
        out_shape=out_shape,
        in_specs=[vm] * 10,
        out_specs=[hb] * 10 + [vm],
        scratch_shapes=[
            pltpu.VMEM(whole, bf),
            pltpu.VMEM(tok.shape, bf),
            pltpu.VMEM((count,) + vec.shape, f32),
        ] + [pltpu.VMEM(s.shape, s.dtype) for s in (saves[5], saves[0], saves[1], saves[2], saves[3], saves[4])] + [
            dma((4,)), dma((1,)), dma((20,)),
            dma((PIECES, 2, depth - 1)), dma((PIECES, 2, depth - 1)),
            dma((FF_NOW, 2, depth - 1)), dma((FF_NOW, 2, depth - 1)),
            dma((PIECES + 1, 8)), dma((PIECES + 1, 8)),
            dma((count,)), dma((count,)),
            dma((2,)), dma((2,)),
        ],
        compiler_params=pltpu.CompilerParams(
            collective_id=1, has_side_effects=True, vmem_limit_bytes=48 << 20
        ),
        name="forward_all",
    )(attn, win, wout, vec, tok, enc, cot, tcol, trow, srow)


def hidden_kernel(
    depth, ff_done,
    act, bias_ref, Win, Wout, g3,
    d_out, y_out, go_out, gbias_out, S_out, YS_out,
    HN, G3, WI, WO, Y, D, S, RF, ACTIVE, SLOPE, BS, BR, CS, CR, CSY, CRY, PS, PR,
    lsem, ps, pr, fs, fr, hs, hr, bs, br, cs, cr, ys, yr, xs, xr,
):
    p = Place()
    z = p.z
    rows, width = HN.shape[3:]
    units = WO.shape[1]
    orow = units // (FF_PIECES // 2)
    done = max(0, ff_done - FF_PIECES // 2) * orow
    loads = [
        pltpu.make_async_copy(act.at[N3], HN.at[p.x, p.c, p.y], lsem.at[0]),
        pltpu.make_async_copy(Win, WI, lsem.at[1]),
        pltpu.make_async_copy(g3, G3, lsem.at[2]),
    ]
    if done:
        loads.append(pltpu.make_async_copy(Wout.at[:, pl.ds(0, done)], WO.at[:, pl.ds(0, done)], lsem.at[3]))
    if done < units:
        rest = pl.ds(done, units - done)
        loads.append(pltpu.make_async_copy(Wout.at[z, rest], WO.at[z, rest], lsem.at[4]))
    for load in loads:
        load.start()
    neighbour_barrier(p, depth)
    half = rows // 2

    def hn_slot(x, c, y, h):
        if h is None:
            return HN.at[x, c, y]
        return HN.at[x, c, y, pl.ds(h * half, half)]

    for load in loads:
        load.wait()
    gather = PlaneGather(p, hn_slot, ps, pr)
    gather.begin()
    BS[...] = jnp.zeros_like(BS)
    lines = []
    for i in range(max(ff_done, FF_PIECES // 2), FF_PIECES):
        at = pl.ds((i - FF_PIECES // 2) * orow, orow)
        n = len(lines)
        lines.append(LineGather(p, depth, lambda b, at=at: WO.at[b, at], fs.at[n], fr.at[n]))
    for it in range(len(lines) + depth - 1 if lines else 0):
        for k in range(depth):
            if 0 <= it - k < len(lines):
                lines[it - k].step(k)

    def bits(code):
        dc, dx, dy = code // 4, lax.rem(code // 2, 2), lax.rem(code, 2)
        return lax.rem(p.x + dx, 2), lax.rem(p.c + dc, 2), lax.rem(p.y + dy, 2)

    arriving = (0, 4, 1, 2, 5, 6, 3, 7)

    def to_core(j, send, land, a, b):
        return remote(send.at[j], land.at[j], a.at[j], b.at[j], p.core())

    def to_chip(j):
        dx, dy = 1 - j // 2, 1 - lax.rem(j, 2)
        return remote(
            PS.at[j], PR.at[j], xs.at[j], xr.at[j], p.at(x=lax.rem(p.x + dx, 2), y=lax.rem(p.y + dy, 2))
        )

    def bias_move(b):
        return remote(BS.at[b], BR.at[z], bs.at[b], br.at[z], p.at(z=b))

    up = remote(S.at[depth - 1], RF, hs.at[0], hr.at[0], p.up())
    down = remote(S.at[0], RF, hs.at[0], hr.at[0], p.down())

    @pl.loop(0, depth)
    def _(s):
        last = s == depth - 1
        b = far_first(z, 0, depth)
        for k in range(1, depth):
            b = jnp.where(s == k, far_first(z, k, depth), b)

        @pl.loop(0, 8)
        def _(i):
            @pl.when((s == 0) & (i == 1))
            def _():
                gather._arrival(4).wait_recv()

            @pl.when((s == 0) & (i == 2))
            def _():
                gather.forward()

            @pl.when((s == 0) & (i == 4))
            def _():
                gather._arrival(5).wait_recv()
                gather._arrival(6).wait_recv()

            @pl.when((s == 0) & (i == 6))
            def _():
                gather.finish()

            @pl.when((s == 0) & (i == 7))
            def _():
                gather._arrival(7).wait_recv()

            code = arriving[0]
            for k in range(1, 8):
                code = jnp.where(i == k, arriving[k], code)
            at = bits(jnp.where(last, 7 - i, code))
            h = HN[at]
            g = G3[at].reshape(rows, width)
            win, wout = WI[b], WO[b]
            before = mm(h, win) + bias_ref[b, 0:1]
            active, slope = gelu_pair(before)
            ACTIVE[at] = active.astype(jnp.bfloat16)
            slope = (mm(g, wout, NT) * slope).astype(jnp.bfloat16)
            SLOPE[at] = slope
            BS[b, 0:1] += jnp.sum(slope.astype(jnp.float32), axis=0, keepdims=True)
            back = mm(slope, win, NT)

            @pl.when(s == 0)
            def _():
                D[at] = back

            @pl.when(s > 0)
            def _():
                D[at] += back

            @pl.when(last & (i < 4))
            def _():
                CS[i] = D[at].astype(jnp.bfloat16)
                to_core(i, CS, CR, cs, cr).start()

            @pl.when(last & (i >= 4))
            def _():
                j = i - 4
                to_core(j, CS, CR, cs, cr).wait_recv()
                total = D[at] + CR[j].astype(jnp.float32)

                @pl.when(j < 3)
                def _():
                    PS[j] = total.astype(jnp.bfloat16)
                    to_chip(j).start()

                @pl.when(j == 3)
                def _():
                    d_out[...] = total

        @pl.loop(0, width // 256)
        def _(n):
            at = pl.ds(pl.multiple_of(n * 256, 256), 256)
            gout = mm(
                ACTIVE[...].reshape(8 * rows, units), G3[:, :, :, :, :, at].reshape(8 * rows, 256), TN
            )
            gin = mm(SLOPE[...].reshape(8 * rows, units), HN[:, :, :, :, at].reshape(8 * rows, 256), TN)
            go_out[0, :, at] = gin
            go_out[1, :, at] = gout
            S[b, 0, :, at] = gin.astype(jnp.bfloat16)
            S[b, 1, :, at] = gout.astype(jnp.bfloat16)

        @pl.when((s == 0) & (z == 0))
        def _():
            up.start()

        @pl.when((s == 0) & (z == depth - 1))
        def _():
            down.start()

        @pl.when(jnp.logical_not(last))
        def _():
            bias_move(b).start()

        @pl.loop(0, 8)
        def _(i):
            at = bits(7 - i)
            more = mm(ACTIVE[at], WO[b])

            @pl.when(s == 0)
            def _():
                Y[at] = more

            @pl.when(s > 0)
            def _():
                Y[at] += more

            @pl.when(last & (i < 4))
            def _():
                CSY[i] = Y[at].astype(jnp.bfloat16)
                to_core(i, CSY, CRY, ys, yr).start()

            @pl.when(last & (i >= 4))
            def _():
                j = i - 4
                to_core(j, CSY, CRY, ys, yr).wait_recv()
                total = Y[at] + CRY[j].astype(jnp.float32)

                to_core(j, CSY, CRY, ys, yr).wait_send()

                @pl.when(j < 3)
                def _():
                    CSY[j] = total.astype(jnp.bfloat16)

                @pl.when(j == 3)
                def _():
                    y_out[...] = total

    @pl.when((z == 1) | (z == depth - 2))
    def _():
        up.wait_recv()
        far = jnp.where(z == 1, depth - 1, 0)
        add_low(S.at[far], RF)

    outs = [
        pltpu.make_async_copy(S, S_out, lsem.at[0]),
        pltpu.make_async_copy(CSY.at[pl.ds(0, 3)], YS_out, lsem.at[1]),
    ]
    for copy in outs:
        copy.start()
    gbias_out[...] = BS[z]

    @pl.loop(1, depth)
    def _(k):
        source = lax.rem(z + k, depth)
        remote(BS.at[source], BR.at[source], bs.at[source], br.at[source], p.at(z=source)).wait()
        gbias_out[...] += BR[source]

    @pl.loop(0, 3)
    def _(j):
        to_chip(j).wait_recv()
        d_out[...] += PR[j].astype(jnp.float32)

    for copy in outs:
        copy.wait()

    @pl.when((z == 0) | (z == depth - 1))
    def _():
        up.wait_send()

    gather.sent()
    for line in lines:
        line.sent()

    @pl.loop(0, 4)
    def _(j):
        to_core(j, CS, CR, cs, cr).wait_send()

    @pl.loop(0, 3)
    def _(j):
        to_chip(j).wait_send()


def hidden_block(act, bias, win, wout, g3):
    depth, width, units = win.shape
    rows = act.shape[1]
    bf, f32 = jnp.bfloat16, jnp.float32
    dma = pltpu.SemaphoreType.DMA
    vm = pl.BlockSpec(memory_space=VMEM)
    hb = pl.BlockSpec(memory_space=HBM)
    later = max(1, FF_PIECES - max(FF_NOW, FF_PIECES // 2))
    return pl.pallas_call(
        functools.partial(hidden_kernel, depth, FF_NOW),
        out_shape=[
            jax.ShapeDtypeStruct((rows, width), f32),
            jax.ShapeDtypeStruct((rows, width), f32),
            jax.ShapeDtypeStruct((2, units, width), f32),
            jax.ShapeDtypeStruct((8, units), f32),
            jax.ShapeDtypeStruct((depth, 2, units, width), bf),
            jax.ShapeDtypeStruct((3, rows, width), bf),
        ],
        in_specs=[hb, vm, hb, hb, hb],
        out_specs=[vm, vm, vm, vm, hb, hb],
        scratch_shapes=[
            pltpu.VMEM((2, 2, 2, rows, width), bf),
            pltpu.VMEM(g3.shape, bf),
            pltpu.VMEM(win.shape, bf),
            pltpu.VMEM(wout.shape, bf),
            pltpu.VMEM((2, 2, 2, rows, width), f32),
            pltpu.VMEM((2, 2, 2, rows, width), f32),
            pltpu.VMEM((depth, 2, units, width), bf),
            pltpu.VMEM((2, units, width), bf),
            pltpu.VMEM((2, 2, 2, rows, units), bf),
            pltpu.VMEM((2, 2, 2, rows, units), bf),
            pltpu.VMEM((depth, 8, units), f32),
            pltpu.VMEM((depth, 8, units), f32),
            pltpu.VMEM((4, rows, width), bf),
            pltpu.VMEM((4, rows, width), bf),
            pltpu.VMEM((4, rows, width), bf),
            pltpu.VMEM((4, rows, width), bf),
            pltpu.VMEM((3, rows, width), bf),
            pltpu.VMEM((3, rows, width), bf),
            dma((5,)),
            dma((8,)), dma((8,)),
            dma((later, 2, depth - 1)), dma((later, 2, depth - 1)),
            dma((1,)), dma((1,)),
            dma((depth,)), dma((depth,)),
            dma((4,)), dma((4,)),
            dma((4,)), dma((4,)),
            dma((3,)), dma((3,)),
        ],
        compiler_params=pltpu.CompilerParams(
            collective_id=2, has_side_effects=True, vmem_limit_bytes=60 << 20
        ),
        name="hidden_block",
    )(act, bias, win, wout, g3)


def norm_back(e, h, gain):
    center = h - jnp.mean(h, axis=-1, keepdims=True)
    inverse = lax.rsqrt(jnp.mean(center * center, axis=-1, keepdims=True) + EPS)
    normal = center * inverse
    scaled = e * gain
    back = inverse * (
        scaled
        - jnp.mean(scaled, axis=-1, keepdims=True)
        - normal * jnp.mean(scaled * normal, axis=-1, keepdims=True)
    )
    return back, jnp.sum(e * normal, axis=0, keepdims=True), jnp.sum(e, axis=0, keepdims=True)


def attend_pairs_back(q_ref, k_ref, v_ref, probs_ref, slope_ref, dq_ref, dk_ref, dv_ref, start, stop):
    rows = q_ref.shape[0]
    first = lax.broadcasted_iota(jnp.int32, (rows, 128), 1) < HEAD

    def stacked(a):
        zero = jnp.zeros_like(a)
        return jnp.concatenate([jnp.where(first, a, zero), jnp.where(first, zero, a)], axis=0)

    @pl.loop(start, stop)
    def _(h):
        at = (slice(None), pl.ds(pl.multiple_of(h * 128, 128), 128))
        up = stacked(slope_ref[at])
        low = probs_ref[h]
        probs = low.astype(jnp.float32)
        dprobs = mm(up, v_ref[at], NT)
        ds = (probs * (dprobs - jnp.sum(probs * dprobs, axis=-1, keepdims=True))).astype(jnp.bfloat16)
        dq = mm(ds, k_ref[at]) * HEAD**-0.5
        dq_ref[at] = jnp.where(first, dq[:rows], dq[rows:]).astype(jnp.bfloat16)
        dk_ref[at] = (mm(ds, stacked(q_ref[at]), TN) * HEAD**-0.5).astype(jnp.bfloat16)
        dv_ref[at] = mm(low, up, TN).astype(jnp.bfloat16)


class HoppedReduce(LineReduce):
    def _down(self, b):
        slot = self.n - 2 + self.p.z - 1 - b
        return remote(self.part(b), self.slots(slot), self.send.at[b], self.recv.at[slot], self.p.down())

    def above(self, b):
        slot = self.n - 2 + self.p.z - b
        return remote(self.slots(slot), self.slots(slot), self.send.at[b], self.recv.at[slot], self.p.down())

    def first(self, b):
        z, n = self.p.z, self.n

        @pl.when((b > z) & (((z == 0) & (b < n - 1)) | ((z == 1) & (b == n - 1))))
        def _():
            self._up(b).start()

        @pl.when((b < z) & (((z == n - 1) & (b > 0)) | ((z == n - 2) & (b == 0))))
        def _():
            self._down(b).start()

    def middle(self, b, add):
        z, n = self.p.z, self.n

        @pl.when((z > 0) & (b > z) & ((z > 1) | (b < n - 1)))
        def _():
            self.below(b).wait_recv()
            add(self.part(b), self.slots(b - z))
            self._up(b).start()

        @pl.when((z < n - 1) & (b < z) & ((z < n - 2) | (b > 0)))
        def _():
            self.above(b).wait_recv()
            add(self.part(b), self.slots(n - 2 + z - b))
            self._down(b).start()

    def last(self, take):
        z, n = self.p.z, self.n

        @pl.when(z > 0)
        def _():
            self.below(z).wait_recv()
            take(self.slots(0))

        @pl.when(z < n - 1)
        def _():
            self.above(z).wait_recv()
            take(self.slots(n - 2))

    def sent(self):
        z, n = self.p.z, self.n

        @pl.loop(0, n)
        def _(b):
            @pl.when((b > z) & ((z > 0) | (b < n - 1)))
            def _():
                self._up(b).wait_send()

            @pl.when((b < z) & ((z < n - 1) | (b > 0)))
            def _():
                self._down(b).wait_send()


SLOTS = 4
FF_PARTS = 8


def backward_kernel(
    depth,
    G, act, ctx, mid, p1, p2, full_ref, g3, d_in, y_in, go_in, S_in, YS_in,
    gw_out, vec_out, res_out, tg_out, eg_out, go_out,
    MY, SEND, CR, PD, PR, R, S, RF, YS, YR, W, ACT, CTX, X, PB1, PB2, UP, LOW, SL, DH, DC, COT, VG, VR, XS, XR, ES, ER,
    lsem, wsem, cs, cr, ds, dr, ps, pr, zs, zr, fs, fr, ys, yr, vs, vr, ss, sr, credit,
):
    p = Place()
    count = 8 * depth
    me = p.dp * 2 + p.y
    ox, oy = 1 - p.x, 1 - p.y
    rows, width = UP.shape
    short = CTX.shape[1]
    cols = width // 2
    part = MY.shape[4]
    half = part // 2
    low_type = jnp.bfloat16

    def load(i, src, dst):
        copy = pltpu.make_async_copy(src, dst, lsem.at[i])
        copy.start()
        return copy

    loads = [
        load(0, mid.at[2], X),
        load(1, d_in, UP),
        load(2, g3.at[p.x, p.c, p.y], COT),
        load(3, y_in.at[pl.ds(0, rows // 2)], res_out.at[0]),
        load(4, y_in.at[pl.ds(rows // 2, rows // 2)], res_out.at[1]),
        load(5, YS_in, YS),
        load(6, act.at[pl.ds(0, 8)], ACT),
        load(7, ctx, CTX),
        load(8, p2, PB2),
        load(9, S_in, S),
        load(10, go_in, go_out),
        load(11, p1, PB1),
    ]
    order = (7, 6, 3, 0, 1, 2, 4, 5)

    def weight(n):
        return pltpu.make_async_copy(G.at[order[n]], W.at[n % 2], wsem.at[n % 2])

    def use(n):
        weight(n).wait()
        if n + 1 < len(order):
            weight(n + 1).start()
        return [W[n % 2, y].reshape(width, cols) for y in range(2)]

    weight(0).start()
    VG[...] = jnp.zeros_like(VG)
    all_barrier(p, count)

    def y_move(j):
        dx, dy = 1 - j // 2, 1 - j % 2
        return remote(
            YS.at[j], YR.at[j], ys.at[j], yr.at[j], p.at(x=lax.rem(p.x + dx, 2), y=lax.rem(p.y + dy, 2))
        )

    loads[5].wait()
    for j in range(3):
        y_move(j).start()

    def core(i):
        return remote(SEND.at[i % 2], CR.at[i % SLOTS], cs.at[i], cr.at[i], p.core())

    def diagonal(i, h):
        return remote(
            MY.at[i, oy, :, ox, pl.ds(h * half, half)], PD.at[i, h], ds.at[i, h], dr.at[i, h],
            p.yn() if h else p.xn(),
        )

    def column(i, h):
        view = MY.at[i, oy, :, p.x] if h else MY.at[i, p.y, :, ox]
        return remote(view, PR.at[i, h], ps.at[i, h], pr.at[i, h], p.yn() if h else p.xn())

    lines = [
        LineReduce(
            p, depth, lambda b, i=i: MY.at[i, p.y, b, p.x], lambda k, i=i: R.at[i, k], zs.at[i], zr.at[i]
        )
        for i in range(PIECES)
    ]
    frows = S.shape[2] // (FF_PARTS // 2)
    ff = []
    for f in range(FF_PARTS):
        at = pl.ds(f // 2 * frows, frows)
        ff.append(
            HoppedReduce(
                p, depth, lambda b, f=f, at=at: S.at[b, f % 2, at], lambda k, f=f, at=at: RF.at[k, f % 2, at],
                fs.at[f], fr.at[f],
            )
        )

    def store_part(i, left, right):
        if i >= 2:
            core(i - 2).wait_send()
        for y in range(2):
            value = mm(left, right[:, y * cols : (y + 1) * cols], TN).reshape(depth, 2, 2, part, cols)
            value = value.astype(low_type)
            even, odd = value[:, :, 0], value[:, :, 1]
            MY[i, y] = jnp.where(p.c == 0, even, odd)
            SEND[i % 2, y] = jnp.where(p.c == 0, odd, even)
        if i >= SLOTS:
            pl.semaphore_wait(credit, 1)
        core(i).start()

    def stage(i, s):
        if s == 1:
            core(i).wait_recv()
            add_low(MY.at[i], CR.at[i % SLOTS])
            if i + SLOTS < PIECES:
                signal(credit, p.core())
            diagonal(i, 0).start()
            diagonal(i, 1).start()
        elif s == 2:
            diagonal(i, 0).wait_recv()
            add_low(MY.at[i, oy, :, p.x, pl.ds(0, half)], PD.at[i, 0])
            column(i, 1).start()
            diagonal(i, 1).wait_recv()
            add_low(MY.at[i, p.y, :, ox, pl.ds(half, half)], PD.at[i, 1])
            column(i, 0).start()
        elif s == 3:
            column(i, 0).wait_recv()
            column(i, 1).wait_recv()
            view = MY.at[i, p.y, :, p.x]
            view[...] = (
                view[...].astype(jnp.float32)
                + PR[i, 0].astype(jnp.float32)
                + PR[i, 1].astype(jnp.float32)
            ).astype(low_type)
            for k in range(depth - 1):
                lines[i].first(far_first(p.z, k, depth))
        elif s < 3 + depth:
            lines[i].middle(far_first(p.z, s - 4, depth), add_low)
        elif s == 3 + depth:
            gw_out[i] = MY[i, p.y, p.z, p.x].astype(jnp.float32)

            def take(slot):
                gw_out[i] += slot[...].astype(jnp.float32)

            lines[i].last(take)

    def ff_stage(f, s):
        if s == 0:
            for k in range(depth - 1):
                ff[f].first(far_first(p.z, k, depth))
        elif s < depth:
            ff[f].middle(far_first(p.z, s - 1, depth), add_low)
        else:
            at = pl.ds(f // 2 * frows, frows)

            def take(slot):
                go_out[f % 2, at] += slot[...].astype(jnp.float32)

            ff[f].last(take)

    clock = [0]

    def tick(*stages):
        n = clock[0]
        clock[0] += 1
        if n == 0:
            loads[9].wait()
            loads[10].wait()
        for f in range(FF_PARTS):
            if (n - f) % 2 == 0 and 0 <= (n - f) // 2 <= depth:
                ff_stage(f, (n - f) // 2)
        for i, s in stages:
            stage(i, s)

    def gain(i):
        return full_ref[i : i + 1]

    def spread(i, values):
        VG[i : i + 1] = values

    tick()
    for i in (0, 1, 2, 3, 4):
        loads[i].wait()
    cot = COT[...].reshape(rows, width).astype(jnp.float32)
    latter = X[...]
    for h in range(2):
        res_out[h] += latter[h * (rows // 2) : (h + 1) * (rows // 2)] + gain(6)
    back, g_gain, g_shift = norm_back(UP[...], latter, gain(4))
    spread(4, g_gain)
    spread(5, g_shift)
    spread(6, jnp.sum(cot, axis=0, keepdims=True))
    UP[...] = cot + back
    LOW[...] = UP[...].astype(low_type)
    next_mid = load(0, mid.at[1], X)
    w = use(0)
    for y in range(2):
        SL[:, y * cols : (y + 1) * cols] = mm(LOW[...], w[y]).astype(low_type)
    loads[6].wait()
    store_part(0, LOW[...], ACT[H2])
    tick()
    loads[7].wait()
    loads[8].wait()
    attend_pairs_back(
        ACT.at[CQ], CTX.at[CK], CTX.at[CV], PB2, SL, DH.at[0], DC.at[0], DC.at[1], 0, width // 128
    )
    store_part(1, ACT[N2], DH[0])
    tick((0, 1))
    w = use(1)
    slope = mm(DH[0, :, :cols], w[0], NT) + mm(DH[0, :, cols:], w[1], NT)
    next_mid.wait()
    back, g_gain, g_shift = norm_back(slope, X[...], gain(2))
    spread(2, g_gain)
    spread(3, g_shift)
    UP[...] += back
    LOW[...] = UP[...].astype(low_type)
    next_mid = load(0, mid.at[0], X)
    store_part(2, CTX[ENC], DC[0])
    tick((1, 1))
    store_part(3, CTX[ENC], DC[1])
    tick((2, 1))
    w = use(2)
    for y in range(2):
        SL[:, y * cols : (y + 1) * cols] = mm(LOW[...], w[y]).astype(low_type)
    store_part(4, LOW[...], ACT[H1])
    tick((3, 1), (0, 2))
    loads[11].wait()
    attend_pairs_back(
        ACT.at[Q], ACT.at[K], ACT.at[V], PB1, SL, DH.at[0], DH.at[1], DH.at[2], 0, width // 256
    )
    tick((4, 1), (1, 2))
    attend_pairs_back(
        ACT.at[Q], ACT.at[K], ACT.at[V], PB1, SL, DH.at[0], DH.at[1], DH.at[2], width // 256, width // 128
    )
    store_part(5, ACT[N1], DH[0])
    tick((0, 3), (2, 2))
    store_part(6, ACT[N1], DH[1])
    tick((5, 1), (1, 3), (3, 2), (0, 4))
    store_part(7, ACT[N1], DH[2])
    tick((6, 1), (2, 3), (4, 2), (1, 4), (0, 5))
    slope = None
    for i in range(3):
        w = use(3 + i)
        term = mm(DH[i, :, :cols], w[0], NT) + mm(DH[i, :, cols:], w[1], NT)
        slope = term if slope is None else slope + term
    tick((7, 1), (3, 3), (5, 2), (2, 4), (1, 5), (0, 6))
    next_mid.wait()
    back, g_gain, g_shift = norm_back(slope, X[...], gain(0))
    spread(0, g_gain)
    spread(1, g_shift)
    back += UP[...]
    for h in range(2):
        tg_out[h] = back[h * (rows // 2) : (h + 1) * (rows // 2)]

    def vec_move(j):
        other = lax.rem(me + j, count)
        at = pl.ds(pl.multiple_of(other * (width // count) // 128 * 128, 128), 128)
        return remote(VG.at[:, at], VR.at[j], vs.at[j], vr.at[j], (other // 2, lax.rem(other, 2)))

    @pl.loop(1, count)
    def _(j):
        vec_move(j).start()

    tick((6, 2), (4, 3), (3, 4), (2, 5), (1, 6), (0, 7))
    slope = None
    for i in range(2):
        w = use(6 + i)
        term = mm(DC[i, :, :cols], w[0], NT) + mm(DC[i, :, cols:], w[1], NT)
        slope = term if slope is None else slope + term
    for h in range(2):
        eg_out[h] = slope[h * (short // 2) : (h + 1) * (short // 2)]
    for j in range(3):
        y_move(j).wait_recv()
        for h in range(2):
            res_out[h] += YR[j, h * (rows // 2) : (h + 1) * (rows // 2)].astype(jnp.float32)
    XS[0] = res_out[oy].astype(low_type)
    XS[1] = tg_out[oy].astype(low_type)
    ES[...] = eg_out[oy].astype(low_type)
    swaps = [
        remote(XS, XR, ss.at[0], sr.at[0], p.yn()),
        remote(ES, ER, ss.at[1], sr.at[1], p.yn()),
    ]
    tick((7, 2), (5, 3), (4, 4), (3, 5), (2, 6), (1, 7))
    for copy in swaps:
        copy.start()
    tick((6, 3), (5, 4), (4, 5), (3, 6), (2, 7))
    tick((7, 3), (6, 4), (5, 5), (4, 6), (3, 7))
    tick((7, 4), (6, 5), (5, 6), (4, 7))
    tick((7, 5), (6, 6), (5, 7))
    tick((7, 6), (6, 7))
    tick((7, 7))
    while clock[0] < FF_PARTS + 2 * depth + 1:
        tick()
    at = pl.ds(pl.multiple_of(me * (width // count) // 128 * 128, 128), 128)
    vec_out[...] = VG[:, at]

    @pl.loop(1, count)
    def _(j):
        vec_move(j).wait()
        vec_out[...] += VR[j]

    for copy in swaps:
        copy.wait()
    res_out[oy] = XR[0].astype(jnp.float32)
    tg_out[oy] = XR[1].astype(jnp.float32)
    eg_out[oy] = ER[...].astype(jnp.float32)
    for i in range(PIECES):
        if i >= PIECES - 2:
            core(i).wait_send()
        for h in range(2):
            diagonal(i, h).wait_send()
            column(i, h).wait_send()
        lines[i].sent()
    for line in ff:
        line.sent()
    for j in range(3):
        y_move(j).wait_send()


def backward_all(G, act, ctx, mid, p1, p2, full, g3, d_in, y_in, go_in, S_in, YS_in):
    depth = G.shape[2]
    count = 8 * depth
    rows, cols = G.shape[5:]
    length, width = d_in.shape
    short = ctx.shape[1]
    bf, f32 = jnp.bfloat16, jnp.float32
    dma = pltpu.SemaphoreType.DMA
    vm = pl.BlockSpec(memory_space=VMEM)
    hb = pl.BlockSpec(memory_space=HBM)
    return pl.pallas_call(
        functools.partial(backward_kernel, depth),
        out_shape=[
            jax.ShapeDtypeStruct((PIECES, rows, cols), f32),
            jax.ShapeDtypeStruct((8, 128), f32),
            jax.ShapeDtypeStruct((2, length // 2, width), f32),
            jax.ShapeDtypeStruct((2, length // 2, width), f32),
            jax.ShapeDtypeStruct((2, short // 2, width), f32),
            jax.ShapeDtypeStruct(go_in.shape, f32),
        ],
        in_specs=[hb] * 6 + [vm] + [hb] * 6,
        out_specs=[vm] * 6,
        scratch_shapes=[
            pltpu.VMEM((PIECES, 2, depth, 2, rows, cols), bf),
            pltpu.VMEM((2, 2, depth, 2, rows, cols), bf),
            pltpu.VMEM((SLOTS, 2, depth, 2, rows, cols), bf),
            pltpu.VMEM((PIECES, 2, depth, rows // 2, cols), bf),
            pltpu.VMEM((PIECES, 2, depth, rows, cols), bf),
            pltpu.VMEM((PIECES, depth + 1, rows, cols), bf),
            pltpu.VMEM(S_in.shape, bf),
            pltpu.VMEM((2 * depth - 4,) + S_in.shape[1:], bf),
            pltpu.VMEM(YS_in.shape, bf),
            pltpu.VMEM(YS_in.shape, bf),
            pltpu.VMEM((2,) + G.shape[1:], bf),
            pltpu.VMEM((8, length, width), bf),
            pltpu.VMEM(ctx.shape, bf),
            pltpu.VMEM((length, width), f32),
            pltpu.VMEM(p1.shape, bf),
            pltpu.VMEM(p2.shape, bf),
            pltpu.VMEM((length, width), f32),
            pltpu.VMEM((length, width), bf),
            pltpu.VMEM((length, width), bf),
            pltpu.VMEM((3, length, width), bf),
            pltpu.VMEM((2, short, width), bf),
            pltpu.VMEM((2, length // 2, width), bf),
            pltpu.VMEM((8, width), f32),
            pltpu.VMEM((count, 8, 128), f32),
            pltpu.VMEM((2, length // 2, width), bf),
            pltpu.VMEM((2, length // 2, width), bf),
            pltpu.VMEM((short // 2, width), bf),
            pltpu.VMEM((short // 2, width), bf),
            dma((12,)), dma((2,)),
            dma((PIECES,)), dma((PIECES,)),
            dma((PIECES, 2)), dma((PIECES, 2)),
            dma((PIECES, 2)), dma((PIECES, 2)),
            dma((PIECES, depth)), dma((PIECES, depth + 1)),
            dma((FF_PARTS, depth)), dma((FF_PARTS, 2 * depth - 4)),
            dma((3,)), dma((3,)),
            dma((count,)), dma((count,)),
            dma((2,)), dma((2,)),
            pltpu.SemaphoreType.REGULAR,
        ],
        compiler_params=pltpu.CompilerParams(
            collective_id=3, has_side_effects=True, vmem_limit_bytes=63 << 20
        ),
        name="backward_all",
    )(G, act, ctx, mid, p1, p2, full, g3, d_in, y_in, go_in, S_in, YS_in)


def fast_local(
    tokens, encoder, target_doc, source_doc, self_proj, self_out, cross_query, cross_pairs, cross_out,
    hidden_in, hidden_in_bias, hidden_out, hidden_out_bias, self_gain, self_shift, cross_gain, cross_shift,
    hidden_gain, hidden_shift, cotangent,
):
    depth = lax.axis_size("dp") // 4
    count = 8 * depth
    place = Place()
    me = place.dp * 2 + place.y
    bf, f32 = jnp.bfloat16, jnp.float32
    attn = jnp.stack([
        self_proj[:, 0], self_proj[:, 1], self_proj[:, 2], self_out.T,
        cross_pairs[:, 0], cross_pairs[:, 1], cross_query, cross_out.T,
    ])
    vectors = jnp.stack(
        [self_gain, self_shift, cross_gain, cross_shift, hidden_gain, hidden_shift, hidden_out_bias]
    )
    span = vectors.shape[1]
    group = 128 // span
    lane = lax.broadcasted_iota(jnp.int32, (1, 128), 1)
    mine = lane // span == lax.rem(me, group)
    vec = jnp.concatenate([
        jnp.where(mine, jnp.tile(vectors, (1, group)), 0.0),
        jnp.zeros((1, 128), f32),
        hidden_in_bias.astype(f32).reshape(-1, 128),
    ])
    vec = jnp.pad(vec, ((0, -vec.shape[0] % 8), (0, 0)))
    length, short, width = 2 * tokens.shape[1], 2 * encoder.shape[1], tokens.shape[2]
    target = lax.dynamic_index_in_dim(target_doc, place.y, 0, keepdims=False)
    source = lax.dynamic_index_in_dim(source_doc, place.y, 0, keepdims=False)
    tcol = jnp.broadcast_to(target[:, None], (length, 128))
    trow = jnp.broadcast_to(target[None, :], (8, length))
    srow = jnp.broadcast_to(source[None, :], (8, short))
    G, win, wout, g3, act, ctx, mid, probs1, probs2, full, bias = forward_all(
        attn, hidden_in, hidden_out, vec, tokens, encoder, cotangent, tcol, trow, srow
    )
    d_in, y_in, go, gbias, S, YS = hidden_block(act, bias, win, wout, g3)
    gw, vout, res, tg, eg, go = backward_all(
        G, act, ctx, mid, probs1, probs2, full, g3, d_in, y_in, go, S, YS
    )
    vout = lax.dynamic_slice_in_dim(vout, lax.rem(me, group) * span, span, axis=1)
    return (
        res, tg, eg,
        jnp.stack([gw[5], gw[6], gw[7]], axis=1),
        gw[4].T, gw[1], jnp.stack([gw[2], gw[3]], axis=1), gw[0].T,
        go[0].T, gbias[0], go[1],
        vout[6], vout[0], vout[1], vout[2], vout[3], vout[4], vout[5],
    )


BLOCK_ROWS = 512


def smooth_gate(values):
    return jax.nn.gelu(values, approximate=True)


def plain_norm_forward(hidden, norm_gain, norm_shift):
    center = hidden - jnp.mean(hidden, axis=-1, keepdims=True)
    inverse = lax.rsqrt(jnp.mean(center * center, axis=-1, keepdims=True) + EPS)
    normal = center * inverse
    return (normal * norm_gain + norm_shift, normal, inverse)


def plain_norm_backward(upward, normal, inverse, norm_gain):
    scaled = upward * norm_gain
    centred = (
        scaled
        - jnp.mean(scaled, axis=-1, keepdims=True)
        - normal * jnp.mean(scaled * normal, axis=-1, keepdims=True)
    )
    return (centred * inverse, jnp.sum(upward * normal, axis=0), jnp.sum(upward, axis=0))


def split_blocks(array):
    row_count = array.shape[0]
    block_size = min(BLOCK_ROWS, row_count)
    return array.reshape((row_count // block_size, block_size) + array.shape[1:])


def block_scores(query_block, key_rows, allow_block):
    query_heads = query_block.reshape(query_block.shape[0], -1, HEAD)
    key_heads = key_rows.reshape(key_rows.shape[0], -1, HEAD)
    scores = jnp.einsum(
        "qhd,khd->hqk", query_heads, key_heads, preferred_element_type=jnp.float32
    ) * HEAD ** (-0.5)
    return jnp.where(allow_block[None], scores, NEGATIVE)


def plain_attend(queries, key_rows, values, allowed):
    columns = queries.shape[1]
    value_heads = values.reshape(values.shape[0], -1, HEAD)

    def one_block(pieces):
        query_block, allow_block = pieces
        scores = block_scores(query_block, key_rows, allow_block)
        highest = jnp.max(scores, axis=-1, keepdims=True)
        exponent = jnp.exp(scores - highest)
        totals = jnp.sum(exponent, axis=-1, keepdims=True)
        softmaxed = (exponent / totals).astype(jnp.bfloat16)
        mixture = jnp.einsum(
            "hqk,khd->qhd", softmaxed, value_heads, preferred_element_type=jnp.float32
        )
        return (
            mixture.reshape(query_block.shape[0], columns).astype(jnp.bfloat16),
            (highest + jnp.log(totals))[..., 0],
        )

    mixture, logsum = lax.map(one_block, (split_blocks(queries), split_blocks(allowed)))
    return (mixture.reshape(queries.shape), logsum)


def plain_attend_backward(queries, key_rows, values, allowed, logsum, slope_heads):
    scaling = HEAD ** (-0.5)
    key_heads = key_rows.reshape(key_rows.shape[0], -1, HEAD)
    value_heads = values.reshape(values.shape[0], -1, HEAD)

    def one_block(running, pieces):
        key_total, value_total = running
        query_block, allow_block, logsum_block, slope_block = pieces
        scores = block_scores(query_block, key_rows, allow_block)
        softmaxed = jnp.exp(scores - logsum_block[..., None])
        query_heads = query_block.reshape(query_block.shape[0], -1, HEAD)
        slope_out = slope_block.reshape(slope_block.shape[0], -1, HEAD)
        slope_probs = jnp.einsum(
            "qhd,khd->hqk", slope_out, value_heads, preferred_element_type=jnp.float32
        )
        centred = jnp.sum(softmaxed * slope_probs, axis=-1, keepdims=True)
        slope_scores = (softmaxed * (slope_probs - centred)).astype(jnp.bfloat16)
        slope_query = (
            jnp.einsum("hqk,khd->qhd", slope_scores, key_heads, preferred_element_type=jnp.float32)
            * scaling
        )
        key_total = (
            key_total
            + jnp.einsum(
                "hqk,qhd->khd", slope_scores, query_heads, preferred_element_type=jnp.float32
            )
            * scaling
        )
        value_total = value_total + jnp.einsum(
            "hqk,qhd->khd",
            softmaxed.astype(jnp.bfloat16),
            slope_out,
            preferred_element_type=jnp.float32,
        )
        return (
            (key_total, value_total),
            slope_query.reshape(query_block.shape[0], -1).astype(jnp.bfloat16),
        )

    empty_heads = jnp.zeros(key_heads.shape, jnp.float32)
    (key_total, value_total), slope_query = lax.scan(
        one_block,
        (empty_heads, empty_heads),
        (split_blocks(queries), split_blocks(allowed), logsum, split_blocks(slope_heads)),
    )
    return (
        slope_query.reshape(queries.shape),
        key_total.reshape(key_rows.shape).astype(jnp.bfloat16),
        value_total.reshape(values.shape).astype(jnp.bfloat16),
    )


def gather_rows(local_rows):
    return lax.all_gather(local_rows, "tensor", axis=0, tiled=True)


def sum_rows(partial_sum):
    return lax.psum_scatter(
        partial_sum.astype(jnp.bfloat16), "tensor", scatter_dimension=0, tiled=True
    ).astype(jnp.float32)


def gather_slopes(local_slopes):
    return lax.all_gather(local_slopes, "tensor", axis=0, tiled=True)


def sum_slopes(partial_sum):
    return lax.psum_scatter(
        partial_sum.astype(jnp.bfloat16), "tensor", scatter_dimension=0, tiled=True
    ).astype(jnp.float32)


def reduce_weights(weight_terms):
    return (
        lax.psum_scatter(weight_terms[0], "dp", scatter_dimension=0, tiled=True),
        lax.psum_scatter(weight_terms[1], "dp", scatter_dimension=1, tiled=True),
        lax.psum_scatter(weight_terms[2], "dp", scatter_dimension=0, tiled=True),
        lax.psum_scatter(weight_terms[3], "dp", scatter_dimension=0, tiled=True),
        lax.psum_scatter(weight_terms[4], "dp", scatter_dimension=1, tiled=True),
        lax.psum_scatter(weight_terms[5], "dp", scatter_dimension=1, tiled=True),
        lax.psum_scatter(weight_terms[6], "dp", scatter_dimension=0, tiled=True),
        lax.psum_scatter(weight_terms[7], "dp", scatter_dimension=0, tiled=True),
    )


def plain_local(
    tokens,
    encoder,
    target_doc,
    source_doc,
    self_proj,
    self_out,
    cross_query,
    cross_pairs,
    cross_out,
    hidden_in,
    hidden_in_bias,
    hidden_out,
    hidden_out_bias,
    self_gain,
    self_shift,
    cross_gain,
    cross_shift,
    hidden_gain,
    hidden_shift,
    cotangent,
):
    (
        full_self_gain,
        full_self_shift,
        full_cross_gain,
        full_cross_shift,
        full_hidden_gain,
        full_hidden_shift,
        full_out_bias,
    ) = (
        lax.all_gather(self_gain, ("dp", "tensor"), axis=0, tiled=True),
        lax.all_gather(self_shift, ("dp", "tensor"), axis=0, tiled=True),
        lax.all_gather(cross_gain, ("dp", "tensor"), axis=0, tiled=True),
        lax.all_gather(cross_shift, ("dp", "tensor"), axis=0, tiled=True),
        lax.all_gather(hidden_gain, ("dp", "tensor"), axis=0, tiled=True),
        lax.all_gather(hidden_shift, ("dp", "tensor"), axis=0, tiled=True),
        lax.all_gather(hidden_out_bias, ("dp", "tensor"), axis=0, tiled=True),
    )
    micro_count = tokens.shape[0]
    row_count = tokens.shape[1] * lax.axis_size("tensor")
    positions = jnp.arange(row_count)
    results = []
    token_grads = []
    encoder_grads = []
    vector_total = None
    weight_total = None
    for step_index in range(micro_count):
        forward_weights = (
            lax.all_gather(self_proj, "dp", axis=0, tiled=True),
            lax.all_gather(self_out, "dp", axis=1, tiled=True),
            lax.all_gather(cross_query, "dp", axis=0, tiled=True),
            lax.all_gather(cross_pairs, "dp", axis=0, tiled=True),
            lax.all_gather(cross_out, "dp", axis=1, tiled=True),
            lax.all_gather(hidden_in, "dp", axis=1, tiled=True),
            lax.all_gather(hidden_in_bias, "dp", axis=0, tiled=True),
            lax.all_gather(hidden_out, "dp", axis=0, tiled=True),
        )
        (
            full_proj,
            full_self_out,
            full_query,
            full_pairs,
            full_cross_out,
            full_in,
            full_in_bias,
            full_out,
        ) = forward_weights
        target_row = target_doc[step_index]
        source_row = source_doc[step_index]
        self_allowed = (target_row[:, None] == target_row[None, :]) & (
            positions[None, :] <= positions[:, None]
        )
        cross_allowed = target_row[:, None] == source_row[None, :]
        start_hidden = tokens[step_index].astype(jnp.float32)
        normed_first, normal_first, inverse_first = plain_norm_forward(
            start_hidden, full_self_gain, full_self_shift
        )
        self_rows = gather_rows(normed_first.astype(jnp.bfloat16))
        triple = jnp.einsum(
            "td,dcj->tcj", self_rows, full_proj, preferred_element_type=jnp.float32
        ).astype(jnp.bfloat16)
        self_heads, self_logsum = plain_attend(triple[:, 0], triple[:, 1], triple[:, 2], self_allowed)
        middle = start_hidden + sum_rows(
            jnp.dot(self_heads, full_self_out, preferred_element_type=jnp.float32)
        )
        normed_second, normal_second, inverse_second = plain_norm_forward(
            middle, full_cross_gain, full_cross_shift
        )
        cross_rows, source_rows = (
            lax.all_gather(normed_second.astype(jnp.bfloat16), "tensor", axis=0, tiled=True),
            lax.all_gather(encoder[step_index], "tensor", axis=0, tiled=True),
        )
        cross_queries = jnp.dot(cross_rows, full_query, preferred_element_type=jnp.float32).astype(
            jnp.bfloat16
        )
        key_value = jnp.einsum(
            "sd,dcj->scj", source_rows, full_pairs, preferred_element_type=jnp.float32
        ).astype(jnp.bfloat16)
        cross_heads, cross_logsum = plain_attend(
            cross_queries, key_value[:, 0], key_value[:, 1], cross_allowed
        )
        latter = middle + sum_rows(
            jnp.dot(cross_heads, full_cross_out, preferred_element_type=jnp.float32)
        )
        normed_third, normal_third, inverse_third = plain_norm_forward(
            latter, full_hidden_gain, full_hidden_shift
        )
        hidden_rows = gather_rows(normed_third.astype(jnp.bfloat16))
        before = jnp.dot(
            hidden_rows, full_in, preferred_element_type=jnp.float32
        ) + full_in_bias.astype(jnp.float32)
        gated, gate_pullback = jax.vjp(smooth_gate, before)
        active = gated.astype(jnp.bfloat16)
        results.append(
            latter
            + sum_rows(jnp.dot(active, full_out, preferred_element_type=jnp.float32))
            + full_out_bias
        )
        back_weights = (
            lax.all_gather(self_proj, "dp", axis=0, tiled=True),
            lax.all_gather(self_out, "dp", axis=1, tiled=True),
            lax.all_gather(cross_query, "dp", axis=0, tiled=True),
            lax.all_gather(cross_pairs, "dp", axis=0, tiled=True),
            lax.all_gather(cross_out, "dp", axis=1, tiled=True),
            lax.all_gather(hidden_in, "dp", axis=1, tiled=True),
            lax.all_gather(hidden_in_bias, "dp", axis=0, tiled=True),
            lax.all_gather(hidden_out, "dp", axis=0, tiled=True),
        )
        (
            back_proj,
            back_self_out,
            back_query,
            back_pairs,
            back_cross_out,
            back_in,
            back_in_bias,
            back_out,
        ) = back_weights
        upward = cotangent[step_index].astype(jnp.float32)
        grad_out_bias = jnp.sum(upward, axis=0)
        slope_rows = gather_slopes(upward.astype(jnp.bfloat16))
        grad_out = jnp.einsum("tf,td->fd", active, slope_rows, preferred_element_type=jnp.float32)
        slope_active = jnp.einsum(
            "td,fd->tf", slope_rows, back_out, preferred_element_type=jnp.float32
        )
        slope_before = gate_pullback(slope_active)[0].astype(jnp.bfloat16)
        grad_in_bias = jnp.sum(slope_before.astype(jnp.float32), axis=0)
        grad_in = jnp.einsum(
            "td,tf->df", hidden_rows, slope_before, preferred_element_type=jnp.float32
        )
        slope_normed = sum_slopes(
            jnp.einsum("tf,df->td", slope_before, back_in, preferred_element_type=jnp.float32)
        )
        slope_hidden, grad_hidden_gain, grad_hidden_shift = plain_norm_backward(
            slope_normed, normal_third, inverse_third, full_hidden_gain
        )
        upward = upward + slope_hidden
        slope_rows = gather_slopes(upward.astype(jnp.bfloat16))
        grad_cross_out = jnp.einsum(
            "tj,td->jd", cross_heads, slope_rows, preferred_element_type=jnp.float32
        )
        slope_heads = jnp.einsum(
            "td,jd->tj", slope_rows, back_cross_out, preferred_element_type=jnp.float32
        ).astype(jnp.bfloat16)
        slope_query, slope_keys, slope_values = plain_attend_backward(
            cross_queries,
            key_value[:, 0],
            key_value[:, 1],
            cross_allowed,
            cross_logsum,
            slope_heads,
        )
        slope_pairs = jnp.stack([slope_keys, slope_values], axis=1)
        grad_query = jnp.einsum(
            "td,tj->dj", cross_rows, slope_query, preferred_element_type=jnp.float32
        )
        grad_pairs = jnp.einsum(
            "sd,scj->dcj", source_rows, slope_pairs, preferred_element_type=jnp.float32
        )
        slope_cross, slope_source = (
            lax.psum_scatter(
                jnp.einsum(
                    "tj,dj->td", slope_query, back_query, preferred_element_type=jnp.float32
                ).astype(jnp.bfloat16),
                "tensor",
                scatter_dimension=0,
                tiled=True,
            ).astype(jnp.float32),
            lax.psum_scatter(
                jnp.einsum(
                    "scj,dcj->sd", slope_pairs, back_pairs, preferred_element_type=jnp.float32
                ).astype(jnp.bfloat16),
                "tensor",
                scatter_dimension=0,
                tiled=True,
            ).astype(jnp.float32),
        )
        slope_hidden, grad_cross_gain, grad_cross_shift = plain_norm_backward(
            slope_cross, normal_second, inverse_second, full_cross_gain
        )
        upward = upward + slope_hidden
        slope_rows = gather_slopes(upward.astype(jnp.bfloat16))
        grad_self_out = jnp.einsum(
            "tj,td->jd", self_heads, slope_rows, preferred_element_type=jnp.float32
        )
        slope_heads = jnp.einsum(
            "td,jd->tj", slope_rows, back_self_out, preferred_element_type=jnp.float32
        ).astype(jnp.bfloat16)
        slope_query, slope_keys, slope_values = plain_attend_backward(
            triple[:, 0], triple[:, 1], triple[:, 2], self_allowed, self_logsum, slope_heads
        )
        slope_triple = jnp.stack([slope_query, slope_keys, slope_values], axis=1)
        grad_proj = jnp.einsum(
            "td,tcj->dcj", self_rows, slope_triple, preferred_element_type=jnp.float32
        )
        slope_self = sum_slopes(
            jnp.einsum("tcj,dcj->td", slope_triple, back_proj, preferred_element_type=jnp.float32)
        )
        slope_hidden, grad_self_gain, grad_self_shift = plain_norm_backward(
            slope_self, normal_first, inverse_first, full_self_gain
        )
        token_grads.append(upward + slope_hidden)
        encoder_grads.append(slope_source)
        vector_terms = (
            grad_self_gain,
            grad_self_shift,
            grad_cross_gain,
            grad_cross_shift,
            grad_hidden_gain,
            grad_hidden_shift,
            grad_out_bias,
        )
        vector_total = (
            vector_terms if step_index == 0 else jax.tree.map(jnp.add, vector_total, vector_terms)
        )
        weight_terms = (
            grad_proj,
            grad_self_out,
            grad_query,
            grad_pairs,
            grad_cross_out,
            grad_in,
            grad_in_bias,
            grad_out,
        )
        shard_terms = reduce_weights(weight_terms)
        weight_total = (
            shard_terms if step_index == 0 else jax.tree.map(jnp.add, weight_total, shard_terms)
        )
    vector_shards = (
        lax.psum_scatter(vector_total[0], ("dp", "tensor"), scatter_dimension=0, tiled=True),
        lax.psum_scatter(vector_total[1], ("dp", "tensor"), scatter_dimension=0, tiled=True),
        lax.psum_scatter(vector_total[2], ("dp", "tensor"), scatter_dimension=0, tiled=True),
        lax.psum_scatter(vector_total[3], ("dp", "tensor"), scatter_dimension=0, tiled=True),
        lax.psum_scatter(vector_total[4], ("dp", "tensor"), scatter_dimension=0, tiled=True),
        lax.psum_scatter(vector_total[5], ("dp", "tensor"), scatter_dimension=0, tiled=True),
        lax.psum_scatter(vector_total[6], ("dp", "tensor"), scatter_dimension=0, tiled=True),
    )
    return (
        jnp.stack(results),
        jnp.stack(token_grads),
        jnp.stack(encoder_grads),
        weight_total[0],
        weight_total[1],
        weight_total[2],
        weight_total[3],
        weight_total[4],
        weight_total[5],
        weight_total[6],
        weight_total[7],
        vector_shards[6],
        vector_shards[0],
        vector_shards[1],
        vector_shards[2],
        vector_shards[3],
        vector_shards[4],
        vector_shards[5],
    )


def solution(mesh):
    in_specs = (
        P("dp", "tensor", None),
        P("dp", "tensor", None),
        P("dp", None),
        P("dp", None),
        P("dp", None, "tensor"),
        P("tensor", "dp"),
        P("dp", "tensor"),
        P("dp", None, "tensor"),
        P("tensor", "dp"),
        P(None, ("dp", "tensor")),
        P(("dp", "tensor")),
        P(("dp", "tensor"), None),
        P(("dp", "tensor")),
        P(("dp", "tensor")),
        P(("dp", "tensor")),
        P(("dp", "tensor")),
        P(("dp", "tensor")),
        P(("dp", "tensor")),
        P(("dp", "tensor")),
        P("dp", "tensor", None),
    )
    out_specs = (
        P("dp", "tensor", None),
        P("dp", "tensor", None),
        P("dp", "tensor", None),
        P("dp", None, "tensor"),
        P("tensor", "dp"),
        P("dp", "tensor"),
        P("dp", None, "tensor"),
        P("tensor", "dp"),
        P(None, ("dp", "tensor")),
        P(("dp", "tensor")),
        P(("dp", "tensor"), None),
        P(("dp", "tensor")),
        P(("dp", "tensor")),
        P(("dp", "tensor")),
        P(("dp", "tensor")),
        P(("dp", "tensor")),
        P(("dp", "tensor")),
        P(("dp", "tensor")),
    )

    def run(*arrays):
        width = arrays[0].shape[2]
        aligned = width // mesh.shape["dp"] % 16 == 0 and mesh.shape["dp"] % 4 == 0
        inner = fast_local if aligned and mesh.shape["tensor"] == 2 else plain_local
        return jax.shard_map(inner, mesh=mesh, in_specs=in_specs, out_specs=out_specs, check_vma=False)(*arrays)

    return run
```

```python
import functools

import jax
import jax.numpy as jnp
from jax import lax
from jax.experimental import pallas as pl
from jax.experimental.pallas import tpu as pltpu
from jax.sharding import PartitionSpec as P

HEAD = 64
EPS = 1e-05
NEGATIVE = -1e30
MESH = pl.DeviceIdType.MESH
HBM = pltpu.HBM
VMEM = pltpu.VMEM
PIECES = 8
FF_PIECES = 16


class Place:
    def __init__(self):
        self.dp = lax.axis_index("dp")
        self.y = lax.axis_index("tensor")
        self.c = lax.rem(self.dp, 2)
        self.x = lax.rem(self.dp // 2, 2)
        self.z = self.dp // 4

    def at(self, z=None, x=None, c=None, y=None):
        z = self.z if z is None else z
        x = self.x if x is None else x
        c = self.c if c is None else c
        y = self.y if y is None else y
        return ((z * 2 + x) * 2 + c, y)

    def core(self):
        return self.at(c=1 - self.c)

    def xn(self):
        return self.at(x=1 - self.x)

    def yn(self):
        return self.at(y=1 - self.y)

    def up(self):
        return self.at(z=self.z + 1)

    def down(self):
        return self.at(z=self.z - 1)


def remote(src, dst, send, recv, device):
    return pltpu.make_async_remote_copy(
        src_ref=src, dst_ref=dst, send_sem=send, recv_sem=recv, device_id=device, device_id_type=MESH
    )


def signal(sem, device):
    pl.semaphore_signal(sem, inc=1, device_id=device, device_id_type=MESH)


class LineGather:
    def __init__(self, place, depth, slot, send, recv):
        self.p, self.n, self.slot, self.send, self.recv = place, depth, slot, send, recv

    def _copy_up(self, k):
        b = self.p.z - k
        return remote(self.slot(b), self.slot(b), self.send.at[0, k], self.recv.at[0, k], self.p.up())

    def _copy_down(self, k):
        b = self.p.z + k
        return remote(self.slot(b), self.slot(b), self.send.at[1, k], self.recv.at[1, k], self.p.down())

    def _from_below(self, k):
        b = self.p.z - k
        return remote(self.slot(b), self.slot(b), self.send.at[0, k - 1], self.recv.at[0, k - 1], self.p.up())

    def _from_above(self, k):
        b = self.p.z + k
        return remote(self.slot(b), self.slot(b), self.send.at[1, k - 1], self.recv.at[1, k - 1], self.p.down())

    def arrive(self, k):
        z = self.p.z

        @pl.when(z - k >= 0)
        def _():
            self._from_below(k).wait_recv()

        @pl.when(z + k <= self.n - 1)
        def _():
            self._from_above(k).wait_recv()

    def step(self, k):
        z = self.p.z
        if k > 0:
            self.arrive(k)
        if k < self.n - 1:

            @pl.when((z - k >= 0) & (z < self.n - 1))
            def _():
                self._copy_up(k).start()

            @pl.when((z + k <= self.n - 1) & (z > 0))
            def _():
                self._copy_down(k).start()

    def sent(self):
        z = self.p.z
        for k in range(self.n - 1):

            @pl.when((z - k >= 0) & (z < self.n - 1))
            def _():
                self._copy_up(k).wait_send()

            @pl.when((z + k <= self.n - 1) & (z > 0))
            def _():
                self._copy_down(k).wait_send()


class PlaneGather:
    def __init__(self, place, slot, send, recv):
        self.p, self.slot, self.send, self.recv = place, slot, send, recv
        p = place
        x, y, c = p.x, p.y, p.c
        ox, oy = 1 - x, 1 - y
        self.moves = [
            ((x, c, y, None), p.xn(), 0),
            ((x, c, y, None), p.yn(), 1),
            ((ox, c, y, 0), p.yn(), 2),
            ((x, c, oy, 1), p.xn(), 3),
            ((x, c, y, None), p.core(), 4),
            ((ox, c, y, None), p.core(), 5),
            ((x, c, oy, None), p.core(), 6),
            ((ox, c, oy, None), p.core(), 7),
        ]
        oc = 1 - c
        self.arrivals = [
            (ox, c, y, None),
            (x, c, oy, None),
            (ox, c, oy, 0),
            (ox, c, oy, 1),
            (x, oc, y, None),
            (ox, oc, y, None),
            (x, oc, oy, None),
            (ox, oc, oy, None),
        ]

    def _move(self, i):
        where, device, s = self.moves[i]
        return remote(self.slot(*where), self.slot(*where), self.send.at[s], self.recv.at[s], device)

    def _arrival(self, i):
        view = self.slot(*self.arrivals[i])
        return remote(view, view, self.send.at[i], self.recv.at[i], self.moves[i][1])

    def begin(self):
        self._move(0).start()
        self._move(1).start()
        self._move(4).start()

    def forward(self):
        self._arrival(0).wait_recv()
        self._move(2).start()
        self._move(5).start()
        self._arrival(1).wait_recv()
        self._move(3).start()
        self._move(6).start()

    def finish(self):
        self._arrival(2).wait_recv()
        self._arrival(3).wait_recv()
        self._move(7).start()

    def end(self):
        for i in range(4, 8):
            self._arrival(i).wait_recv()

    def sent(self):
        for i in range(8):
            self._move(i).wait_send()


def all_barrier(place, count):
    sem = pltpu.get_barrier_semaphore()
    me = place.dp * 2 + place.y

    @pl.loop(1, count)
    def _(j):
        other = lax.rem(me + j, count)
        signal(sem, (other // 2, lax.rem(other, 2)))

    pl.semaphore_wait(sem, count - 1)


def far_first(z, s, depth):
    b = 0
    for place in range(depth):
        order = sorted(range(depth), key=lambda k: (-abs(k - place), k))
        b = jnp.where(z == place, order[s], b)
    return b


class LineReduce:
    def __init__(self, place, depth, part, slots, send, recv):
        self.p, self.n, self.part, self.slots, self.send, self.recv = place, depth, part, slots, send, recv

    def _up(self, b):
        slot = b - (self.p.z + 1)
        return remote(self.part(b), self.slots(slot), self.send.at[b], self.recv.at[slot], self.p.up())

    def _down(self, b):
        slot = self.n - b
        return remote(self.part(b), self.slots(slot), self.send.at[b], self.recv.at[slot], self.p.down())

    def below(self, b):
        slot = b - self.p.z
        return remote(self.slots(slot), self.slots(slot), self.send.at[b], self.recv.at[slot], self.p.up())

    def above(self, b):
        slot = self.n - b
        return remote(self.slots(slot), self.slots(slot), self.send.at[b], self.recv.at[slot], self.p.down())

    def first(self, b):
        z = self.p.z

        @pl.when((z == 0) & (b > z))
        def _():
            self._up(b).start()

        @pl.when((z == self.n - 1) & (b < z))
        def _():
            self._down(b).start()

    def middle(self, b, add):
        z = self.p.z

        @pl.when((z > 0) & (b > z))
        def _():
            self.below(b).wait_recv()
            add(self.part(b), self.slots(b - z))
            self._up(b).start()

        @pl.when((z < self.n - 1) & (b < z))
        def _():
            self.above(b).wait_recv()
            add(self.part(b), self.slots(self.n - b))
            self._down(b).start()

    def last(self, take):
        z = self.p.z

        @pl.when(z > 0)
        def _():
            self.below(z).wait_recv()
            take(self.slots(0))

        @pl.when(z < self.n - 1)
        def _():
            self.above(z).wait_recv()
            take(self.slots(self.n - z))

    def sent(self):
        z = self.p.z

        @pl.loop(0, self.n)
        def _(b):
            @pl.when(b > z)
            def _():
                self._up(b).wait_send()

            @pl.when(b < z)
            def _():
                self._down(b).wait_send()


def add_low(part, other):
    part[...] = (part[...].astype(jnp.float32) + other[...].astype(jnp.float32)).astype(part.dtype)


def gelu_pair(x):
    a, b = 0.7978845608028654, 0.044715
    square = x * x
    t = jnp.tanh(a * x * (1.0 + b * square))
    half = 0.5 * (1.0 + t)
    return x * half, half + 0.5 * x * (1.0 - t * t) * (a * (1.0 + 3.0 * b * square))


NN = (((1,), (0,)), ((), ()))
NT = (((1,), (1,)), ((), ()))
TN = (((0,), (0,)), ((), ()))


def mm(left, right, form=NN):
    return lax.dot_general(left, right, form, preferred_element_type=jnp.float32)


def neighbour_barrier(p, depth):
    sem = pltpu.get_barrier_semaphore()
    for dx in range(2):
        for dc in range(2):
            for dy in range(2):
                if dx + dc + dy:
                    signal(sem, p.at(x=lax.rem(p.x + dx, 2), c=lax.rem(p.c + dc, 2), y=lax.rem(p.y + dy, 2)))

    @pl.loop(1, depth)
    def _(k):
        signal(sem, p.at(z=lax.rem(p.z + k, depth)))

    pl.semaphore_wait(sem, 7 + depth - 1)


def layer_norm(x, gain, shift):
    center = x - jnp.mean(x, axis=-1, keepdims=True)
    inverse = lax.rsqrt(jnp.mean(center * center, axis=-1, keepdims=True) + EPS)
    return center * inverse * gain + shift


def attend_pairs(q_ref, k_ref, v_ref, allowed, probs_ref, heads_ref, start, stop):
    rows = q_ref.shape[0]
    first = lax.broadcasted_iota(jnp.int32, (rows, 128), 1) < HEAD
    both = jnp.concatenate([allowed, allowed], axis=0)

    @pl.loop(start, stop)
    def _(h):
        at = (slice(None), pl.ds(pl.multiple_of(h * 128, 128), 128))
        q, k, v = q_ref[at], k_ref[at], v_ref[at]
        zero = jnp.zeros_like(q)
        pair = jnp.concatenate([jnp.where(first, q, zero), jnp.where(first, zero, q)], axis=0)
        scores = jnp.where(both, mm(pair, k, NT) * HEAD**-0.5, NEGATIVE)
        weights = jnp.exp(scores - jnp.max(scores, axis=-1, keepdims=True))
        probs = (weights * (1.0 / jnp.sum(weights, axis=-1, keepdims=True))).astype(jnp.bfloat16)
        probs_ref[h] = probs
        mix = mm(probs, v)
        heads_ref[at] = jnp.where(first, mix[:rows], mix[rows:]).astype(jnp.bfloat16)


Q, K, V, CQ, H1, H2, N1, N2, N3 = range(9)
CK, CV, ENC = range(3)


def forward_kernel(
    depth,
    proj, so, pairs_in, query, co, win, wout, vec, tok_in, enc_in, cot, target, source,
    G, act_out, ctx_out, mid_out, p1_out, p2_out, full_out, cot_out,
    d_out, y_out, go_out, gbias_out, S_out, YS_out,
    ATT, W, TOK, VEC, FULL, BIAS, ACT, CTX, MID, P1, P2, TARGET, SOURCE, OWN_T, OWN_E,
    HN, G3, WI, WO, S, RF, ACTIVE, SLOPE, BS, BR, CS, CR, CSY, CRY, PS, PR, DSUM, YSUM, GO, GB, LATS, LATR,
    lsem, wsem, osem, zs, zr, fs, fr, ps, pr, vs, vr, ss, sr, gs, gr, hs, hr, bs, br, cs, cr, ys, yr, xs, xr,
):
    p = Place()
    z = p.z
    count = 8 * depth
    me = p.dp * 2 + p.y
    rows, width = ACT.shape[1:]
    short = CTX.shape[1]
    units = WO.shape[1]
    half, few = rows // 2, short // 2
    part = ATT.shape[1]
    mine = pl.ds(pl.multiple_of(p.y * few, few), few)
    local = []

    def keep(src, dst):
        copy = pltpu.make_async_copy(src, dst, lsem.at[len(local)])
        copy.start()
        local.append(copy)

    keep(vec, VEC.at[me])
    keep(tok_in, OWN_T)
    keep(enc_in, OWN_E)
    keep(proj, ATT.at[pl.ds(0, 3)])
    keep(so, ATT.at[3])
    keep(pairs_in, ATT.at[pl.ds(4, 2)])
    keep(query, ATT.at[6])
    keep(co, ATT.at[7])
    keep(cot, G3.at[p.x, p.c, :, p.y])
    keep(win, WI.at[:, pl.ds(pl.multiple_of(z * units, units), units)])
    keep(wout, WO.at[z])
    keep(target, TARGET)
    keep(source, SOURCE)
    BS[...] = jnp.zeros_like(BS)
    all_barrier(p, count)
    for copy in local:
        copy.wait()
    TOK[p.y] = OWN_T[p.y]
    CTX[ENC, mine] = OWN_E[p.y]
    own = pltpu.make_async_copy(ATT, G.at[:, p.y, z, p.x, p.c], lsem.at[0])
    own.start()

    lines = []
    for i in range(PIECES):
        lines.append(LineGather(p, depth, lambda b, i=i: G.at[i, p.y, b, p.x, p.c], zs.at[i], zr.at[i]))
    wr = WI.shape[0] // (FF_PIECES // 2)
    orow = units // (FF_PIECES // 2)
    ff = []
    for i in range(FF_PIECES):
        if i < FF_PIECES // 2:
            slot = lambda b, i=i: WI.at[pl.ds(i * wr, wr), pl.ds(pl.multiple_of(b * units, units), units)]
        else:
            slot = lambda b, i=i: WO.at[b, pl.ds((i - FF_PIECES // 2) * orow, orow)]
        ff.append(LineGather(p, depth, slot, fs.at[i], fr.at[i]))

    def plane_slot(i):
        def slot(x, c, y, h):
            if h is None:
                return G.at[i, y, :, x, c]
            return G.at[i, y, :, x, c, pl.ds(h * (part // 2), part // 2)]

        return slot

    def g3_slot(r):
        few_rows = G3.shape[4] // 2

        def slot(x, c, y, h):
            if h is None:
                return G3.at[x, c, r, y]
            return G3.at[x, c, r, y, pl.ds(h * few_rows, few_rows)]

        return slot

    slots = [g3_slot(0)] + [plane_slot(i) for i in range(PIECES)] + [g3_slot(1)]
    planes = [PlaneGather(p, slot, ps.at[i], pr.at[i]) for i, slot in enumerate(slots)]
    swaps = [
        remote(OWN_T.at[1 - p.y], TOK.at[p.y], ss.at[0], sr.at[0], p.yn()),
        remote(OWN_E.at[1 - p.y], CTX.at[ENC, mine], ss.at[1], sr.at[1], p.yn()),
    ]

    def swapped(i):
        if i == 0:
            view = TOK.at[1 - p.y]
        else:
            view = CTX.at[ENC, pl.ds(pl.multiple_of((1 - p.y) * few, few), few)]
        remote(view, view, ss.at[i], sr.at[i], p.yn()).wait_recv()

    swaps[0].start()

    def vec_move(j):
        other = lax.rem(me + j, count)
        return remote(VEC.at[me], VEC.at[me], vs.at[j], vr.at[j], (other // 2, lax.rem(other, 2)))

    @pl.loop(1, count)
    def _(j):
        vec_move(j).start()

    own.wait()

    saved = []

    def save(src, dst):
        copy = pltpu.make_async_copy(src, dst, osem.at[len(saved)])
        copy.start()
        saved.append(copy)

    def vector(i):
        return FULL[i : i + 1]

    def weight(i):
        copy = pltpu.make_async_copy(G.at[i], W, wsem.at[0])
        copy.start()
        copy.wait()

    def project(a, store):
        for y in range(2):
            store(y * (width // 2), mm(a, W[y].reshape(width, width // 2)))

    def project_back(a_ref):
        total = None
        for y in range(2):
            term = mm(a_ref[:, y * (width // 2) : (y + 1) * (width // 2)], W[y].reshape(width, width // 2), NT)
            total = term if total is None else total + term
        return total

    def into(ref, i):
        def store(at, value):
            ref[i, :, at : at + width // 2] = value.astype(jnp.bfloat16)

        return store

    def first_norm():
        @pl.loop(1, count)
        def _(j):
            other = lax.rem(me + count - j, count)
            remote(VEC.at[other], VEC.at[other], vs.at[j], vr.at[j], p.yn()).wait_recv()

        group = count * 128 // width
        for k in range(width // 128):
            piece = VEC[group * k, 0:8]
            for j in range(1, group):
                piece += VEC[group * k + j, 0:8]
            FULL[:, k * 128 : (k + 1) * 128] = piece
        save(FULL, full_out)
        for b in range(depth):
            held = VEC[((b * 2 + p.x) * 2 + p.c) * 2 + p.y]
            for k in range(units // 128):
                at = b * units + k * 128
                BIAS[:, at : at + 128] = jnp.broadcast_to(held[8 + k : 9 + k], (8, 128))
        swapped(0)
        tok = TOK[...].reshape(rows, width).astype(jnp.float32)
        MID[0] = tok
        ACT[N1] = layer_norm(tok, vector(0), vector(1)).astype(jnp.bfloat16)
        save(ACT.at[N1], act_out.at[N1])

    def qkv(i):
        weight(i)
        project(ACT[N1], into(ACT, (Q, K, V)[i]))
        save(ACT.at[(Q, K, V)[i]], act_out.at[(Q, K, V)[i]])

    def same(left, right):
        def pair(ref):
            row = ref[pl.ds(p.y, 1)].astype(jnp.float32)
            rest = jnp.zeros((14, row.shape[1]), jnp.float32)
            return jnp.concatenate([row, 1.0 - row, rest], axis=0).astype(jnp.bfloat16)

        return mm(pair(left), pair(right), TN) > 0.5

    pairs_of_heads = width // 128

    def self_attention(start, stop):
        back = lax.broadcasted_iota(jnp.int32, (rows, rows), 1) <= lax.broadcasted_iota(jnp.int32, (rows, rows), 0)
        attend_pairs(
            ACT.at[Q], ACT.at[K], ACT.at[V], same(TARGET, TARGET) & back, P1, ACT.at[H1], start, stop
        )

    def self_project():
        self_attention(pairs_of_heads // 2, pairs_of_heads)
        save(P1, p1_out)
        save(ACT.at[H1], act_out.at[H1])
        weight(3)
        middle = MID[0] + project_back(ACT.at[H1])
        MID[1] = middle
        ACT[N2] = layer_norm(middle, vector(2), vector(3)).astype(jnp.bfloat16)
        save(MID.at[pl.ds(0, 2)], mid_out.at[pl.ds(0, 2)])
        save(ACT.at[N2], act_out.at[N2])

    def pairs(i):
        if i == 0:
            swapped(1)
        weight(4 + i)
        project(CTX[ENC], into(CTX, (CK, CV)[i]))

    def cross_attention():
        save(CTX, ctx_out)
        weight(6)
        project(ACT[N2], into(ACT, CQ))
        save(ACT.at[CQ], act_out.at[CQ])
        attend_pairs(
            ACT.at[CQ], CTX.at[CK], CTX.at[CV], same(TARGET, SOURCE), P2, ACT.at[H2], 0, pairs_of_heads
        )
        save(P2, p2_out)
        save(ACT.at[H2], act_out.at[H2])

    def hn_slot(x, c, y, h):
        if h is None:
            return HN.at[x, c, y]
        return HN.at[x, c, y, pl.ds(h * half, half)]

    gather = PlaneGather(p, hn_slot, gs, gr)

    def cross_project():
        weight(7)
        latter = MID[1] + project_back(ACT.at[H2])
        HN[p.x, p.c, p.y] = layer_norm(latter, vector(4), vector(5)).astype(jnp.bfloat16)
        gather.begin()
        MID[2] = latter
        save(MID.at[2], mid_out.at[2])
        LATS[...] = MID[2, pl.ds(pl.multiple_of((1 - p.y) * half, half), half)].astype(jnp.bfloat16)

    work = {
        0: [functools.partial(qkv, 0)],
        1: [functools.partial(qkv, 1)],
        2: [functools.partial(qkv, 2), functools.partial(self_attention, 0, pairs_of_heads // 2)],
        3: [self_project],
        4: [functools.partial(pairs, 0)],
        5: [functools.partial(pairs, 1)],
        6: [cross_attention],
        7: [cross_project],
    }
    lead = depth - 2
    turns = 2 * (lead + len(planes) + 3)
    early, late = 2 * lead, 2 * lead + 2 * PIECES - 2
    starts = list(range(early)) + list(range(early, late, 3))
    starts += list(range(late, late + FF_PIECES - len(starts)))

    def turn(n):
        for f in range(FF_PIECES):
            k = n - starts[f]
            if k % 2 == 0 and 0 <= k < 2 * depth:
                ff[f].step(k // 2)

    for it in range(-lead, len(planes) + 3):
        for i in range(PIECES):
            if 0 <= it - i + lead < depth:
                lines[i].step(it - i + lead)
        if 0 <= it < len(planes):
            planes[it].begin()
        turn(2 * (it + lead))
        if it == 0:
            swaps[1].start()
        if 0 <= it - 1 < len(planes):
            planes[it - 1].forward()
        if 0 <= it - 2 < len(planes):
            planes[it - 2].finish()
        turn(2 * (it + lead) + 1)
        if 0 <= it - 3 < len(planes):
            planes[it - 3].end()
        if it == 1:
            first_norm()
        for task in work.get(it - 4, []):
            task()

    def bits(code):
        dc, dx, dy = code // 4, lax.rem(code // 2, 2), lax.rem(code, 2)
        return lax.rem(p.x + dx, 2), lax.rem(p.c + dc, 2), lax.rem(p.y + dy, 2)

    arriving = (0, 4, 1, 2, 5, 6, 3, 7)

    def to_core(j, send, land, a, b):
        return remote(send.at[j], land.at[j], a.at[j], b.at[j], p.core())

    def to_chip(j):
        dx, dy = 1 - j // 2, 1 - lax.rem(j, 2)
        return remote(
            PS.at[j], PR.at[j], xs.at[j], xr.at[j], p.at(x=lax.rem(p.x + dx, 2), y=lax.rem(p.y + dy, 2))
        )

    latter_move = remote(LATS, LATR, ss.at[2], sr.at[2], p.yn())

    def bias_move(b):
        return remote(BS.at[b], BR.at[z], bs.at[b], br.at[z], p.at(z=b))

    up = remote(S.at[depth - 1, 0], RF, hs.at[0], hr.at[0], p.up())
    down = remote(S.at[0, 0], RF, hs.at[0], hr.at[0], p.down())

    @pl.loop(0, 8)
    def _(i):
        @pl.when(i == 1)
        def _():
            gather._arrival(4).wait_recv()

        @pl.when(i == 2)
        def _():
            gather.forward()

        @pl.when(i == 4)
        def _():
            gather._arrival(5).wait_recv()
            gather._arrival(6).wait_recv()

        @pl.when(i == 6)
        def _():
            gather.finish()

        @pl.when(i == 7)
        def _():
            gather._arrival(7).wait_recv()

        code = arriving[0]
        for k in range(1, 8):
            code = jnp.where(i == k, arriving[k], code)
        at = bits(code)
        before = mm(HN[at], WI[...]) + BIAS[0:1]
        active, slope = gelu_pair(before)
        ACTIVE[at] = active.astype(jnp.bfloat16)
        SLOPE[at] = slope.astype(jnp.bfloat16)

    for n in range(turns, max(starts) + 2 * depth):
        turn(n)

    @pl.loop(0, 8)
    def _(i):
        at = bits(3 - i // 2 + 4 * (1 - lax.rem(i, 2)))
        slope = mm(G3[at].reshape(rows, width), WO[...].reshape(depth * units, width), NT)
        slope = (slope * SLOPE[at].astype(jnp.float32)).astype(jnp.bfloat16)
        SLOPE[at] = slope
        total = jnp.sum(slope.astype(jnp.float32), axis=0, keepdims=True)
        for b in range(depth):
            BS[b, 0:1] += total[:, b * units : (b + 1) * units]
        back = mm(slope, WI[...], NT)
        j = i // 2

        @pl.when(lax.rem(i, 2) == 0)
        def _():
            CS[j] = back.astype(jnp.bfloat16)
            to_core(j, CS, CR, cs, cr).start()

        @pl.when(lax.rem(i, 2) == 1)
        def _():
            to_core(j, CS, CR, cs, cr).wait_recv()
            total = back + CR[j].astype(jnp.float32)

            @pl.when(j < 3)
            def _():
                PS[j] = total.astype(jnp.bfloat16)
                to_chip(j).start()

            @pl.when(j == 3)
            def _():
                DSUM[...] = total

    @pl.loop(1, depth)
    def _(k):
        bias_move(lax.rem(z + k, depth)).start()

    @pl.loop(0, depth)
    def _(s):
        b = far_first(z, 0, depth)
        for k in range(1, depth):
            b = jnp.where(s == k, far_first(z, k, depth), b)
        cols = pl.ds(pl.multiple_of(b * units, units), units)

        gin = mm(SLOPE[:, :, :, :, cols].reshape(8 * rows, units), HN[...].reshape(8 * rows, width), TN)
        GO[0] = gin
        S[b, 0] = gin.astype(jnp.bfloat16)
        @pl.when((s == 0) & (z == 0))
        def _():
            up.start()

        @pl.when((s == 0) & (z == depth - 1))
        def _():
            down.start()

        gout = mm(ACTIVE[:, :, :, :, cols].reshape(8 * rows, units), G3[...].reshape(8 * rows, width), TN)
        GO[1] = gout
        S[b, 1] = gout.astype(jnp.bfloat16)

    latter_move.start()

    @pl.loop(0, 8)
    def _(i):
        ox, oc, oh = bits(7 - i)
        active = ACTIVE[ox, oc, :, pl.ds(pl.multiple_of(oh * half, half), half)].reshape(rows, depth * units)
        more = mm(active, WO[...].reshape(depth * units, width))

        @pl.when(i < 4)
        def _():
            CSY[i] = more.astype(jnp.bfloat16)
            to_core(i, CSY, CRY, ys, yr).start()

        @pl.when(i >= 4)
        def _():
            j = i - 4
            to_core(j, CSY, CRY, ys, yr).wait()
            total = more + CRY[j].astype(jnp.float32)

            @pl.when(j < 3)
            def _():
                CSY[j] = total.astype(jnp.bfloat16)

            @pl.when(j == 3)
            def _():
                YSUM[...] = total.reshape(2, half, width)

    save(GO, go_out)
    save(G3.at[p.x, p.c, p.y], cot_out)

    GB[...] = BS[z]

    @pl.loop(1, depth)
    def _(k):
        other = lax.rem(z + k, depth)
        remote(BS.at[other], BR.at[other], bs.at[other], br.at[other], p.at(z=other)).wait()
        GB[...] += BR[other]

    save(GB, gbias_out)

    @pl.loop(0, 3)
    def _(j):
        to_chip(j).wait_recv()
        DSUM[...] += PR[j].astype(jnp.float32)

    save(DSUM, d_out)

    @pl.when((z == 1) | (z == depth - 2))
    def _():
        up.wait_recv()
        far = jnp.where(z == 1, depth - 1, 0)
        add_low(S.at[far, 0], RF)

    save(S, S_out)
    latter_move.wait()
    YSUM[p.y] += MID[2, pl.ds(pl.multiple_of(p.y * half, half), half)] + vector(6)
    YSUM[1 - p.y] += LATR[...].astype(jnp.float32) + vector(6)

    save(CSY.at[pl.ds(0, 3)], YS_out)
    save(YSUM, y_out)

    @pl.when((z == 0) | (z == depth - 1))
    def _():
        up.wait_send()

    for line in lines + ff:
        line.sent()
    for plane in planes + [gather]:
        plane.sent()
    for copy in swaps:
        copy.wait_send()

    @pl.loop(1, count)
    def _(j):
        vec_move(j).wait_send()

    @pl.loop(0, 4)
    def _(j):
        to_core(j, CS, CR, cs, cr).wait_send()

    @pl.loop(0, 3)
    def _(j):
        to_chip(j).wait_send()

    for copy in saved:
        copy.wait()


def forward_all(proj, so, pairs, query, co, win, wout, vec, tok, enc, cot, target, source):
    depth = lax.axis_size("dp") // 4
    rows, cols = query.shape
    bf, f32 = jnp.bfloat16, jnp.float32
    count = 8 * depth
    length, short, d = 2 * tok.shape[1], 2 * enc.shape[1], tok.shape[2]
    units = wout.shape[0]
    heads = d // 128
    whole = (2, depth, 2, 2, rows, cols)
    shapes = {
        "G": ((PIECES,) + whole, bf),
        "ACT": ((9, length, d), bf),
        "CTX": ((3, short, d), bf),
        "MID": ((3, length, d), f32),
        "P1": ((heads, 2 * length, length), bf),
        "P2": ((heads, 2 * length, short), bf),
        "FULL": ((8, d), f32),
        "COT": (cot.shape, bf),
        "DSUM": ((length, d), f32),
        "YSUM": ((2, length // 2, d), f32),
        "GO": ((2, units, d), f32),
        "GB": ((8, units), f32),
        "S": ((depth, 2, units, d), bf),
        "YS": ((3, length, d), bf),
    }
    outs = [jax.ShapeDtypeStruct(*shape) for shape in shapes.values()]

    def held(name):
        return pltpu.VMEM(*shapes[name])

    dma = pltpu.SemaphoreType.DMA
    hb = pl.BlockSpec(memory_space=HBM)
    tokens = (2, 2, 2, length, d)
    four = pltpu.VMEM((4, length, d), bf)
    three = pltpu.VMEM((3, length, d), bf)
    scratch = [
        pltpu.VMEM((PIECES, rows, cols), bf),
        pltpu.VMEM(whole, bf),
        pltpu.VMEM(tok.shape, bf),
        pltpu.VMEM((count,) + vec.shape, f32),
        held("FULL"),
        pltpu.VMEM((8, depth * units), f32),
        held("ACT"), held("CTX"), held("MID"), held("P1"), held("P2"),
        pltpu.VMEM(target.shape, jnp.int32), pltpu.VMEM(source.shape, jnp.int32),
        pltpu.VMEM(tok.shape, bf), pltpu.VMEM(enc.shape, bf),
        pltpu.VMEM(tokens, bf),
        pltpu.VMEM((2, 2, 2, 2) + cot.shape[1:], bf),
        pltpu.VMEM((d, depth * units), bf),
        pltpu.VMEM((depth, units, d), bf),
        held("S"),
        pltpu.VMEM((units, d), bf),
        pltpu.VMEM(tokens[:4] + (depth * units,), bf),
        pltpu.VMEM(tokens[:4] + (depth * units,), bf),
        pltpu.VMEM((depth, 8, units), f32),
        pltpu.VMEM((depth, 8, units), f32),
        four, four, four, four, three, three,
        held("DSUM"), held("YSUM"), held("GO"), held("GB"),
        pltpu.VMEM((length // 2, d), bf), pltpu.VMEM((length // 2, d), bf),
        dma((13,)), dma((1,)), dma((24,)),
        dma((PIECES, 2, depth - 1)), dma((PIECES, 2, depth - 1)),
        dma((FF_PIECES, 2, depth - 1)), dma((FF_PIECES, 2, depth - 1)),
        dma((PIECES + 2, 8)), dma((PIECES + 2, 8)),
        dma((count,)), dma((count,)),
        dma((3,)), dma((3,)),
        dma((8,)), dma((8,)),
        dma((1,)), dma((1,)),
        dma((depth,)), dma((depth,)),
        dma((4,)), dma((4,)),
        dma((4,)), dma((4,)),
        dma((3,)), dma((3,)),
    ]
    return pl.pallas_call(
        functools.partial(forward_kernel, depth),
        out_shape=outs,
        in_specs=[hb] * 13,
        out_specs=[hb] * len(outs),
        scratch_shapes=scratch,
        compiler_params=pltpu.CompilerParams(
            collective_id=1, has_side_effects=True, vmem_limit_bytes=63 << 20
        ),
        name="forward_all",
    )(proj, so, pairs, query, co, win, wout, vec, tok, enc, cot, target, source)


def norm_back(e, h, gain):
    center = h - jnp.mean(h, axis=-1, keepdims=True)
    inverse = lax.rsqrt(jnp.mean(center * center, axis=-1, keepdims=True) + EPS)
    normal = center * inverse
    scaled = e * gain
    back = inverse * (
        scaled
        - jnp.mean(scaled, axis=-1, keepdims=True)
        - normal * jnp.mean(scaled * normal, axis=-1, keepdims=True)
    )
    return back, jnp.sum(e * normal, axis=0, keepdims=True), jnp.sum(e, axis=0, keepdims=True)


def attend_pairs_back(q_ref, k_ref, v_ref, probs_ref, slope_ref, dq_ref, dk_ref, dv_ref, start, stop):
    rows = q_ref.shape[0]
    first = lax.broadcasted_iota(jnp.int32, (rows, 128), 1) < HEAD

    def stacked(a):
        zero = jnp.zeros_like(a)
        return jnp.concatenate([jnp.where(first, a, zero), jnp.where(first, zero, a)], axis=0)

    @pl.loop(start, stop)
    def _(h):
        at = (slice(None), pl.ds(pl.multiple_of(h * 128, 128), 128))
        up = stacked(slope_ref[at])
        low = probs_ref[h]
        probs = low.astype(jnp.float32)
        dprobs = mm(up, v_ref[at], NT)
        ds = (probs * (dprobs - jnp.sum(probs * dprobs, axis=-1, keepdims=True))).astype(jnp.bfloat16)
        dq = mm(ds, k_ref[at]) * HEAD**-0.5
        dq_ref[at] = jnp.where(first, dq[:rows], dq[rows:]).astype(jnp.bfloat16)
        dk_ref[at] = (mm(ds, stacked(q_ref[at]), TN) * HEAD**-0.5).astype(jnp.bfloat16)
        dv_ref[at] = mm(low, up, TN).astype(jnp.bfloat16)


class HoppedReduce(LineReduce):
    def _down(self, b):
        slot = self.n - 2 + self.p.z - 1 - b
        return remote(self.part(b), self.slots(slot), self.send.at[b], self.recv.at[slot], self.p.down())

    def above(self, b):
        slot = self.n - 2 + self.p.z - b
        return remote(self.slots(slot), self.slots(slot), self.send.at[b], self.recv.at[slot], self.p.down())

    def first(self, b):
        z, n = self.p.z, self.n

        @pl.when((b > z) & (((z == 0) & (b < n - 1)) | ((z == 1) & (b == n - 1))))
        def _():
            self._up(b).start()

        @pl.when((b < z) & (((z == n - 1) & (b > 0)) | ((z == n - 2) & (b == 0))))
        def _():
            self._down(b).start()

    def middle(self, b, add):
        z, n = self.p.z, self.n

        @pl.when((z > 0) & (b > z) & ((z > 1) | (b < n - 1)))
        def _():
            self.below(b).wait_recv()
            add(self.part(b), self.slots(b - z))
            self._up(b).start()

        @pl.when((z < n - 1) & (b < z) & ((z < n - 2) | (b > 0)))
        def _():
            self.above(b).wait_recv()
            add(self.part(b), self.slots(n - 2 + z - b))
            self._down(b).start()

    def last(self, take):
        z, n = self.p.z, self.n

        @pl.when(z > 0)
        def _():
            self.below(z).wait_recv()
            take(self.slots(0))

        @pl.when(z < n - 1)
        def _():
            self.above(z).wait_recv()
            take(self.slots(n - 2))

    def sent(self):
        z, n = self.p.z, self.n

        @pl.loop(0, n)
        def _(b):
            @pl.when((b > z) & ((z > 0) | (b < n - 1)))
            def _():
                self._up(b).wait_send()

            @pl.when((b < z) & ((z < n - 1) | (b > 0)))
            def _():
                self._down(b).wait_send()


SLOTS = 4
FF_PARTS = 8
FF_GAP = 2


def backward_kernel(
    depth,
    G, act, ctx, mid, p1, p2, full, cot_in, d_in, y_in, go_in, S_in, YS_in,
    gw_out, vec_out, res_out, tg_out, eg_out, go_out,
    MY, SEND, CR, PD, PR, R, S, RF0, RF1, YS, YR, W, ACT, CTX, X, PB1, PB2, UP, LOW, SL, DH, DC, COT, FULL, VG, VR, XS, XR, ES, ER,
    lsem, wsem, cs, cr, ds, dr, ps, pr, zs, zr, fs, fr, ys, yr, vs, vr, ss, sr, credit,
):
    p = Place()
    count = 8 * depth
    me = p.dp * 2 + p.y
    ox, oy = 1 - p.x, 1 - p.y
    rows, width = UP.shape
    short = CTX.shape[1]
    cols = width // 2
    part = MY.shape[4]
    low_type = jnp.bfloat16

    def load(i, src, dst):
        copy = pltpu.make_async_copy(src, dst, lsem.at[i])
        copy.start()
        return copy

    loads = [
        load(0, mid.at[2], X),
        load(1, d_in, UP),
        load(2, cot_in, COT),
        load(3, full, FULL),
        load(4, act.at[pl.ds(0, 8)], ACT),
        load(5, ctx, CTX),
        load(6, p2, PB2),
        load(7, S_in, S),
        load(8, go_in, go_out),
        load(9, p1, PB1),
        load(10, YS_in, YS),
        load(11, y_in, res_out),
    ]
    order = (7, 6, 3, 0, 1, 2, 4, 5)

    def weight(n):
        return pltpu.make_async_copy(G.at[order[n]], W.at[n % 2], wsem.at[n % 2])

    def use(n):
        weight(n).wait()
        if n + 1 < len(order):
            weight(n + 1).start()
        return [W[n % 2, y].reshape(width, cols) for y in range(2)]

    weight(0).start()
    VG[...] = jnp.zeros_like(VG)
    all_barrier(p, count)

    def y_move(j):
        dx, dy = 1 - j // 2, 1 - j % 2
        return remote(
            YS.at[j], YR.at[j], ys.at[j], yr.at[j], p.at(x=lax.rem(p.x + dx, 2), y=lax.rem(p.y + dy, 2))
        )

    loads[10].wait()
    for j in range(3):
        y_move(j).start()

    def core(i):
        return remote(SEND.at[i % 2], CR.at[i % SLOTS], cs.at[i], cr.at[i], p.core())

    def cut(i, h):
        by_x = part // 2
        return pl.ds(by_x, part - by_x) if h else pl.ds(0, by_x)

    def diagonal(i, h):
        return remote(
            MY.at[i, oy, :, ox, cut(i, h)], PD.at[i, :, cut(i, h)], ds.at[i, h], dr.at[i, h],
            p.yn() if h else p.xn(),
        )

    def column(i, h):
        view = MY.at[i, oy, :, p.x] if h else MY.at[i, p.y, :, ox]
        return remote(view, PR.at[i, h], ps.at[i, h], pr.at[i, h], p.yn() if h else p.xn())

    lines = [
        LineReduce(
            p, depth, lambda b, i=i: MY.at[i, p.y, b, p.x], lambda k, i=i: R.at[i, k], zs.at[i], zr.at[i]
        )
        for i in range(PIECES)
    ]
    frows = S.shape[2] // (FF_PARTS // 2)
    ff = []
    for f in range(FF_PARTS):
        at = pl.ds(f // 2 * frows, frows)
        kind, land = (LineReduce, RF1) if f % 2 else (HoppedReduce, RF0)
        ff.append(
            kind(
                p, depth, lambda b, f=f, at=at: S.at[b, f % 2, at], lambda k, at=at, land=land: land.at[k, at],
                fs.at[f], fr.at[f],
            )
        )

    def store_part(i, left, right):
        if i >= 2:
            core(i - 2).wait_send()
        for y in range(2):
            value = mm(left, right[:, y * cols : (y + 1) * cols], TN).reshape(depth, 2, 2, part, cols)
            value = value.astype(low_type)
            even, odd = value[:, :, 0], value[:, :, 1]
            MY[i, y] = jnp.where(p.c == 0, even, odd)
            SEND[i % 2, y] = jnp.where(p.c == 0, odd, even)
        if i >= SLOTS:
            pl.semaphore_wait(credit, 1)
        core(i).start()

    def stage(i, s):
        if s == 1:
            core(i).wait_recv()
            add_low(MY.at[i], CR.at[i % SLOTS])
            if i + SLOTS < PIECES:
                signal(credit, p.core())
            diagonal(i, 0).start()
            diagonal(i, 1).start()
        elif s == 2:
            diagonal(i, 0).wait_recv()
            add_low(MY.at[i, oy, :, p.x, cut(i, 0)], PD.at[i, :, cut(i, 0)])
            column(i, 1).start()
            diagonal(i, 1).wait_recv()
            add_low(MY.at[i, p.y, :, ox, cut(i, 1)], PD.at[i, :, cut(i, 1)])
            column(i, 0).start()
        elif s == 3:
            column(i, 0).wait_recv()
            column(i, 1).wait_recv()
            view = MY.at[i, p.y, :, p.x]
            view[...] = (
                view[...].astype(jnp.float32)
                + PR[i, 0].astype(jnp.float32)
                + PR[i, 1].astype(jnp.float32)
            ).astype(low_type)
            for k in range(depth - 1):
                lines[i].first(far_first(p.z, k, depth))
        elif s < 3 + depth:
            lines[i].middle(far_first(p.z, s - 4, depth), add_low)
        elif s == 3 + depth:
            gw_out[i] = MY[i, p.y, p.z, p.x].astype(jnp.float32)

            def take(slot):
                gw_out[i] += slot[...].astype(jnp.float32)

            lines[i].last(take)

    def ff_stage(f, s):
        if s == 0:
            for k in range(depth - 1):
                ff[f].first(far_first(p.z, k, depth))
        elif s < depth:
            ff[f].middle(far_first(p.z, s - 1, depth), add_low)
        else:
            at = pl.ds(f // 2 * frows, frows)

            def take(slot):
                go_out[f % 2, at] += slot[...].astype(jnp.float32)

            ff[f].last(take)

    clock = [0]

    def tick(*stages):
        n = clock[0]
        clock[0] += 1
        if n == 0:
            loads[7].wait()
            loads[8].wait()
        for f in range(FF_PARTS):
            if (n - f) % FF_GAP == 0 and 0 <= (n - f) // FF_GAP <= depth:
                ff_stage(f, (n - f) // FF_GAP)
        for i, s in stages:
            stage(i, s)

    def gain(i):
        return FULL[i : i + 1]

    def spread(i, values):
        VG[i : i + 1] = values

    tick()
    for i in (0, 1, 2, 3):
        loads[i].wait()
    cot = COT[...].reshape(rows, width).astype(jnp.float32)
    latter = X[...]
    back, g_gain, g_shift = norm_back(UP[...], latter, gain(4))
    spread(4, g_gain)
    spread(5, g_shift)
    spread(6, jnp.sum(cot, axis=0, keepdims=True))
    UP[...] = cot + back
    LOW[...] = UP[...].astype(low_type)
    next_mid = load(0, mid.at[1], X)
    w = use(0)
    for y in range(2):
        SL[:, y * cols : (y + 1) * cols] = mm(LOW[...], w[y]).astype(low_type)
    loads[4].wait()
    store_part(0, LOW[...], ACT[H2])
    tick()
    loads[5].wait()
    loads[6].wait()
    attend_pairs_back(
        ACT.at[CQ], CTX.at[CK], CTX.at[CV], PB2, SL, DH.at[0], DC.at[0], DC.at[1], 0, width // 128
    )
    store_part(1, ACT[N2], DH[0])
    tick((0, 1))
    w = use(1)
    slope = mm(DH[0, :, :cols], w[0], NT) + mm(DH[0, :, cols:], w[1], NT)
    next_mid.wait()
    back, g_gain, g_shift = norm_back(slope, X[...], gain(2))
    spread(2, g_gain)
    spread(3, g_shift)
    UP[...] += back
    LOW[...] = UP[...].astype(low_type)
    next_mid = load(0, mid.at[0], X)
    store_part(2, CTX[ENC], DC[0])
    tick((1, 1))
    store_part(3, CTX[ENC], DC[1])
    tick((2, 1))
    w = use(2)
    for y in range(2):
        SL[:, y * cols : (y + 1) * cols] = mm(LOW[...], w[y]).astype(low_type)
    store_part(4, LOW[...], ACT[H1])
    tick((3, 1), (0, 2))
    loads[9].wait()
    attend_pairs_back(
        ACT.at[Q], ACT.at[K], ACT.at[V], PB1, SL, DH.at[0], DH.at[1], DH.at[2], 0, width // 256
    )
    tick((4, 1), (1, 2))
    attend_pairs_back(
        ACT.at[Q], ACT.at[K], ACT.at[V], PB1, SL, DH.at[0], DH.at[1], DH.at[2], width // 256, width // 128
    )
    store_part(5, ACT[N1], DH[0])
    tick((0, 3), (2, 2))
    store_part(6, ACT[N1], DH[1])
    tick((5, 1), (1, 3), (3, 2), (0, 4))
    store_part(7, ACT[N1], DH[2])
    tick((6, 1), (2, 3), (4, 2), (1, 4), (0, 5))
    slope = None
    for i in range(3):
        w = use(3 + i)
        term = mm(DH[i, :, :cols], w[0], NT) + mm(DH[i, :, cols:], w[1], NT)
        slope = term if slope is None else slope + term
    tick((7, 1), (3, 3), (5, 2), (2, 4), (1, 5), (0, 6))
    next_mid.wait()
    back, g_gain, g_shift = norm_back(slope, X[...], gain(0))
    spread(0, g_gain)
    spread(1, g_shift)
    back += UP[...]
    for h in range(2):
        tg_out[h] = back[h * (rows // 2) : (h + 1) * (rows // 2)]

    def vec_move(j):
        other = lax.rem(me + j, count)
        at = pl.ds(pl.multiple_of(other * (width // count) // 128 * 128, 128), 128)
        return remote(VG.at[:, at], VR.at[j], vs.at[j], vr.at[j], (other // 2, lax.rem(other, 2)))

    @pl.loop(1, count)
    def _(j):
        vec_move(j).start()

    tick((6, 2), (4, 3), (3, 4), (2, 5), (1, 6), (0, 7))
    slope = None
    for i in range(2):
        w = use(6 + i)
        term = mm(DC[i, :, :cols], w[0], NT) + mm(DC[i, :, cols:], w[1], NT)
        slope = term if slope is None else slope + term
    for h in range(2):
        eg_out[h] = slope[h * (short // 2) : (h + 1) * (short // 2)]
    XS[...] = tg_out[oy].astype(low_type)
    loads[11].wait()
    for j in range(3):
        y_move(j).wait_recv()
        res_out[...] += YR[j].astype(jnp.float32).reshape(res_out.shape)
    ES[...] = eg_out[oy].astype(low_type)
    swaps = [
        remote(XS, XR, ss.at[0], sr.at[0], p.yn()),
        remote(ES, ER, ss.at[1], sr.at[1], p.yn()),
    ]
    tick((7, 2), (5, 3), (4, 4), (3, 5), (2, 6), (1, 7))
    for copy in swaps:
        copy.start()
    tick((6, 3), (5, 4), (4, 5), (3, 6), (2, 7))
    tick((7, 3), (6, 4), (5, 5), (4, 6), (3, 7))
    tick((7, 4), (6, 5), (5, 6), (4, 7))
    tick((7, 5), (6, 6), (5, 7))
    tick((7, 6), (6, 7))
    tick((7, 7))
    while clock[0] < FF_PARTS + FF_GAP * depth + 1:
        tick()
    at = pl.ds(pl.multiple_of(me * (width // count) // 128 * 128, 128), 128)
    vec_out[...] = VG[:, at]

    @pl.loop(1, count)
    def _(j):
        vec_move(j).wait()
        vec_out[...] += VR[j]

    for copy in swaps:
        copy.wait()
    tg_out[oy] = XR[...].astype(jnp.float32)
    eg_out[oy] = ER[...].astype(jnp.float32)
    for i in range(PIECES):
        if i >= PIECES - 2:
            core(i).wait_send()
        for h in range(2):
            diagonal(i, h).wait_send()
            column(i, h).wait_send()
        lines[i].sent()
    for line in ff:
        line.sent()
    for j in range(3):
        y_move(j).wait_send()


def backward_all(G, act, ctx, mid, p1, p2, full, cot, d_in, y_in, go_in, S_in, YS_in):
    depth = G.shape[2]
    count = 8 * depth
    rows, cols = G.shape[5:]
    length, width = d_in.shape
    short = ctx.shape[1]
    bf, f32 = jnp.bfloat16, jnp.float32
    dma = pltpu.SemaphoreType.DMA
    vm = pl.BlockSpec(memory_space=VMEM)
    hb = pl.BlockSpec(memory_space=HBM)
    return pl.pallas_call(
        functools.partial(backward_kernel, depth),
        out_shape=[
            jax.ShapeDtypeStruct((PIECES, rows, cols), f32),
            jax.ShapeDtypeStruct((8, 128), f32),
            jax.ShapeDtypeStruct((2, length // 2, width), f32),
            jax.ShapeDtypeStruct((2, length // 2, width), f32),
            jax.ShapeDtypeStruct((2, short // 2, width), f32),
            jax.ShapeDtypeStruct(go_in.shape, f32),
        ],
        in_specs=[hb] * 13,
        out_specs=[vm] * 6,
        scratch_shapes=[
            pltpu.VMEM((PIECES, 2, depth, 2, rows, cols), bf),
            pltpu.VMEM((2, 2, depth, 2, rows, cols), bf),
            pltpu.VMEM((SLOTS, 2, depth, 2, rows, cols), bf),
            pltpu.VMEM((PIECES, depth, rows, cols), bf),
            pltpu.VMEM((PIECES, 2, depth, rows, cols), bf),
            pltpu.VMEM((PIECES, depth + 1, rows, cols), bf),
            pltpu.VMEM(S_in.shape, bf),
            pltpu.VMEM((2 * depth - 4,) + S_in.shape[2:], bf),
            pltpu.VMEM((depth + 1,) + S_in.shape[2:], bf),
            pltpu.VMEM(YS_in.shape, bf),
            pltpu.VMEM(YS_in.shape, bf),
            pltpu.VMEM((2,) + G.shape[1:], bf),
            pltpu.VMEM((8, length, width), bf),
            pltpu.VMEM(ctx.shape, bf),
            pltpu.VMEM((length, width), f32),
            pltpu.VMEM(p1.shape, bf),
            pltpu.VMEM(p2.shape, bf),
            pltpu.VMEM((length, width), f32),
            pltpu.VMEM((length, width), bf),
            pltpu.VMEM((length, width), bf),
            pltpu.VMEM((3, length, width), bf),
            pltpu.VMEM((2, short, width), bf),
            pltpu.VMEM((2, length // 2, width), bf),
            pltpu.VMEM((8, width), f32),
            pltpu.VMEM((8, width), f32),
            pltpu.VMEM((count, 8, 128), f32),
            pltpu.VMEM((length // 2, width), bf),
            pltpu.VMEM((length // 2, width), bf),
            pltpu.VMEM((short // 2, width), bf),
            pltpu.VMEM((short // 2, width), bf),
            dma((12,)), dma((2,)),
            dma((PIECES,)), dma((PIECES,)),
            dma((PIECES, 2)), dma((PIECES, 2)),
            dma((PIECES, 2)), dma((PIECES, 2)),
            dma((PIECES, depth)), dma((PIECES, depth + 1)),
            dma((FF_PARTS, depth)), dma((FF_PARTS, 2 * depth)),
            dma((3,)), dma((3,)),
            dma((count,)), dma((count,)),
            dma((2,)), dma((2,)),
            pltpu.SemaphoreType.REGULAR,
        ],
        compiler_params=pltpu.CompilerParams(
            collective_id=3, has_side_effects=True, vmem_limit_bytes=63 << 20
        ),
        name="backward_all",
    )(G, act, ctx, mid, p1, p2, full, cot, d_in, y_in, go_in, S_in, YS_in)


def fast_local(
    tokens, encoder, target_doc, source_doc, self_proj, self_out, cross_query, cross_pairs, cross_out,
    hidden_in, hidden_in_bias, hidden_out, hidden_out_bias, self_gain, self_shift, cross_gain, cross_shift,
    hidden_gain, hidden_shift, cotangent,
):
    depth = lax.axis_size("dp") // 4
    count = 8 * depth
    place = Place()
    me = place.dp * 2 + place.y
    bf, f32 = jnp.bfloat16, jnp.float32
    vectors = jnp.stack(
        [self_gain, self_shift, cross_gain, cross_shift, hidden_gain, hidden_shift, hidden_out_bias]
    )
    span = vectors.shape[1]
    group = 128 // span
    lane = lax.broadcasted_iota(jnp.int32, (1, 128), 1)
    mine = lane // span == lax.rem(me, group)
    vec = jnp.concatenate([
        jnp.where(mine, jnp.tile(vectors, (1, group)), 0.0),
        jnp.zeros((1, 128), f32),
        hidden_in_bias.astype(f32).reshape(-1, 128),
    ])
    vec = jnp.pad(vec, ((0, -vec.shape[0] % 8), (0, 0)))
    G, act, ctx, mid, probs1, probs2, full, cot, d_in, y_in, go, gbias, S, YS = forward_all(
        self_proj.transpose(1, 0, 2), self_out.T, cross_pairs.transpose(1, 0, 2), cross_query, cross_out.T,
        hidden_in, hidden_out, vec, tokens, encoder, cotangent, target_doc, source_doc,
    )
    gw, vout, res, tg, eg, go = backward_all(
        G, act, ctx, mid, probs1, probs2, full, cot, d_in, y_in, go, S, YS
    )
    vout = lax.dynamic_slice_in_dim(vout, lax.rem(me, group) * span, span, axis=1)
    return (
        res, tg, eg,
        jnp.stack([gw[5], gw[6], gw[7]], axis=1),
        gw[4].T, gw[1], jnp.stack([gw[2], gw[3]], axis=1), gw[0].T,
        go[0].T, gbias[0], go[1],
        vout[6], vout[0], vout[1], vout[2], vout[3], vout[4], vout[5],
    )


BLOCK_ROWS = 512


def smooth_gate(values):
    return jax.nn.gelu(values, approximate=True)


def plain_norm_forward(hidden, norm_gain, norm_shift):
    center = hidden - jnp.mean(hidden, axis=-1, keepdims=True)
    inverse = lax.rsqrt(jnp.mean(center * center, axis=-1, keepdims=True) + EPS)
    normal = center * inverse
    return (normal * norm_gain + norm_shift, normal, inverse)


def plain_norm_backward(upward, normal, inverse, norm_gain):
    scaled = upward * norm_gain
    centred = (
        scaled
        - jnp.mean(scaled, axis=-1, keepdims=True)
        - normal * jnp.mean(scaled * normal, axis=-1, keepdims=True)
    )
    return (centred * inverse, jnp.sum(upward * normal, axis=0), jnp.sum(upward, axis=0))


def split_blocks(array):
    row_count = array.shape[0]
    block_size = min(BLOCK_ROWS, row_count)
    return array.reshape((row_count // block_size, block_size) + array.shape[1:])


def block_scores(query_block, key_rows, allow_block):
    query_heads = query_block.reshape(query_block.shape[0], -1, HEAD)
    key_heads = key_rows.reshape(key_rows.shape[0], -1, HEAD)
    scores = jnp.einsum(
        "qhd,khd->hqk", query_heads, key_heads, preferred_element_type=jnp.float32
    ) * HEAD ** (-0.5)
    return jnp.where(allow_block[None], scores, NEGATIVE)


def plain_attend(queries, key_rows, values, allowed):
    columns = queries.shape[1]
    value_heads = values.reshape(values.shape[0], -1, HEAD)

    def one_block(pieces):
        query_block, allow_block = pieces
        scores = block_scores(query_block, key_rows, allow_block)
        highest = jnp.max(scores, axis=-1, keepdims=True)
        exponent = jnp.exp(scores - highest)
        totals = jnp.sum(exponent, axis=-1, keepdims=True)
        softmaxed = (exponent / totals).astype(jnp.bfloat16)
        mixture = jnp.einsum(
            "hqk,khd->qhd", softmaxed, value_heads, preferred_element_type=jnp.float32
        )
        return (
            mixture.reshape(query_block.shape[0], columns).astype(jnp.bfloat16),
            (highest + jnp.log(totals))[..., 0],
        )

    mixture, logsum = lax.map(one_block, (split_blocks(queries), split_blocks(allowed)))
    return (mixture.reshape(queries.shape), logsum)


def plain_attend_backward(queries, key_rows, values, allowed, logsum, slope_heads):
    scaling = HEAD ** (-0.5)
    key_heads = key_rows.reshape(key_rows.shape[0], -1, HEAD)
    value_heads = values.reshape(values.shape[0], -1, HEAD)

    def one_block(running, pieces):
        key_total, value_total = running
        query_block, allow_block, logsum_block, slope_block = pieces
        scores = block_scores(query_block, key_rows, allow_block)
        softmaxed = jnp.exp(scores - logsum_block[..., None])
        query_heads = query_block.reshape(query_block.shape[0], -1, HEAD)
        slope_out = slope_block.reshape(slope_block.shape[0], -1, HEAD)
        slope_probs = jnp.einsum(
            "qhd,khd->hqk", slope_out, value_heads, preferred_element_type=jnp.float32
        )
        centred = jnp.sum(softmaxed * slope_probs, axis=-1, keepdims=True)
        slope_scores = (softmaxed * (slope_probs - centred)).astype(jnp.bfloat16)
        slope_query = (
            jnp.einsum("hqk,khd->qhd", slope_scores, key_heads, preferred_element_type=jnp.float32)
            * scaling
        )
        key_total = (
            key_total
            + jnp.einsum(
                "hqk,qhd->khd", slope_scores, query_heads, preferred_element_type=jnp.float32
            )
            * scaling
        )
        value_total = value_total + jnp.einsum(
            "hqk,qhd->khd",
            softmaxed.astype(jnp.bfloat16),
            slope_out,
            preferred_element_type=jnp.float32,
        )
        return (
            (key_total, value_total),
            slope_query.reshape(query_block.shape[0], -1).astype(jnp.bfloat16),
        )

    empty_heads = jnp.zeros(key_heads.shape, jnp.float32)
    (key_total, value_total), slope_query = lax.scan(
        one_block,
        (empty_heads, empty_heads),
        (split_blocks(queries), split_blocks(allowed), logsum, split_blocks(slope_heads)),
    )
    return (
        slope_query.reshape(queries.shape),
        key_total.reshape(key_rows.shape).astype(jnp.bfloat16),
        value_total.reshape(values.shape).astype(jnp.bfloat16),
    )


def gather_rows(local_rows):
    return lax.all_gather(local_rows, "tensor", axis=0, tiled=True)


def sum_rows(partial_sum):
    return lax.psum_scatter(
        partial_sum.astype(jnp.bfloat16), "tensor", scatter_dimension=0, tiled=True
    ).astype(jnp.float32)


def gather_slopes(local_slopes):
    return lax.all_gather(local_slopes, "tensor", axis=0, tiled=True)


def sum_slopes(partial_sum):
    return lax.psum_scatter(
        partial_sum.astype(jnp.bfloat16), "tensor", scatter_dimension=0, tiled=True
    ).astype(jnp.float32)


def reduce_weights(weight_terms):
    return (
        lax.psum_scatter(weight_terms[0], "dp", scatter_dimension=0, tiled=True),
        lax.psum_scatter(weight_terms[1], "dp", scatter_dimension=1, tiled=True),
        lax.psum_scatter(weight_terms[2], "dp", scatter_dimension=0, tiled=True),
        lax.psum_scatter(weight_terms[3], "dp", scatter_dimension=0, tiled=True),
        lax.psum_scatter(weight_terms[4], "dp", scatter_dimension=1, tiled=True),
        lax.psum_scatter(weight_terms[5], "dp", scatter_dimension=1, tiled=True),
        lax.psum_scatter(weight_terms[6], "dp", scatter_dimension=0, tiled=True),
        lax.psum_scatter(weight_terms[7], "dp", scatter_dimension=0, tiled=True),
    )


def plain_local(
    tokens,
    encoder,
    target_doc,
    source_doc,
    self_proj,
    self_out,
    cross_query,
    cross_pairs,
    cross_out,
    hidden_in,
    hidden_in_bias,
    hidden_out,
    hidden_out_bias,
    self_gain,
    self_shift,
    cross_gain,
    cross_shift,
    hidden_gain,
    hidden_shift,
    cotangent,
):
    (
        full_self_gain,
        full_self_shift,
        full_cross_gain,
        full_cross_shift,
        full_hidden_gain,
        full_hidden_shift,
        full_out_bias,
    ) = (
        lax.all_gather(self_gain, ("dp", "tensor"), axis=0, tiled=True),
        lax.all_gather(self_shift, ("dp", "tensor"), axis=0, tiled=True),
        lax.all_gather(cross_gain, ("dp", "tensor"), axis=0, tiled=True),
        lax.all_gather(cross_shift, ("dp", "tensor"), axis=0, tiled=True),
        lax.all_gather(hidden_gain, ("dp", "tensor"), axis=0, tiled=True),
        lax.all_gather(hidden_shift, ("dp", "tensor"), axis=0, tiled=True),
        lax.all_gather(hidden_out_bias, ("dp", "tensor"), axis=0, tiled=True),
    )
    micro_count = tokens.shape[0]
    row_count = tokens.shape[1] * lax.axis_size("tensor")
    positions = jnp.arange(row_count)
    results = []
    token_grads = []
    encoder_grads = []
    vector_total = None
    weight_total = None
    for step_index in range(micro_count):
        forward_weights = (
            lax.all_gather(self_proj, "dp", axis=0, tiled=True),
            lax.all_gather(self_out, "dp", axis=1, tiled=True),
            lax.all_gather(cross_query, "dp", axis=0, tiled=True),
            lax.all_gather(cross_pairs, "dp", axis=0, tiled=True),
            lax.all_gather(cross_out, "dp", axis=1, tiled=True),
            lax.all_gather(hidden_in, "dp", axis=1, tiled=True),
            lax.all_gather(hidden_in_bias, "dp", axis=0, tiled=True),
            lax.all_gather(hidden_out, "dp", axis=0, tiled=True),
        )
        (
            full_proj,
            full_self_out,
            full_query,
            full_pairs,
            full_cross_out,
            full_in,
            full_in_bias,
            full_out,
        ) = forward_weights
        target_row = target_doc[step_index]
        source_row = source_doc[step_index]
        self_allowed = (target_row[:, None] == target_row[None, :]) & (
            positions[None, :] <= positions[:, None]
        )
        cross_allowed = target_row[:, None] == source_row[None, :]
        start_hidden = tokens[step_index].astype(jnp.float32)
        normed_first, normal_first, inverse_first = plain_norm_forward(
            start_hidden, full_self_gain, full_self_shift
        )
        self_rows = gather_rows(normed_first.astype(jnp.bfloat16))
        triple = jnp.einsum(
            "td,dcj->tcj", self_rows, full_proj, preferred_element_type=jnp.float32
        ).astype(jnp.bfloat16)
        self_heads, self_logsum = plain_attend(triple[:, 0], triple[:, 1], triple[:, 2], self_allowed)
        middle = start_hidden + sum_rows(
            jnp.dot(self_heads, full_self_out, preferred_element_type=jnp.float32)
        )
        normed_second, normal_second, inverse_second = plain_norm_forward(
            middle, full_cross_gain, full_cross_shift
        )
        cross_rows, source_rows = (
            lax.all_gather(normed_second.astype(jnp.bfloat16), "tensor", axis=0, tiled=True),
            lax.all_gather(encoder[step_index], "tensor", axis=0, tiled=True),
        )
        cross_queries = jnp.dot(cross_rows, full_query, preferred_element_type=jnp.float32).astype(
            jnp.bfloat16
        )
        key_value = jnp.einsum(
            "sd,dcj->scj", source_rows, full_pairs, preferred_element_type=jnp.float32
        ).astype(jnp.bfloat16)
        cross_heads, cross_logsum = plain_attend(
            cross_queries, key_value[:, 0], key_value[:, 1], cross_allowed
        )
        latter = middle + sum_rows(
            jnp.dot(cross_heads, full_cross_out, preferred_element_type=jnp.float32)
        )
        normed_third, normal_third, inverse_third = plain_norm_forward(
            latter, full_hidden_gain, full_hidden_shift
        )
        hidden_rows = gather_rows(normed_third.astype(jnp.bfloat16))
        before = jnp.dot(
            hidden_rows, full_in, preferred_element_type=jnp.float32
        ) + full_in_bias.astype(jnp.float32)
        gated, gate_pullback = jax.vjp(smooth_gate, before)
        active = gated.astype(jnp.bfloat16)
        results.append(
            latter
            + sum_rows(jnp.dot(active, full_out, preferred_element_type=jnp.float32))
            + full_out_bias
        )
        back_weights = (
            lax.all_gather(self_proj, "dp", axis=0, tiled=True),
            lax.all_gather(self_out, "dp", axis=1, tiled=True),
            lax.all_gather(cross_query, "dp", axis=0, tiled=True),
            lax.all_gather(cross_pairs, "dp", axis=0, tiled=True),
            lax.all_gather(cross_out, "dp", axis=1, tiled=True),
            lax.all_gather(hidden_in, "dp", axis=1, tiled=True),
            lax.all_gather(hidden_in_bias, "dp", axis=0, tiled=True),
            lax.all_gather(hidden_out, "dp", axis=0, tiled=True),
        )
        (
            back_proj,
            back_self_out,
            back_query,
            back_pairs,
            back_cross_out,
            back_in,
            back_in_bias,
            back_out,
        ) = back_weights
        upward = cotangent[step_index].astype(jnp.float32)
        grad_out_bias = jnp.sum(upward, axis=0)
        slope_rows = gather_slopes(upward.astype(jnp.bfloat16))
        grad_out = jnp.einsum("tf,td->fd", active, slope_rows, preferred_element_type=jnp.float32)
        slope_active = jnp.einsum(
            "td,fd->tf", slope_rows, back_out, preferred_element_type=jnp.float32
        )
        slope_before = gate_pullback(slope_active)[0].astype(jnp.bfloat16)
        grad_in_bias = jnp.sum(slope_before.astype(jnp.float32), axis=0)
        grad_in = jnp.einsum(
            "td,tf->df", hidden_rows, slope_before, preferred_element_type=jnp.float32
        )
        slope_normed = sum_slopes(
            jnp.einsum("tf,df->td", slope_before, back_in, preferred_element_type=jnp.float32)
        )
        slope_hidden, grad_hidden_gain, grad_hidden_shift = plain_norm_backward(
            slope_normed, normal_third, inverse_third, full_hidden_gain
        )
        upward = upward + slope_hidden
        slope_rows = gather_slopes(upward.astype(jnp.bfloat16))
        grad_cross_out = jnp.einsum(
            "tj,td->jd", cross_heads, slope_rows, preferred_element_type=jnp.float32
        )
        slope_heads = jnp.einsum(
            "td,jd->tj", slope_rows, back_cross_out, preferred_element_type=jnp.float32
        ).astype(jnp.bfloat16)
        slope_query, slope_keys, slope_values = plain_attend_backward(
            cross_queries,
            key_value[:, 0],
            key_value[:, 1],
            cross_allowed,
            cross_logsum,
            slope_heads,
        )
        slope_pairs = jnp.stack([slope_keys, slope_values], axis=1)
        grad_query = jnp.einsum(
            "td,tj->dj", cross_rows, slope_query, preferred_element_type=jnp.float32
        )
        grad_pairs = jnp.einsum(
            "sd,scj->dcj", source_rows, slope_pairs, preferred_element_type=jnp.float32
        )
        slope_cross, slope_source = (
            lax.psum_scatter(
                jnp.einsum(
                    "tj,dj->td", slope_query, back_query, preferred_element_type=jnp.float32
                ).astype(jnp.bfloat16),
                "tensor",
                scatter_dimension=0,
                tiled=True,
            ).astype(jnp.float32),
            lax.psum_scatter(
                jnp.einsum(
                    "scj,dcj->sd", slope_pairs, back_pairs, preferred_element_type=jnp.float32
                ).astype(jnp.bfloat16),
                "tensor",
                scatter_dimension=0,
                tiled=True,
            ).astype(jnp.float32),
        )
        slope_hidden, grad_cross_gain, grad_cross_shift = plain_norm_backward(
            slope_cross, normal_second, inverse_second, full_cross_gain
        )
        upward = upward + slope_hidden
        slope_rows = gather_slopes(upward.astype(jnp.bfloat16))
        grad_self_out = jnp.einsum(
            "tj,td->jd", self_heads, slope_rows, preferred_element_type=jnp.float32
        )
        slope_heads = jnp.einsum(
            "td,jd->tj", slope_rows, back_self_out, preferred_element_type=jnp.float32
        ).astype(jnp.bfloat16)
        slope_query, slope_keys, slope_values = plain_attend_backward(
            triple[:, 0], triple[:, 1], triple[:, 2], self_allowed, self_logsum, slope_heads
        )
        slope_triple = jnp.stack([slope_query, slope_keys, slope_values], axis=1)
        grad_proj = jnp.einsum(
            "td,tcj->dcj", self_rows, slope_triple, preferred_element_type=jnp.float32
        )
        slope_self = sum_slopes(
            jnp.einsum("tcj,dcj->td", slope_triple, back_proj, preferred_element_type=jnp.float32)
        )
        slope_hidden, grad_self_gain, grad_self_shift = plain_norm_backward(
            slope_self, normal_first, inverse_first, full_self_gain
        )
        token_grads.append(upward + slope_hidden)
        encoder_grads.append(slope_source)
        vector_terms = (
            grad_self_gain,
            grad_self_shift,
            grad_cross_gain,
            grad_cross_shift,
            grad_hidden_gain,
            grad_hidden_shift,
            grad_out_bias,
        )
        vector_total = (
            vector_terms if step_index == 0 else jax.tree.map(jnp.add, vector_total, vector_terms)
        )
        weight_terms = (
            grad_proj,
            grad_self_out,
            grad_query,
            grad_pairs,
            grad_cross_out,
            grad_in,
            grad_in_bias,
            grad_out,
        )
        shard_terms = reduce_weights(weight_terms)
        weight_total = (
            shard_terms if step_index == 0 else jax.tree.map(jnp.add, weight_total, shard_terms)
        )
    vector_shards = (
        lax.psum_scatter(vector_total[0], ("dp", "tensor"), scatter_dimension=0, tiled=True),
        lax.psum_scatter(vector_total[1], ("dp", "tensor"), scatter_dimension=0, tiled=True),
        lax.psum_scatter(vector_total[2], ("dp", "tensor"), scatter_dimension=0, tiled=True),
        lax.psum_scatter(vector_total[3], ("dp", "tensor"), scatter_dimension=0, tiled=True),
        lax.psum_scatter(vector_total[4], ("dp", "tensor"), scatter_dimension=0, tiled=True),
        lax.psum_scatter(vector_total[5], ("dp", "tensor"), scatter_dimension=0, tiled=True),
        lax.psum_scatter(vector_total[6], ("dp", "tensor"), scatter_dimension=0, tiled=True),
    )
    return (
        jnp.stack(results),
        jnp.stack(token_grads),
        jnp.stack(encoder_grads),
        weight_total[0],
        weight_total[1],
        weight_total[2],
        weight_total[3],
        weight_total[4],
        weight_total[5],
        weight_total[6],
        weight_total[7],
        vector_shards[6],
        vector_shards[0],
        vector_shards[1],
        vector_shards[2],
        vector_shards[3],
        vector_shards[4],
        vector_shards[5],
    )


def solution(mesh):
    in_specs = (
        P("dp", "tensor", None),
        P("dp", "tensor", None),
        P("dp", None),
        P("dp", None),
        P("dp", None, "tensor"),
        P("tensor", "dp"),
        P("dp", "tensor"),
        P("dp", None, "tensor"),
        P("tensor", "dp"),
        P(None, ("dp", "tensor")),
        P(("dp", "tensor")),
        P(("dp", "tensor"), None),
        P(("dp", "tensor")),
        P(("dp", "tensor")),
        P(("dp", "tensor")),
        P(("dp", "tensor")),
        P(("dp", "tensor")),
        P(("dp", "tensor")),
        P(("dp", "tensor")),
        P("dp", "tensor", None),
    )
    out_specs = (
        P("dp", "tensor", None),
        P("dp", "tensor", None),
        P("dp", "tensor", None),
        P("dp", None, "tensor"),
        P("tensor", "dp"),
        P("dp", "tensor"),
        P("dp", None, "tensor"),
        P("tensor", "dp"),
        P(None, ("dp", "tensor")),
        P(("dp", "tensor")),
        P(("dp", "tensor"), None),
        P(("dp", "tensor")),
        P(("dp", "tensor")),
        P(("dp", "tensor")),
        P(("dp", "tensor")),
        P(("dp", "tensor")),
        P(("dp", "tensor")),
        P(("dp", "tensor")),
    )

    def run(*arrays):
        width = arrays[0].shape[2]
        aligned = width // mesh.shape["dp"] % 16 == 0 and mesh.shape["dp"] % 4 == 0
        inner = fast_local if aligned and mesh.shape["tensor"] == 2 else plain_local
        return jax.shard_map(inner, mesh=mesh, in_specs=in_specs, out_specs=out_specs, check_vma=False)(*arrays)

    return run
```

```python
import functools

import jax
import jax.numpy as jnp
from jax import lax
from jax.experimental import pallas as pl
from jax.experimental.pallas import tpu as pltpu
from jax.sharding import PartitionSpec as P

HEAD = 64
EPS = 1e-05
NEGATIVE = -1e30
MESH = pl.DeviceIdType.MESH
HBM = pltpu.HBM
VMEM = pltpu.VMEM
PIECES = 8
FF_PIECES = 16


class Place:
    def __init__(self):
        self.dp = lax.axis_index("dp")
        self.y = lax.axis_index("tensor")
        self.c = lax.rem(self.dp, 2)
        self.x = lax.rem(self.dp // 2, 2)
        self.z = self.dp // 4

    def at(self, z=None, x=None, c=None, y=None):
        z = self.z if z is None else z
        x = self.x if x is None else x
        c = self.c if c is None else c
        y = self.y if y is None else y
        return ((z * 2 + x) * 2 + c, y)

    def core(self):
        return self.at(c=1 - self.c)

    def xn(self):
        return self.at(x=1 - self.x)

    def yn(self):
        return self.at(y=1 - self.y)

    def up(self):
        return self.at(z=self.z + 1)

    def down(self):
        return self.at(z=self.z - 1)


def remote(src, dst, send, recv, device):
    return pltpu.make_async_remote_copy(
        src_ref=src, dst_ref=dst, send_sem=send, recv_sem=recv, device_id=device, device_id_type=MESH
    )


def signal(sem, device):
    pl.semaphore_signal(sem, inc=1, device_id=device, device_id_type=MESH)


class LineGather:
    def __init__(self, place, depth, slot, send, recv):
        self.p, self.n, self.slot, self.send, self.recv = place, depth, slot, send, recv

    def _copy_up(self, k):
        b = self.p.z - k
        return remote(self.slot(b), self.slot(b), self.send.at[0, k], self.recv.at[0, k], self.p.up())

    def _copy_down(self, k):
        b = self.p.z + k
        return remote(self.slot(b), self.slot(b), self.send.at[1, k], self.recv.at[1, k], self.p.down())

    def _from_below(self, k):
        b = self.p.z - k
        return remote(self.slot(b), self.slot(b), self.send.at[0, k - 1], self.recv.at[0, k - 1], self.p.up())

    def _from_above(self, k):
        b = self.p.z + k
        return remote(self.slot(b), self.slot(b), self.send.at[1, k - 1], self.recv.at[1, k - 1], self.p.down())

    def arrive(self, k):
        z = self.p.z

        @pl.when(z - k >= 0)
        def _():
            self._from_below(k).wait_recv()

        @pl.when(z + k <= self.n - 1)
        def _():
            self._from_above(k).wait_recv()

    def step(self, k):
        z = self.p.z
        if k > 0:
            self.arrive(k)
        if k < self.n - 1:

            @pl.when((z - k >= 0) & (z < self.n - 1))
            def _():
                self._copy_up(k).start()

            @pl.when((z + k <= self.n - 1) & (z > 0))
            def _():
                self._copy_down(k).start()

    def sent(self):
        z = self.p.z
        for k in range(self.n - 1):

            @pl.when((z - k >= 0) & (z < self.n - 1))
            def _():
                self._copy_up(k).wait_send()

            @pl.when((z + k <= self.n - 1) & (z > 0))
            def _():
                self._copy_down(k).wait_send()


class PlaneGather:
    def __init__(self, place, slot, send, recv):
        self.p, self.slot, self.send, self.recv = place, slot, send, recv
        p = place
        x, y, c = p.x, p.y, p.c
        ox, oy = 1 - x, 1 - y
        self.moves = [
            ((x, c, y, None), p.xn(), 0),
            ((x, c, y, None), p.yn(), 1),
            ((ox, c, y, 0), p.yn(), 2),
            ((x, c, oy, 1), p.xn(), 3),
            ((x, c, y, None), p.core(), 4),
            ((ox, c, y, None), p.core(), 5),
            ((x, c, oy, None), p.core(), 6),
            ((ox, c, oy, None), p.core(), 7),
        ]
        oc = 1 - c
        self.arrivals = [
            (ox, c, y, None),
            (x, c, oy, None),
            (ox, c, oy, 0),
            (ox, c, oy, 1),
            (x, oc, y, None),
            (ox, oc, y, None),
            (x, oc, oy, None),
            (ox, oc, oy, None),
        ]

    def _move(self, i):
        where, device, s = self.moves[i]
        return remote(self.slot(*where), self.slot(*where), self.send.at[s], self.recv.at[s], device)

    def _arrival(self, i):
        view = self.slot(*self.arrivals[i])
        return remote(view, view, self.send.at[i], self.recv.at[i], self.moves[i][1])

    def begin(self):
        self._move(0).start()
        self._move(1).start()
        self._move(4).start()

    def forward(self):
        self._arrival(0).wait_recv()
        self._move(2).start()
        self._move(5).start()
        self._arrival(1).wait_recv()
        self._move(3).start()
        self._move(6).start()

    def finish(self):
        self._arrival(2).wait_recv()
        self._arrival(3).wait_recv()
        self._move(7).start()

    def end(self):
        for i in range(4, 8):
            self._arrival(i).wait_recv()

    def sent(self):
        for i in range(8):
            self._move(i).wait_send()


def all_barrier(place, count):
    sem = pltpu.get_barrier_semaphore()
    me = place.dp * 2 + place.y

    @pl.loop(1, count)
    def _(j):
        other = lax.rem(me + j, count)
        signal(sem, (other // 2, lax.rem(other, 2)))

    pl.semaphore_wait(sem, count - 1)


def far_first(z, s, depth):
    b = 0
    for place in range(depth):
        order = sorted(range(depth), key=lambda k: (-abs(k - place), k))
        b = jnp.where(z == place, order[s], b)
    return b


class LineReduce:
    def __init__(self, place, depth, part, slots, send, recv):
        self.p, self.n, self.part, self.slots, self.send, self.recv = place, depth, part, slots, send, recv

    def _up(self, b):
        slot = b - (self.p.z + 1)
        return remote(self.part(b), self.slots(slot), self.send.at[b], self.recv.at[slot], self.p.up())

    def _down(self, b):
        slot = self.n - b
        return remote(self.part(b), self.slots(slot), self.send.at[b], self.recv.at[slot], self.p.down())

    def below(self, b):
        slot = b - self.p.z
        return remote(self.slots(slot), self.slots(slot), self.send.at[b], self.recv.at[slot], self.p.up())

    def above(self, b):
        slot = self.n - b
        return remote(self.slots(slot), self.slots(slot), self.send.at[b], self.recv.at[slot], self.p.down())

    def first(self, b):
        z = self.p.z

        @pl.when((z == 0) & (b > z))
        def _():
            self._up(b).start()

        @pl.when((z == self.n - 1) & (b < z))
        def _():
            self._down(b).start()

    def middle(self, b, add):
        z = self.p.z

        @pl.when((z > 0) & (b > z))
        def _():
            self.below(b).wait_recv()
            add(self.part(b), self.slots(b - z))
            self._up(b).start()

        @pl.when((z < self.n - 1) & (b < z))
        def _():
            self.above(b).wait_recv()
            add(self.part(b), self.slots(self.n - b))
            self._down(b).start()

    def last(self, take):
        z = self.p.z

        @pl.when(z > 0)
        def _():
            self.below(z).wait_recv()
            take(self.slots(0))

        @pl.when(z < self.n - 1)
        def _():
            self.above(z).wait_recv()
            take(self.slots(self.n - z))

    def sent(self):
        z = self.p.z

        @pl.loop(0, self.n)
        def _(b):
            @pl.when(b > z)
            def _():
                self._up(b).wait_send()

            @pl.when(b < z)
            def _():
                self._down(b).wait_send()


def add_low(part, other):
    part[...] = (part[...].astype(jnp.float32) + other[...].astype(jnp.float32)).astype(part.dtype)


def gelu_pair(x):
    a, b = 0.7978845608028654, 0.044715
    square = x * x
    t = jnp.tanh(a * x * (1.0 + b * square))
    half = 0.5 * (1.0 + t)
    return x * half, half + 0.5 * x * (1.0 - t * t) * (a * (1.0 + 3.0 * b * square))


NN = (((1,), (0,)), ((), ()))
NT = (((1,), (1,)), ((), ()))
TN = (((0,), (0,)), ((), ()))


def mm(left, right, form=NN):
    return lax.dot_general(left, right, form, preferred_element_type=jnp.float32)


def neighbour_barrier(p, depth):
    sem = pltpu.get_barrier_semaphore()
    for dx in range(2):
        for dc in range(2):
            for dy in range(2):
                if dx + dc + dy:
                    signal(sem, p.at(x=lax.rem(p.x + dx, 2), c=lax.rem(p.c + dc, 2), y=lax.rem(p.y + dy, 2)))

    @pl.loop(1, depth)
    def _(k):
        signal(sem, p.at(z=lax.rem(p.z + k, depth)))

    pl.semaphore_wait(sem, 7 + depth - 1)


def layer_norm(x, gain, shift):
    center = x - jnp.mean(x, axis=-1, keepdims=True)
    inverse = lax.rsqrt(jnp.mean(center * center, axis=-1, keepdims=True) + EPS)
    return center * inverse * gain + shift


def attend_pairs(q_ref, k_ref, v_ref, allowed, probs_ref, heads_ref, start, stop):
    rows = q_ref.shape[0]
    first = lax.broadcasted_iota(jnp.int32, (rows, 128), 1) < HEAD
    both = jnp.concatenate([allowed, allowed], axis=0)

    @pl.loop(start, stop)
    def _(h):
        at = (slice(None), pl.ds(pl.multiple_of(h * 128, 128), 128))
        q, k, v = q_ref[at], k_ref[at], v_ref[at]
        zero = jnp.zeros_like(q)
        pair = jnp.concatenate([jnp.where(first, q, zero), jnp.where(first, zero, q)], axis=0)
        scores = jnp.where(both, mm(pair, k, NT) * HEAD**-0.5, NEGATIVE)
        weights = jnp.exp(scores - jnp.max(scores, axis=-1, keepdims=True))
        probs = (weights * (1.0 / jnp.sum(weights, axis=-1, keepdims=True))).astype(jnp.bfloat16)
        probs_ref[h] = probs
        mix = mm(probs, v)
        heads_ref[at] = jnp.where(first, mix[:rows], mix[rows:]).astype(jnp.bfloat16)


Q, K, V, CQ, H1, H2, N1, N2, N3 = range(9)
CK, CV, ENC = range(3)


def forward_kernel(
    depth,
    proj, so, pairs_in, query, co, win, wout, vec, tok_in, enc_in, cot, target, source,
    G, act_out, ctx_out, mid_out, p1_out, p2_out, full_out, cot_out,
    d_out, y_out, go_out, gbias_out, S_out, YS_out,
    ATT, W, TOK, VEC, FULL, BIAS, ACT, CTX, MID, P1, P2, TARGET, SOURCE, OWN_T, OWN_E,
    HN, G3, WI, WO, S, RF, ACTIVE, SLOPE, BS, BR, CS, CR, CSY, CRY, PS, PR, DA, YA, DSUM, YSUM, GO, GB, LATS, LATR,
    lsem, wsem, osem, zs, zr, fs, fr, ps, pr, vs, vr, ss, sr, gs, gr, hs, hr, bs, br, cs, cr, ys, yr, xs, xr, us, ur,
):
    p = Place()
    z = p.z
    count = 8 * depth
    me = p.dp * 2 + p.y
    rows, width = ACT.shape[1:]
    short = CTX.shape[1]
    units = WO.shape[1]
    half, few = rows // 2, short // 2
    part = ATT.shape[1]
    mine = pl.ds(pl.multiple_of(p.y * few, few), few)
    local = []

    def keep(src, dst):
        copy = pltpu.make_async_copy(src, dst, lsem.at[len(local)])
        copy.start()
        local.append(copy)

    keep(vec, VEC.at[me])
    keep(tok_in, OWN_T)
    keep(enc_in, OWN_E)
    keep(proj, ATT.at[pl.ds(0, 3)])
    keep(so, ATT.at[3])
    keep(pairs_in, ATT.at[pl.ds(4, 2)])
    keep(query, ATT.at[6])
    keep(co, ATT.at[7])
    keep(cot, G3.at[p.x, p.c, :, p.y])
    keep(win, WI.at[:, pl.ds(pl.multiple_of(z * units, units), units)])
    keep(wout, WO.at[z])
    keep(target, TARGET)
    keep(source, SOURCE)
    BS[...] = jnp.zeros_like(BS)
    all_barrier(p, count)
    for copy in local:
        copy.wait()
    TOK[p.y] = OWN_T[p.y]
    CTX[ENC, mine] = OWN_E[p.y]
    own = pltpu.make_async_copy(ATT, G.at[:, p.y, z, p.x, p.c], lsem.at[0])
    own.start()

    lines = []
    for i in range(PIECES):
        lines.append(LineGather(p, depth, lambda b, i=i: G.at[i, p.y, b, p.x, p.c], zs.at[i], zr.at[i]))
    wr = WI.shape[0] // (FF_PIECES // 2)
    orow = units // (FF_PIECES // 2)
    ff = []
    for i in range(FF_PIECES):
        if i < FF_PIECES // 2:
            slot = lambda b, i=i: WI.at[pl.ds(i * wr, wr), pl.ds(pl.multiple_of(b * units, units), units)]
        else:
            slot = lambda b, i=i: WO.at[b, pl.ds((i - FF_PIECES // 2) * orow, orow)]
        ff.append(LineGather(p, depth, slot, fs.at[i], fr.at[i]))

    def plane_slot(i):
        def slot(x, c, y, h):
            if h is None:
                return G.at[i, y, :, x, c]
            return G.at[i, y, :, x, c, pl.ds(h * (part // 2), part // 2)]

        return slot

    def g3_slot(r):
        few_rows = G3.shape[4] // 2

        def slot(x, c, y, h):
            if h is None:
                return G3.at[x, c, r, y]
            return G3.at[x, c, r, y, pl.ds(h * few_rows, few_rows)]

        return slot

    slots = [g3_slot(0)] + [plane_slot(i) for i in range(PIECES)] + [g3_slot(1)]
    planes = [PlaneGather(p, slot, ps.at[i], pr.at[i]) for i, slot in enumerate(slots)]
    swaps = [
        remote(OWN_T.at[1 - p.y], TOK.at[p.y], ss.at[0], sr.at[0], p.yn()),
        remote(OWN_E.at[1 - p.y], CTX.at[ENC, mine], ss.at[1], sr.at[1], p.yn()),
    ]

    def swapped(i):
        if i == 0:
            view = TOK.at[1 - p.y]
        else:
            view = CTX.at[ENC, pl.ds(pl.multiple_of((1 - p.y) * few, few), few)]
        remote(view, view, ss.at[i], sr.at[i], p.yn()).wait_recv()

    swaps[0].start()

    def vec_move(j):
        other = lax.rem(me + j, count)
        return remote(VEC.at[me], VEC.at[me], vs.at[j], vr.at[j], (other // 2, lax.rem(other, 2)))

    @pl.loop(1, count)
    def _(j):
        vec_move(j).start()

    own.wait()

    saved = []

    def save(src, dst):
        copy = pltpu.make_async_copy(src, dst, osem.at[len(saved)])
        copy.start()
        saved.append(copy)

    def vector(i):
        return FULL[i : i + 1]

    def weight(i):
        copy = pltpu.make_async_copy(G.at[i], W, wsem.at[0])
        copy.start()
        copy.wait()

    def project(a, store):
        for y in range(2):
            store(y * (width // 2), mm(a, W[y].reshape(width, width // 2)))

    def project_back(a_ref):
        total = None
        for y in range(2):
            term = mm(a_ref[:, y * (width // 2) : (y + 1) * (width // 2)], W[y].reshape(width, width // 2), NT)
            total = term if total is None else total + term
        return total

    def into(ref, i):
        def store(at, value):
            ref[i, :, at : at + width // 2] = value.astype(jnp.bfloat16)

        return store

    def first_norm():
        @pl.loop(1, count)
        def _(j):
            other = lax.rem(me + count - j, count)
            remote(VEC.at[other], VEC.at[other], vs.at[j], vr.at[j], p.yn()).wait_recv()

        group = count * 128 // width
        for k in range(width // 128):
            piece = VEC[group * k, 0:8]
            for j in range(1, group):
                piece += VEC[group * k + j, 0:8]
            FULL[:, k * 128 : (k + 1) * 128] = piece
        save(FULL, full_out)
        for b in range(depth):
            held = VEC[((b * 2 + p.x) * 2 + p.c) * 2 + p.y]
            for k in range(units // 128):
                at = b * units + k * 128
                BIAS[:, at : at + 128] = jnp.broadcast_to(held[8 + k : 9 + k], (8, 128))
        swapped(0)
        tok = TOK[...].reshape(rows, width).astype(jnp.float32)
        MID[0] = tok
        ACT[N1] = layer_norm(tok, vector(0), vector(1)).astype(jnp.bfloat16)
        save(ACT.at[N1], act_out.at[N1])

    def qkv(i):
        weight(i)
        project(ACT[N1], into(ACT, (Q, K, V)[i]))
        save(ACT.at[(Q, K, V)[i]], act_out.at[(Q, K, V)[i]])

    def same(left, right):
        def pair(ref):
            row = ref[pl.ds(p.y, 1)].astype(jnp.float32)
            rest = jnp.zeros((14, row.shape[1]), jnp.float32)
            return jnp.concatenate([row, 1.0 - row, rest], axis=0).astype(jnp.bfloat16)

        return mm(pair(left), pair(right), TN) > 0.5

    pairs_of_heads = width // 128

    def self_attention(start, stop):
        back = lax.broadcasted_iota(jnp.int32, (rows, rows), 1) <= lax.broadcasted_iota(jnp.int32, (rows, rows), 0)
        attend_pairs(
            ACT.at[Q], ACT.at[K], ACT.at[V], same(TARGET, TARGET) & back, P1, ACT.at[H1], start, stop
        )

    def self_project():
        self_attention(pairs_of_heads // 2, pairs_of_heads)
        save(P1, p1_out)
        save(ACT.at[H1], act_out.at[H1])
        weight(3)
        middle = MID[0] + project_back(ACT.at[H1])
        MID[1] = middle
        ACT[N2] = layer_norm(middle, vector(2), vector(3)).astype(jnp.bfloat16)
        save(MID.at[pl.ds(0, 2)], mid_out.at[pl.ds(0, 2)])
        save(ACT.at[N2], act_out.at[N2])

    def pairs(i):
        if i == 0:
            swapped(1)
        weight(4 + i)
        project(CTX[ENC], into(CTX, (CK, CV)[i]))

    def cross_attention():
        save(CTX, ctx_out)
        weight(6)
        project(ACT[N2], into(ACT, CQ))
        save(ACT.at[CQ], act_out.at[CQ])
        attend_pairs(
            ACT.at[CQ], CTX.at[CK], CTX.at[CV], same(TARGET, SOURCE), P2, ACT.at[H2], 0, pairs_of_heads
        )
        save(P2, p2_out)
        save(ACT.at[H2], act_out.at[H2])

    def hn_slot(x, c, y, h):
        if h is None:
            return HN.at[x, c, y]
        return HN.at[x, c, y, pl.ds(h * half, half)]

    gather = PlaneGather(p, hn_slot, gs, gr)

    def cross_project():
        weight(7)
        latter = MID[1] + project_back(ACT.at[H2])
        HN[p.x, p.c, p.y] = layer_norm(latter, vector(4), vector(5)).astype(jnp.bfloat16)
        gather.begin()
        MID[2] = latter
        save(MID.at[2], mid_out.at[2])
        LATS[...] = MID[2, pl.ds(pl.multiple_of((1 - p.y) * half, half), half)].astype(jnp.bfloat16)

    work = {
        0: [functools.partial(qkv, 0)],
        1: [functools.partial(qkv, 1)],
        2: [functools.partial(qkv, 2), functools.partial(self_attention, 0, pairs_of_heads // 2)],
        3: [self_project],
        4: [functools.partial(pairs, 0)],
        5: [functools.partial(pairs, 1)],
        6: [cross_attention],
        7: [cross_project],
    }
    lead = depth - 2
    turns = 2 * (lead + len(planes) + 3)
    early, late = 2 * lead, 2 * lead + 2 * PIECES - 2
    starts = list(range(early)) + list(range(early, late, 3))
    starts += list(range(late, late + FF_PIECES - len(starts)))

    def turn(n):
        for f in range(FF_PIECES):
            k = n - starts[f]
            if k % 2 == 0 and 0 <= k < 2 * depth:
                ff[f].step(k // 2)

    for it in range(-lead, len(planes) + 3):
        for i in range(PIECES):
            if 0 <= it - i + lead < depth:
                lines[i].step(it - i + lead)
        if 0 <= it < len(planes):
            planes[it].begin()
        turn(2 * (it + lead))
        if it == 0:
            swaps[1].start()
        if 0 <= it - 1 < len(planes):
            planes[it - 1].forward()
        if 0 <= it - 2 < len(planes):
            planes[it - 2].finish()
        turn(2 * (it + lead) + 1)
        if 0 <= it - 3 < len(planes):
            planes[it - 3].end()
        if it == 1:
            first_norm()
        for task in work.get(it - 4, []):
            task()

    def bits(code):
        dc, dx, dy = code // 4, lax.rem(code // 2, 2), lax.rem(code, 2)
        return lax.rem(p.x + dx, 2), lax.rem(p.c + dc, 2), lax.rem(p.y + dy, 2)

    arriving = (0, 4, 1, 2, 5, 6, 3, 7)
    leaving = (7, 6, 3, 5, 2, 1, 4, 0)
    for_core = (1, 1, 0, 1, 0, 0, 1, 0)
    turn_of = (0, 1, 0, 2, 1, 2, 3, 3)

    def pick(i, table):
        value = table[0]
        for k in range(1, 8):
            value = jnp.where(i == k, table[k], value)
        return value

    def to_core(j, send, land, a, b):
        return remote(send.at[j], land.at[j], a.at[j], b.at[j], p.core())

    def to_chip(j):
        dx, dy = 1 - j // 2, 1 - lax.rem(j, 2)
        return remote(
            PS.at[j], PR.at[j], xs.at[j], xr.at[j], p.at(x=lax.rem(p.x + dx, 2), y=lax.rem(p.y + dy, 2))
        )

    def diagonal(src, land, n, h):
        return remote(
            src.at[0, pl.ds(h * half, half)], land.at[h], us.at[n, h], ur.at[n, h], p.yn() if h else p.xn()
        )

    def merge(parts, land, n):
        diagonal(parts, land, n, 0).wait_recv()
        add_low(parts.at[2, pl.ds(0, half)], land.at[0])
        diagonal(parts, land, n, 1).wait_recv()
        add_low(parts.at[1, pl.ds(half, half)], land.at[1])

    latter_move = remote(LATS, LATR, ss.at[2], sr.at[2], p.yn())

    def bias_move(b):
        return remote(BS.at[b], BR.at[z], bs.at[b], br.at[z], p.at(z=b))

    def up(h):
        return remote(S.at[depth - 1, h], RF.at[h], hs.at[h], hr.at[h], p.up())

    def down(h):
        return remote(S.at[0, h], RF.at[h], hs.at[h], hr.at[h], p.down())

    def hop(s, h):
        @pl.when(jnp.logical_and(s == 0, z == 0))
        def _():
            up(h).start()

        @pl.when(jnp.logical_and(s == 0, z == depth - 1))
        def _():
            down(h).start()


    @pl.loop(0, 8)
    def _(i):
        @pl.when(i == 1)
        def _():
            gather._arrival(4).wait_recv()

        @pl.when(i == 2)
        def _():
            gather.forward()

        @pl.when(i == 4)
        def _():
            gather._arrival(5).wait_recv()
            gather._arrival(6).wait_recv()

        @pl.when(i == 6)
        def _():
            gather.finish()

        @pl.when(i == 7)
        def _():
            gather._arrival(7).wait_recv()

        at = bits(pick(i, arriving))
        before = mm(HN[at], WI[...]) + BIAS[0:1]
        active, slope = gelu_pair(before)
        ACTIVE[at] = active.astype(jnp.bfloat16)
        SLOPE[at] = slope.astype(jnp.bfloat16)

    def block(s):
        b = far_first(z, 0, depth)
        for k in range(1, depth):
            b = jnp.where(s == k, far_first(z, k, depth), b)
        return b, pl.ds(pl.multiple_of(b * units, units), units)

    def out_sums(s):
        b, cols = block(s)
        gout = mm(ACTIVE[:, :, :, :, cols].reshape(8 * rows, units), G3[...].reshape(8 * rows, width), TN)
        GO[1] = gout
        S[b, 1] = gout.astype(jnp.bfloat16)
        hop(s, 1)

    out_sums(0)
    for n in range(turns, max(starts) + 2 * depth):
        turn(n)

    @pl.loop(0, 8)
    def _(i):
        at = bits(pick(i, leaving))
        slope = mm(G3[at].reshape(rows, width), WO[...].reshape(depth * units, width), NT)
        slope = (slope * SLOPE[at].astype(jnp.float32)).astype(jnp.bfloat16)
        SLOPE[at] = slope
        total = jnp.sum(slope.astype(jnp.float32), axis=0, keepdims=True)
        for b in range(depth):
            BS[b, 0:1] += total[:, b * units : (b + 1) * units]
        back = mm(slope, WI[...], NT)
        j = pick(i, turn_of)

        @pl.when(pick(i, for_core) == 1)
        def _():
            CS[j] = back.astype(jnp.bfloat16)
            to_core(j, CS, CR, cs, cr).start()

        @pl.when(pick(i, for_core) == 0)
        def _():
            to_core(j, CS, CR, cs, cr).wait_recv()
            total = back + CR[j].astype(jnp.float32)

            @pl.when(j < 3)
            def _():
                PS[j] = total.astype(jnp.bfloat16)

            @pl.when(j == 0)
            def _():
                diagonal(PS, DA, 0, 0).start()
                diagonal(PS, DA, 0, 1).start()

            @pl.when(j == 3)
            def _():
                DSUM[...] = total

        @pl.when(i == 6)
        def _():
            merge(PS, DA, 0)
            to_chip(1).start()
            to_chip(2).start()

    @pl.loop(1, depth)
    def _(k):
        bias_move(lax.rem(z + k, depth)).start()

    def in_sums(s):
        b, cols = block(s)
        gin = mm(SLOPE[:, :, :, :, cols].reshape(8 * rows, units), HN[...].reshape(8 * rows, width), TN)
        GO[0] = gin
        S[b, 0] = gin.astype(jnp.bfloat16)
        hop(s, 0)


    in_sums(0)
    latter_move.start()

    @pl.loop(0, 8)
    def _(i):
        ox, oc, oh = bits(pick(i, leaving))
        active = ACTIVE[ox, oc, :, pl.ds(pl.multiple_of(oh * half, half), half)].reshape(rows, depth * units)
        more = mm(active, WO[...].reshape(depth * units, width))

        j = pick(i, turn_of)

        @pl.when(pick(i, for_core) == 1)
        def _():
            CSY[j] = more.astype(jnp.bfloat16)
            to_core(j, CSY, CRY, ys, yr).start()

        @pl.when(pick(i, for_core) == 0)
        def _():
            to_core(j, CSY, CRY, ys, yr).wait()
            total = more + CRY[j].astype(jnp.float32)

            @pl.when(j < 3)
            def _():
                CSY[j] = total.astype(jnp.bfloat16)

            @pl.when(j == 0)
            def _():
                diagonal(CSY, YA, 1, 0).start()
                diagonal(CSY, YA, 1, 1).start()

            @pl.when(j == 3)
            def _():
                YSUM[...] = total.reshape(2, half, width)

    @pl.loop(1, depth)
    def _(s):
        in_sums(s)
        out_sums(s)

    save(GO, go_out)
    save(G3.at[p.x, p.c, p.y], cot_out)

    GB[...] = BS[z]

    @pl.loop(1, depth)
    def _(k):
        other = lax.rem(z + k, depth)
        remote(BS.at[other], BR.at[other], bs.at[other], br.at[other], p.at(z=other)).wait()
        GB[...] += BR[other]

    save(GB, gbias_out)

    @pl.loop(1, 3)
    def _(j):
        to_chip(j).wait_recv()
        DSUM[...] += PR[j].astype(jnp.float32)

    save(DSUM, d_out)

    @pl.when((z == 1) | (z == depth - 2))
    def _():
        far = jnp.where(z == 1, depth - 1, 0)
        for h in range(2):
            up(h).wait_recv()
            add_low(S.at[far, h], RF.at[h])

    save(S, S_out)
    latter_move.wait()
    YSUM[p.y] += MID[2, pl.ds(pl.multiple_of(p.y * half, half), half)] + vector(6)
    YSUM[1 - p.y] += LATR[...].astype(jnp.float32) + vector(6)

    merge(CSY, YA, 1)
    save(CSY.at[pl.ds(1, 2)], YS_out)
    save(YSUM, y_out)

    @pl.when((z == 0) | (z == depth - 1))
    def _():
        for h in range(2):
            up(h).wait_send()

    for line in lines + ff:
        line.sent()
    for plane in planes + [gather]:
        plane.sent()
    for copy in swaps:
        copy.wait_send()

    @pl.loop(1, count)
    def _(j):
        vec_move(j).wait_send()

    @pl.loop(0, 4)
    def _(j):
        to_core(j, CS, CR, cs, cr).wait_send()

    @pl.loop(1, 3)
    def _(j):
        to_chip(j).wait_send()

    for h in range(2):
        diagonal(PS, DA, 0, h).wait_send()
        diagonal(CSY, YA, 1, h).wait_send()

    for copy in saved:
        copy.wait()


def forward_all(proj, so, pairs, query, co, win, wout, vec, tok, enc, cot, target, source):
    depth = lax.axis_size("dp") // 4
    rows, cols = query.shape
    bf, f32 = jnp.bfloat16, jnp.float32
    count = 8 * depth
    length, short, d = 2 * tok.shape[1], 2 * enc.shape[1], tok.shape[2]
    units = wout.shape[0]
    heads = d // 128
    whole = (2, depth, 2, 2, rows, cols)
    shapes = {
        "G": ((PIECES,) + whole, bf),
        "ACT": ((9, length, d), bf),
        "CTX": ((3, short, d), bf),
        "MID": ((3, length, d), f32),
        "P1": ((heads, 2 * length, length), bf),
        "P2": ((heads, 2 * length, short), bf),
        "FULL": ((8, d), f32),
        "COT": (cot.shape, bf),
        "DSUM": ((length, d), f32),
        "YSUM": ((2, length // 2, d), f32),
        "GO": ((2, units, d), f32),
        "GB": ((8, units), f32),
        "S": ((depth, 2, units, d), bf),
        "YS": ((2, length, d), bf),
    }
    outs = [jax.ShapeDtypeStruct(*shape) for shape in shapes.values()]

    def held(name):
        return pltpu.VMEM(*shapes[name])

    dma = pltpu.SemaphoreType.DMA
    hb = pl.BlockSpec(memory_space=HBM)
    tokens = (2, 2, 2, length, d)
    four = pltpu.VMEM((4, length, d), bf)
    three = pltpu.VMEM((3, length, d), bf)
    scratch = [
        pltpu.VMEM((PIECES, rows, cols), bf),
        pltpu.VMEM(whole, bf),
        pltpu.VMEM(tok.shape, bf),
        pltpu.VMEM((count,) + vec.shape, f32),
        held("FULL"),
        pltpu.VMEM((8, depth * units), f32),
        held("ACT"), held("CTX"), held("MID"), held("P1"), held("P2"),
        pltpu.VMEM(target.shape, jnp.int32), pltpu.VMEM(source.shape, jnp.int32),
        pltpu.VMEM(tok.shape, bf), pltpu.VMEM(enc.shape, bf),
        pltpu.VMEM(tokens, bf),
        pltpu.VMEM((2, 2, 2, 2) + cot.shape[1:], bf),
        pltpu.VMEM((d, depth * units), bf),
        pltpu.VMEM((depth, units, d), bf),
        held("S"),
        pltpu.VMEM((2, units, d), bf),
        pltpu.VMEM(tokens[:4] + (depth * units,), bf),
        pltpu.VMEM(tokens[:4] + (depth * units,), bf),
        pltpu.VMEM((depth, 8, units), f32),
        pltpu.VMEM((depth, 8, units), f32),
        four, four, four, four, three, three,
        pltpu.VMEM((2, length // 2, d), bf), pltpu.VMEM((2, length // 2, d), bf),
        held("DSUM"), held("YSUM"), held("GO"), held("GB"),
        pltpu.VMEM((length // 2, d), bf), pltpu.VMEM((length // 2, d), bf),
        dma((13,)), dma((1,)), dma((24,)),
        dma((PIECES, 2, depth - 1)), dma((PIECES, 2, depth - 1)),
        dma((FF_PIECES, 2, depth - 1)), dma((FF_PIECES, 2, depth - 1)),
        dma((PIECES + 2, 8)), dma((PIECES + 2, 8)),
        dma((count,)), dma((count,)),
        dma((3,)), dma((3,)),
        dma((8,)), dma((8,)),
        dma((2,)), dma((2,)),
        dma((depth,)), dma((depth,)),
        dma((4,)), dma((4,)),
        dma((4,)), dma((4,)),
        dma((3,)), dma((3,)),
        dma((2, 2)), dma((2, 2)),
    ]
    return pl.pallas_call(
        functools.partial(forward_kernel, depth),
        out_shape=outs,
        in_specs=[hb] * 13,
        out_specs=[hb] * len(outs),
        scratch_shapes=scratch,
        compiler_params=pltpu.CompilerParams(
            collective_id=1, has_side_effects=True, vmem_limit_bytes=63 << 20
        ),
        name="forward_all",
    )(proj, so, pairs, query, co, win, wout, vec, tok, enc, cot, target, source)


def norm_back(e, h, gain):
    center = h - jnp.mean(h, axis=-1, keepdims=True)
    inverse = lax.rsqrt(jnp.mean(center * center, axis=-1, keepdims=True) + EPS)
    normal = center * inverse
    scaled = e * gain
    back = inverse * (
        scaled
        - jnp.mean(scaled, axis=-1, keepdims=True)
        - normal * jnp.mean(scaled * normal, axis=-1, keepdims=True)
    )
    return back, jnp.sum(e * normal, axis=0, keepdims=True), jnp.sum(e, axis=0, keepdims=True)


def attend_pairs_back(q_ref, k_ref, v_ref, probs_ref, slope_ref, dq_ref, dk_ref, dv_ref, start, stop):
    rows = q_ref.shape[0]
    first = lax.broadcasted_iota(jnp.int32, (rows, 128), 1) < HEAD

    def stacked(a):
        zero = jnp.zeros_like(a)
        return jnp.concatenate([jnp.where(first, a, zero), jnp.where(first, zero, a)], axis=0)

    @pl.loop(start, stop)
    def _(h):
        at = (slice(None), pl.ds(pl.multiple_of(h * 128, 128), 128))
        up = stacked(slope_ref[at])
        low = probs_ref[h]
        probs = low.astype(jnp.float32)
        dprobs = mm(up, v_ref[at], NT)
        ds = (probs * (dprobs - jnp.sum(probs * dprobs, axis=-1, keepdims=True))).astype(jnp.bfloat16)
        dq = mm(ds, k_ref[at]) * HEAD**-0.5
        dq_ref[at] = jnp.where(first, dq[:rows], dq[rows:]).astype(jnp.bfloat16)
        dk_ref[at] = (mm(ds, stacked(q_ref[at]), TN) * HEAD**-0.5).astype(jnp.bfloat16)
        dv_ref[at] = mm(low, up, TN).astype(jnp.bfloat16)


class HoppedReduce(LineReduce):
    def _down(self, b):
        slot = self.n - 2 + self.p.z - 1 - b
        return remote(self.part(b), self.slots(slot), self.send.at[b], self.recv.at[slot], self.p.down())

    def above(self, b):
        slot = self.n - 2 + self.p.z - b
        return remote(self.slots(slot), self.slots(slot), self.send.at[b], self.recv.at[slot], self.p.down())

    def first(self, b):
        z, n = self.p.z, self.n

        @pl.when((b > z) & (((z == 0) & (b < n - 1)) | ((z == 1) & (b == n - 1))))
        def _():
            self._up(b).start()

        @pl.when((b < z) & (((z == n - 1) & (b > 0)) | ((z == n - 2) & (b == 0))))
        def _():
            self._down(b).start()

    def middle(self, b, add):
        z, n = self.p.z, self.n

        @pl.when((z > 0) & (b > z) & ((z > 1) | (b < n - 1)))
        def _():
            self.below(b).wait_recv()
            add(self.part(b), self.slots(b - z))
            self._up(b).start()

        @pl.when((z < n - 1) & (b < z) & ((z < n - 2) | (b > 0)))
        def _():
            self.above(b).wait_recv()
            add(self.part(b), self.slots(n - 2 + z - b))
            self._down(b).start()

    def last(self, take):
        z, n = self.p.z, self.n

        @pl.when(z > 0)
        def _():
            self.below(z).wait_recv()
            take(self.slots(0))

        @pl.when(z < n - 1)
        def _():
            self.above(z).wait_recv()
            take(self.slots(n - 2))

    def sent(self):
        z, n = self.p.z, self.n

        @pl.loop(0, n)
        def _(b):
            @pl.when((b > z) & ((z > 0) | (b < n - 1)))
            def _():
                self._up(b).wait_send()

            @pl.when((b < z) & ((z < n - 1) | (b > 0)))
            def _():
                self._down(b).wait_send()


SLOTS = 4
FF_PARTS = 8
FF_GAP = 2


def backward_kernel(
    depth,
    G, act, ctx, mid, p1, p2, full, cot_in, d_in, y_in, go_in, S_in, YS_in,
    gw_hbm, vec_hbm, res_hbm, tg_hbm, eg_hbm, go_hbm,
    gw_out, vec_out, res_out, tg_out, eg_out, go_out,
    MY, SEND, CR, PD, PR, R, S, RF, YS, YR, W, ACT, CTX, X, PB1, PB2, UP, LOW, SL, DH, DC, COT, FULL, VG, VR, XS, XR, ES, ER,
    lsem, wsem, cs, cr, ds, dr, ps, pr, zs, zr, fs, fr, ys, yr, vs, vr, ss, sr, osem, credit,
):
    p = Place()
    count = 8 * depth
    me = p.dp * 2 + p.y
    ox, oy = 1 - p.x, 1 - p.y
    rows, width = UP.shape
    short = CTX.shape[1]
    cols = width // 2
    part = MY.shape[4]
    low_type = jnp.bfloat16

    def load(i, src, dst):
        copy = pltpu.make_async_copy(src, dst, lsem.at[i])
        copy.start()
        return copy

    loads = [
        load(0, mid.at[2], X),
        load(1, d_in, UP),
        load(2, cot_in, COT),
        load(3, full, FULL),
        load(4, act.at[pl.ds(0, 8)], ACT),
        load(5, ctx, CTX),
        load(6, p2, PB2),
        load(7, S_in, S),
        load(8, go_in, go_out),
        load(9, p1, PB1),
        load(10, YS_in, YS),
        load(11, y_in, res_out),
    ]
    order = (7, 6, 3, 0, 1, 2, 4, 5)

    def weight(n):
        return pltpu.make_async_copy(G.at[order[n]], W.at[n % 2], wsem.at[n % 2])

    def use(n):
        weight(n).wait()
        if n + 1 < len(order):
            weight(n + 1).start()
        return [W[n % 2, y].reshape(width, cols) for y in range(2)]

    weight(0).start()
    VG[...] = jnp.zeros_like(VG)
    all_barrier(p, count)

    def y_move(j):
        return remote(YS.at[j], YR.at[j], ys.at[j], yr.at[j], p.yn() if j else p.xn())

    loads[10].wait()
    for j in range(2):
        y_move(j).start()

    def core(i):
        return remote(SEND.at[i % 2], CR.at[i % SLOTS], cs.at[i], cr.at[i], p.core())

    def cut(i, h):
        by_x = part // 2
        return pl.ds(by_x, part - by_x) if h else pl.ds(0, by_x)

    def diagonal(i, h):
        return remote(
            MY.at[i, oy, :, ox, cut(i, h)], PD.at[i, :, cut(i, h)], ds.at[i, h], dr.at[i, h],
            p.yn() if h else p.xn(),
        )

    def column(i, h):
        view = MY.at[i, oy, :, p.x] if h else MY.at[i, p.y, :, ox]
        return remote(view, PR.at[i, h], ps.at[i, h], pr.at[i, h], p.yn() if h else p.xn())

    lines = [
        LineReduce(
            p, depth, lambda b, i=i: MY.at[i, p.y, b, p.x], lambda k, i=i: R.at[i, k], zs.at[i], zr.at[i]
        )
        for i in range(PIECES)
    ]
    frows = S.shape[2] // (FF_PARTS // 2)
    ff = []
    for f in range(FF_PARTS):
        at = pl.ds(f // 2 * frows, frows)
        ff.append(
            HoppedReduce(
                p, depth, lambda b, f=f, at=at: S.at[b, f % 2, at], lambda k, f=f, at=at: RF.at[k, f % 2, at],
                fs.at[f], fr.at[f],
            )
        )

    def store_part(i, left, right):
        if i >= 2:
            core(i - 2).wait_send()
        for y in range(2):
            value = mm(left, right[:, y * cols : (y + 1) * cols], TN).reshape(depth, 2, 2, part, cols)
            value = value.astype(low_type)
            even, odd = value[:, :, 0], value[:, :, 1]
            MY[i, y] = jnp.where(p.c == 0, even, odd)
            SEND[i % 2, y] = jnp.where(p.c == 0, odd, even)
        if i >= SLOTS:
            pl.semaphore_wait(credit, 1)
        core(i).start()

    def stage(i, s):
        if s == 1:
            core(i).wait_recv()
            add_low(MY.at[i], CR.at[i % SLOTS])
            if i + SLOTS < PIECES:
                signal(credit, p.core())
            diagonal(i, 0).start()
            diagonal(i, 1).start()
        elif s == 2:
            diagonal(i, 0).wait_recv()
            add_low(MY.at[i, oy, :, p.x, cut(i, 0)], PD.at[i, :, cut(i, 0)])
            column(i, 1).start()
            diagonal(i, 1).wait_recv()
            add_low(MY.at[i, p.y, :, ox, cut(i, 1)], PD.at[i, :, cut(i, 1)])
            column(i, 0).start()
        elif s == 3:
            column(i, 0).wait_recv()
            column(i, 1).wait_recv()
            view = MY.at[i, p.y, :, p.x]
            view[...] = (
                view[...].astype(jnp.float32)
                + PR[i, 0].astype(jnp.float32)
                + PR[i, 1].astype(jnp.float32)
            ).astype(low_type)
            for k in range(depth - 1):
                lines[i].first(far_first(p.z, k, depth))
        elif s < 3 + depth:
            lines[i].middle(far_first(p.z, s - 4, depth), add_low)
        elif s == 3 + depth:
            gw_out[i] = MY[i, p.y, p.z, p.x].astype(jnp.float32)

            def take(slot):
                gw_out[i] += slot[...].astype(jnp.float32)

            lines[i].last(take)

    def ff_stage(f, s):
        if s == 0:
            for k in range(depth - 1):
                ff[f].first(far_first(p.z, k, depth))
        elif s < depth:
            ff[f].middle(far_first(p.z, s - 1, depth), add_low)
        else:
            at = pl.ds(f // 2 * frows, frows)

            def take(slot):
                go_out[f % 2, at] += slot[...].astype(jnp.float32)

            ff[f].last(take)

    clock = [0]

    def tick(*stages):
        n = clock[0]
        clock[0] += 1
        if n == 0:
            loads[7].wait()
            loads[8].wait()
        for f in range(FF_PARTS):
            if (n - f) % FF_GAP == 0 and 0 <= (n - f) // FF_GAP <= depth:
                ff_stage(f, (n - f) // FF_GAP)
        for i, s in stages:
            stage(i, s)

    def gain(i):
        return FULL[i : i + 1]

    def spread(i, values):
        VG[i : i + 1] = values

    tick()
    for i in (0, 1, 2, 3):
        loads[i].wait()
    cot = COT[...].reshape(rows, width).astype(jnp.float32)
    latter = X[...]
    back, g_gain, g_shift = norm_back(UP[...], latter, gain(4))
    spread(4, g_gain)
    spread(5, g_shift)
    spread(6, jnp.sum(cot, axis=0, keepdims=True))
    UP[...] = cot + back
    LOW[...] = UP[...].astype(low_type)
    next_mid = load(0, mid.at[1], X)
    w = use(0)
    for y in range(2):
        SL[:, y * cols : (y + 1) * cols] = mm(LOW[...], w[y]).astype(low_type)
    loads[4].wait()
    store_part(0, LOW[...], ACT[H2])
    tick()
    loads[5].wait()
    loads[6].wait()
    attend_pairs_back(
        ACT.at[CQ], CTX.at[CK], CTX.at[CV], PB2, SL, DH.at[0], DC.at[0], DC.at[1], 0, width // 128
    )
    store_part(1, ACT[N2], DH[0])
    tick((0, 1))
    w = use(1)
    slope = mm(DH[0, :, :cols], w[0], NT) + mm(DH[0, :, cols:], w[1], NT)
    next_mid.wait()
    back, g_gain, g_shift = norm_back(slope, X[...], gain(2))
    spread(2, g_gain)
    spread(3, g_shift)
    UP[...] += back
    LOW[...] = UP[...].astype(low_type)
    next_mid = load(0, mid.at[0], X)
    store_part(2, CTX[ENC], DC[0])
    tick((1, 1))
    store_part(3, CTX[ENC], DC[1])
    tick((2, 1))
    w = use(2)
    for y in range(2):
        SL[:, y * cols : (y + 1) * cols] = mm(LOW[...], w[y]).astype(low_type)
    store_part(4, LOW[...], ACT[H1])
    tick((3, 1), (0, 2))
    loads[9].wait()
    attend_pairs_back(
        ACT.at[Q], ACT.at[K], ACT.at[V], PB1, SL, DH.at[0], DH.at[1], DH.at[2], 0, width // 256
    )
    tick((4, 1), (1, 2))
    attend_pairs_back(
        ACT.at[Q], ACT.at[K], ACT.at[V], PB1, SL, DH.at[0], DH.at[1], DH.at[2], width // 256, width // 128
    )
    store_part(5, ACT[N1], DH[0])
    tick((0, 3), (2, 2))
    store_part(6, ACT[N1], DH[1])
    tick((5, 1), (1, 3), (3, 2), (0, 4))
    store_part(7, ACT[N1], DH[2])
    tick((6, 1), (2, 3), (4, 2), (1, 4), (0, 5))
    slope = None
    for i in range(3):
        w = use(3 + i)
        term = mm(DH[i, :, :cols], w[0], NT) + mm(DH[i, :, cols:], w[1], NT)
        slope = term if slope is None else slope + term
    tick((7, 1), (3, 3), (5, 2), (2, 4), (1, 5), (0, 6))
    next_mid.wait()
    back, g_gain, g_shift = norm_back(slope, X[...], gain(0))
    spread(0, g_gain)
    spread(1, g_shift)
    back += UP[...]
    for h in range(2):
        tg_out[h] = back[h * (rows // 2) : (h + 1) * (rows // 2)]

    def vec_move(j):
        other = lax.rem(me + j, count)
        at = pl.ds(pl.multiple_of(other * (width // count) // 128 * 128, 128), 128)
        return remote(VG.at[:, at], VR.at[j], vs.at[j], vr.at[j], (other // 2, lax.rem(other, 2)))

    @pl.loop(1, count)
    def _(j):
        vec_move(j).start()

    tick((6, 2), (4, 3), (3, 4), (2, 5), (1, 6), (0, 7))
    slope = None
    for i in range(2):
        w = use(6 + i)
        term = mm(DC[i, :, :cols], w[0], NT) + mm(DC[i, :, cols:], w[1], NT)
        slope = term if slope is None else slope + term
    for h in range(2):
        eg_out[h] = slope[h * (short // 2) : (h + 1) * (short // 2)]
    stores = []

    def store(src, dst):
        copy = pltpu.make_async_copy(src, dst, osem.at[len(stores)])
        copy.start()
        stores.append(copy)

    XS[...] = tg_out[oy].astype(low_type)
    loads[11].wait()
    for j in range(2):
        y_move(j).wait_recv()
        res_out[...] += YR[j].astype(jnp.float32).reshape(res_out.shape)
    ES[...] = eg_out[oy].astype(low_type)
    store(res_out, res_hbm)
    swaps = [
        remote(XS, XR, ss.at[0], sr.at[0], p.yn()),
        remote(ES, ER, ss.at[1], sr.at[1], p.yn()),
    ]
    tick((7, 2), (5, 3), (4, 4), (3, 5), (2, 6), (1, 7))
    for copy in swaps:
        copy.start()
    tick((6, 3), (5, 4), (4, 5), (3, 6), (2, 7))
    tick((7, 3), (6, 4), (5, 5), (4, 6), (3, 7))
    tick((7, 4), (6, 5), (5, 6), (4, 7))
    tick((7, 5), (6, 6), (5, 7))
    tick((7, 6), (6, 7))
    tick((7, 7))
    while clock[0] < FF_PARTS + FF_GAP * depth + 1:
        tick()
    store(gw_out, gw_hbm)
    store(go_out, go_hbm)
    at = pl.ds(pl.multiple_of(me * (width // count) // 128 * 128, 128), 128)
    vec_out[...] = VG[:, at]

    @pl.loop(1, count)
    def _(j):
        vec_move(j).wait()
        vec_out[...] += VR[j]

    store(vec_out, vec_hbm)

    for copy in swaps:
        copy.wait()
    tg_out[oy] = XR[...].astype(jnp.float32)
    eg_out[oy] = ER[...].astype(jnp.float32)
    store(tg_out, tg_hbm)
    store(eg_out, eg_hbm)
    for i in range(PIECES):
        if i >= PIECES - 2:
            core(i).wait_send()
        for h in range(2):
            diagonal(i, h).wait_send()
            column(i, h).wait_send()
        lines[i].sent()
    for line in ff:
        line.sent()
    for j in range(2):
        y_move(j).wait_send()
    for copy in stores:
        copy.wait()


def backward_all(G, act, ctx, mid, p1, p2, full, cot, d_in, y_in, go_in, S_in, YS_in):
    depth = G.shape[2]
    count = 8 * depth
    rows, cols = G.shape[5:]
    length, width = d_in.shape
    short = ctx.shape[1]
    bf, f32 = jnp.bfloat16, jnp.float32
    dma = pltpu.SemaphoreType.DMA
    hb = pl.BlockSpec(memory_space=HBM)
    outs = [
            jax.ShapeDtypeStruct((PIECES, rows, cols), f32),
            jax.ShapeDtypeStruct((8, 128), f32),
            jax.ShapeDtypeStruct((2, length // 2, width), f32),
            jax.ShapeDtypeStruct((2, length // 2, width), f32),
            jax.ShapeDtypeStruct((2, short // 2, width), f32),
            jax.ShapeDtypeStruct(go_in.shape, f32),
    ]
    return pl.pallas_call(
        functools.partial(backward_kernel, depth),
        out_shape=outs,
        in_specs=[hb] * 13,
        out_specs=[hb] * 6,
        scratch_shapes=[pltpu.VMEM(o.shape, o.dtype) for o in outs] + [
            pltpu.VMEM((PIECES, 2, depth, 2, rows, cols), bf),
            pltpu.VMEM((2, 2, depth, 2, rows, cols), bf),
            pltpu.VMEM((SLOTS, 2, depth, 2, rows, cols), bf),
            pltpu.VMEM((PIECES, depth, rows, cols), bf),
            pltpu.VMEM((PIECES, 2, depth, rows, cols), bf),
            pltpu.VMEM((PIECES, depth + 1, rows, cols), bf),
            pltpu.VMEM(S_in.shape, bf),
            pltpu.VMEM((2 * depth - 4,) + S_in.shape[1:], bf),
            pltpu.VMEM(YS_in.shape, bf),
            pltpu.VMEM(YS_in.shape, bf),
            pltpu.VMEM((2,) + G.shape[1:], bf),
            pltpu.VMEM((8, length, width), bf),
            pltpu.VMEM(ctx.shape, bf),
            pltpu.VMEM((length, width), f32),
            pltpu.VMEM(p1.shape, bf),
            pltpu.VMEM(p2.shape, bf),
            pltpu.VMEM((length, width), f32),
            pltpu.VMEM((length, width), bf),
            pltpu.VMEM((length, width), bf),
            pltpu.VMEM((3, length, width), bf),
            pltpu.VMEM((2, short, width), bf),
            pltpu.VMEM((2, length // 2, width), bf),
            pltpu.VMEM((8, width), f32),
            pltpu.VMEM((8, width), f32),
            pltpu.VMEM((count, 8, 128), f32),
            pltpu.VMEM((length // 2, width), bf),
            pltpu.VMEM((length // 2, width), bf),
            pltpu.VMEM((short // 2, width), bf),
            pltpu.VMEM((short // 2, width), bf),
            dma((12,)), dma((2,)),
            dma((PIECES,)), dma((PIECES,)),
            dma((PIECES, 2)), dma((PIECES, 2)),
            dma((PIECES, 2)), dma((PIECES, 2)),
            dma((PIECES, depth)), dma((PIECES, depth + 1)),
            dma((FF_PARTS, depth)), dma((FF_PARTS, 2 * depth - 4)),
            dma((2,)), dma((2,)),
            dma((count,)), dma((count,)),
            dma((2,)), dma((2,)),
            dma((6,)),
            pltpu.SemaphoreType.REGULAR,
        ],
        compiler_params=pltpu.CompilerParams(
            collective_id=3, has_side_effects=True, vmem_limit_bytes=63 << 20
        ),
        name="backward_all",
    )(G, act, ctx, mid, p1, p2, full, cot, d_in, y_in, go_in, S_in, YS_in)


def fast_local(
    tokens, encoder, target_doc, source_doc, self_proj, self_out, cross_query, cross_pairs, cross_out,
    hidden_in, hidden_in_bias, hidden_out, hidden_out_bias, self_gain, self_shift, cross_gain, cross_shift,
    hidden_gain, hidden_shift, cotangent,
):
    depth = lax.axis_size("dp") // 4
    count = 8 * depth
    place = Place()
    me = place.dp * 2 + place.y
    bf, f32 = jnp.bfloat16, jnp.float32
    vectors = jnp.stack(
        [self_gain, self_shift, cross_gain, cross_shift, hidden_gain, hidden_shift, hidden_out_bias]
    )
    span = vectors.shape[1]
    group = 128 // span
    lane = lax.broadcasted_iota(jnp.int32, (1, 128), 1)
    mine = lane // span == lax.rem(me, group)
    vec = jnp.concatenate([
        jnp.where(mine, jnp.tile(vectors, (1, group)), 0.0),
        jnp.zeros((1, 128), f32),
        hidden_in_bias.astype(f32).reshape(-1, 128),
    ])
    vec = jnp.pad(vec, ((0, -vec.shape[0] % 8), (0, 0)))
    G, act, ctx, mid, probs1, probs2, full, cot, d_in, y_in, go, gbias, S, YS = forward_all(
        self_proj.transpose(1, 0, 2), self_out.T, cross_pairs.transpose(1, 0, 2), cross_query, cross_out.T,
        hidden_in, hidden_out, vec, tokens, encoder, cotangent, target_doc, source_doc,
    )
    gw, vout, res, tg, eg, go = backward_all(
        G, act, ctx, mid, probs1, probs2, full, cot, d_in, y_in, go, S, YS
    )
    vout = lax.dynamic_slice_in_dim(vout, lax.rem(me, group) * span, span, axis=1)
    return (
        res, tg, eg,
        jnp.stack([gw[5], gw[6], gw[7]], axis=1),
        gw[4].T, gw[1], jnp.stack([gw[2], gw[3]], axis=1), gw[0].T,
        go[0].T, gbias[0], go[1],
        vout[6], vout[0], vout[1], vout[2], vout[3], vout[4], vout[5],
    )


BLOCK_ROWS = 512


def smooth_gate(values):
    return jax.nn.gelu(values, approximate=True)


def plain_norm_forward(hidden, norm_gain, norm_shift):
    center = hidden - jnp.mean(hidden, axis=-1, keepdims=True)
    inverse = lax.rsqrt(jnp.mean(center * center, axis=-1, keepdims=True) + EPS)
    normal = center * inverse
    return (normal * norm_gain + norm_shift, normal, inverse)


def plain_norm_backward(upward, normal, inverse, norm_gain):
    scaled = upward * norm_gain
    centred = (
        scaled
        - jnp.mean(scaled, axis=-1, keepdims=True)
        - normal * jnp.mean(scaled * normal, axis=-1, keepdims=True)
    )
    return (centred * inverse, jnp.sum(upward * normal, axis=0), jnp.sum(upward, axis=0))


def split_blocks(array):
    row_count = array.shape[0]
    block_size = min(BLOCK_ROWS, row_count)
    return array.reshape((row_count // block_size, block_size) + array.shape[1:])


def block_scores(query_block, key_rows, allow_block):
    query_heads = query_block.reshape(query_block.shape[0], -1, HEAD)
    key_heads = key_rows.reshape(key_rows.shape[0], -1, HEAD)
    scores = jnp.einsum(
        "qhd,khd->hqk", query_heads, key_heads, preferred_element_type=jnp.float32
    ) * HEAD ** (-0.5)
    return jnp.where(allow_block[None], scores, NEGATIVE)


def plain_attend(queries, key_rows, values, allowed):
    columns = queries.shape[1]
    value_heads = values.reshape(values.shape[0], -1, HEAD)

    def one_block(pieces):
        query_block, allow_block = pieces
        scores = block_scores(query_block, key_rows, allow_block)
        highest = jnp.max(scores, axis=-1, keepdims=True)
        exponent = jnp.exp(scores - highest)
        totals = jnp.sum(exponent, axis=-1, keepdims=True)
        softmaxed = (exponent / totals).astype(jnp.bfloat16)
        mixture = jnp.einsum(
            "hqk,khd->qhd", softmaxed, value_heads, preferred_element_type=jnp.float32
        )
        return (
            mixture.reshape(query_block.shape[0], columns).astype(jnp.bfloat16),
            (highest + jnp.log(totals))[..., 0],
        )

    mixture, logsum = lax.map(one_block, (split_blocks(queries), split_blocks(allowed)))
    return (mixture.reshape(queries.shape), logsum)


def plain_attend_backward(queries, key_rows, values, allowed, logsum, slope_heads):
    scaling = HEAD ** (-0.5)
    key_heads = key_rows.reshape(key_rows.shape[0], -1, HEAD)
    value_heads = values.reshape(values.shape[0], -1, HEAD)

    def one_block(running, pieces):
        key_total, value_total = running
        query_block, allow_block, logsum_block, slope_block = pieces
        scores = block_scores(query_block, key_rows, allow_block)
        softmaxed = jnp.exp(scores - logsum_block[..., None])
        query_heads = query_block.reshape(query_block.shape[0], -1, HEAD)
        slope_out = slope_block.reshape(slope_block.shape[0], -1, HEAD)
        slope_probs = jnp.einsum(
            "qhd,khd->hqk", slope_out, value_heads, preferred_element_type=jnp.float32
        )
        centred = jnp.sum(softmaxed * slope_probs, axis=-1, keepdims=True)
        slope_scores = (softmaxed * (slope_probs - centred)).astype(jnp.bfloat16)
        slope_query = (
            jnp.einsum("hqk,khd->qhd", slope_scores, key_heads, preferred_element_type=jnp.float32)
            * scaling
        )
        key_total = (
            key_total
            + jnp.einsum(
                "hqk,qhd->khd", slope_scores, query_heads, preferred_element_type=jnp.float32
            )
            * scaling
        )
        value_total = value_total + jnp.einsum(
            "hqk,qhd->khd",
            softmaxed.astype(jnp.bfloat16),
            slope_out,
            preferred_element_type=jnp.float32,
        )
        return (
            (key_total, value_total),
            slope_query.reshape(query_block.shape[0], -1).astype(jnp.bfloat16),
        )

    empty_heads = jnp.zeros(key_heads.shape, jnp.float32)
    (key_total, value_total), slope_query = lax.scan(
        one_block,
        (empty_heads, empty_heads),
        (split_blocks(queries), split_blocks(allowed), logsum, split_blocks(slope_heads)),
    )
    return (
        slope_query.reshape(queries.shape),
        key_total.reshape(key_rows.shape).astype(jnp.bfloat16),
        value_total.reshape(values.shape).astype(jnp.bfloat16),
    )


def gather_rows(local_rows):
    return lax.all_gather(local_rows, "tensor", axis=0, tiled=True)


def sum_rows(partial_sum):
    return lax.psum_scatter(
        partial_sum.astype(jnp.bfloat16), "tensor", scatter_dimension=0, tiled=True
    ).astype(jnp.float32)


def gather_slopes(local_slopes):
    return lax.all_gather(local_slopes, "tensor", axis=0, tiled=True)


def sum_slopes(partial_sum):
    return lax.psum_scatter(
        partial_sum.astype(jnp.bfloat16), "tensor", scatter_dimension=0, tiled=True
    ).astype(jnp.float32)


def reduce_weights(weight_terms):
    return (
        lax.psum_scatter(weight_terms[0], "dp", scatter_dimension=0, tiled=True),
        lax.psum_scatter(weight_terms[1], "dp", scatter_dimension=1, tiled=True),
        lax.psum_scatter(weight_terms[2], "dp", scatter_dimension=0, tiled=True),
        lax.psum_scatter(weight_terms[3], "dp", scatter_dimension=0, tiled=True),
        lax.psum_scatter(weight_terms[4], "dp", scatter_dimension=1, tiled=True),
        lax.psum_scatter(weight_terms[5], "dp", scatter_dimension=1, tiled=True),
        lax.psum_scatter(weight_terms[6], "dp", scatter_dimension=0, tiled=True),
        lax.psum_scatter(weight_terms[7], "dp", scatter_dimension=0, tiled=True),
    )


def plain_local(
    tokens,
    encoder,
    target_doc,
    source_doc,
    self_proj,
    self_out,
    cross_query,
    cross_pairs,
    cross_out,
    hidden_in,
    hidden_in_bias,
    hidden_out,
    hidden_out_bias,
    self_gain,
    self_shift,
    cross_gain,
    cross_shift,
    hidden_gain,
    hidden_shift,
    cotangent,
):
    (
        full_self_gain,
        full_self_shift,
        full_cross_gain,
        full_cross_shift,
        full_hidden_gain,
        full_hidden_shift,
        full_out_bias,
    ) = (
        lax.all_gather(self_gain, ("dp", "tensor"), axis=0, tiled=True),
        lax.all_gather(self_shift, ("dp", "tensor"), axis=0, tiled=True),
        lax.all_gather(cross_gain, ("dp", "tensor"), axis=0, tiled=True),
        lax.all_gather(cross_shift, ("dp", "tensor"), axis=0, tiled=True),
        lax.all_gather(hidden_gain, ("dp", "tensor"), axis=0, tiled=True),
        lax.all_gather(hidden_shift, ("dp", "tensor"), axis=0, tiled=True),
        lax.all_gather(hidden_out_bias, ("dp", "tensor"), axis=0, tiled=True),
    )
    micro_count = tokens.shape[0]
    row_count = tokens.shape[1] * lax.axis_size("tensor")
    positions = jnp.arange(row_count)
    results = []
    token_grads = []
    encoder_grads = []
    vector_total = None
    weight_total = None
    for step_index in range(micro_count):
        forward_weights = (
            lax.all_gather(self_proj, "dp", axis=0, tiled=True),
            lax.all_gather(self_out, "dp", axis=1, tiled=True),
            lax.all_gather(cross_query, "dp", axis=0, tiled=True),
            lax.all_gather(cross_pairs, "dp", axis=0, tiled=True),
            lax.all_gather(cross_out, "dp", axis=1, tiled=True),
            lax.all_gather(hidden_in, "dp", axis=1, tiled=True),
            lax.all_gather(hidden_in_bias, "dp", axis=0, tiled=True),
            lax.all_gather(hidden_out, "dp", axis=0, tiled=True),
        )
        (
            full_proj,
            full_self_out,
            full_query,
            full_pairs,
            full_cross_out,
            full_in,
            full_in_bias,
            full_out,
        ) = forward_weights
        target_row = target_doc[step_index]
        source_row = source_doc[step_index]
        self_allowed = (target_row[:, None] == target_row[None, :]) & (
            positions[None, :] <= positions[:, None]
        )
        cross_allowed = target_row[:, None] == source_row[None, :]
        start_hidden = tokens[step_index].astype(jnp.float32)
        normed_first, normal_first, inverse_first = plain_norm_forward(
            start_hidden, full_self_gain, full_self_shift
        )
        self_rows = gather_rows(normed_first.astype(jnp.bfloat16))
        triple = jnp.einsum(
            "td,dcj->tcj", self_rows, full_proj, preferred_element_type=jnp.float32
        ).astype(jnp.bfloat16)
        self_heads, self_logsum = plain_attend(triple[:, 0], triple[:, 1], triple[:, 2], self_allowed)
        middle = start_hidden + sum_rows(
            jnp.dot(self_heads, full_self_out, preferred_element_type=jnp.float32)
        )
        normed_second, normal_second, inverse_second = plain_norm_forward(
            middle, full_cross_gain, full_cross_shift
        )
        cross_rows, source_rows = (
            lax.all_gather(normed_second.astype(jnp.bfloat16), "tensor", axis=0, tiled=True),
            lax.all_gather(encoder[step_index], "tensor", axis=0, tiled=True),
        )
        cross_queries = jnp.dot(cross_rows, full_query, preferred_element_type=jnp.float32).astype(
            jnp.bfloat16
        )
        key_value = jnp.einsum(
            "sd,dcj->scj", source_rows, full_pairs, preferred_element_type=jnp.float32
        ).astype(jnp.bfloat16)
        cross_heads, cross_logsum = plain_attend(
            cross_queries, key_value[:, 0], key_value[:, 1], cross_allowed
        )
        latter = middle + sum_rows(
            jnp.dot(cross_heads, full_cross_out, preferred_element_type=jnp.float32)
        )
        normed_third, normal_third, inverse_third = plain_norm_forward(
            latter, full_hidden_gain, full_hidden_shift
        )
        hidden_rows = gather_rows(normed_third.astype(jnp.bfloat16))
        before = jnp.dot(
            hidden_rows, full_in, preferred_element_type=jnp.float32
        ) + full_in_bias.astype(jnp.float32)
        gated, gate_pullback = jax.vjp(smooth_gate, before)
        active = gated.astype(jnp.bfloat16)
        results.append(
            latter
            + sum_rows(jnp.dot(active, full_out, preferred_element_type=jnp.float32))
            + full_out_bias
        )
        back_weights = (
            lax.all_gather(self_proj, "dp", axis=0, tiled=True),
            lax.all_gather(self_out, "dp", axis=1, tiled=True),
            lax.all_gather(cross_query, "dp", axis=0, tiled=True),
            lax.all_gather(cross_pairs, "dp", axis=0, tiled=True),
            lax.all_gather(cross_out, "dp", axis=1, tiled=True),
            lax.all_gather(hidden_in, "dp", axis=1, tiled=True),
            lax.all_gather(hidden_in_bias, "dp", axis=0, tiled=True),
            lax.all_gather(hidden_out, "dp", axis=0, tiled=True),
        )
        (
            back_proj,
            back_self_out,
            back_query,
            back_pairs,
            back_cross_out,
            back_in,
            back_in_bias,
            back_out,
        ) = back_weights
        upward = cotangent[step_index].astype(jnp.float32)
        grad_out_bias = jnp.sum(upward, axis=0)
        slope_rows = gather_slopes(upward.astype(jnp.bfloat16))
        grad_out = jnp.einsum("tf,td->fd", active, slope_rows, preferred_element_type=jnp.float32)
        slope_active = jnp.einsum(
            "td,fd->tf", slope_rows, back_out, preferred_element_type=jnp.float32
        )
        slope_before = gate_pullback(slope_active)[0].astype(jnp.bfloat16)
        grad_in_bias = jnp.sum(slope_before.astype(jnp.float32), axis=0)
        grad_in = jnp.einsum(
            "td,tf->df", hidden_rows, slope_before, preferred_element_type=jnp.float32
        )
        slope_normed = sum_slopes(
            jnp.einsum("tf,df->td", slope_before, back_in, preferred_element_type=jnp.float32)
        )
        slope_hidden, grad_hidden_gain, grad_hidden_shift = plain_norm_backward(
            slope_normed, normal_third, inverse_third, full_hidden_gain
        )
        upward = upward + slope_hidden
        slope_rows = gather_slopes(upward.astype(jnp.bfloat16))
        grad_cross_out = jnp.einsum(
            "tj,td->jd", cross_heads, slope_rows, preferred_element_type=jnp.float32
        )
        slope_heads = jnp.einsum(
            "td,jd->tj", slope_rows, back_cross_out, preferred_element_type=jnp.float32
        ).astype(jnp.bfloat16)
        slope_query, slope_keys, slope_values = plain_attend_backward(
            cross_queries,
            key_value[:, 0],
            key_value[:, 1],
            cross_allowed,
            cross_logsum,
            slope_heads,
        )
        slope_pairs = jnp.stack([slope_keys, slope_values], axis=1)
        grad_query = jnp.einsum(
            "td,tj->dj", cross_rows, slope_query, preferred_element_type=jnp.float32
        )
        grad_pairs = jnp.einsum(
            "sd,scj->dcj", source_rows, slope_pairs, preferred_element_type=jnp.float32
        )
        slope_cross, slope_source = (
            lax.psum_scatter(
                jnp.einsum(
                    "tj,dj->td", slope_query, back_query, preferred_element_type=jnp.float32
                ).astype(jnp.bfloat16),
                "tensor",
                scatter_dimension=0,
                tiled=True,
            ).astype(jnp.float32),
            lax.psum_scatter(
                jnp.einsum(
                    "scj,dcj->sd", slope_pairs, back_pairs, preferred_element_type=jnp.float32
                ).astype(jnp.bfloat16),
                "tensor",
                scatter_dimension=0,
                tiled=True,
            ).astype(jnp.float32),
        )
        slope_hidden, grad_cross_gain, grad_cross_shift = plain_norm_backward(
            slope_cross, normal_second, inverse_second, full_cross_gain
        )
        upward = upward + slope_hidden
        slope_rows = gather_slopes(upward.astype(jnp.bfloat16))
        grad_self_out = jnp.einsum(
            "tj,td->jd", self_heads, slope_rows, preferred_element_type=jnp.float32
        )
        slope_heads = jnp.einsum(
            "td,jd->tj", slope_rows, back_self_out, preferred_element_type=jnp.float32
        ).astype(jnp.bfloat16)
        slope_query, slope_keys, slope_values = plain_attend_backward(
            triple[:, 0], triple[:, 1], triple[:, 2], self_allowed, self_logsum, slope_heads
        )
        slope_triple = jnp.stack([slope_query, slope_keys, slope_values], axis=1)
        grad_proj = jnp.einsum(
            "td,tcj->dcj", self_rows, slope_triple, preferred_element_type=jnp.float32
        )
        slope_self = sum_slopes(
            jnp.einsum("tcj,dcj->td", slope_triple, back_proj, preferred_element_type=jnp.float32)
        )
        slope_hidden, grad_self_gain, grad_self_shift = plain_norm_backward(
            slope_self, normal_first, inverse_first, full_self_gain
        )
        token_grads.append(upward + slope_hidden)
        encoder_grads.append(slope_source)
        vector_terms = (
            grad_self_gain,
            grad_self_shift,
            grad_cross_gain,
            grad_cross_shift,
            grad_hidden_gain,
            grad_hidden_shift,
            grad_out_bias,
        )
        vector_total = (
            vector_terms if step_index == 0 else jax.tree.map(jnp.add, vector_total, vector_terms)
        )
        weight_terms = (
            grad_proj,
            grad_self_out,
            grad_query,
            grad_pairs,
            grad_cross_out,
            grad_in,
            grad_in_bias,
            grad_out,
        )
        shard_terms = reduce_weights(weight_terms)
        weight_total = (
            shard_terms if step_index == 0 else jax.tree.map(jnp.add, weight_total, shard_terms)
        )
    vector_shards = (
        lax.psum_scatter(vector_total[0], ("dp", "tensor"), scatter_dimension=0, tiled=True),
        lax.psum_scatter(vector_total[1], ("dp", "tensor"), scatter_dimension=0, tiled=True),
        lax.psum_scatter(vector_total[2], ("dp", "tensor"), scatter_dimension=0, tiled=True),
        lax.psum_scatter(vector_total[3], ("dp", "tensor"), scatter_dimension=0, tiled=True),
        lax.psum_scatter(vector_total[4], ("dp", "tensor"), scatter_dimension=0, tiled=True),
        lax.psum_scatter(vector_total[5], ("dp", "tensor"), scatter_dimension=0, tiled=True),
        lax.psum_scatter(vector_total[6], ("dp", "tensor"), scatter_dimension=0, tiled=True),
    )
    return (
        jnp.stack(results),
        jnp.stack(token_grads),
        jnp.stack(encoder_grads),
        weight_total[0],
        weight_total[1],
        weight_total[2],
        weight_total[3],
        weight_total[4],
        weight_total[5],
        weight_total[6],
        weight_total[7],
        vector_shards[6],
        vector_shards[0],
        vector_shards[1],
        vector_shards[2],
        vector_shards[3],
        vector_shards[4],
        vector_shards[5],
    )


def solution(mesh):
    in_specs = (
        P("dp", "tensor", None),
        P("dp", "tensor", None),
        P("dp", None),
        P("dp", None),
        P("dp", None, "tensor"),
        P("tensor", "dp"),
        P("dp", "tensor"),
        P("dp", None, "tensor"),
        P("tensor", "dp"),
        P(None, ("dp", "tensor")),
        P(("dp", "tensor")),
        P(("dp", "tensor"), None),
        P(("dp", "tensor")),
        P(("dp", "tensor")),
        P(("dp", "tensor")),
        P(("dp", "tensor")),
        P(("dp", "tensor")),
        P(("dp", "tensor")),
        P(("dp", "tensor")),
        P("dp", "tensor", None),
    )
    out_specs = (
        P("dp", "tensor", None),
        P("dp", "tensor", None),
        P("dp", "tensor", None),
        P("dp", None, "tensor"),
        P("tensor", "dp"),
        P("dp", "tensor"),
        P("dp", None, "tensor"),
        P("tensor", "dp"),
        P(None, ("dp", "tensor")),
        P(("dp", "tensor")),
        P(("dp", "tensor"), None),
        P(("dp", "tensor")),
        P(("dp", "tensor")),
        P(("dp", "tensor")),
        P(("dp", "tensor")),
        P(("dp", "tensor")),
        P(("dp", "tensor")),
        P(("dp", "tensor")),
    )

    def run(*arrays):
        width = arrays[0].shape[2]
        aligned = width // mesh.shape["dp"] % 16 == 0 and mesh.shape["dp"] % 4 == 0
        inner = fast_local if aligned and mesh.shape["tensor"] == 2 else plain_local
        return jax.shard_map(inner, mesh=mesh, in_specs=in_specs, out_specs=out_specs, check_vma=False)(*arrays)

    return run
```

```python
import functools

import jax
import jax.numpy as jnp
from jax import lax
from jax.experimental import pallas as pl
from jax.experimental.pallas import tpu as pltpu
from jax.sharding import PartitionSpec as P

HEAD = 64
EPS = 1e-05
NEGATIVE = -1e30
MESH = pl.DeviceIdType.MESH
HBM = pltpu.HBM
VMEM = pltpu.VMEM
PIECES = 8
FF_PIECES = 16


class Place:
    def __init__(self):
        self.dp = lax.axis_index("dp")
        self.y = lax.axis_index("tensor")
        self.c = lax.rem(self.dp, 2)
        self.x = lax.rem(self.dp // 2, 2)
        self.z = self.dp // 4

    def at(self, z=None, x=None, c=None, y=None):
        z = self.z if z is None else z
        x = self.x if x is None else x
        c = self.c if c is None else c
        y = self.y if y is None else y
        return ((z * 2 + x) * 2 + c, y)

    def core(self):
        return self.at(c=1 - self.c)

    def xn(self):
        return self.at(x=1 - self.x)

    def yn(self):
        return self.at(y=1 - self.y)

    def up(self):
        return self.at(z=self.z + 1)

    def down(self):
        return self.at(z=self.z - 1)


def remote(src, dst, send, recv, device):
    return pltpu.make_async_remote_copy(
        src_ref=src, dst_ref=dst, send_sem=send, recv_sem=recv, device_id=device, device_id_type=MESH
    )


def signal(sem, device):
    pl.semaphore_signal(sem, inc=1, device_id=device, device_id_type=MESH)


class LineGather:
    def __init__(self, place, depth, slot, send, recv):
        self.p, self.n, self.slot, self.send, self.recv = place, depth, slot, send, recv

    def _copy_up(self, k):
        b = self.p.z - k
        return remote(self.slot(b), self.slot(b), self.send.at[0, k], self.recv.at[0, k], self.p.up())

    def _copy_down(self, k):
        b = self.p.z + k
        return remote(self.slot(b), self.slot(b), self.send.at[1, k], self.recv.at[1, k], self.p.down())

    def _from_below(self, k):
        b = self.p.z - k
        return remote(self.slot(b), self.slot(b), self.send.at[0, k - 1], self.recv.at[0, k - 1], self.p.up())

    def _from_above(self, k):
        b = self.p.z + k
        return remote(self.slot(b), self.slot(b), self.send.at[1, k - 1], self.recv.at[1, k - 1], self.p.down())

    def arrive(self, k):
        z = self.p.z

        @pl.when(z - k >= 0)
        def _():
            self._from_below(k).wait_recv()

        @pl.when(z + k <= self.n - 1)
        def _():
            self._from_above(k).wait_recv()

    def step(self, k):
        z = self.p.z
        if k > 0:
            self.arrive(k)
        if k < self.n - 1:

            @pl.when((z - k >= 0) & (z < self.n - 1))
            def _():
                self._copy_up(k).start()

            @pl.when((z + k <= self.n - 1) & (z > 0))
            def _():
                self._copy_down(k).start()

    def sent(self):
        z = self.p.z
        for k in range(self.n - 1):

            @pl.when((z - k >= 0) & (z < self.n - 1))
            def _():
                self._copy_up(k).wait_send()

            @pl.when((z + k <= self.n - 1) & (z > 0))
            def _():
                self._copy_down(k).wait_send()


class PlaneGather:
    def __init__(self, place, slot, send, recv):
        self.p, self.slot, self.send, self.recv = place, slot, send, recv
        p = place
        x, y, c = p.x, p.y, p.c
        ox, oy = 1 - x, 1 - y
        self.moves = [
            ((x, c, y, None), p.xn(), 0),
            ((x, c, y, None), p.yn(), 1),
            ((ox, c, y, 0), p.yn(), 2),
            ((x, c, oy, 1), p.xn(), 3),
            ((x, c, y, None), p.core(), 4),
            ((ox, c, y, None), p.core(), 5),
            ((x, c, oy, None), p.core(), 6),
            ((ox, c, oy, None), p.core(), 7),
        ]
        oc = 1 - c
        self.arrivals = [
            (ox, c, y, None),
            (x, c, oy, None),
            (ox, c, oy, 0),
            (ox, c, oy, 1),
            (x, oc, y, None),
            (ox, oc, y, None),
            (x, oc, oy, None),
            (ox, oc, oy, None),
        ]

    def _move(self, i):
        where, device, s = self.moves[i]
        return remote(self.slot(*where), self.slot(*where), self.send.at[s], self.recv.at[s], device)

    def _arrival(self, i):
        view = self.slot(*self.arrivals[i])
        return remote(view, view, self.send.at[i], self.recv.at[i], self.moves[i][1])

    def begin(self):
        self._move(0).start()
        self._move(1).start()
        self._move(4).start()

    def forward(self):
        self._arrival(0).wait_recv()
        self._move(2).start()
        self._move(5).start()
        self._arrival(1).wait_recv()
        self._move(3).start()
        self._move(6).start()

    def finish(self):
        self._arrival(2).wait_recv()
        self._arrival(3).wait_recv()
        self._move(7).start()

    def end(self):
        for i in range(4, 8):
            self._arrival(i).wait_recv()

    def sent(self):
        for i in range(8):
            self._move(i).wait_send()


def all_barrier(place, count):
    sem = pltpu.get_barrier_semaphore()
    me = place.dp * 2 + place.y

    @pl.loop(1, count)
    def _(j):
        other = lax.rem(me + j, count)
        signal(sem, (other // 2, lax.rem(other, 2)))

    pl.semaphore_wait(sem, count - 1)


def far_first(z, s, depth):
    b = 0
    for place in range(depth):
        order = sorted(range(depth), key=lambda k: (-abs(k - place), k))
        b = jnp.where(z == place, order[s], b)
    return b


class LineReduce:
    def __init__(self, place, depth, part, slots, send, recv):
        self.p, self.n, self.part, self.slots, self.send, self.recv = place, depth, part, slots, send, recv

    def _up(self, b):
        slot = b - (self.p.z + 1)
        return remote(self.part(b), self.slots(slot), self.send.at[b], self.recv.at[slot], self.p.up())

    def _down(self, b):
        slot = self.n - b
        return remote(self.part(b), self.slots(slot), self.send.at[b], self.recv.at[slot], self.p.down())

    def below(self, b):
        slot = b - self.p.z
        return remote(self.slots(slot), self.slots(slot), self.send.at[b], self.recv.at[slot], self.p.up())

    def above(self, b):
        slot = self.n - b
        return remote(self.slots(slot), self.slots(slot), self.send.at[b], self.recv.at[slot], self.p.down())

    def first(self, b):
        z = self.p.z

        @pl.when((z == 0) & (b > z))
        def _():
            self._up(b).start()

        @pl.when((z == self.n - 1) & (b < z))
        def _():
            self._down(b).start()

    def middle(self, b, add):
        z = self.p.z

        @pl.when((z > 0) & (b > z))
        def _():
            self.below(b).wait_recv()
            add(self.part(b), self.slots(b - z))
            self._up(b).start()

        @pl.when((z < self.n - 1) & (b < z))
        def _():
            self.above(b).wait_recv()
            add(self.part(b), self.slots(self.n - b))
            self._down(b).start()

    def last(self, take):
        z = self.p.z

        @pl.when(z > 0)
        def _():
            self.below(z).wait_recv()
            take(self.slots(0))

        @pl.when(z < self.n - 1)
        def _():
            self.above(z).wait_recv()
            take(self.slots(self.n - z))

    def sent(self):
        z = self.p.z

        @pl.loop(0, self.n)
        def _(b):
            @pl.when(b > z)
            def _():
                self._up(b).wait_send()

            @pl.when(b < z)
            def _():
                self._down(b).wait_send()


def add_low(part, other):
    part[...] = (part[...].astype(jnp.float32) + other[...].astype(jnp.float32)).astype(part.dtype)


def gelu_pair(x):
    a, b = 0.7978845608028654, 0.044715
    square = x * x
    t = jnp.tanh(a * x * (1.0 + b * square))
    half = 0.5 * (1.0 + t)
    return x * half, half + 0.5 * x * (1.0 - t * t) * (a * (1.0 + 3.0 * b * square))


NN = (((1,), (0,)), ((), ()))
NT = (((1,), (1,)), ((), ()))
TN = (((0,), (0,)), ((), ()))


def mm(left, right, form=NN):
    return lax.dot_general(left, right, form, preferred_element_type=jnp.float32)


def neighbour_barrier(p, depth):
    sem = pltpu.get_barrier_semaphore()
    for dx in range(2):
        for dc in range(2):
            for dy in range(2):
                if dx + dc + dy:
                    signal(sem, p.at(x=lax.rem(p.x + dx, 2), c=lax.rem(p.c + dc, 2), y=lax.rem(p.y + dy, 2)))

    @pl.loop(1, depth)
    def _(k):
        signal(sem, p.at(z=lax.rem(p.z + k, depth)))

    pl.semaphore_wait(sem, 7 + depth - 1)


def layer_norm(x, gain, shift):
    center = x - jnp.mean(x, axis=-1, keepdims=True)
    inverse = lax.rsqrt(jnp.mean(center * center, axis=-1, keepdims=True) + EPS)
    return center * inverse * gain + shift


def attend_pairs(q_ref, k_ref, v_ref, allowed, probs_ref, heads_ref, start, stop):
    rows = q_ref.shape[0]
    first = lax.broadcasted_iota(jnp.int32, (rows, 128), 1) < HEAD
    both = jnp.concatenate([allowed, allowed], axis=0)

    @pl.loop(start, stop)
    def _(h):
        at = (slice(None), pl.ds(pl.multiple_of(h * 128, 128), 128))
        q, k, v = q_ref[at], k_ref[at], v_ref[at]
        zero = jnp.zeros_like(q)
        pair = jnp.concatenate([jnp.where(first, q, zero), jnp.where(first, zero, q)], axis=0)
        scores = jnp.where(both, mm(pair, k, NT) * HEAD**-0.5, NEGATIVE)
        weights = jnp.exp(scores - jnp.max(scores, axis=-1, keepdims=True))
        probs = (weights * (1.0 / jnp.sum(weights, axis=-1, keepdims=True))).astype(jnp.bfloat16)
        probs_ref[h] = probs
        mix = mm(probs, v)
        heads_ref[at] = jnp.where(first, mix[:rows], mix[rows:]).astype(jnp.bfloat16)


Q, K, V, CQ, H1, H2, N1, N2, N3 = range(9)
CK, CV, ENC = range(3)


def forward_kernel(
    depth,
    proj, so, pairs_in, query, co, win, wout, vec, tok_in, enc_in, cot, target, source,
    G, act_out, ctx_out, mid_out, p1_out, p2_out, full_out, cot_out,
    d_out, y_out, go_out, gbias_out, S_out, YS_out,
    ATT, W, TOK, VEC, FULL, BIAS, ACT, CTX, MID, P1, P2, TARGET, SOURCE, OWN_T, OWN_E,
    HN, G3, WI, WO, S, RF, ACTIVE, SLOPE, BS, BR, CS, CR, CSY, CRY, PS, PR, DA, YA, DSUM, YSUM, GO, GB, LATS, LATR,
    lsem, wsem, osem, zs, zr, fs, fr, ps, pr, vs, vr, ss, sr, gs, gr, hs, hr, bs, br, cs, cr, ys, yr, xs, xr, us, ur,
):
    p = Place()
    z = p.z
    count = 8 * depth
    me = p.dp * 2 + p.y
    rows, width = ACT.shape[1:]
    short = CTX.shape[1]
    units = WO.shape[1]
    half, few = rows // 2, short // 2
    part = ATT.shape[1]
    mine = pl.ds(pl.multiple_of(p.y * few, few), few)
    local = []

    def keep(src, dst):
        copy = pltpu.make_async_copy(src, dst, lsem.at[len(local)])
        copy.start()
        local.append(copy)

    keep(vec, VEC.at[me])
    keep(tok_in, OWN_T)
    keep(enc_in, OWN_E)
    keep(proj, ATT.at[pl.ds(0, 3)])
    keep(so, ATT.at[3])
    keep(pairs_in, ATT.at[pl.ds(4, 2)])
    keep(query, ATT.at[6])
    keep(co, ATT.at[7])
    keep(cot, G3.at[p.x, p.c, :, p.y])
    keep(win, WI.at[:, pl.ds(pl.multiple_of(z * units, units), units)])
    keep(wout, WO.at[z])
    keep(target, TARGET)
    keep(source, SOURCE)
    BS[...] = jnp.zeros_like(BS)
    all_barrier(p, count)
    for copy in local:
        copy.wait()
    TOK[p.y] = OWN_T[p.y]
    CTX[ENC, mine] = OWN_E[p.y]
    own = pltpu.make_async_copy(ATT, G.at[:, p.y, z, p.x, p.c], lsem.at[0])
    own.start()

    lines = []
    for i in range(PIECES):
        lines.append(LineGather(p, depth, lambda b, i=i: G.at[i, p.y, b, p.x, p.c], zs.at[i], zr.at[i]))
    wr = WI.shape[0] // (FF_PIECES // 2)
    orow = units // (FF_PIECES // 2)
    ff = []
    for i in range(FF_PIECES):
        if i < FF_PIECES // 2:
            slot = lambda b, i=i: WI.at[pl.ds(i * wr, wr), pl.ds(pl.multiple_of(b * units, units), units)]
        else:
            slot = lambda b, i=i: WO.at[b, pl.ds((i - FF_PIECES // 2) * orow, orow)]
        ff.append(LineGather(p, depth, slot, fs.at[i], fr.at[i]))

    def plane_slot(i):
        def slot(x, c, y, h):
            if h is None:
                return G.at[i, y, :, x, c]
            return G.at[i, y, :, x, c, pl.ds(h * (part // 2), part // 2)]

        return slot

    def g3_slot(r):
        few_rows = G3.shape[4] // 2

        def slot(x, c, y, h):
            if h is None:
                return G3.at[x, c, r, y]
            return G3.at[x, c, r, y, pl.ds(h * few_rows, few_rows)]

        return slot

    slots = [g3_slot(0)] + [plane_slot(i) for i in range(PIECES)] + [g3_slot(1)]
    planes = [PlaneGather(p, slot, ps.at[i], pr.at[i]) for i, slot in enumerate(slots)]
    swaps = [
        remote(OWN_T.at[1 - p.y], TOK.at[p.y], ss.at[0], sr.at[0], p.yn()),
        remote(OWN_E.at[1 - p.y], CTX.at[ENC, mine], ss.at[1], sr.at[1], p.yn()),
    ]

    def swapped(i):
        if i == 0:
            view = TOK.at[1 - p.y]
        else:
            view = CTX.at[ENC, pl.ds(pl.multiple_of((1 - p.y) * few, few), few)]
        remote(view, view, ss.at[i], sr.at[i], p.yn()).wait_recv()

    swaps[0].start()

    def vec_move(j):
        other = lax.rem(me + j, count)
        return remote(VEC.at[me], VEC.at[me], vs.at[j], vr.at[j], (other // 2, lax.rem(other, 2)))

    @pl.loop(1, count)
    def _(j):
        vec_move(j).start()

    own.wait()

    saved = []

    def save(src, dst):
        copy = pltpu.make_async_copy(src, dst, osem.at[len(saved)])
        copy.start()
        saved.append(copy)

    def vector(i):
        return FULL[i : i + 1]

    def weight(i):
        copy = pltpu.make_async_copy(G.at[i], W, wsem.at[0])
        copy.start()
        copy.wait()

    def project(a, store):
        for y in range(2):
            store(y * (width // 2), mm(a, W[y].reshape(width, width // 2)))

    def project_back(a_ref):
        total = None
        for y in range(2):
            term = mm(a_ref[:, y * (width // 2) : (y + 1) * (width // 2)], W[y].reshape(width, width // 2), NT)
            total = term if total is None else total + term
        return total

    def into(ref, i):
        def store(at, value):
            ref[i, :, at : at + width // 2] = value.astype(jnp.bfloat16)

        return store

    def first_norm():
        @pl.loop(1, count)
        def _(j):
            other = lax.rem(me + count - j, count)
            remote(VEC.at[other], VEC.at[other], vs.at[j], vr.at[j], p.yn()).wait_recv()

        group = count * 128 // width
        for k in range(width // 128):
            piece = VEC[group * k, 0:8]
            for j in range(1, group):
                piece += VEC[group * k + j, 0:8]
            FULL[:, k * 128 : (k + 1) * 128] = piece
        save(FULL, full_out)
        for b in range(depth):
            held = VEC[((b * 2 + p.x) * 2 + p.c) * 2 + p.y]
            for k in range(units // 128):
                at = b * units + k * 128
                BIAS[:, at : at + 128] = jnp.broadcast_to(held[8 + k : 9 + k], (8, 128))
        swapped(0)
        tok = TOK[...].reshape(rows, width).astype(jnp.float32)
        MID[0] = tok
        ACT[N1] = layer_norm(tok, vector(0), vector(1)).astype(jnp.bfloat16)
        save(ACT.at[N1], act_out.at[N1])

    def qkv(i):
        weight(i)
        project(ACT[N1], into(ACT, (Q, K, V)[i]))
        save(ACT.at[(Q, K, V)[i]], act_out.at[(Q, K, V)[i]])

    def same(left, right):
        def pair(ref):
            row = ref[pl.ds(p.y, 1)].astype(jnp.float32)
            rest = jnp.zeros((14, row.shape[1]), jnp.float32)
            return jnp.concatenate([row, 1.0 - row, rest], axis=0).astype(jnp.bfloat16)

        return mm(pair(left), pair(right), TN) > 0.5

    pairs_of_heads = width // 128

    def self_attention(start, stop):
        back = lax.broadcasted_iota(jnp.int32, (rows, rows), 1) <= lax.broadcasted_iota(jnp.int32, (rows, rows), 0)
        attend_pairs(
            ACT.at[Q], ACT.at[K], ACT.at[V], same(TARGET, TARGET) & back, P1, ACT.at[H1], start, stop
        )

    def self_project():
        self_attention(pairs_of_heads // 2, pairs_of_heads)
        save(P1, p1_out)
        save(ACT.at[H1], act_out.at[H1])
        weight(3)
        middle = MID[0] + project_back(ACT.at[H1])
        MID[1] = middle
        ACT[N2] = layer_norm(middle, vector(2), vector(3)).astype(jnp.bfloat16)
        save(MID.at[pl.ds(0, 2)], mid_out.at[pl.ds(0, 2)])
        save(ACT.at[N2], act_out.at[N2])

    def pairs(i):
        if i == 0:
            swapped(1)
        weight(4 + i)
        project(CTX[ENC], into(CTX, (CK, CV)[i]))

    def cross_attention():
        save(CTX, ctx_out)
        weight(6)
        project(ACT[N2], into(ACT, CQ))
        save(ACT.at[CQ], act_out.at[CQ])
        attend_pairs(
            ACT.at[CQ], CTX.at[CK], CTX.at[CV], same(TARGET, SOURCE), P2, ACT.at[H2], 0, pairs_of_heads
        )
        save(P2, p2_out)
        save(ACT.at[H2], act_out.at[H2])

    def hn_slot(x, c, y, h):
        if h is None:
            return HN.at[x, c, y]
        return HN.at[x, c, y, pl.ds(h * half, half)]

    gather = PlaneGather(p, hn_slot, gs, gr)

    def cross_project():
        weight(7)
        latter = MID[1] + project_back(ACT.at[H2])
        HN[p.x, p.c, p.y] = layer_norm(latter, vector(4), vector(5)).astype(jnp.bfloat16)
        gather.begin()
        MID[2] = latter
        save(MID.at[2], mid_out.at[2])
        LATS[...] = MID[2, pl.ds(pl.multiple_of((1 - p.y) * half, half), half)].astype(jnp.bfloat16)

    work = {
        0: [functools.partial(qkv, 0)],
        1: [functools.partial(qkv, 1)],
        2: [functools.partial(qkv, 2), functools.partial(self_attention, 0, pairs_of_heads // 2)],
        3: [self_project],
        4: [functools.partial(pairs, 0)],
        5: [functools.partial(pairs, 1)],
        6: [cross_attention],
        7: [cross_project],
    }
    lead = depth - 2
    turns = 2 * (lead + len(planes) + 3)
    early, late = 2 * lead, 2 * lead + 2 * PIECES - 2
    starts = list(range(early)) + list(range(early, late, 3))
    starts += list(range(late, late + FF_PIECES - len(starts)))

    def turn(n):
        for f in range(FF_PIECES):
            k = n - starts[f]
            if k % 2 == 0 and 0 <= k < 2 * depth:
                ff[f].step(k // 2)

    for it in range(-lead, len(planes) + 3):
        for i in range(PIECES):
            if 0 <= it - i + lead < depth:
                lines[i].step(it - i + lead)
        if 0 <= it < len(planes):
            planes[it].begin()
        turn(2 * (it + lead))
        if it == 0:
            swaps[1].start()
        if 0 <= it - 1 < len(planes):
            planes[it - 1].forward()
        if 0 <= it - 2 < len(planes):
            planes[it - 2].finish()
        turn(2 * (it + lead) + 1)
        if 0 <= it - 3 < len(planes):
            planes[it - 3].end()
        if it == 1:
            first_norm()
        for task in work.get(it - 4, []):
            task()

    def bits(code):
        dc, dx, dy = code // 4, lax.rem(code // 2, 2), lax.rem(code, 2)
        return lax.rem(p.x + dx, 2), lax.rem(p.c + dc, 2), lax.rem(p.y + dy, 2)

    arriving = (0, 4, 1, 2, 5, 6, 3, 7)
    leaving = (7, 6, 3, 5, 2, 1, 4, 0)
    for_core = (1, 1, 0, 1, 0, 0, 1, 0)
    turn_of = (0, 1, 0, 2, 1, 2, 3, 3)

    def pick(i, table):
        value = table[0]
        for k in range(1, 8):
            value = jnp.where(i == k, table[k], value)
        return value

    def to_core(j, send, land, a, b):
        return remote(send.at[j], land.at[j], a.at[j], b.at[j], p.core())

    def to_chip(j):
        dx, dy = 1 - j // 2, 1 - lax.rem(j, 2)
        return remote(
            PS.at[j], PR.at[j], xs.at[j], xr.at[j], p.at(x=lax.rem(p.x + dx, 2), y=lax.rem(p.y + dy, 2))
        )

    def diagonal(src, land, n, h):
        return remote(
            src.at[0, pl.ds(h * half, half)], land.at[h], us.at[n, h], ur.at[n, h], p.yn() if h else p.xn()
        )

    def merge(parts, land, n):
        diagonal(parts, land, n, 0).wait_recv()
        add_low(parts.at[2, pl.ds(0, half)], land.at[0])
        diagonal(parts, land, n, 1).wait_recv()
        add_low(parts.at[1, pl.ds(half, half)], land.at[1])

    latter_move = remote(LATS, LATR, ss.at[2], sr.at[2], p.yn())

    def bias_move(b):
        return remote(BS.at[b], BR.at[z], bs.at[b], br.at[z], p.at(z=b))

    def up(h):
        return remote(S.at[depth - 1, h], RF.at[h], hs.at[h], hr.at[h], p.up())

    def down(h):
        return remote(S.at[0, h], RF.at[h], hs.at[h], hr.at[h], p.down())

    def hop(s, h):
        @pl.when(jnp.logical_and(s == 0, z == 0))
        def _():
            up(h).start()

        @pl.when(jnp.logical_and(s == 0, z == depth - 1))
        def _():
            down(h).start()


    @pl.loop(0, 8)
    def _(i):
        @pl.when(i == 1)
        def _():
            gather._arrival(4).wait_recv()

        @pl.when(i == 2)
        def _():
            gather.forward()

        @pl.when(i == 4)
        def _():
            gather._arrival(5).wait_recv()
            gather._arrival(6).wait_recv()

        @pl.when(i == 6)
        def _():
            gather.finish()

        @pl.when(i == 7)
        def _():
            gather._arrival(7).wait_recv()

        at = bits(pick(i, arriving))
        before = mm(HN[at], WI[...]) + BIAS[0:1]
        active, slope = gelu_pair(before)
        ACTIVE[at] = active.astype(jnp.bfloat16)
        SLOPE[at] = slope.astype(jnp.bfloat16)

    def block(s):
        b = far_first(z, 0, depth)
        for k in range(1, depth):
            b = jnp.where(s == k, far_first(z, k, depth), b)
        return b, pl.ds(pl.multiple_of(b * units, units), units)

    def out_sums(s):
        b, cols = block(s)
        gout = mm(ACTIVE[:, :, :, :, cols].reshape(8 * rows, units), G3[...].reshape(8 * rows, width), TN)
        GO[1] = gout
        S[b, 1] = gout.astype(jnp.bfloat16)
        hop(s, 1)

    out_sums(0)
    for n in range(turns, max(starts) + 2 * depth):
        turn(n)

    @pl.loop(0, 8)
    def _(i):
        at = bits(pick(i, leaving))
        slope = mm(G3[at].reshape(rows, width), WO[...].reshape(depth * units, width), NT)
        slope = (slope * SLOPE[at].astype(jnp.float32)).astype(jnp.bfloat16)
        SLOPE[at] = slope
        total = jnp.sum(slope.astype(jnp.float32), axis=0, keepdims=True)
        for b in range(depth):
            BS[b, 0:1] += total[:, b * units : (b + 1) * units]
        back = mm(slope, WI[...], NT)
        j = pick(i, turn_of)

        @pl.when(pick(i, for_core) == 1)
        def _():
            CS[j] = back.astype(jnp.bfloat16)
            to_core(j, CS, CR, cs, cr).start()

        @pl.when(pick(i, for_core) == 0)
        def _():
            to_core(j, CS, CR, cs, cr).wait_recv()
            total = back + CR[j].astype(jnp.float32)

            @pl.when(j < 3)
            def _():
                PS[j] = total.astype(jnp.bfloat16)

            @pl.when(j == 0)
            def _():
                diagonal(PS, DA, 0, 0).start()
                diagonal(PS, DA, 0, 1).start()

            @pl.when(j == 3)
            def _():
                DSUM[...] = total

        @pl.when(i == 6)
        def _():
            merge(PS, DA, 0)
            to_chip(1).start()
            to_chip(2).start()

    @pl.loop(1, depth)
    def _(k):
        bias_move(lax.rem(z + k, depth)).start()

    def in_sums(s):
        b, cols = block(s)
        gin = mm(SLOPE[:, :, :, :, cols].reshape(8 * rows, units), HN[...].reshape(8 * rows, width), TN)
        GO[0] = gin
        S[b, 0] = gin.astype(jnp.bfloat16)
        hop(s, 0)


    in_sums(0)
    latter_move.start()

    @pl.loop(0, 8)
    def _(i):
        ox, oc, oh = bits(pick(i, leaving))
        active = ACTIVE[ox, oc, :, pl.ds(pl.multiple_of(oh * half, half), half)].reshape(rows, depth * units)
        more = mm(active, WO[...].reshape(depth * units, width))

        j = pick(i, turn_of)

        @pl.when(pick(i, for_core) == 1)
        def _():
            CSY[j] = more.astype(jnp.bfloat16)
            to_core(j, CSY, CRY, ys, yr).start()

        @pl.when(pick(i, for_core) == 0)
        def _():
            to_core(j, CSY, CRY, ys, yr).wait()
            total = more + CRY[j].astype(jnp.float32)

            @pl.when(j < 3)
            def _():
                CSY[j] = total.astype(jnp.bfloat16)

            @pl.when(j == 0)
            def _():
                diagonal(CSY, YA, 1, 0).start()
                diagonal(CSY, YA, 1, 1).start()

            @pl.when(j == 3)
            def _():
                YSUM[...] = total.reshape(2, half, width)

    @pl.loop(1, depth)
    def _(s):
        in_sums(s)
        out_sums(s)

    save(GO, go_out)
    save(G3.at[p.x, p.c, p.y], cot_out)

    GB[...] = BS[z]

    @pl.loop(1, depth)
    def _(k):
        other = lax.rem(z + k, depth)
        remote(BS.at[other], BR.at[other], bs.at[other], br.at[other], p.at(z=other)).wait()
        GB[...] += BR[other]

    save(GB, gbias_out)

    @pl.loop(1, 3)
    def _(j):
        to_chip(j).wait_recv()
        DSUM[...] += PR[j].astype(jnp.float32)

    save(DSUM, d_out)

    @pl.when((z == 1) | (z == depth - 2))
    def _():
        far = jnp.where(z == 1, depth - 1, 0)
        for h in range(2):
            up(h).wait_recv()
            add_low(S.at[far, h], RF.at[h])

    save(S, S_out)
    latter_move.wait()
    YSUM[p.y] += MID[2, pl.ds(pl.multiple_of(p.y * half, half), half)] + vector(6)
    YSUM[1 - p.y] += LATR[...].astype(jnp.float32) + vector(6)

    merge(CSY, YA, 1)
    save(CSY.at[pl.ds(1, 2)], YS_out)
    save(YSUM, y_out)

    @pl.when((z == 0) | (z == depth - 1))
    def _():
        for h in range(2):
            up(h).wait_send()

    for line in lines + ff:
        line.sent()
    for plane in planes + [gather]:
        plane.sent()
    for copy in swaps:
        copy.wait_send()

    @pl.loop(1, count)
    def _(j):
        vec_move(j).wait_send()

    @pl.loop(0, 4)
    def _(j):
        to_core(j, CS, CR, cs, cr).wait_send()

    @pl.loop(1, 3)
    def _(j):
        to_chip(j).wait_send()

    for h in range(2):
        diagonal(PS, DA, 0, h).wait_send()
        diagonal(CSY, YA, 1, h).wait_send()

    for copy in saved:
        copy.wait()


def forward_all(proj, so, pairs, query, co, win, wout, vec, tok, enc, cot, target, source):
    depth = lax.axis_size("dp") // 4
    rows, cols = query.shape
    bf, f32 = jnp.bfloat16, jnp.float32
    count = 8 * depth
    length, short, d = 2 * tok.shape[1], 2 * enc.shape[1], tok.shape[2]
    units = wout.shape[0]
    heads = d // 128
    whole = (2, depth, 2, 2, rows, cols)
    shapes = {
        "G": ((PIECES,) + whole, bf),
        "ACT": ((9, length, d), bf),
        "CTX": ((3, short, d), bf),
        "MID": ((3, length, d), f32),
        "P1": ((heads, 2 * length, length), bf),
        "P2": ((heads, 2 * length, short), bf),
        "FULL": ((8, d), f32),
        "COT": (cot.shape, bf),
        "DSUM": ((length, d), f32),
        "YSUM": ((2, length // 2, d), f32),
        "GO": ((2, units, d), f32),
        "GB": ((8, units), f32),
        "S": ((depth, 2, units, d), bf),
        "YS": ((2, length, d), bf),
    }
    outs = [jax.ShapeDtypeStruct(*shape) for shape in shapes.values()]

    def held(name):
        return pltpu.VMEM(*shapes[name])

    dma = pltpu.SemaphoreType.DMA
    hb = pl.BlockSpec(memory_space=HBM)
    tokens = (2, 2, 2, length, d)
    four = pltpu.VMEM((4, length, d), bf)
    three = pltpu.VMEM((3, length, d), bf)
    scratch = [
        pltpu.VMEM((PIECES, rows, cols), bf),
        pltpu.VMEM(whole, bf),
        pltpu.VMEM(tok.shape, bf),
        pltpu.VMEM((count,) + vec.shape, f32),
        held("FULL"),
        pltpu.VMEM((8, depth * units), f32),
        held("ACT"), held("CTX"), held("MID"), held("P1"), held("P2"),
        pltpu.VMEM(target.shape, jnp.int32), pltpu.VMEM(source.shape, jnp.int32),
        pltpu.VMEM(tok.shape, bf), pltpu.VMEM(enc.shape, bf),
        pltpu.VMEM(tokens, bf),
        pltpu.VMEM((2, 2, 2, 2) + cot.shape[1:], bf),
        pltpu.VMEM((d, depth * units), bf),
        pltpu.VMEM((depth, units, d), bf),
        held("S"),
        pltpu.VMEM((2, units, d), bf),
        pltpu.VMEM(tokens[:4] + (depth * units,), bf),
        pltpu.VMEM(tokens[:4] + (depth * units,), bf),
        pltpu.VMEM((depth, 8, units), f32),
        pltpu.VMEM((depth, 8, units), f32),
        four, four, four, four, three, three,
        pltpu.VMEM((2, length // 2, d), bf), pltpu.VMEM((2, length // 2, d), bf),
        held("DSUM"), held("YSUM"), held("GO"), held("GB"),
        pltpu.VMEM((length // 2, d), bf), pltpu.VMEM((length // 2, d), bf),
        dma((13,)), dma((1,)), dma((24,)),
        dma((PIECES, 2, depth - 1)), dma((PIECES, 2, depth - 1)),
        dma((FF_PIECES, 2, depth - 1)), dma((FF_PIECES, 2, depth - 1)),
        dma((PIECES + 2, 8)), dma((PIECES + 2, 8)),
        dma((count,)), dma((count,)),
        dma((3,)), dma((3,)),
        dma((8,)), dma((8,)),
        dma((2,)), dma((2,)),
        dma((depth,)), dma((depth,)),
        dma((4,)), dma((4,)),
        dma((4,)), dma((4,)),
        dma((3,)), dma((3,)),
        dma((2, 2)), dma((2, 2)),
    ]
    return pl.pallas_call(
        functools.partial(forward_kernel, depth),
        out_shape=outs,
        in_specs=[hb] * 13,
        out_specs=[hb] * len(outs),
        scratch_shapes=scratch,
        compiler_params=pltpu.CompilerParams(
            collective_id=1, has_side_effects=True, vmem_limit_bytes=63 << 20
        ),
        name="forward_all",
    )(proj, so, pairs, query, co, win, wout, vec, tok, enc, cot, target, source)


def norm_back(e, h, gain):
    center = h - jnp.mean(h, axis=-1, keepdims=True)
    inverse = lax.rsqrt(jnp.mean(center * center, axis=-1, keepdims=True) + EPS)
    normal = center * inverse
    scaled = e * gain
    back = inverse * (
        scaled
        - jnp.mean(scaled, axis=-1, keepdims=True)
        - normal * jnp.mean(scaled * normal, axis=-1, keepdims=True)
    )
    return back, jnp.sum(e * normal, axis=0, keepdims=True), jnp.sum(e, axis=0, keepdims=True)


def attend_pairs_back(q_ref, k_ref, v_ref, probs_ref, slope_ref, dq_ref, dk_ref, dv_ref, start, stop):
    rows = q_ref.shape[0]
    first = lax.broadcasted_iota(jnp.int32, (rows, 128), 1) < HEAD

    def stacked(a):
        zero = jnp.zeros_like(a)
        return jnp.concatenate([jnp.where(first, a, zero), jnp.where(first, zero, a)], axis=0)

    @pl.loop(start, stop)
    def _(h):
        at = (slice(None), pl.ds(pl.multiple_of(h * 128, 128), 128))
        up = stacked(slope_ref[at])
        low = probs_ref[h]
        probs = low.astype(jnp.float32)
        dprobs = mm(up, v_ref[at], NT)
        ds = (probs * (dprobs - jnp.sum(probs * dprobs, axis=-1, keepdims=True))).astype(jnp.bfloat16)
        dq = mm(ds, k_ref[at]) * HEAD**-0.5
        dq_ref[at] = jnp.where(first, dq[:rows], dq[rows:]).astype(jnp.bfloat16)
        dk_ref[at] = (mm(ds, stacked(q_ref[at]), TN) * HEAD**-0.5).astype(jnp.bfloat16)
        dv_ref[at] = mm(low, up, TN).astype(jnp.bfloat16)


class HoppedReduce(LineReduce):
    def _down(self, b):
        slot = self.n - 2 + self.p.z - 1 - b
        return remote(self.part(b), self.slots(slot), self.send.at[b], self.recv.at[slot], self.p.down())

    def above(self, b):
        slot = self.n - 2 + self.p.z - b
        return remote(self.slots(slot), self.slots(slot), self.send.at[b], self.recv.at[slot], self.p.down())

    def first(self, b):
        z, n = self.p.z, self.n

        @pl.when((b > z) & (((z == 0) & (b < n - 1)) | ((z == 1) & (b == n - 1))))
        def _():
            self._up(b).start()

        @pl.when((b < z) & (((z == n - 1) & (b > 0)) | ((z == n - 2) & (b == 0))))
        def _():
            self._down(b).start()

    def middle(self, b, add):
        z, n = self.p.z, self.n

        @pl.when((z > 0) & (b > z) & ((z > 1) | (b < n - 1)))
        def _():
            self.below(b).wait_recv()
            add(self.part(b), self.slots(b - z))
            self._up(b).start()

        @pl.when((z < n - 1) & (b < z) & ((z < n - 2) | (b > 0)))
        def _():
            self.above(b).wait_recv()
            add(self.part(b), self.slots(n - 2 + z - b))
            self._down(b).start()

    def last(self, take):
        z, n = self.p.z, self.n

        @pl.when(z > 0)
        def _():
            self.below(z).wait_recv()
            take(self.slots(0))

        @pl.when(z < n - 1)
        def _():
            self.above(z).wait_recv()
            take(self.slots(n - 2))

    def sent(self):
        z, n = self.p.z, self.n

        @pl.loop(0, n)
        def _(b):
            @pl.when((b > z) & ((z > 0) | (b < n - 1)))
            def _():
                self._up(b).wait_send()

            @pl.when((b < z) & ((z < n - 1) | (b > 0)))
            def _():
                self._down(b).wait_send()


SLOTS = 4
FF_PARTS = 8
FF_GAP = 2


def backward_kernel(
    depth,
    G, act, ctx, mid, p1, p2, full, cot_in, d_in, y_in, go_in, S_in, YS_in,
    gw_hbm, vec_hbm, res_hbm, tg_hbm, eg_hbm, go_hbm,
    gw_out, vec_out, res_out, tg_out, eg_out, go_out,
    MY, SEND, CR, PD, PR, R, S, RF, YS, YR, W, ACT, CTX, X, PB1, PB2, UP, LOW, SL, DH, DC, COT, FULL, VG, VR, XS, XR, ES, ER,
    lsem, wsem, cs, cr, ds, dr, ps, pr, zs, zr, fs, fr, ys, yr, vs, vr, ss, sr, osem, credit,
):
    p = Place()
    count = 8 * depth
    me = p.dp * 2 + p.y
    ox, oy = 1 - p.x, 1 - p.y
    rows, width = UP.shape
    short = CTX.shape[1]
    cols = width // 2
    part = MY.shape[4]
    low_type = jnp.bfloat16

    def load(i, src, dst):
        copy = pltpu.make_async_copy(src, dst, lsem.at[i])
        copy.start()
        return copy

    loads = [
        load(0, mid.at[2], X),
        load(1, d_in, UP),
        load(2, cot_in, COT),
        load(3, full, FULL),
        load(4, act.at[pl.ds(0, 8)], ACT),
        load(5, ctx, CTX),
        load(6, p2, PB2),
        load(7, S_in, S),
        load(8, go_in, go_out),
        load(9, p1, PB1),
        load(10, YS_in, YS),
        load(11, y_in, res_out),
    ]
    order = (7, 6, 3, 0, 1, 2, 4, 5)

    def weight(n):
        return pltpu.make_async_copy(G.at[order[n]], W.at[n % 2], wsem.at[n % 2])

    def use(n):
        weight(n).wait()
        if n + 1 < len(order):
            weight(n + 1).start()
        return [W[n % 2, y].reshape(width, cols) for y in range(2)]

    weight(0).start()
    VG[...] = jnp.zeros_like(VG)
    all_barrier(p, count)

    def y_move(j):
        return remote(YS.at[j], YR.at[j], ys.at[j], yr.at[j], p.yn() if j else p.xn())

    loads[10].wait()
    for j in range(2):
        y_move(j).start()

    def core(i):
        return remote(SEND.at[i % 2], CR.at[i % SLOTS], cs.at[i], cr.at[i], p.core())

    def cut(i, h):
        by_x = part // 2
        return pl.ds(by_x, part - by_x) if h else pl.ds(0, by_x)

    def diagonal(i, h):
        return remote(
            MY.at[i, oy, :, ox, cut(i, h)], PD.at[i, :, cut(i, h)], ds.at[i, h], dr.at[i, h],
            p.yn() if h else p.xn(),
        )

    def column(i, h):
        view = MY.at[i, oy, :, p.x] if h else MY.at[i, p.y, :, ox]
        return remote(view, PR.at[i, h], ps.at[i, h], pr.at[i, h], p.yn() if h else p.xn())

    lines = [
        LineReduce(
            p, depth, lambda b, i=i: MY.at[i, p.y, b, p.x], lambda k, i=i: R.at[i, k], zs.at[i], zr.at[i]
        )
        for i in range(PIECES)
    ]
    frows = S.shape[2] // (FF_PARTS // 2)
    ff = []
    for f in range(FF_PARTS):
        at = pl.ds(f // 2 * frows, frows)
        ff.append(
            HoppedReduce(
                p, depth, lambda b, f=f, at=at: S.at[b, f % 2, at], lambda k, f=f, at=at: RF.at[k, f % 2, at],
                fs.at[f], fr.at[f],
            )
        )

    def store_part(i, left, right):
        if i >= 2:
            core(i - 2).wait_send()
        for y in range(2):
            value = mm(left, right[:, y * cols : (y + 1) * cols], TN).reshape(depth, 2, 2, part, cols)
            value = value.astype(low_type)
            even, odd = value[:, :, 0], value[:, :, 1]
            MY[i, y] = jnp.where(p.c == 0, even, odd)
            SEND[i % 2, y] = jnp.where(p.c == 0, odd, even)
        if i >= SLOTS:
            pl.semaphore_wait(credit, 1)
        core(i).start()

    def stage(i, s):
        if s == 1:
            core(i).wait_recv()
            add_low(MY.at[i], CR.at[i % SLOTS])
            if i + SLOTS < PIECES:
                signal(credit, p.core())
            diagonal(i, 0).start()
            diagonal(i, 1).start()
        elif s == 2:
            diagonal(i, 0).wait_recv()
            add_low(MY.at[i, oy, :, p.x, cut(i, 0)], PD.at[i, :, cut(i, 0)])
            column(i, 1).start()
            diagonal(i, 1).wait_recv()
            add_low(MY.at[i, p.y, :, ox, cut(i, 1)], PD.at[i, :, cut(i, 1)])
            column(i, 0).start()
        elif s == 3:
            column(i, 0).wait_recv()
            column(i, 1).wait_recv()
            view = MY.at[i, p.y, :, p.x]
            view[...] = (
                view[...].astype(jnp.float32)
                + PR[i, 0].astype(jnp.float32)
                + PR[i, 1].astype(jnp.float32)
            ).astype(low_type)
            for k in range(depth - 1):
                lines[i].first(far_first(p.z, k, depth))
        elif s < 3 + depth:
            lines[i].middle(far_first(p.z, s - 4, depth), add_low)
        elif s == 3 + depth:
            gw_out[i] = MY[i, p.y, p.z, p.x].astype(jnp.float32)

            def take(slot):
                gw_out[i] += slot[...].astype(jnp.float32)

            lines[i].last(take)

    def ff_stage(f, s):
        if s == 0:
            for k in range(depth - 1):
                ff[f].first(far_first(p.z, k, depth))
        elif s < depth:
            ff[f].middle(far_first(p.z, s - 1, depth), add_low)
        else:
            at = pl.ds(f // 2 * frows, frows)

            def take(slot):
                go_out[f % 2, at] += slot[...].astype(jnp.float32)

            ff[f].last(take)

    clock = [0]

    def tick(*stages):
        n = clock[0]
        clock[0] += 1
        if n == 0:
            loads[7].wait()
            loads[8].wait()
        for f in range(FF_PARTS):
            if (n - f) % FF_GAP == 0 and 0 <= (n - f) // FF_GAP <= depth:
                ff_stage(f, (n - f) // FF_GAP)
        for i, s in stages:
            stage(i, s)

    def gain(i):
        return FULL[i : i + 1]

    def spread(i, values):
        VG[i : i + 1] = values

    tick()
    for i in (0, 1, 2, 3):
        loads[i].wait()
    cot = COT[...].reshape(rows, width).astype(jnp.float32)
    latter = X[...]
    back, g_gain, g_shift = norm_back(UP[...], latter, gain(4))
    spread(4, g_gain)
    spread(5, g_shift)
    spread(6, jnp.sum(cot, axis=0, keepdims=True))
    UP[...] = cot + back
    LOW[...] = UP[...].astype(low_type)
    next_mid = load(0, mid.at[1], X)
    w = use(0)
    for y in range(2):
        SL[:, y * cols : (y + 1) * cols] = mm(LOW[...], w[y]).astype(low_type)
    loads[4].wait()
    store_part(0, LOW[...], ACT[H2])
    tick()
    loads[5].wait()
    loads[6].wait()
    attend_pairs_back(
        ACT.at[CQ], CTX.at[CK], CTX.at[CV], PB2, SL, DH.at[0], DC.at[0], DC.at[1], 0, width // 128
    )
    store_part(1, ACT[N2], DH[0])
    tick((0, 1))
    w = use(1)
    slope = mm(DH[0, :, :cols], w[0], NT) + mm(DH[0, :, cols:], w[1], NT)
    next_mid.wait()
    back, g_gain, g_shift = norm_back(slope, X[...], gain(2))
    spread(2, g_gain)
    spread(3, g_shift)
    UP[...] += back
    LOW[...] = UP[...].astype(low_type)
    next_mid = load(0, mid.at[0], X)
    store_part(2, CTX[ENC], DC[0])
    tick((1, 1))
    store_part(3, CTX[ENC], DC[1])
    tick((2, 1))
    w = use(2)
    for y in range(2):
        SL[:, y * cols : (y + 1) * cols] = mm(LOW[...], w[y]).astype(low_type)
    store_part(4, LOW[...], ACT[H1])
    tick((3, 1), (0, 2))
    loads[9].wait()
    attend_pairs_back(
        ACT.at[Q], ACT.at[K], ACT.at[V], PB1, SL, DH.at[0], DH.at[1], DH.at[2], 0, width // 256
    )
    tick((4, 1), (1, 2))
    attend_pairs_back(
        ACT.at[Q], ACT.at[K], ACT.at[V], PB1, SL, DH.at[0], DH.at[1], DH.at[2], width // 256, width // 128
    )
    store_part(5, ACT[N1], DH[0])
    tick((0, 3), (2, 2))
    store_part(6, ACT[N1], DH[1])
    tick((5, 1), (1, 3), (3, 2), (0, 4))
    store_part(7, ACT[N1], DH[2])
    tick((6, 1), (2, 3), (4, 2), (1, 4), (0, 5))
    slope = None
    for i in range(3):
        w = use(3 + i)
        term = mm(DH[i, :, :cols], w[0], NT) + mm(DH[i, :, cols:], w[1], NT)
        slope = term if slope is None else slope + term
    tick((7, 1), (3, 3), (5, 2), (2, 4), (1, 5), (0, 6))
    next_mid.wait()
    back, g_gain, g_shift = norm_back(slope, X[...], gain(0))
    spread(0, g_gain)
    spread(1, g_shift)
    back += UP[...]
    for h in range(2):
        tg_out[h] = back[h * (rows // 2) : (h + 1) * (rows // 2)]

    def vec_move(j):
        other = lax.rem(me + j, count)
        at = pl.ds(pl.multiple_of(other * (width // count) // 128 * 128, 128), 128)
        return remote(VG.at[:, at], VR.at[j], vs.at[j], vr.at[j], (other // 2, lax.rem(other, 2)))

    @pl.loop(1, count)
    def _(j):
        vec_move(j).start()

    tick((6, 2), (4, 3), (3, 4), (2, 5), (1, 6), (0, 7))
    slope = None
    for i in range(2):
        w = use(6 + i)
        term = mm(DC[i, :, :cols], w[0], NT) + mm(DC[i, :, cols:], w[1], NT)
        slope = term if slope is None else slope + term
    for h in range(2):
        eg_out[h] = slope[h * (short // 2) : (h + 1) * (short // 2)]
    stores = []

    def store(src, dst):
        copy = pltpu.make_async_copy(src, dst, osem.at[len(stores)])
        copy.start()
        stores.append(copy)

    XS[...] = tg_out[oy].astype(low_type)
    loads[11].wait()
    for j in range(2):
        y_move(j).wait_recv()
        res_out[...] += YR[j].astype(jnp.float32).reshape(res_out.shape)
    ES[...] = eg_out[oy].astype(low_type)
    store(res_out, res_hbm)
    swaps = [
        remote(XS, XR, ss.at[0], sr.at[0], p.yn()),
        remote(ES, ER, ss.at[1], sr.at[1], p.yn()),
    ]
    tick((7, 2), (5, 3), (4, 4), (3, 5), (2, 6), (1, 7))
    for copy in swaps:
        copy.start()
    tick((6, 3), (5, 4), (4, 5), (3, 6), (2, 7))
    tick((7, 3), (6, 4), (5, 5), (4, 6), (3, 7))
    tick((7, 4), (6, 5), (5, 6), (4, 7))
    tick((7, 5), (6, 6), (5, 7))
    tick((7, 6), (6, 7))
    tick((7, 7))
    while clock[0] < FF_PARTS + FF_GAP * depth + 1:
        tick()
    store(gw_out, gw_hbm)
    store(go_out, go_hbm)
    at = pl.ds(pl.multiple_of(me * (width // count) // 128 * 128, 128), 128)
    vec_out[...] = VG[:, at]

    @pl.loop(1, count)
    def _(j):
        vec_move(j).wait()
        vec_out[...] += VR[j]

    store(vec_out, vec_hbm)

    for copy in swaps:
        copy.wait()
    tg_out[oy] = XR[...].astype(jnp.float32)
    eg_out[oy] = ER[...].astype(jnp.float32)
    store(tg_out, tg_hbm)
    store(eg_out, eg_hbm)
    for i in range(PIECES):
        if i >= PIECES - 2:
            core(i).wait_send()
        for h in range(2):
            diagonal(i, h).wait_send()
            column(i, h).wait_send()
        lines[i].sent()
    for line in ff:
        line.sent()
    for j in range(2):
        y_move(j).wait_send()
    for copy in stores:
        copy.wait()


def backward_all(G, act, ctx, mid, p1, p2, full, cot, d_in, y_in, go_in, S_in, YS_in):
    depth = G.shape[2]
    count = 8 * depth
    rows, cols = G.shape[5:]
    length, width = d_in.shape
    short = ctx.shape[1]
    bf, f32 = jnp.bfloat16, jnp.float32
    dma = pltpu.SemaphoreType.DMA
    hb = pl.BlockSpec(memory_space=HBM)
    outs = [
            jax.ShapeDtypeStruct((PIECES, rows, cols), f32),
            jax.ShapeDtypeStruct((8, 128), f32),
            jax.ShapeDtypeStruct((2, length // 2, width), f32),
            jax.ShapeDtypeStruct((2, length // 2, width), f32),
            jax.ShapeDtypeStruct((2, short // 2, width), f32),
            jax.ShapeDtypeStruct(go_in.shape, f32),
    ]
    return pl.pallas_call(
        functools.partial(backward_kernel, depth),
        out_shape=outs,
        in_specs=[hb] * 13,
        out_specs=[hb] * 6,
        scratch_shapes=[pltpu.VMEM(o.shape, o.dtype) for o in outs] + [
            pltpu.VMEM((PIECES, 2, depth, 2, rows, cols), bf),
            pltpu.VMEM((2, 2, depth, 2, rows, cols), bf),
            pltpu.VMEM((SLOTS, 2, depth, 2, rows, cols), bf),
            pltpu.VMEM((PIECES, depth, rows, cols), bf),
            pltpu.VMEM((PIECES, 2, depth, rows, cols), bf),
            pltpu.VMEM((PIECES, depth + 1, rows, cols), bf),
            pltpu.VMEM(S_in.shape, bf),
            pltpu.VMEM((2 * depth - 4,) + S_in.shape[1:], bf),
            pltpu.VMEM(YS_in.shape, bf),
            pltpu.VMEM(YS_in.shape, bf),
            pltpu.VMEM((2,) + G.shape[1:], bf),
            pltpu.VMEM((8, length, width), bf),
            pltpu.VMEM(ctx.shape, bf),
            pltpu.VMEM((length, width), f32),
            pltpu.VMEM(p1.shape, bf),
            pltpu.VMEM(p2.shape, bf),
            pltpu.VMEM((length, width), f32),
            pltpu.VMEM((length, width), bf),
            pltpu.VMEM((length, width), bf),
            pltpu.VMEM((3, length, width), bf),
            pltpu.VMEM((2, short, width), bf),
            pltpu.VMEM((2, length // 2, width), bf),
            pltpu.VMEM((8, width), f32),
            pltpu.VMEM((8, width), f32),
            pltpu.VMEM((count, 8, 128), f32),
            pltpu.VMEM((length // 2, width), bf),
            pltpu.VMEM((length // 2, width), bf),
            pltpu.VMEM((short // 2, width), bf),
            pltpu.VMEM((short // 2, width), bf),
            dma((12,)), dma((2,)),
            dma((PIECES,)), dma((PIECES,)),
            dma((PIECES, 2)), dma((PIECES, 2)),
            dma((PIECES, 2)), dma((PIECES, 2)),
            dma((PIECES, depth)), dma((PIECES, depth + 1)),
            dma((FF_PARTS, depth)), dma((FF_PARTS, 2 * depth - 4)),
            dma((2,)), dma((2,)),
            dma((count,)), dma((count,)),
            dma((2,)), dma((2,)),
            dma((6,)),
            pltpu.SemaphoreType.REGULAR,
        ],
        compiler_params=pltpu.CompilerParams(
            collective_id=3, has_side_effects=True, vmem_limit_bytes=63 << 20
        ),
        name="backward_all",
    )(G, act, ctx, mid, p1, p2, full, cot, d_in, y_in, go_in, S_in, YS_in)


def finish_kernel(gw, res, tg, eg, go, res_out, tg_out, eg_out, proj_out, so_out, query_out, co_out, in_out, out_out, A, B, lsem, osem):
    moves = []

    def load(src, dst):
        copy = pltpu.make_async_copy(src, dst, lsem.at[len(moves)])
        copy.start()
        moves.append(copy)

    IN, RES, TG, EG, GW, OUT = A
    load(go.at[0], IN)
    load(res, RES)
    load(tg, TG)
    load(gw, GW)
    load(go.at[1], OUT)
    load(eg, EG)
    done = []

    def store(src, dst):
        copy = pltpu.make_async_copy(src, dst, osem.at[len(done)])
        copy.start()
        done.append(copy)

    moves[0].wait()
    B[...] = IN[...].T
    store(B, in_out)
    moves[1].wait()
    store(RES, res_out)
    moves[2].wait()
    store(TG, tg_out)
    moves[3].wait()
    store(GW.at[pl.ds(5, 3)], proj_out)
    store(GW.at[4], so_out)
    store(GW.at[1], query_out)
    store(GW.at[0], co_out)
    moves[4].wait()
    store(OUT, out_out)
    moves[5].wait()
    store(EG, eg_out)
    for copy in done:
        copy.wait()


def finish(gw, res, tg, eg, go):
    f32 = jnp.float32
    rows, cols = gw.shape[1:]
    units, width = go.shape[1:]
    one = jax.ShapeDtypeStruct((rows, cols), f32)
    hb = pl.BlockSpec(memory_space=HBM)
    return pl.pallas_call(
        finish_kernel,
        out_shape=[
            jax.ShapeDtypeStruct(res.shape, f32),
            jax.ShapeDtypeStruct(tg.shape, f32),
            jax.ShapeDtypeStruct(eg.shape, f32),
            jax.ShapeDtypeStruct((3, rows, cols), f32),
            one, one, one,
            jax.ShapeDtypeStruct((width, units), f32),
            jax.ShapeDtypeStruct((units, width), f32),
        ],
        in_specs=[hb] * 5,
        out_specs=[hb] * 9,
        scratch_shapes=[
            (
                pltpu.VMEM((units, width), f32),
                pltpu.VMEM(res.shape, f32),
                pltpu.VMEM(tg.shape, f32),
                pltpu.VMEM(eg.shape, f32),
                pltpu.VMEM(gw.shape, f32),
                pltpu.VMEM((units, width), f32),
            ),
            pltpu.VMEM((width, units), f32),
            pltpu.SemaphoreType.DMA((6,)),
            pltpu.SemaphoreType.DMA((9,)),
        ],
        compiler_params=pltpu.CompilerParams(vmem_limit_bytes=62 << 20),
        name="finish",
    )(gw, res, tg, eg, go)


def fast_local(
    tokens, encoder, target_doc, source_doc, self_proj, self_out, cross_query, cross_pairs, cross_out,
    hidden_in, hidden_in_bias, hidden_out, hidden_out_bias, self_gain, self_shift, cross_gain, cross_shift,
    hidden_gain, hidden_shift, cotangent,
):
    depth = lax.axis_size("dp") // 4
    count = 8 * depth
    place = Place()
    me = place.dp * 2 + place.y
    bf, f32 = jnp.bfloat16, jnp.float32
    vectors = jnp.stack(
        [self_gain, self_shift, cross_gain, cross_shift, hidden_gain, hidden_shift, hidden_out_bias]
    )
    span = vectors.shape[1]
    group = 128 // span
    lane = lax.broadcasted_iota(jnp.int32, (1, 128), 1)
    mine = lane // span == lax.rem(me, group)
    vec = jnp.concatenate([
        jnp.where(mine, jnp.tile(vectors, (1, group)), 0.0),
        jnp.zeros((1, 128), f32),
        hidden_in_bias.astype(f32).reshape(-1, 128),
    ])
    vec = jnp.pad(vec, ((0, -vec.shape[0] % 8), (0, 0)))
    G, act, ctx, mid, probs1, probs2, full, cot, d_in, y_in, go, gbias, S, YS = forward_all(
        self_proj.transpose(1, 0, 2), self_out.T, cross_pairs.transpose(1, 0, 2), cross_query, cross_out.T,
        hidden_in, hidden_out, vec, tokens, encoder, cotangent, target_doc, source_doc,
    )
    gw, vout, res, tg, eg, go = backward_all(
        G, act, ctx, mid, probs1, probs2, full, cot, d_in, y_in, go, S, YS
    )
    vout = lax.dynamic_slice_in_dim(vout, lax.rem(me, group) * span, span, axis=1)
    res, tg, eg, g_proj, g_so, g_query, g_co, g_in, g_out = finish(gw, res, tg, eg, go)
    return (
        res, tg, eg,
        g_proj.transpose(1, 0, 2), g_so.T, g_query, jnp.stack([gw[2], gw[3]], axis=1), g_co.T,
        g_in, gbias[0], g_out,
        vout[6], vout[0], vout[1], vout[2], vout[3], vout[4], vout[5],
    )


BLOCK_ROWS = 512


def smooth_gate(values):
    return jax.nn.gelu(values, approximate=True)


def plain_norm_forward(hidden, norm_gain, norm_shift):
    center = hidden - jnp.mean(hidden, axis=-1, keepdims=True)
    inverse = lax.rsqrt(jnp.mean(center * center, axis=-1, keepdims=True) + EPS)
    normal = center * inverse
    return (normal * norm_gain + norm_shift, normal, inverse)


def plain_norm_backward(upward, normal, inverse, norm_gain):
    scaled = upward * norm_gain
    centred = (
        scaled
        - jnp.mean(scaled, axis=-1, keepdims=True)
        - normal * jnp.mean(scaled * normal, axis=-1, keepdims=True)
    )
    return (centred * inverse, jnp.sum(upward * normal, axis=0), jnp.sum(upward, axis=0))


def split_blocks(array):
    row_count = array.shape[0]
    block_size = min(BLOCK_ROWS, row_count)
    return array.reshape((row_count // block_size, block_size) + array.shape[1:])


def block_scores(query_block, key_rows, allow_block):
    query_heads = query_block.reshape(query_block.shape[0], -1, HEAD)
    key_heads = key_rows.reshape(key_rows.shape[0], -1, HEAD)
    scores = jnp.einsum(
        "qhd,khd->hqk", query_heads, key_heads, preferred_element_type=jnp.float32
    ) * HEAD ** (-0.5)
    return jnp.where(allow_block[None], scores, NEGATIVE)


def plain_attend(queries, key_rows, values, allowed):
    columns = queries.shape[1]
    value_heads = values.reshape(values.shape[0], -1, HEAD)

    def one_block(pieces):
        query_block, allow_block = pieces
        scores = block_scores(query_block, key_rows, allow_block)
        highest = jnp.max(scores, axis=-1, keepdims=True)
        exponent = jnp.exp(scores - highest)
        totals = jnp.sum(exponent, axis=-1, keepdims=True)
        softmaxed = (exponent / totals).astype(jnp.bfloat16)
        mixture = jnp.einsum(
            "hqk,khd->qhd", softmaxed, value_heads, preferred_element_type=jnp.float32
        )
        return (
            mixture.reshape(query_block.shape[0], columns).astype(jnp.bfloat16),
            (highest + jnp.log(totals))[..., 0],
        )

    mixture, logsum = lax.map(one_block, (split_blocks(queries), split_blocks(allowed)))
    return (mixture.reshape(queries.shape), logsum)


def plain_attend_backward(queries, key_rows, values, allowed, logsum, slope_heads):
    scaling = HEAD ** (-0.5)
    key_heads = key_rows.reshape(key_rows.shape[0], -1, HEAD)
    value_heads = values.reshape(values.shape[0], -1, HEAD)

    def one_block(running, pieces):
        key_total, value_total = running
        query_block, allow_block, logsum_block, slope_block = pieces
        scores = block_scores(query_block, key_rows, allow_block)
        softmaxed = jnp.exp(scores - logsum_block[..., None])
        query_heads = query_block.reshape(query_block.shape[0], -1, HEAD)
        slope_out = slope_block.reshape(slope_block.shape[0], -1, HEAD)
        slope_probs = jnp.einsum(
            "qhd,khd->hqk", slope_out, value_heads, preferred_element_type=jnp.float32
        )
        centred = jnp.sum(softmaxed * slope_probs, axis=-1, keepdims=True)
        slope_scores = (softmaxed * (slope_probs - centred)).astype(jnp.bfloat16)
        slope_query = (
            jnp.einsum("hqk,khd->qhd", slope_scores, key_heads, preferred_element_type=jnp.float32)
            * scaling
        )
        key_total = (
            key_total
            + jnp.einsum(
                "hqk,qhd->khd", slope_scores, query_heads, preferred_element_type=jnp.float32
            )
            * scaling
        )
        value_total = value_total + jnp.einsum(
            "hqk,qhd->khd",
            softmaxed.astype(jnp.bfloat16),
            slope_out,
            preferred_element_type=jnp.float32,
        )
        return (
            (key_total, value_total),
            slope_query.reshape(query_block.shape[0], -1).astype(jnp.bfloat16),
        )

    empty_heads = jnp.zeros(key_heads.shape, jnp.float32)
    (key_total, value_total), slope_query = lax.scan(
        one_block,
        (empty_heads, empty_heads),
        (split_blocks(queries), split_blocks(allowed), logsum, split_blocks(slope_heads)),
    )
    return (
        slope_query.reshape(queries.shape),
        key_total.reshape(key_rows.shape).astype(jnp.bfloat16),
        value_total.reshape(values.shape).astype(jnp.bfloat16),
    )


def gather_rows(local_rows):
    return lax.all_gather(local_rows, "tensor", axis=0, tiled=True)


def sum_rows(partial_sum):
    return lax.psum_scatter(
        partial_sum.astype(jnp.bfloat16), "tensor", scatter_dimension=0, tiled=True
    ).astype(jnp.float32)


def gather_slopes(local_slopes):
    return lax.all_gather(local_slopes, "tensor", axis=0, tiled=True)


def sum_slopes(partial_sum):
    return lax.psum_scatter(
        partial_sum.astype(jnp.bfloat16), "tensor", scatter_dimension=0, tiled=True
    ).astype(jnp.float32)


def reduce_weights(weight_terms):
    return (
        lax.psum_scatter(weight_terms[0], "dp", scatter_dimension=0, tiled=True),
        lax.psum_scatter(weight_terms[1], "dp", scatter_dimension=1, tiled=True),
        lax.psum_scatter(weight_terms[2], "dp", scatter_dimension=0, tiled=True),
        lax.psum_scatter(weight_terms[3], "dp", scatter_dimension=0, tiled=True),
        lax.psum_scatter(weight_terms[4], "dp", scatter_dimension=1, tiled=True),
        lax.psum_scatter(weight_terms[5], "dp", scatter_dimension=1, tiled=True),
        lax.psum_scatter(weight_terms[6], "dp", scatter_dimension=0, tiled=True),
        lax.psum_scatter(weight_terms[7], "dp", scatter_dimension=0, tiled=True),
    )


def plain_local(
    tokens,
    encoder,
    target_doc,
    source_doc,
    self_proj,
    self_out,
    cross_query,
    cross_pairs,
    cross_out,
    hidden_in,
    hidden_in_bias,
    hidden_out,
    hidden_out_bias,
    self_gain,
    self_shift,
    cross_gain,
    cross_shift,
    hidden_gain,
    hidden_shift,
    cotangent,
):
    (
        full_self_gain,
        full_self_shift,
        full_cross_gain,
        full_cross_shift,
        full_hidden_gain,
        full_hidden_shift,
        full_out_bias,
    ) = (
        lax.all_gather(self_gain, ("dp", "tensor"), axis=0, tiled=True),
        lax.all_gather(self_shift, ("dp", "tensor"), axis=0, tiled=True),
        lax.all_gather(cross_gain, ("dp", "tensor"), axis=0, tiled=True),
        lax.all_gather(cross_shift, ("dp", "tensor"), axis=0, tiled=True),
        lax.all_gather(hidden_gain, ("dp", "tensor"), axis=0, tiled=True),
        lax.all_gather(hidden_shift, ("dp", "tensor"), axis=0, tiled=True),
        lax.all_gather(hidden_out_bias, ("dp", "tensor"), axis=0, tiled=True),
    )
    micro_count = tokens.shape[0]
    row_count = tokens.shape[1] * lax.axis_size("tensor")
    positions = jnp.arange(row_count)
    results = []
    token_grads = []
    encoder_grads = []
    vector_total = None
    weight_total = None
    for step_index in range(micro_count):
        forward_weights = (
            lax.all_gather(self_proj, "dp", axis=0, tiled=True),
            lax.all_gather(self_out, "dp", axis=1, tiled=True),
            lax.all_gather(cross_query, "dp", axis=0, tiled=True),
            lax.all_gather(cross_pairs, "dp", axis=0, tiled=True),
            lax.all_gather(cross_out, "dp", axis=1, tiled=True),
            lax.all_gather(hidden_in, "dp", axis=1, tiled=True),
            lax.all_gather(hidden_in_bias, "dp", axis=0, tiled=True),
            lax.all_gather(hidden_out, "dp", axis=0, tiled=True),
        )
        (
            full_proj,
            full_self_out,
            full_query,
            full_pairs,
            full_cross_out,
            full_in,
            full_in_bias,
            full_out,
        ) = forward_weights
        target_row = target_doc[step_index]
        source_row = source_doc[step_index]
        self_allowed = (target_row[:, None] == target_row[None, :]) & (
            positions[None, :] <= positions[:, None]
        )
        cross_allowed = target_row[:, None] == source_row[None, :]
        start_hidden = tokens[step_index].astype(jnp.float32)
        normed_first, normal_first, inverse_first = plain_norm_forward(
            start_hidden, full_self_gain, full_self_shift
        )
        self_rows = gather_rows(normed_first.astype(jnp.bfloat16))
        triple = jnp.einsum(
            "td,dcj->tcj", self_rows, full_proj, preferred_element_type=jnp.float32
        ).astype(jnp.bfloat16)
        self_heads, self_logsum = plain_attend(triple[:, 0], triple[:, 1], triple[:, 2], self_allowed)
        middle = start_hidden + sum_rows(
            jnp.dot(self_heads, full_self_out, preferred_element_type=jnp.float32)
        )
        normed_second, normal_second, inverse_second = plain_norm_forward(
            middle, full_cross_gain, full_cross_shift
        )
        cross_rows, source_rows = (
            lax.all_gather(normed_second.astype(jnp.bfloat16), "tensor", axis=0, tiled=True),
            lax.all_gather(encoder[step_index], "tensor", axis=0, tiled=True),
        )
        cross_queries = jnp.dot(cross_rows, full_query, preferred_element_type=jnp.float32).astype(
            jnp.bfloat16
        )
        key_value = jnp.einsum(
            "sd,dcj->scj", source_rows, full_pairs, preferred_element_type=jnp.float32
        ).astype(jnp.bfloat16)
        cross_heads, cross_logsum = plain_attend(
            cross_queries, key_value[:, 0], key_value[:, 1], cross_allowed
        )
        latter = middle + sum_rows(
            jnp.dot(cross_heads, full_cross_out, preferred_element_type=jnp.float32)
        )
        normed_third, normal_third, inverse_third = plain_norm_forward(
            latter, full_hidden_gain, full_hidden_shift
        )
        hidden_rows = gather_rows(normed_third.astype(jnp.bfloat16))
        before = jnp.dot(
            hidden_rows, full_in, preferred_element_type=jnp.float32
        ) + full_in_bias.astype(jnp.float32)
        gated, gate_pullback = jax.vjp(smooth_gate, before)
        active = gated.astype(jnp.bfloat16)
        results.append(
            latter
            + sum_rows(jnp.dot(active, full_out, preferred_element_type=jnp.float32))
            + full_out_bias
        )
        back_weights = (
            lax.all_gather(self_proj, "dp", axis=0, tiled=True),
            lax.all_gather(self_out, "dp", axis=1, tiled=True),
            lax.all_gather(cross_query, "dp", axis=0, tiled=True),
            lax.all_gather(cross_pairs, "dp", axis=0, tiled=True),
            lax.all_gather(cross_out, "dp", axis=1, tiled=True),
            lax.all_gather(hidden_in, "dp", axis=1, tiled=True),
            lax.all_gather(hidden_in_bias, "dp", axis=0, tiled=True),
            lax.all_gather(hidden_out, "dp", axis=0, tiled=True),
        )
        (
            back_proj,
            back_self_out,
            back_query,
            back_pairs,
            back_cross_out,
            back_in,
            back_in_bias,
            back_out,
        ) = back_weights
        upward = cotangent[step_index].astype(jnp.float32)
        grad_out_bias = jnp.sum(upward, axis=0)
        slope_rows = gather_slopes(upward.astype(jnp.bfloat16))
        grad_out = jnp.einsum("tf,td->fd", active, slope_rows, preferred_element_type=jnp.float32)
        slope_active = jnp.einsum(
            "td,fd->tf", slope_rows, back_out, preferred_element_type=jnp.float32
        )
        slope_before = gate_pullback(slope_active)[0].astype(jnp.bfloat16)
        grad_in_bias = jnp.sum(slope_before.astype(jnp.float32), axis=0)
        grad_in = jnp.einsum(
            "td,tf->df", hidden_rows, slope_before, preferred_element_type=jnp.float32
        )
        slope_normed = sum_slopes(
            jnp.einsum("tf,df->td", slope_before, back_in, preferred_element_type=jnp.float32)
        )
        slope_hidden, grad_hidden_gain, grad_hidden_shift = plain_norm_backward(
            slope_normed, normal_third, inverse_third, full_hidden_gain
        )
        upward = upward + slope_hidden
        slope_rows = gather_slopes(upward.astype(jnp.bfloat16))
        grad_cross_out = jnp.einsum(
            "tj,td->jd", cross_heads, slope_rows, preferred_element_type=jnp.float32
        )
        slope_heads = jnp.einsum(
            "td,jd->tj", slope_rows, back_cross_out, preferred_element_type=jnp.float32
        ).astype(jnp.bfloat16)
        slope_query, slope_keys, slope_values = plain_attend_backward(
            cross_queries,
            key_value[:, 0],
            key_value[:, 1],
            cross_allowed,
            cross_logsum,
            slope_heads,
        )
        slope_pairs = jnp.stack([slope_keys, slope_values], axis=1)
        grad_query = jnp.einsum(
            "td,tj->dj", cross_rows, slope_query, preferred_element_type=jnp.float32
        )
        grad_pairs = jnp.einsum(
            "sd,scj->dcj", source_rows, slope_pairs, preferred_element_type=jnp.float32
        )
        slope_cross, slope_source = (
            lax.psum_scatter(
                jnp.einsum(
                    "tj,dj->td", slope_query, back_query, preferred_element_type=jnp.float32
                ).astype(jnp.bfloat16),
                "tensor",
                scatter_dimension=0,
                tiled=True,
            ).astype(jnp.float32),
            lax.psum_scatter(
                jnp.einsum(
                    "scj,dcj->sd", slope_pairs, back_pairs, preferred_element_type=jnp.float32
                ).astype(jnp.bfloat16),
                "tensor",
                scatter_dimension=0,
                tiled=True,
            ).astype(jnp.float32),
        )
        slope_hidden, grad_cross_gain, grad_cross_shift = plain_norm_backward(
            slope_cross, normal_second, inverse_second, full_cross_gain
        )
        upward = upward + slope_hidden
        slope_rows = gather_slopes(upward.astype(jnp.bfloat16))
        grad_self_out = jnp.einsum(
            "tj,td->jd", self_heads, slope_rows, preferred_element_type=jnp.float32
        )
        slope_heads = jnp.einsum(
            "td,jd->tj", slope_rows, back_self_out, preferred_element_type=jnp.float32
        ).astype(jnp.bfloat16)
        slope_query, slope_keys, slope_values = plain_attend_backward(
            triple[:, 0], triple[:, 1], triple[:, 2], self_allowed, self_logsum, slope_heads
        )
        slope_triple = jnp.stack([slope_query, slope_keys, slope_values], axis=1)
        grad_proj = jnp.einsum(
            "td,tcj->dcj", self_rows, slope_triple, preferred_element_type=jnp.float32
        )
        slope_self = sum_slopes(
            jnp.einsum("tcj,dcj->td", slope_triple, back_proj, preferred_element_type=jnp.float32)
        )
        slope_hidden, grad_self_gain, grad_self_shift = plain_norm_backward(
            slope_self, normal_first, inverse_first, full_self_gain
        )
        token_grads.append(upward + slope_hidden)
        encoder_grads.append(slope_source)
        vector_terms = (
            grad_self_gain,
            grad_self_shift,
            grad_cross_gain,
            grad_cross_shift,
            grad_hidden_gain,
            grad_hidden_shift,
            grad_out_bias,
        )
        vector_total = (
            vector_terms if step_index == 0 else jax.tree.map(jnp.add, vector_total, vector_terms)
        )
        weight_terms = (
            grad_proj,
            grad_self_out,
            grad_query,
            grad_pairs,
            grad_cross_out,
            grad_in,
            grad_in_bias,
            grad_out,
        )
        shard_terms = reduce_weights(weight_terms)
        weight_total = (
            shard_terms if step_index == 0 else jax.tree.map(jnp.add, weight_total, shard_terms)
        )
    vector_shards = (
        lax.psum_scatter(vector_total[0], ("dp", "tensor"), scatter_dimension=0, tiled=True),
        lax.psum_scatter(vector_total[1], ("dp", "tensor"), scatter_dimension=0, tiled=True),
        lax.psum_scatter(vector_total[2], ("dp", "tensor"), scatter_dimension=0, tiled=True),
        lax.psum_scatter(vector_total[3], ("dp", "tensor"), scatter_dimension=0, tiled=True),
        lax.psum_scatter(vector_total[4], ("dp", "tensor"), scatter_dimension=0, tiled=True),
        lax.psum_scatter(vector_total[5], ("dp", "tensor"), scatter_dimension=0, tiled=True),
        lax.psum_scatter(vector_total[6], ("dp", "tensor"), scatter_dimension=0, tiled=True),
    )
    return (
        jnp.stack(results),
        jnp.stack(token_grads),
        jnp.stack(encoder_grads),
        weight_total[0],
        weight_total[1],
        weight_total[2],
        weight_total[3],
        weight_total[4],
        weight_total[5],
        weight_total[6],
        weight_total[7],
        vector_shards[6],
        vector_shards[0],
        vector_shards[1],
        vector_shards[2],
        vector_shards[3],
        vector_shards[4],
        vector_shards[5],
    )


def solution(mesh):
    in_specs = (
        P("dp", "tensor", None),
        P("dp", "tensor", None),
        P("dp", None),
        P("dp", None),
        P("dp", None, "tensor"),
        P("tensor", "dp"),
        P("dp", "tensor"),
        P("dp", None, "tensor"),
        P("tensor", "dp"),
        P(None, ("dp", "tensor")),
        P(("dp", "tensor")),
        P(("dp", "tensor"), None),
        P(("dp", "tensor")),
        P(("dp", "tensor")),
        P(("dp", "tensor")),
        P(("dp", "tensor")),
        P(("dp", "tensor")),
        P(("dp", "tensor")),
        P(("dp", "tensor")),
        P("dp", "tensor", None),
    )
    out_specs = (
        P("dp", "tensor", None),
        P("dp", "tensor", None),
        P("dp", "tensor", None),
        P("dp", None, "tensor"),
        P("tensor", "dp"),
        P("dp", "tensor"),
        P("dp", None, "tensor"),
        P("tensor", "dp"),
        P(None, ("dp", "tensor")),
        P(("dp", "tensor")),
        P(("dp", "tensor"), None),
        P(("dp", "tensor")),
        P(("dp", "tensor")),
        P(("dp", "tensor")),
        P(("dp", "tensor")),
        P(("dp", "tensor")),
        P(("dp", "tensor")),
        P(("dp", "tensor")),
    )

    def run(*arrays):
        width = arrays[0].shape[2]
        aligned = width // mesh.shape["dp"] % 16 == 0 and mesh.shape["dp"] % 4 == 0
        inner = fast_local if aligned and mesh.shape["tensor"] == 2 else plain_local
        return jax.shard_map(inner, mesh=mesh, in_specs=in_specs, out_specs=out_specs, check_vma=False)(*arrays)

    return run
```

```python
import functools

import jax
import jax.numpy as jnp
from jax import lax
from jax.experimental import pallas as pl
from jax.experimental.pallas import tpu as pltpu
from jax.sharding import PartitionSpec as P

HEAD = 64
EPS = 1e-05
NEGATIVE = -1e30
MESH = pl.DeviceIdType.MESH
HBM = pltpu.HBM
VMEM = pltpu.VMEM
PIECES = 8
FF_PIECES = 16


class Place:
    def __init__(self):
        self.dp = lax.axis_index("dp")
        self.y = lax.axis_index("tensor")
        self.c = lax.rem(self.dp, 2)
        self.x = lax.rem(self.dp // 2, 2)
        self.z = self.dp // 4

    def at(self, z=None, x=None, c=None, y=None):
        z = self.z if z is None else z
        x = self.x if x is None else x
        c = self.c if c is None else c
        y = self.y if y is None else y
        return ((z * 2 + x) * 2 + c, y)

    def core(self):
        return self.at(c=1 - self.c)

    def xn(self):
        return self.at(x=1 - self.x)

    def yn(self):
        return self.at(y=1 - self.y)

    def up(self):
        return self.at(z=self.z + 1)

    def down(self):
        return self.at(z=self.z - 1)


def remote(src, dst, send, recv, device):
    return pltpu.make_async_remote_copy(
        src_ref=src, dst_ref=dst, send_sem=send, recv_sem=recv, device_id=device, device_id_type=MESH
    )


def signal(sem, device):
    pl.semaphore_signal(sem, inc=1, device_id=device, device_id_type=MESH)


class LineGather:
    def __init__(self, place, depth, slot, send, recv):
        self.p, self.n, self.slot, self.send, self.recv = place, depth, slot, send, recv

    def _copy_up(self, k):
        b = self.p.z - k
        return remote(self.slot(b), self.slot(b), self.send.at[0, k], self.recv.at[0, k], self.p.up())

    def _copy_down(self, k):
        b = self.p.z + k
        return remote(self.slot(b), self.slot(b), self.send.at[1, k], self.recv.at[1, k], self.p.down())

    def _from_below(self, k):
        b = self.p.z - k
        return remote(self.slot(b), self.slot(b), self.send.at[0, k - 1], self.recv.at[0, k - 1], self.p.up())

    def _from_above(self, k):
        b = self.p.z + k
        return remote(self.slot(b), self.slot(b), self.send.at[1, k - 1], self.recv.at[1, k - 1], self.p.down())

    def arrive(self, k):
        z = self.p.z

        @pl.when(z - k >= 0)
        def _():
            self._from_below(k).wait_recv()

        @pl.when(z + k <= self.n - 1)
        def _():
            self._from_above(k).wait_recv()

    def step(self, k):
        z = self.p.z
        if k > 0:
            self.arrive(k)
        if k < self.n - 1:

            @pl.when((z - k >= 0) & (z < self.n - 1))
            def _():
                self._copy_up(k).start()

            @pl.when((z + k <= self.n - 1) & (z > 0))
            def _():
                self._copy_down(k).start()

    def sent(self):
        z = self.p.z
        for k in range(self.n - 1):

            @pl.when((z - k >= 0) & (z < self.n - 1))
            def _():
                self._copy_up(k).wait_send()

            @pl.when((z + k <= self.n - 1) & (z > 0))
            def _():
                self._copy_down(k).wait_send()


class PlaneGather:
    def __init__(self, place, slot, send, recv):
        self.p, self.slot, self.send, self.recv = place, slot, send, recv
        p = place
        x, y, c = p.x, p.y, p.c
        ox, oy = 1 - x, 1 - y
        self.moves = [
            ((x, c, y, None), p.xn(), 0),
            ((x, c, y, None), p.yn(), 1),
            ((ox, c, y, 0), p.yn(), 2),
            ((x, c, oy, 1), p.xn(), 3),
            ((x, c, y, None), p.core(), 4),
            ((ox, c, y, None), p.core(), 5),
            ((x, c, oy, None), p.core(), 6),
            ((ox, c, oy, None), p.core(), 7),
        ]
        oc = 1 - c
        self.arrivals = [
            (ox, c, y, None),
            (x, c, oy, None),
            (ox, c, oy, 0),
            (ox, c, oy, 1),
            (x, oc, y, None),
            (ox, oc, y, None),
            (x, oc, oy, None),
            (ox, oc, oy, None),
        ]

    def _move(self, i):
        where, device, s = self.moves[i]
        return remote(self.slot(*where), self.slot(*where), self.send.at[s], self.recv.at[s], device)

    def _arrival(self, i):
        view = self.slot(*self.arrivals[i])
        return remote(view, view, self.send.at[i], self.recv.at[i], self.moves[i][1])

    def begin(self):
        self._move(0).start()
        self._move(1).start()
        self._move(4).start()

    def forward(self):
        self._arrival(0).wait_recv()
        self._move(2).start()
        self._move(5).start()
        self._arrival(1).wait_recv()
        self._move(3).start()
        self._move(6).start()

    def finish(self):
        self._arrival(2).wait_recv()
        self._arrival(3).wait_recv()
        self._move(7).start()

    def end(self):
        for i in range(4, 8):
            self._arrival(i).wait_recv()

    def sent(self):
        for i in range(8):
            self._move(i).wait_send()


def all_barrier(place, count):
    sem = pltpu.get_barrier_semaphore()
    me = place.dp * 2 + place.y

    @pl.loop(1, count)
    def _(j):
        other = lax.rem(me + j, count)
        signal(sem, (other // 2, lax.rem(other, 2)))

    pl.semaphore_wait(sem, count - 1)


def far_first(z, s, depth):
    b = 0
    for place in range(depth):
        order = sorted(range(depth), key=lambda k: (-abs(k - place), k))
        b = jnp.where(z == place, order[s], b)
    return b


class LineReduce:
    def __init__(self, place, depth, part, slots, send, recv):
        self.p, self.n, self.part, self.slots, self.send, self.recv = place, depth, part, slots, send, recv

    def _up(self, b):
        slot = b - (self.p.z + 1)
        return remote(self.part(b), self.slots(slot), self.send.at[b], self.recv.at[slot], self.p.up())

    def _down(self, b):
        slot = self.n - b
        return remote(self.part(b), self.slots(slot), self.send.at[b], self.recv.at[slot], self.p.down())

    def below(self, b):
        slot = b - self.p.z
        return remote(self.slots(slot), self.slots(slot), self.send.at[b], self.recv.at[slot], self.p.up())

    def above(self, b):
        slot = self.n - b
        return remote(self.slots(slot), self.slots(slot), self.send.at[b], self.recv.at[slot], self.p.down())

    def first(self, b):
        z = self.p.z

        @pl.when((z == 0) & (b > z))
        def _():
            self._up(b).start()

        @pl.when((z == self.n - 1) & (b < z))
        def _():
            self._down(b).start()

    def middle(self, b, add):
        z = self.p.z

        @pl.when((z > 0) & (b > z))
        def _():
            self.below(b).wait_recv()
            add(self.part(b), self.slots(b - z))
            self._up(b).start()

        @pl.when((z < self.n - 1) & (b < z))
        def _():
            self.above(b).wait_recv()
            add(self.part(b), self.slots(self.n - b))
            self._down(b).start()

    def last(self, take):
        z = self.p.z

        @pl.when(z > 0)
        def _():
            self.below(z).wait_recv()
            take(self.slots(0))

        @pl.when(z < self.n - 1)
        def _():
            self.above(z).wait_recv()
            take(self.slots(self.n - z))

    def sent(self):
        z = self.p.z

        @pl.loop(0, self.n)
        def _(b):
            @pl.when(b > z)
            def _():
                self._up(b).wait_send()

            @pl.when(b < z)
            def _():
                self._down(b).wait_send()


def add_low(part, other):
    part[...] = (part[...].astype(jnp.float32) + other[...].astype(jnp.float32)).astype(part.dtype)


def gelu_pair(x):
    a, b = 0.7978845608028654, 0.044715
    square = x * x
    t = jnp.tanh(a * x * (1.0 + b * square))
    half = 0.5 * (1.0 + t)
    return x * half, half + 0.5 * x * (1.0 - t * t) * (a * (1.0 + 3.0 * b * square))


NN = (((1,), (0,)), ((), ()))
NT = (((1,), (1,)), ((), ()))
TN = (((0,), (0,)), ((), ()))


def mm(left, right, form=NN):
    return lax.dot_general(left, right, form, preferred_element_type=jnp.float32)


def neighbour_barrier(p, depth):
    sem = pltpu.get_barrier_semaphore()
    for dx in range(2):
        for dc in range(2):
            for dy in range(2):
                if dx + dc + dy:
                    signal(sem, p.at(x=lax.rem(p.x + dx, 2), c=lax.rem(p.c + dc, 2), y=lax.rem(p.y + dy, 2)))

    @pl.loop(1, depth)
    def _(k):
        signal(sem, p.at(z=lax.rem(p.z + k, depth)))

    pl.semaphore_wait(sem, 7 + depth - 1)


def layer_norm(x, gain, shift):
    center = x - jnp.mean(x, axis=-1, keepdims=True)
    inverse = lax.rsqrt(jnp.mean(center * center, axis=-1, keepdims=True) + EPS)
    return center * inverse * gain + shift


def attend_pairs(q_ref, k_ref, v_ref, allowed, probs_ref, heads_ref, start, stop):
    rows = q_ref.shape[0]
    first = lax.broadcasted_iota(jnp.int32, (rows, 128), 1) < HEAD
    both = jnp.concatenate([allowed, allowed], axis=0)

    @pl.loop(start, stop)
    def _(h):
        at = (slice(None), pl.ds(pl.multiple_of(h * 128, 128), 128))
        q, k, v = q_ref[at], k_ref[at], v_ref[at]
        zero = jnp.zeros_like(q)
        pair = jnp.concatenate([jnp.where(first, q, zero), jnp.where(first, zero, q)], axis=0)
        scores = jnp.where(both, mm(pair, k, NT) * HEAD**-0.5, NEGATIVE)
        weights = jnp.exp(scores - jnp.max(scores, axis=-1, keepdims=True))
        probs = (weights * (1.0 / jnp.sum(weights, axis=-1, keepdims=True))).astype(jnp.bfloat16)
        probs_ref[h] = probs
        mix = mm(probs, v)
        heads_ref[at] = jnp.where(first, mix[:rows], mix[rows:]).astype(jnp.bfloat16)


Q, K, V, CQ, H1, H2, N1, N2, N3 = range(9)
CK, CV, ENC = range(3)


def forward_kernel(
    depth,
    proj, so, pairs_in, query, co, win, wout, vec, tok_in, enc_in, cot, target, source,
    G, act_out, ctx_out, mid_out, p1_out, p2_out, full_out, cot_out,
    d_out, y_out, go_out, gbias_out, S_out, YS_out,
    ATT, W, TOK, VEC, FULL, BIAS, ACT, CTX, MID, P1, P2, TARGET, SOURCE, OWN_T, OWN_E,
    HN, G3, WI, WO, S, RF, ACTIVE, SLOPE, BS, BR, CS, CR, CSY, CRY, PS, PR, DA, YA, DSUM, YSUM, GO, GB, LATS, LATR,
    lsem, wsem, osem, zs, zr, fs, fr, ps, pr, vs, vr, ss, sr, gs, gr, hs, hr, bs, br, cs, cr, ys, yr, xs, xr, us, ur,
):
    p = Place()
    z = p.z
    count = 8 * depth
    me = p.dp * 2 + p.y
    rows, width = ACT.shape[1:]
    short = CTX.shape[1]
    units = WO.shape[1]
    half, few = rows // 2, short // 2
    part = ATT.shape[1]
    mine = pl.ds(pl.multiple_of(p.y * few, few), few)
    local = []

    def keep(src, dst):
        copy = pltpu.make_async_copy(src, dst, lsem.at[len(local)])
        copy.start()
        local.append(copy)

    keep(vec, VEC.at[me])
    keep(tok_in, OWN_T)
    keep(enc_in, OWN_E)
    keep(proj, ATT.at[pl.ds(0, 3)])
    keep(so, ATT.at[3])
    keep(pairs_in, ATT.at[pl.ds(4, 2)])
    keep(query, ATT.at[6])
    keep(co, ATT.at[7])
    keep(cot, G3.at[p.x, p.c, :, p.y])
    keep(win, WI.at[:, pl.ds(pl.multiple_of(z * units, units), units)])
    keep(wout, WO.at[z])
    keep(target, TARGET)
    keep(source, SOURCE)
    BS[...] = jnp.zeros_like(BS)
    all_barrier(p, count)
    for copy in local:
        copy.wait()
    TOK[p.y] = OWN_T[p.y]
    CTX[ENC, mine] = OWN_E[p.y]
    own = pltpu.make_async_copy(ATT, G.at[:, p.y, z, p.x, p.c], lsem.at[0])
    own.start()

    lines = []
    for i in range(PIECES):
        lines.append(LineGather(p, depth, lambda b, i=i: G.at[i, p.y, b, p.x, p.c], zs.at[i], zr.at[i]))
    wr = WI.shape[0] // (FF_PIECES // 2)
    orow = units // (FF_PIECES // 2)
    ff = []
    for i in range(FF_PIECES):
        if i < FF_PIECES // 2:
            slot = lambda b, i=i: WI.at[pl.ds(i * wr, wr), pl.ds(pl.multiple_of(b * units, units), units)]
        else:
            slot = lambda b, i=i: WO.at[b, pl.ds((i - FF_PIECES // 2) * orow, orow)]
        ff.append(LineGather(p, depth, slot, fs.at[i], fr.at[i]))

    def plane_slot(i):
        def slot(x, c, y, h):
            if h is None:
                return G.at[i, y, :, x, c]
            return G.at[i, y, :, x, c, pl.ds(h * (part // 2), part // 2)]

        return slot

    def g3_slot(r):
        few_rows = G3.shape[4] // 2

        def slot(x, c, y, h):
            if h is None:
                return G3.at[x, c, r, y]
            return G3.at[x, c, r, y, pl.ds(h * few_rows, few_rows)]

        return slot

    slots = [g3_slot(0)] + [plane_slot(i) for i in range(PIECES)] + [g3_slot(1)]
    planes = [PlaneGather(p, slot, ps.at[i], pr.at[i]) for i, slot in enumerate(slots)]
    swaps = [
        remote(OWN_T.at[1 - p.y], TOK.at[p.y], ss.at[0], sr.at[0], p.yn()),
        remote(OWN_E.at[1 - p.y], CTX.at[ENC, mine], ss.at[1], sr.at[1], p.yn()),
    ]

    def swapped(i):
        if i == 0:
            view = TOK.at[1 - p.y]
        else:
            view = CTX.at[ENC, pl.ds(pl.multiple_of((1 - p.y) * few, few), few)]
        remote(view, view, ss.at[i], sr.at[i], p.yn()).wait_recv()

    swaps[0].start()

    def vec_move(j):
        other = lax.rem(me + j, count)
        return remote(VEC.at[me], VEC.at[me], vs.at[j], vr.at[j], (other // 2, lax.rem(other, 2)))

    @pl.loop(1, count)
    def _(j):
        vec_move(j).start()

    own.wait()

    saved = []

    def save(src, dst):
        copy = pltpu.make_async_copy(src, dst, osem.at[len(saved)])
        copy.start()
        saved.append(copy)

    def vector(i):
        return FULL[i : i + 1]

    def weight(i):
        copy = pltpu.make_async_copy(G.at[i], W, wsem.at[0])
        copy.start()
        copy.wait()

    def project(a, store):
        for y in range(2):
            store(y * (width // 2), mm(a, W[y].reshape(width, width // 2)))

    def project_back(a_ref):
        total = None
        for y in range(2):
            term = mm(a_ref[:, y * (width // 2) : (y + 1) * (width // 2)], W[y].reshape(width, width // 2), NT)
            total = term if total is None else total + term
        return total

    def into(ref, i):
        def store(at, value):
            ref[i, :, at : at + width // 2] = value.astype(jnp.bfloat16)

        return store

    def first_norm():
        @pl.loop(1, count)
        def _(j):
            other = lax.rem(me + count - j, count)
            remote(VEC.at[other], VEC.at[other], vs.at[j], vr.at[j], p.yn()).wait_recv()

        group = count * 128 // width
        for k in range(width // 128):
            piece = VEC[group * k, 0:8]
            for j in range(1, group):
                piece += VEC[group * k + j, 0:8]
            FULL[:, k * 128 : (k + 1) * 128] = piece
        save(FULL, full_out)
        for b in range(depth):
            held = VEC[((b * 2 + p.x) * 2 + p.c) * 2 + p.y]
            for k in range(units // 128):
                at = b * units + k * 128
                BIAS[:, at : at + 128] = jnp.broadcast_to(held[8 + k : 9 + k], (8, 128))
        swapped(0)
        tok = TOK[...].reshape(rows, width).astype(jnp.float32)
        MID[0] = tok
        ACT[N1] = layer_norm(tok, vector(0), vector(1)).astype(jnp.bfloat16)
        save(ACT.at[N1], act_out.at[N1])

    def qkv(i):
        weight(i)
        project(ACT[N1], into(ACT, (Q, K, V)[i]))
        save(ACT.at[(Q, K, V)[i]], act_out.at[(Q, K, V)[i]])

    def same(left, right):
        def pair(ref):
            row = ref[pl.ds(p.y, 1)].astype(jnp.float32)
            rest = jnp.zeros((14, row.shape[1]), jnp.float32)
            return jnp.concatenate([row, 1.0 - row, rest], axis=0).astype(jnp.bfloat16)

        return mm(pair(left), pair(right), TN) > 0.5

    pairs_of_heads = width // 128

    def self_attention(start, stop):
        back = lax.broadcasted_iota(jnp.int32, (rows, rows), 1) <= lax.broadcasted_iota(jnp.int32, (rows, rows), 0)
        attend_pairs(
            ACT.at[Q], ACT.at[K], ACT.at[V], same(TARGET, TARGET) & back, P1, ACT.at[H1], start, stop
        )

    def self_project():
        self_attention(pairs_of_heads // 2, pairs_of_heads)
        save(P1, p1_out)
        save(ACT.at[H1], act_out.at[H1])
        weight(3)
        middle = MID[0] + project_back(ACT.at[H1])
        MID[1] = middle
        ACT[N2] = layer_norm(middle, vector(2), vector(3)).astype(jnp.bfloat16)
        save(MID.at[pl.ds(0, 2)], mid_out.at[pl.ds(0, 2)])
        save(ACT.at[N2], act_out.at[N2])

    def pairs(i):
        if i == 0:
            swapped(1)
        weight(4 + i)
        project(CTX[ENC], into(CTX, (CK, CV)[i]))

    def cross_attention():
        save(CTX, ctx_out)
        weight(6)
        project(ACT[N2], into(ACT, CQ))
        save(ACT.at[CQ], act_out.at[CQ])
        attend_pairs(
            ACT.at[CQ], CTX.at[CK], CTX.at[CV], same(TARGET, SOURCE), P2, ACT.at[H2], 0, pairs_of_heads
        )
        save(P2, p2_out)
        save(ACT.at[H2], act_out.at[H2])

    def hn_slot(x, c, y, h):
        if h is None:
            return HN.at[x, c, y]
        return HN.at[x, c, y, pl.ds(h * half, half)]

    gather = PlaneGather(p, hn_slot, gs, gr)

    def cross_project():
        weight(7)
        latter = MID[1] + project_back(ACT.at[H2])
        HN[p.x, p.c, p.y] = layer_norm(latter, vector(4), vector(5)).astype(jnp.bfloat16)
        gather.begin()
        MID[2] = latter
        save(MID.at[2], mid_out.at[2])
        LATS[...] = MID[2, pl.ds(pl.multiple_of((1 - p.y) * half, half), half)].astype(jnp.bfloat16)

    work = {
        0: [functools.partial(qkv, 0)],
        1: [functools.partial(qkv, 1)],
        2: [functools.partial(qkv, 2), functools.partial(self_attention, 0, pairs_of_heads // 2)],
        3: [self_project],
        4: [functools.partial(pairs, 0)],
        5: [functools.partial(pairs, 1)],
        6: [cross_attention],
        7: [cross_project],
    }
    lead = depth - 2
    turns = 2 * (lead + len(planes) + 3)
    early, late = 2 * lead, 2 * lead + 2 * PIECES - 2
    starts = list(range(early)) + list(range(early, late, 3))
    starts += list(range(late, late + FF_PIECES - len(starts)))

    def turn(n):
        for f in range(FF_PIECES):
            k = n - starts[f]
            if k % 2 == 0 and 0 <= k < 2 * depth:
                ff[f].step(k // 2)

    for it in range(-lead, len(planes) + 3):
        for i in range(PIECES):
            if 0 <= it - i + lead < depth:
                lines[i].step(it - i + lead)
        if 0 <= it < len(planes):
            planes[it].begin()
        turn(2 * (it + lead))
        if it == 0:
            swaps[1].start()
        if 0 <= it - 1 < len(planes):
            planes[it - 1].forward()
        if 0 <= it - 2 < len(planes):
            planes[it - 2].finish()
        turn(2 * (it + lead) + 1)
        if 0 <= it - 3 < len(planes):
            planes[it - 3].end()
        if it == 1:
            first_norm()
        for task in work.get(it - 4, []):
            task()

    def bits(code):
        dc, dx, dy = code // 4, lax.rem(code // 2, 2), lax.rem(code, 2)
        return lax.rem(p.x + dx, 2), lax.rem(p.c + dc, 2), lax.rem(p.y + dy, 2)

    arriving = (0, 4, 1, 2, 5, 6, 3, 7)
    leaving = (7, 6, 3, 5, 2, 1, 4, 0)
    for_core = (1, 1, 0, 1, 0, 0, 1, 0)
    turn_of = (0, 1, 0, 2, 1, 2, 3, 3)

    def pick(i, table):
        value = table[0]
        for k in range(1, 8):
            value = jnp.where(i == k, table[k], value)
        return value

    def to_core(j, send, land, a, b):
        return remote(send.at[j], land.at[j], a.at[j], b.at[j], p.core())

    def to_chip(j):
        dx, dy = 1 - j // 2, 1 - lax.rem(j, 2)
        return remote(
            PS.at[j], PR.at[j], xs.at[j], xr.at[j], p.at(x=lax.rem(p.x + dx, 2), y=lax.rem(p.y + dy, 2))
        )

    def diagonal(src, land, n, h):
        return remote(
            src.at[0, pl.ds(h * half, half)], land.at[h], us.at[n, h], ur.at[n, h], p.yn() if h else p.xn()
        )

    def merge(parts, land, n):
        diagonal(parts, land, n, 0).wait_recv()
        add_low(parts.at[2, pl.ds(0, half)], land.at[0])
        diagonal(parts, land, n, 1).wait_recv()
        add_low(parts.at[1, pl.ds(half, half)], land.at[1])

    latter_move = remote(LATS, LATR, ss.at[2], sr.at[2], p.yn())

    def bias_move(b):
        return remote(BS.at[b], BR.at[z], bs.at[b], br.at[z], p.at(z=b))

    def up(h):
        return remote(S.at[depth - 1, h], RF.at[h], hs.at[h], hr.at[h], p.up())

    def down(h):
        return remote(S.at[0, h], RF.at[h], hs.at[h], hr.at[h], p.down())

    def hop(s, h):
        @pl.when(jnp.logical_and(s == 0, z == 0))
        def _():
            up(h).start()

        @pl.when(jnp.logical_and(s == 0, z == depth - 1))
        def _():
            down(h).start()


    @pl.loop(0, 8)
    def _(i):
        @pl.when(i == 1)
        def _():
            gather._arrival(4).wait_recv()

        @pl.when(i == 2)
        def _():
            gather.forward()

        @pl.when(i == 4)
        def _():
            gather._arrival(5).wait_recv()
            gather._arrival(6).wait_recv()

        @pl.when(i == 6)
        def _():
            gather.finish()

        @pl.when(i == 7)
        def _():
            gather._arrival(7).wait_recv()

        at = bits(pick(i, arriving))
        before = mm(HN[at], WI[...]) + BIAS[0:1]
        active, slope = gelu_pair(before)
        ACTIVE[at] = active.astype(jnp.bfloat16)
        SLOPE[at] = slope.astype(jnp.bfloat16)

    def block(s):
        b = far_first(z, 0, depth)
        for k in range(1, depth):
            b = jnp.where(s == k, far_first(z, k, depth), b)
        return b, pl.ds(pl.multiple_of(b * units, units), units)

    def out_sums(s):
        b, cols = block(s)
        gout = mm(ACTIVE[:, :, :, :, cols].reshape(8 * rows, units), G3[...].reshape(8 * rows, width), TN)
        GO[1] = gout
        S[b, 1] = gout.astype(jnp.bfloat16)
        hop(s, 1)

    out_sums(0)
    for n in range(turns, max(starts) + 2 * depth):
        turn(n)

    @pl.loop(0, 8)
    def _(i):
        at = bits(pick(i, leaving))
        slope = mm(G3[at].reshape(rows, width), WO[...].reshape(depth * units, width), NT)
        slope = (slope * SLOPE[at].astype(jnp.float32)).astype(jnp.bfloat16)
        SLOPE[at] = slope
        total = jnp.sum(slope.astype(jnp.float32), axis=0, keepdims=True)
        for b in range(depth):
            BS[b, 0:1] += total[:, b * units : (b + 1) * units]
        back = mm(slope, WI[...], NT)
        j = pick(i, turn_of)

        @pl.when(pick(i, for_core) == 1)
        def _():
            CS[j] = back.astype(jnp.bfloat16)
            to_core(j, CS, CR, cs, cr).start()

        @pl.when(pick(i, for_core) == 0)
        def _():
            to_core(j, CS, CR, cs, cr).wait_recv()
            total = back + CR[j].astype(jnp.float32)

            @pl.when(j < 3)
            def _():
                PS[j] = total.astype(jnp.bfloat16)

            @pl.when(j == 0)
            def _():
                diagonal(PS, DA, 0, 0).start()
                diagonal(PS, DA, 0, 1).start()

            @pl.when(j == 3)
            def _():
                DSUM[...] = total

        @pl.when(i == 6)
        def _():
            merge(PS, DA, 0)
            to_chip(1).start()
            to_chip(2).start()

    @pl.loop(1, depth)
    def _(k):
        bias_move(lax.rem(z + k, depth)).start()

    def in_sums(s):
        b, cols = block(s)
        gin = mm(SLOPE[:, :, :, :, cols].reshape(8 * rows, units), HN[...].reshape(8 * rows, width), TN)
        GO[0] = gin
        S[b, 0] = gin.astype(jnp.bfloat16)
        hop(s, 0)


    in_sums(0)
    latter_move.start()

    @pl.loop(0, 8)
    def _(i):
        ox, oc, oh = bits(pick(i, leaving))
        active = ACTIVE[ox, oc, :, pl.ds(pl.multiple_of(oh * half, half), half)].reshape(rows, depth * units)
        more = mm(active, WO[...].reshape(depth * units, width))

        j = pick(i, turn_of)

        @pl.when(pick(i, for_core) == 1)
        def _():
            CSY[j] = more.astype(jnp.bfloat16)
            to_core(j, CSY, CRY, ys, yr).start()

        @pl.when(pick(i, for_core) == 0)
        def _():
            to_core(j, CSY, CRY, ys, yr).wait()
            total = more + CRY[j].astype(jnp.float32)

            @pl.when(j < 3)
            def _():
                CSY[j] = total.astype(jnp.bfloat16)

            @pl.when(j == 0)
            def _():
                diagonal(CSY, YA, 1, 0).start()
                diagonal(CSY, YA, 1, 1).start()

            @pl.when(j == 3)
            def _():
                YSUM[...] = total.reshape(2, half, width)

    @pl.loop(1, depth)
    def _(s):
        in_sums(s)
        out_sums(s)

    save(GO, go_out)
    save(G3.at[p.x, p.c, p.y], cot_out)

    GB[...] = BS[z]

    @pl.loop(1, depth)
    def _(k):
        other = lax.rem(z + k, depth)
        remote(BS.at[other], BR.at[other], bs.at[other], br.at[other], p.at(z=other)).wait()
        GB[...] += BR[other]

    save(GB, gbias_out)

    @pl.loop(1, 3)
    def _(j):
        to_chip(j).wait_recv()
        DSUM[...] += PR[j].astype(jnp.float32)

    save(DSUM, d_out)

    @pl.when((z == 1) | (z == depth - 2))
    def _():
        far = jnp.where(z == 1, depth - 1, 0)
        for h in range(2):
            up(h).wait_recv()
            add_low(S.at[far, h], RF.at[h])

    save(S, S_out)
    latter_move.wait()
    YSUM[p.y] += MID[2, pl.ds(pl.multiple_of(p.y * half, half), half)] + vector(6)
    YSUM[1 - p.y] += LATR[...].astype(jnp.float32) + vector(6)

    merge(CSY, YA, 1)
    save(CSY.at[pl.ds(1, 2)], YS_out)
    save(YSUM, y_out)

    @pl.when((z == 0) | (z == depth - 1))
    def _():
        for h in range(2):
            up(h).wait_send()

    for line in lines + ff:
        line.sent()
    for plane in planes + [gather]:
        plane.sent()
    for copy in swaps:
        copy.wait_send()

    @pl.loop(1, count)
    def _(j):
        vec_move(j).wait_send()

    @pl.loop(0, 4)
    def _(j):
        to_core(j, CS, CR, cs, cr).wait_send()

    @pl.loop(1, 3)
    def _(j):
        to_chip(j).wait_send()

    for h in range(2):
        diagonal(PS, DA, 0, h).wait_send()
        diagonal(CSY, YA, 1, h).wait_send()

    for copy in saved:
        copy.wait()


def forward_all(proj, so, pairs, query, co, win, wout, vec, tok, enc, cot, target, source):
    depth = lax.axis_size("dp") // 4
    rows, cols = query.shape
    bf, f32 = jnp.bfloat16, jnp.float32
    count = 8 * depth
    length, short, d = 2 * tok.shape[1], 2 * enc.shape[1], tok.shape[2]
    units = wout.shape[0]
    heads = d // 128
    whole = (2, depth, 2, 2, rows, cols)
    shapes = {
        "G": ((PIECES,) + whole, bf),
        "ACT": ((9, length, d), bf),
        "CTX": ((3, short, d), bf),
        "MID": ((3, length, d), f32),
        "P1": ((heads, 2 * length, length), bf),
        "P2": ((heads, 2 * length, short), bf),
        "FULL": ((8, d), f32),
        "COT": (cot.shape, bf),
        "DSUM": ((length, d), f32),
        "YSUM": ((2, length // 2, d), f32),
        "GO": ((2, units, d), f32),
        "GB": ((8, units), f32),
        "S": ((depth, 2, units, d), bf),
        "YS": ((2, length, d), bf),
    }
    outs = [jax.ShapeDtypeStruct(*shape) for shape in shapes.values()]

    def held(name):
        return pltpu.VMEM(*shapes[name])

    dma = pltpu.SemaphoreType.DMA
    hb = pl.BlockSpec(memory_space=HBM)
    tokens = (2, 2, 2, length, d)
    four = pltpu.VMEM((4, length, d), bf)
    three = pltpu.VMEM((3, length, d), bf)
    scratch = [
        pltpu.VMEM((PIECES, rows, cols), bf),
        pltpu.VMEM(whole, bf),
        pltpu.VMEM(tok.shape, bf),
        pltpu.VMEM((count,) + vec.shape, f32),
        held("FULL"),
        pltpu.VMEM((8, depth * units), f32),
        held("ACT"), held("CTX"), held("MID"), held("P1"), held("P2"),
        pltpu.VMEM(target.shape, jnp.int32), pltpu.VMEM(source.shape, jnp.int32),
        pltpu.VMEM(tok.shape, bf), pltpu.VMEM(enc.shape, bf),
        pltpu.VMEM(tokens, bf),
        pltpu.VMEM((2, 2, 2, 2) + cot.shape[1:], bf),
        pltpu.VMEM((d, depth * units), bf),
        pltpu.VMEM((depth, units, d), bf),
        held("S"),
        pltpu.VMEM((2, units, d), bf),
        pltpu.VMEM(tokens[:4] + (depth * units,), bf),
        pltpu.VMEM(tokens[:4] + (depth * units,), bf),
        pltpu.VMEM((depth, 8, units), f32),
        pltpu.VMEM((depth, 8, units), f32),
        four, four, four, four, three, three,
        pltpu.VMEM((2, length // 2, d), bf), pltpu.VMEM((2, length // 2, d), bf),
        held("DSUM"), held("YSUM"), held("GO"), held("GB"),
        pltpu.VMEM((length // 2, d), bf), pltpu.VMEM((length // 2, d), bf),
        dma((13,)), dma((1,)), dma((24,)),
        dma((PIECES, 2, depth - 1)), dma((PIECES, 2, depth - 1)),
        dma((FF_PIECES, 2, depth - 1)), dma((FF_PIECES, 2, depth - 1)),
        dma((PIECES + 2, 8)), dma((PIECES + 2, 8)),
        dma((count,)), dma((count,)),
        dma((3,)), dma((3,)),
        dma((8,)), dma((8,)),
        dma((2,)), dma((2,)),
        dma((depth,)), dma((depth,)),
        dma((4,)), dma((4,)),
        dma((4,)), dma((4,)),
        dma((3,)), dma((3,)),
        dma((2, 2)), dma((2, 2)),
    ]
    return pl.pallas_call(
        functools.partial(forward_kernel, depth),
        out_shape=outs,
        in_specs=[hb] * 13,
        out_specs=[hb] * len(outs),
        scratch_shapes=scratch,
        compiler_params=pltpu.CompilerParams(
            collective_id=1, has_side_effects=True, vmem_limit_bytes=63 << 20
        ),
        name="forward_all",
    )(proj, so, pairs, query, co, win, wout, vec, tok, enc, cot, target, source)


def norm_back(e, h, gain):
    center = h - jnp.mean(h, axis=-1, keepdims=True)
    inverse = lax.rsqrt(jnp.mean(center * center, axis=-1, keepdims=True) + EPS)
    normal = center * inverse
    scaled = e * gain
    back = inverse * (
        scaled
        - jnp.mean(scaled, axis=-1, keepdims=True)
        - normal * jnp.mean(scaled * normal, axis=-1, keepdims=True)
    )
    return back, jnp.sum(e * normal, axis=0, keepdims=True), jnp.sum(e, axis=0, keepdims=True)


def attend_pairs_back(q_ref, k_ref, v_ref, probs_ref, slope_ref, dq_ref, dk_ref, dv_ref, start, stop):
    rows = q_ref.shape[0]
    first = lax.broadcasted_iota(jnp.int32, (rows, 128), 1) < HEAD

    def stacked(a):
        zero = jnp.zeros_like(a)
        return jnp.concatenate([jnp.where(first, a, zero), jnp.where(first, zero, a)], axis=0)

    @pl.loop(start, stop)
    def _(h):
        at = (slice(None), pl.ds(pl.multiple_of(h * 128, 128), 128))
        up = stacked(slope_ref[at])
        low = probs_ref[h]
        probs = low.astype(jnp.float32)
        dprobs = mm(up, v_ref[at], NT)
        ds = (probs * (dprobs - jnp.sum(probs * dprobs, axis=-1, keepdims=True))).astype(jnp.bfloat16)
        dq = mm(ds, k_ref[at]) * HEAD**-0.5
        dq_ref[at] = jnp.where(first, dq[:rows], dq[rows:]).astype(jnp.bfloat16)
        dk_ref[at] = (mm(ds, stacked(q_ref[at]), TN) * HEAD**-0.5).astype(jnp.bfloat16)
        dv_ref[at] = mm(low, up, TN).astype(jnp.bfloat16)


class HoppedReduce(LineReduce):
    def _down(self, b):
        slot = self.n - 2 + self.p.z - 1 - b
        return remote(self.part(b), self.slots(slot), self.send.at[b], self.recv.at[slot], self.p.down())

    def above(self, b):
        slot = self.n - 2 + self.p.z - b
        return remote(self.slots(slot), self.slots(slot), self.send.at[b], self.recv.at[slot], self.p.down())

    def first(self, b):
        z, n = self.p.z, self.n

        @pl.when((b > z) & (((z == 0) & (b < n - 1)) | ((z == 1) & (b == n - 1))))
        def _():
            self._up(b).start()

        @pl.when((b < z) & (((z == n - 1) & (b > 0)) | ((z == n - 2) & (b == 0))))
        def _():
            self._down(b).start()

    def middle(self, b, add):
        z, n = self.p.z, self.n

        @pl.when((z > 0) & (b > z) & ((z > 1) | (b < n - 1)))
        def _():
            self.below(b).wait_recv()
            add(self.part(b), self.slots(b - z))
            self._up(b).start()

        @pl.when((z < n - 1) & (b < z) & ((z < n - 2) | (b > 0)))
        def _():
            self.above(b).wait_recv()
            add(self.part(b), self.slots(n - 2 + z - b))
            self._down(b).start()

    def last(self, take):
        z, n = self.p.z, self.n

        @pl.when(z > 0)
        def _():
            self.below(z).wait_recv()
            take(self.slots(0))

        @pl.when(z < n - 1)
        def _():
            self.above(z).wait_recv()
            take(self.slots(n - 2))

    def sent(self):
        z, n = self.p.z, self.n

        @pl.loop(0, n)
        def _(b):
            @pl.when((b > z) & ((z > 0) | (b < n - 1)))
            def _():
                self._up(b).wait_send()

            @pl.when((b < z) & ((z < n - 1) | (b > 0)))
            def _():
                self._down(b).wait_send()


SLOTS = 4
FF_PARTS = 16
FF_GAP = 1


def backward_kernel(
    depth,
    G, act, ctx, mid, p1, p2, full, cot_in, d_in, y_in, go_in, S_in, YS_in,
    gw_hbm, vec_hbm, res_hbm, tg_hbm, eg_hbm, go_hbm,
    gw_out, vec_out, res_out, tg_out, eg_out, go_out,
    MY, SEND, CR, PD, PR, R, S, RF, YS, YR, W, ACT, CTX, X, PB1, PB2, UP, LOW, SL, DH, DC, COT, FULL, VG, VR, XS, XR, ES, ER,
    lsem, wsem, cs, cr, ds, dr, ps, pr, zs, zr, fs, fr, ys, yr, vs, vr, ss, sr, osem, credit,
):
    p = Place()
    count = 8 * depth
    me = p.dp * 2 + p.y
    ox, oy = 1 - p.x, 1 - p.y
    rows, width = UP.shape
    short = CTX.shape[1]
    cols = width // 2
    part = MY.shape[4]
    low_type = jnp.bfloat16

    def load(i, src, dst):
        copy = pltpu.make_async_copy(src, dst, lsem.at[i])
        copy.start()
        return copy

    loads = [
        load(0, mid.at[2], X),
        load(1, d_in, UP),
        load(2, cot_in, COT),
        load(3, full, FULL),
        load(4, act.at[pl.ds(0, 8)], ACT),
        load(5, ctx, CTX),
        load(6, p2, PB2),
        load(7, S_in, S),
        load(8, go_in, go_out),
        load(9, p1, PB1),
        load(10, YS_in, YS),
        load(11, y_in, res_out),
    ]
    order = (7, 6, 3, 0, 1, 2, 4, 5)

    def weight(n):
        return pltpu.make_async_copy(G.at[order[n]], W.at[n % 2], wsem.at[n % 2])

    def use(n):
        weight(n).wait()
        if n + 1 < len(order):
            weight(n + 1).start()
        return [W[n % 2, y].reshape(width, cols) for y in range(2)]

    weight(0).start()
    VG[...] = jnp.zeros_like(VG)
    all_barrier(p, count)

    def y_move(j):
        return remote(YS.at[j], YR.at[j], ys.at[j], yr.at[j], p.yn() if j else p.xn())

    loads[10].wait()
    for j in range(2):
        y_move(j).start()

    def core(i):
        return remote(SEND.at[i % 2], CR.at[i % SLOTS], cs.at[i], cr.at[i], p.core())

    def cut(i, h):
        by_x = part // 2
        return pl.ds(by_x, part - by_x) if h else pl.ds(0, by_x)

    def diagonal(i, h):
        return remote(
            MY.at[i, oy, :, ox, cut(i, h)], PD.at[i, :, cut(i, h)], ds.at[i, h], dr.at[i, h],
            p.yn() if h else p.xn(),
        )

    def column(i, h):
        view = MY.at[i, oy, :, p.x] if h else MY.at[i, p.y, :, ox]
        return remote(view, PR.at[i, h], ps.at[i, h], pr.at[i, h], p.yn() if h else p.xn())

    lines = [
        LineReduce(
            p, depth, lambda b, i=i: MY.at[i, p.y, b, p.x], lambda k, i=i: R.at[i, k], zs.at[i], zr.at[i]
        )
        for i in range(PIECES)
    ]
    frows = S.shape[2] // (FF_PARTS // 2)
    ff = []
    for f in range(FF_PARTS):
        at = pl.ds(f // 2 * frows, frows)
        ff.append(
            HoppedReduce(
                p, depth, lambda b, f=f, at=at: S.at[b, f % 2, at], lambda k, f=f, at=at: RF.at[k, f % 2, at],
                fs.at[f], fr.at[f],
            )
        )

    def store_part(i, left, right):
        if i >= 2:
            core(i - 2).wait_send()
        for y in range(2):
            value = mm(left, right[:, y * cols : (y + 1) * cols], TN).reshape(depth, 2, 2, part, cols)
            value = value.astype(low_type)
            even, odd = value[:, :, 0], value[:, :, 1]
            MY[i, y] = jnp.where(p.c == 0, even, odd)
            SEND[i % 2, y] = jnp.where(p.c == 0, odd, even)
        if i >= SLOTS:
            pl.semaphore_wait(credit, 1)
        core(i).start()

    def stage(i, s):
        if s == 1:
            core(i).wait_recv()
            add_low(MY.at[i], CR.at[i % SLOTS])
            if i + SLOTS < PIECES:
                signal(credit, p.core())
            diagonal(i, 0).start()
            diagonal(i, 1).start()
        elif s == 2:
            diagonal(i, 0).wait_recv()
            add_low(MY.at[i, oy, :, p.x, cut(i, 0)], PD.at[i, :, cut(i, 0)])
            column(i, 1).start()
            diagonal(i, 1).wait_recv()
            add_low(MY.at[i, p.y, :, ox, cut(i, 1)], PD.at[i, :, cut(i, 1)])
            column(i, 0).start()
        elif s == 3:
            column(i, 0).wait_recv()
            column(i, 1).wait_recv()
            view = MY.at[i, p.y, :, p.x]
            view[...] = (
                view[...].astype(jnp.float32)
                + PR[i, 0].astype(jnp.float32)
                + PR[i, 1].astype(jnp.float32)
            ).astype(low_type)
            for k in range(depth - 1):
                lines[i].first(far_first(p.z, k, depth))
        elif s < 3 + depth:
            lines[i].middle(far_first(p.z, s - 4, depth), add_low)
        elif s == 3 + depth:
            gw_out[i] = MY[i, p.y, p.z, p.x].astype(jnp.float32)

            def take(slot):
                gw_out[i] += slot[...].astype(jnp.float32)

            lines[i].last(take)

    def ff_stage(f, s):
        if s == 0:
            for k in range(depth - 1):
                ff[f].first(far_first(p.z, k, depth))
        elif s < depth:
            ff[f].middle(far_first(p.z, s - 1, depth), add_low)
        else:
            at = pl.ds(f // 2 * frows, frows)

            def take(slot):
                go_out[f % 2, at] += slot[...].astype(jnp.float32)

            ff[f].last(take)

    clock = [0]

    def tick(*stages):
        n = clock[0]
        clock[0] += 1
        if n == 0:
            loads[7].wait()
            loads[8].wait()
        for f in range(FF_PARTS):
            if (n - f) % FF_GAP == 0 and 0 <= (n - f) // FF_GAP <= depth:
                ff_stage(f, (n - f) // FF_GAP)
        for i, s in stages:
            stage(i, s)

    def gain(i):
        return FULL[i : i + 1]

    def spread(i, values):
        VG[i : i + 1] = values

    tick()
    for i in (0, 1, 2, 3):
        loads[i].wait()
    cot = COT[...].reshape(rows, width).astype(jnp.float32)
    latter = X[...]
    back, g_gain, g_shift = norm_back(UP[...], latter, gain(4))
    spread(4, g_gain)
    spread(5, g_shift)
    spread(6, jnp.sum(cot, axis=0, keepdims=True))
    UP[...] = cot + back
    LOW[...] = UP[...].astype(low_type)
    next_mid = load(0, mid.at[1], X)
    w = use(0)
    for y in range(2):
        SL[:, y * cols : (y + 1) * cols] = mm(LOW[...], w[y]).astype(low_type)
    loads[4].wait()
    store_part(0, LOW[...], ACT[H2])
    tick()
    loads[5].wait()
    loads[6].wait()
    attend_pairs_back(
        ACT.at[CQ], CTX.at[CK], CTX.at[CV], PB2, SL, DH.at[0], DC.at[0], DC.at[1], 0, width // 128
    )
    store_part(1, ACT[N2], DH[0])
    tick((0, 1))
    w = use(1)
    slope = mm(DH[0, :, :cols], w[0], NT) + mm(DH[0, :, cols:], w[1], NT)
    next_mid.wait()
    back, g_gain, g_shift = norm_back(slope, X[...], gain(2))
    spread(2, g_gain)
    spread(3, g_shift)
    UP[...] += back
    LOW[...] = UP[...].astype(low_type)
    next_mid = load(0, mid.at[0], X)
    store_part(2, CTX[ENC], DC[0])
    tick((1, 1))
    store_part(3, CTX[ENC], DC[1])
    tick((2, 1))
    w = use(2)
    for y in range(2):
        SL[:, y * cols : (y + 1) * cols] = mm(LOW[...], w[y]).astype(low_type)
    store_part(4, LOW[...], ACT[H1])
    tick((3, 1), (0, 2))
    loads[9].wait()
    attend_pairs_back(
        ACT.at[Q], ACT.at[K], ACT.at[V], PB1, SL, DH.at[0], DH.at[1], DH.at[2], 0, width // 256
    )
    tick((4, 1), (1, 2))
    attend_pairs_back(
        ACT.at[Q], ACT.at[K], ACT.at[V], PB1, SL, DH.at[0], DH.at[1], DH.at[2], width // 256, width // 128
    )
    store_part(5, ACT[N1], DH[0])
    tick((0, 3), (2, 2))
    store_part(6, ACT[N1], DH[1])
    tick((5, 1), (1, 3), (3, 2), (0, 4))
    store_part(7, ACT[N1], DH[2])
    tick((6, 1), (2, 3), (4, 2), (1, 4), (0, 5))
    slope = None
    for i in range(3):
        w = use(3 + i)
        term = mm(DH[i, :, :cols], w[0], NT) + mm(DH[i, :, cols:], w[1], NT)
        slope = term if slope is None else slope + term
    tick((7, 1), (3, 3), (5, 2), (2, 4), (1, 5), (0, 6))
    next_mid.wait()
    back, g_gain, g_shift = norm_back(slope, X[...], gain(0))
    spread(0, g_gain)
    spread(1, g_shift)
    back += UP[...]
    for h in range(2):
        tg_out[h] = back[h * (rows // 2) : (h + 1) * (rows // 2)]

    def vec_move(j):
        other = lax.rem(me + j, count)
        at = pl.ds(pl.multiple_of(other * (width // count) // 128 * 128, 128), 128)
        return remote(VG.at[:, at], VR.at[j], vs.at[j], vr.at[j], (other // 2, lax.rem(other, 2)))

    @pl.loop(1, count)
    def _(j):
        vec_move(j).start()

    tick((6, 2), (4, 3), (3, 4), (2, 5), (1, 6), (0, 7))
    slope = None
    for i in range(2):
        w = use(6 + i)
        term = mm(DC[i, :, :cols], w[0], NT) + mm(DC[i, :, cols:], w[1], NT)
        slope = term if slope is None else slope + term
    for h in range(2):
        eg_out[h] = slope[h * (short // 2) : (h + 1) * (short // 2)]
    stores = []

    def store(src, dst):
        copy = pltpu.make_async_copy(src, dst, osem.at[len(stores)])
        copy.start()
        stores.append(copy)

    XS[...] = tg_out[oy].astype(low_type)
    loads[11].wait()
    for j in range(2):
        y_move(j).wait_recv()
        res_out[...] += YR[j].astype(jnp.float32).reshape(res_out.shape)
    ES[...] = eg_out[oy].astype(low_type)
    store(res_out, res_hbm)
    swaps = [
        remote(XS, XR, ss.at[0], sr.at[0], p.yn()),
        remote(ES, ER, ss.at[1], sr.at[1], p.yn()),
    ]
    tick((7, 2), (5, 3), (4, 4), (3, 5), (2, 6), (1, 7))
    for copy in swaps:
        copy.start()
    tick((6, 3), (5, 4), (4, 5), (3, 6), (2, 7))
    tick((7, 3), (6, 4), (5, 5), (4, 6), (3, 7))
    tick((7, 4), (6, 5), (5, 6), (4, 7))
    tick((7, 5), (6, 6), (5, 7))
    tick((7, 6), (6, 7))
    tick((7, 7))
    while clock[0] < FF_PARTS + FF_GAP * depth + 1:
        tick()
    store(gw_out, gw_hbm)
    store(go_out, go_hbm)
    at = pl.ds(pl.multiple_of(me * (width // count) // 128 * 128, 128), 128)
    vec_out[...] = VG[:, at]

    @pl.loop(1, count)
    def _(j):
        vec_move(j).wait()
        vec_out[...] += VR[j]

    store(vec_out, vec_hbm)

    for copy in swaps:
        copy.wait()
    tg_out[oy] = XR[...].astype(jnp.float32)
    eg_out[oy] = ER[...].astype(jnp.float32)
    store(tg_out, tg_hbm)
    store(eg_out, eg_hbm)
    for i in range(PIECES):
        if i >= PIECES - 2:
            core(i).wait_send()
        for h in range(2):
            diagonal(i, h).wait_send()
            column(i, h).wait_send()
        lines[i].sent()
    for line in ff:
        line.sent()
    for j in range(2):
        y_move(j).wait_send()
    for copy in stores:
        copy.wait()


def backward_all(G, act, ctx, mid, p1, p2, full, cot, d_in, y_in, go_in, S_in, YS_in):
    depth = G.shape[2]
    count = 8 * depth
    rows, cols = G.shape[5:]
    length, width = d_in.shape
    short = ctx.shape[1]
    bf, f32 = jnp.bfloat16, jnp.float32
    dma = pltpu.SemaphoreType.DMA
    hb = pl.BlockSpec(memory_space=HBM)
    outs = [
            jax.ShapeDtypeStruct((PIECES, rows, cols), f32),
            jax.ShapeDtypeStruct((8, 128), f32),
            jax.ShapeDtypeStruct((2, length // 2, width), f32),
            jax.ShapeDtypeStruct((2, length // 2, width), f32),
            jax.ShapeDtypeStruct((2, short // 2, width), f32),
            jax.ShapeDtypeStruct(go_in.shape, f32),
    ]
    return pl.pallas_call(
        functools.partial(backward_kernel, depth),
        out_shape=outs,
        in_specs=[hb] * 13,
        out_specs=[hb] * 6,
        scratch_shapes=[pltpu.VMEM(o.shape, o.dtype) for o in outs] + [
            pltpu.VMEM((PIECES, 2, depth, 2, rows, cols), bf),
            pltpu.VMEM((2, 2, depth, 2, rows, cols), bf),
            pltpu.VMEM((SLOTS, 2, depth, 2, rows, cols), bf),
            pltpu.VMEM((PIECES, depth, rows, cols), bf),
            pltpu.VMEM((PIECES, 2, depth, rows, cols), bf),
            pltpu.VMEM((PIECES, depth + 1, rows, cols), bf),
            pltpu.VMEM(S_in.shape, bf),
            pltpu.VMEM((2 * depth - 4,) + S_in.shape[1:], bf),
            pltpu.VMEM(YS_in.shape, bf),
            pltpu.VMEM(YS_in.shape, bf),
            pltpu.VMEM((2,) + G.shape[1:], bf),
            pltpu.VMEM((8, length, width), bf),
            pltpu.VMEM(ctx.shape, bf),
            pltpu.VMEM((length, width), f32),
            pltpu.VMEM(p1.shape, bf),
            pltpu.VMEM(p2.shape, bf),
            pltpu.VMEM((length, width), f32),
            pltpu.VMEM((length, width), bf),
            pltpu.VMEM((length, width), bf),
            pltpu.VMEM((3, length, width), bf),
            pltpu.VMEM((2, short, width), bf),
            pltpu.VMEM((2, length // 2, width), bf),
            pltpu.VMEM((8, width), f32),
            pltpu.VMEM((8, width), f32),
            pltpu.VMEM((count, 8, 128), f32),
            pltpu.VMEM((length // 2, width), bf),
            pltpu.VMEM((length // 2, width), bf),
            pltpu.VMEM((short // 2, width), bf),
            pltpu.VMEM((short // 2, width), bf),
            dma((12,)), dma((2,)),
            dma((PIECES,)), dma((PIECES,)),
            dma((PIECES, 2)), dma((PIECES, 2)),
            dma((PIECES, 2)), dma((PIECES, 2)),
            dma((PIECES, depth)), dma((PIECES, depth + 1)),
            dma((FF_PARTS, depth)), dma((FF_PARTS, 2 * depth - 4)),
            dma((2,)), dma((2,)),
            dma((count,)), dma((count,)),
            dma((2,)), dma((2,)),
            dma((6,)),
            pltpu.SemaphoreType.REGULAR,
        ],
        compiler_params=pltpu.CompilerParams(
            collective_id=3, has_side_effects=True, vmem_limit_bytes=63 << 20
        ),
        name="backward_all",
    )(G, act, ctx, mid, p1, p2, full, cot, d_in, y_in, go_in, S_in, YS_in)


def finish_kernel(gw, res, tg, eg, go, res_out, tg_out, eg_out, proj_out, so_out, query_out, co_out, in_out, out_out, A, B, lsem, osem):
    moves = []

    def load(src, dst):
        copy = pltpu.make_async_copy(src, dst, lsem.at[len(moves)])
        copy.start()
        moves.append(copy)

    IN, RES, TG, EG, GW, OUT = A
    load(go.at[0], IN)
    load(res, RES)
    load(tg, TG)
    load(gw, GW)
    load(go.at[1], OUT)
    load(eg, EG)
    done = []

    def store(src, dst):
        copy = pltpu.make_async_copy(src, dst, osem.at[len(done)])
        copy.start()
        done.append(copy)

    moves[0].wait()
    B[...] = IN[...].T
    store(B, in_out)
    moves[1].wait()
    store(RES, res_out)
    moves[2].wait()
    store(TG, tg_out)
    moves[3].wait()
    store(GW.at[pl.ds(5, 3)], proj_out)
    store(GW.at[4], so_out)
    store(GW.at[1], query_out)
    store(GW.at[0], co_out)
    moves[4].wait()
    store(OUT, out_out)
    moves[5].wait()
    store(EG, eg_out)
    for copy in done:
        copy.wait()


def finish(gw, res, tg, eg, go):
    f32 = jnp.float32
    rows, cols = gw.shape[1:]
    units, width = go.shape[1:]
    one = jax.ShapeDtypeStruct((rows, cols), f32)
    hb = pl.BlockSpec(memory_space=HBM)
    return pl.pallas_call(
        finish_kernel,
        out_shape=[
            jax.ShapeDtypeStruct(res.shape, f32),
            jax.ShapeDtypeStruct(tg.shape, f32),
            jax.ShapeDtypeStruct(eg.shape, f32),
            jax.ShapeDtypeStruct((3, rows, cols), f32),
            one, one, one,
            jax.ShapeDtypeStruct((width, units), f32),
            jax.ShapeDtypeStruct((units, width), f32),
        ],
        in_specs=[hb] * 5,
        out_specs=[hb] * 9,
        scratch_shapes=[
            (
                pltpu.VMEM((units, width), f32),
                pltpu.VMEM(res.shape, f32),
                pltpu.VMEM(tg.shape, f32),
                pltpu.VMEM(eg.shape, f32),
                pltpu.VMEM(gw.shape, f32),
                pltpu.VMEM((units, width), f32),
            ),
            pltpu.VMEM((width, units), f32),
            pltpu.SemaphoreType.DMA((6,)),
            pltpu.SemaphoreType.DMA((9,)),
        ],
        compiler_params=pltpu.CompilerParams(vmem_limit_bytes=62 << 20),
        name="finish",
    )(gw, res, tg, eg, go)


def fast_local(
    tokens, encoder, target_doc, source_doc, self_proj, self_out, cross_query, cross_pairs, cross_out,
    hidden_in, hidden_in_bias, hidden_out, hidden_out_bias, self_gain, self_shift, cross_gain, cross_shift,
    hidden_gain, hidden_shift, cotangent,
):
    depth = lax.axis_size("dp") // 4
    count = 8 * depth
    place = Place()
    me = place.dp * 2 + place.y
    bf, f32 = jnp.bfloat16, jnp.float32
    vectors = jnp.stack(
        [self_gain, self_shift, cross_gain, cross_shift, hidden_gain, hidden_shift, hidden_out_bias]
    )
    span = vectors.shape[1]
    group = 128 // span
    lane = lax.broadcasted_iota(jnp.int32, (1, 128), 1)
    mine = lane // span == lax.rem(me, group)
    vec = jnp.concatenate([
        jnp.where(mine, jnp.tile(vectors, (1, group)), 0.0),
        jnp.zeros((1, 128), f32),
        hidden_in_bias.astype(f32).reshape(-1, 128),
    ])
    vec = jnp.pad(vec, ((0, -vec.shape[0] % 8), (0, 0)))
    G, act, ctx, mid, probs1, probs2, full, cot, d_in, y_in, go, gbias, S, YS = forward_all(
        self_proj.transpose(1, 0, 2), self_out.T, cross_pairs.transpose(1, 0, 2), cross_query, cross_out.T,
        hidden_in, hidden_out, vec, tokens, encoder, cotangent, target_doc, source_doc,
    )
    gw, vout, res, tg, eg, go = backward_all(
        G, act, ctx, mid, probs1, probs2, full, cot, d_in, y_in, go, S, YS
    )
    vout = lax.dynamic_slice_in_dim(vout, lax.rem(me, group) * span, span, axis=1)
    res, tg, eg, g_proj, g_so, g_query, g_co, g_in, g_out = finish(gw, res, tg, eg, go)
    return (
        res, tg, eg,
        g_proj.transpose(1, 0, 2), g_so.T, g_query, jnp.stack([gw[2], gw[3]], axis=1), g_co.T,
        g_in, gbias[0], g_out,
        vout[6], vout[0], vout[1], vout[2], vout[3], vout[4], vout[5],
    )


BLOCK_ROWS = 512


def smooth_gate(values):
    return jax.nn.gelu(values, approximate=True)


def plain_norm_forward(hidden, norm_gain, norm_shift):
    center = hidden - jnp.mean(hidden, axis=-1, keepdims=True)
    inverse = lax.rsqrt(jnp.mean(center * center, axis=-1, keepdims=True) + EPS)
    normal = center * inverse
    return (normal * norm_gain + norm_shift, normal, inverse)


def plain_norm_backward(upward, normal, inverse, norm_gain):
    scaled = upward * norm_gain
    centred = (
        scaled
        - jnp.mean(scaled, axis=-1, keepdims=True)
        - normal * jnp.mean(scaled * normal, axis=-1, keepdims=True)
    )
    return (centred * inverse, jnp.sum(upward * normal, axis=0), jnp.sum(upward, axis=0))


def split_blocks(array):
    row_count = array.shape[0]
    block_size = min(BLOCK_ROWS, row_count)
    return array.reshape((row_count // block_size, block_size) + array.shape[1:])


def block_scores(query_block, key_rows, allow_block):
    query_heads = query_block.reshape(query_block.shape[0], -1, HEAD)
    key_heads = key_rows.reshape(key_rows.shape[0], -1, HEAD)
    scores = jnp.einsum(
        "qhd,khd->hqk", query_heads, key_heads, preferred_element_type=jnp.float32
    ) * HEAD ** (-0.5)
    return jnp.where(allow_block[None], scores, NEGATIVE)


def plain_attend(queries, key_rows, values, allowed):
    columns = queries.shape[1]
    value_heads = values.reshape(values.shape[0], -1, HEAD)

    def one_block(pieces):
        query_block, allow_block = pieces
        scores = block_scores(query_block, key_rows, allow_block)
        highest = jnp.max(scores, axis=-1, keepdims=True)
        exponent = jnp.exp(scores - highest)
        totals = jnp.sum(exponent, axis=-1, keepdims=True)
        softmaxed = (exponent / totals).astype(jnp.bfloat16)
        mixture = jnp.einsum(
            "hqk,khd->qhd", softmaxed, value_heads, preferred_element_type=jnp.float32
        )
        return (
            mixture.reshape(query_block.shape[0], columns).astype(jnp.bfloat16),
            (highest + jnp.log(totals))[..., 0],
        )

    mixture, logsum = lax.map(one_block, (split_blocks(queries), split_blocks(allowed)))
    return (mixture.reshape(queries.shape), logsum)


def plain_attend_backward(queries, key_rows, values, allowed, logsum, slope_heads):
    scaling = HEAD ** (-0.5)
    key_heads = key_rows.reshape(key_rows.shape[0], -1, HEAD)
    value_heads = values.reshape(values.shape[0], -1, HEAD)

    def one_block(running, pieces):
        key_total, value_total = running
        query_block, allow_block, logsum_block, slope_block = pieces
        scores = block_scores(query_block, key_rows, allow_block)
        softmaxed = jnp.exp(scores - logsum_block[..., None])
        query_heads = query_block.reshape(query_block.shape[0], -1, HEAD)
        slope_out = slope_block.reshape(slope_block.shape[0], -1, HEAD)
        slope_probs = jnp.einsum(
            "qhd,khd->hqk", slope_out, value_heads, preferred_element_type=jnp.float32
        )
        centred = jnp.sum(softmaxed * slope_probs, axis=-1, keepdims=True)
        slope_scores = (softmaxed * (slope_probs - centred)).astype(jnp.bfloat16)
        slope_query = (
            jnp.einsum("hqk,khd->qhd", slope_scores, key_heads, preferred_element_type=jnp.float32)
            * scaling
        )
        key_total = (
            key_total
            + jnp.einsum(
                "hqk,qhd->khd", slope_scores, query_heads, preferred_element_type=jnp.float32
            )
            * scaling
        )
        value_total = value_total + jnp.einsum(
            "hqk,qhd->khd",
            softmaxed.astype(jnp.bfloat16),
            slope_out,
            preferred_element_type=jnp.float32,
        )
        return (
            (key_total, value_total),
            slope_query.reshape(query_block.shape[0], -1).astype(jnp.bfloat16),
        )

    empty_heads = jnp.zeros(key_heads.shape, jnp.float32)
    (key_total, value_total), slope_query = lax.scan(
        one_block,
        (empty_heads, empty_heads),
        (split_blocks(queries), split_blocks(allowed), logsum, split_blocks(slope_heads)),
    )
    return (
        slope_query.reshape(queries.shape),
        key_total.reshape(key_rows.shape).astype(jnp.bfloat16),
        value_total.reshape(values.shape).astype(jnp.bfloat16),
    )


def gather_rows(local_rows):
    return lax.all_gather(local_rows, "tensor", axis=0, tiled=True)


def sum_rows(partial_sum):
    return lax.psum_scatter(
        partial_sum.astype(jnp.bfloat16), "tensor", scatter_dimension=0, tiled=True
    ).astype(jnp.float32)


def gather_slopes(local_slopes):
    return lax.all_gather(local_slopes, "tensor", axis=0, tiled=True)


def sum_slopes(partial_sum):
    return lax.psum_scatter(
        partial_sum.astype(jnp.bfloat16), "tensor", scatter_dimension=0, tiled=True
    ).astype(jnp.float32)


def reduce_weights(weight_terms):
    return (
        lax.psum_scatter(weight_terms[0], "dp", scatter_dimension=0, tiled=True),
        lax.psum_scatter(weight_terms[1], "dp", scatter_dimension=1, tiled=True),
        lax.psum_scatter(weight_terms[2], "dp", scatter_dimension=0, tiled=True),
        lax.psum_scatter(weight_terms[3], "dp", scatter_dimension=0, tiled=True),
        lax.psum_scatter(weight_terms[4], "dp", scatter_dimension=1, tiled=True),
        lax.psum_scatter(weight_terms[5], "dp", scatter_dimension=1, tiled=True),
        lax.psum_scatter(weight_terms[6], "dp", scatter_dimension=0, tiled=True),
        lax.psum_scatter(weight_terms[7], "dp", scatter_dimension=0, tiled=True),
    )


def plain_local(
    tokens,
    encoder,
    target_doc,
    source_doc,
    self_proj,
    self_out,
    cross_query,
    cross_pairs,
    cross_out,
    hidden_in,
    hidden_in_bias,
    hidden_out,
    hidden_out_bias,
    self_gain,
    self_shift,
    cross_gain,
    cross_shift,
    hidden_gain,
    hidden_shift,
    cotangent,
):
    (
        full_self_gain,
        full_self_shift,
        full_cross_gain,
        full_cross_shift,
        full_hidden_gain,
        full_hidden_shift,
        full_out_bias,
    ) = (
        lax.all_gather(self_gain, ("dp", "tensor"), axis=0, tiled=True),
        lax.all_gather(self_shift, ("dp", "tensor"), axis=0, tiled=True),
        lax.all_gather(cross_gain, ("dp", "tensor"), axis=0, tiled=True),
        lax.all_gather(cross_shift, ("dp", "tensor"), axis=0, tiled=True),
        lax.all_gather(hidden_gain, ("dp", "tensor"), axis=0, tiled=True),
        lax.all_gather(hidden_shift, ("dp", "tensor"), axis=0, tiled=True),
        lax.all_gather(hidden_out_bias, ("dp", "tensor"), axis=0, tiled=True),
    )
    micro_count = tokens.shape[0]
    row_count = tokens.shape[1] * lax.axis_size("tensor")
    positions = jnp.arange(row_count)
    results = []
    token_grads = []
    encoder_grads = []
    vector_total = None
    weight_total = None
    for step_index in range(micro_count):
        forward_weights = (
            lax.all_gather(self_proj, "dp", axis=0, tiled=True),
            lax.all_gather(self_out, "dp", axis=1, tiled=True),
            lax.all_gather(cross_query, "dp", axis=0, tiled=True),
            lax.all_gather(cross_pairs, "dp", axis=0, tiled=True),
            lax.all_gather(cross_out, "dp", axis=1, tiled=True),
            lax.all_gather(hidden_in, "dp", axis=1, tiled=True),
            lax.all_gather(hidden_in_bias, "dp", axis=0, tiled=True),
            lax.all_gather(hidden_out, "dp", axis=0, tiled=True),
        )
        (
            full_proj,
            full_self_out,
            full_query,
            full_pairs,
            full_cross_out,
            full_in,
            full_in_bias,
            full_out,
        ) = forward_weights
        target_row = target_doc[step_index]
        source_row = source_doc[step_index]
        self_allowed = (target_row[:, None] == target_row[None, :]) & (
            positions[None, :] <= positions[:, None]
        )
        cross_allowed = target_row[:, None] == source_row[None, :]
        start_hidden = tokens[step_index].astype(jnp.float32)
        normed_first, normal_first, inverse_first = plain_norm_forward(
            start_hidden, full_self_gain, full_self_shift
        )
        self_rows = gather_rows(normed_first.astype(jnp.bfloat16))
        triple = jnp.einsum(
            "td,dcj->tcj", self_rows, full_proj, preferred_element_type=jnp.float32
        ).astype(jnp.bfloat16)
        self_heads, self_logsum = plain_attend(triple[:, 0], triple[:, 1], triple[:, 2], self_allowed)
        middle = start_hidden + sum_rows(
            jnp.dot(self_heads, full_self_out, preferred_element_type=jnp.float32)
        )
        normed_second, normal_second, inverse_second = plain_norm_forward(
            middle, full_cross_gain, full_cross_shift
        )
        cross_rows, source_rows = (
            lax.all_gather(normed_second.astype(jnp.bfloat16), "tensor", axis=0, tiled=True),
            lax.all_gather(encoder[step_index], "tensor", axis=0, tiled=True),
        )
        cross_queries = jnp.dot(cross_rows, full_query, preferred_element_type=jnp.float32).astype(
            jnp.bfloat16
        )
        key_value = jnp.einsum(
            "sd,dcj->scj", source_rows, full_pairs, preferred_element_type=jnp.float32
        ).astype(jnp.bfloat16)
        cross_heads, cross_logsum = plain_attend(
            cross_queries, key_value[:, 0], key_value[:, 1], cross_allowed
        )
        latter = middle + sum_rows(
            jnp.dot(cross_heads, full_cross_out, preferred_element_type=jnp.float32)
        )
        normed_third, normal_third, inverse_third = plain_norm_forward(
            latter, full_hidden_gain, full_hidden_shift
        )
        hidden_rows = gather_rows(normed_third.astype(jnp.bfloat16))
        before = jnp.dot(
            hidden_rows, full_in, preferred_element_type=jnp.float32
        ) + full_in_bias.astype(jnp.float32)
        gated, gate_pullback = jax.vjp(smooth_gate, before)
        active = gated.astype(jnp.bfloat16)
        results.append(
            latter
            + sum_rows(jnp.dot(active, full_out, preferred_element_type=jnp.float32))
            + full_out_bias
        )
        back_weights = (
            lax.all_gather(self_proj, "dp", axis=0, tiled=True),
            lax.all_gather(self_out, "dp", axis=1, tiled=True),
            lax.all_gather(cross_query, "dp", axis=0, tiled=True),
            lax.all_gather(cross_pairs, "dp", axis=0, tiled=True),
            lax.all_gather(cross_out, "dp", axis=1, tiled=True),
            lax.all_gather(hidden_in, "dp", axis=1, tiled=True),
            lax.all_gather(hidden_in_bias, "dp", axis=0, tiled=True),
            lax.all_gather(hidden_out, "dp", axis=0, tiled=True),
        )
        (
            back_proj,
            back_self_out,
            back_query,
            back_pairs,
            back_cross_out,
            back_in,
            back_in_bias,
            back_out,
        ) = back_weights
        upward = cotangent[step_index].astype(jnp.float32)
        grad_out_bias = jnp.sum(upward, axis=0)
        slope_rows = gather_slopes(upward.astype(jnp.bfloat16))
        grad_out = jnp.einsum("tf,td->fd", active, slope_rows, preferred_element_type=jnp.float32)
        slope_active = jnp.einsum(
            "td,fd->tf", slope_rows, back_out, preferred_element_type=jnp.float32
        )
        slope_before = gate_pullback(slope_active)[0].astype(jnp.bfloat16)
        grad_in_bias = jnp.sum(slope_before.astype(jnp.float32), axis=0)
        grad_in = jnp.einsum(
            "td,tf->df", hidden_rows, slope_before, preferred_element_type=jnp.float32
        )
        slope_normed = sum_slopes(
            jnp.einsum("tf,df->td", slope_before, back_in, preferred_element_type=jnp.float32)
        )
        slope_hidden, grad_hidden_gain, grad_hidden_shift = plain_norm_backward(
            slope_normed, normal_third, inverse_third, full_hidden_gain
        )
        upward = upward + slope_hidden
        slope_rows = gather_slopes(upward.astype(jnp.bfloat16))
        grad_cross_out = jnp.einsum(
            "tj,td->jd", cross_heads, slope_rows, preferred_element_type=jnp.float32
        )
        slope_heads = jnp.einsum(
            "td,jd->tj", slope_rows, back_cross_out, preferred_element_type=jnp.float32
        ).astype(jnp.bfloat16)
        slope_query, slope_keys, slope_values = plain_attend_backward(
            cross_queries,
            key_value[:, 0],
            key_value[:, 1],
            cross_allowed,
            cross_logsum,
            slope_heads,
        )
        slope_pairs = jnp.stack([slope_keys, slope_values], axis=1)
        grad_query = jnp.einsum(
            "td,tj->dj", cross_rows, slope_query, preferred_element_type=jnp.float32
        )
        grad_pairs = jnp.einsum(
            "sd,scj->dcj", source_rows, slope_pairs, preferred_element_type=jnp.float32
        )
        slope_cross, slope_source = (
            lax.psum_scatter(
                jnp.einsum(
                    "tj,dj->td", slope_query, back_query, preferred_element_type=jnp.float32
                ).astype(jnp.bfloat16),
                "tensor",
                scatter_dimension=0,
                tiled=True,
            ).astype(jnp.float32),
            lax.psum_scatter(
                jnp.einsum(
                    "scj,dcj->sd", slope_pairs, back_pairs, preferred_element_type=jnp.float32
                ).astype(jnp.bfloat16),
                "tensor",
                scatter_dimension=0,
                tiled=True,
            ).astype(jnp.float32),
        )
        slope_hidden, grad_cross_gain, grad_cross_shift = plain_norm_backward(
            slope_cross, normal_second, inverse_second, full_cross_gain
        )
        upward = upward + slope_hidden
        slope_rows = gather_slopes(upward.astype(jnp.bfloat16))
        grad_self_out = jnp.einsum(
            "tj,td->jd", self_heads, slope_rows, preferred_element_type=jnp.float32
        )
        slope_heads = jnp.einsum(
            "td,jd->tj", slope_rows, back_self_out, preferred_element_type=jnp.float32
        ).astype(jnp.bfloat16)
        slope_query, slope_keys, slope_values = plain_attend_backward(
            triple[:, 0], triple[:, 1], triple[:, 2], self_allowed, self_logsum, slope_heads
        )
        slope_triple = jnp.stack([slope_query, slope_keys, slope_values], axis=1)
        grad_proj = jnp.einsum(
            "td,tcj->dcj", self_rows, slope_triple, preferred_element_type=jnp.float32
        )
        slope_self = sum_slopes(
            jnp.einsum("tcj,dcj->td", slope_triple, back_proj, preferred_element_type=jnp.float32)
        )
        slope_hidden, grad_self_gain, grad_self_shift = plain_norm_backward(
            slope_self, normal_first, inverse_first, full_self_gain
        )
        token_grads.append(upward + slope_hidden)
        encoder_grads.append(slope_source)
        vector_terms = (
            grad_self_gain,
            grad_self_shift,
            grad_cross_gain,
            grad_cross_shift,
            grad_hidden_gain,
            grad_hidden_shift,
            grad_out_bias,
        )
        vector_total = (
            vector_terms if step_index == 0 else jax.tree.map(jnp.add, vector_total, vector_terms)
        )
        weight_terms = (
            grad_proj,
            grad_self_out,
            grad_query,
            grad_pairs,
            grad_cross_out,
            grad_in,
            grad_in_bias,
            grad_out,
        )
        shard_terms = reduce_weights(weight_terms)
        weight_total = (
            shard_terms if step_index == 0 else jax.tree.map(jnp.add, weight_total, shard_terms)
        )
    vector_shards = (
        lax.psum_scatter(vector_total[0], ("dp", "tensor"), scatter_dimension=0, tiled=True),
        lax.psum_scatter(vector_total[1], ("dp", "tensor"), scatter_dimension=0, tiled=True),
        lax.psum_scatter(vector_total[2], ("dp", "tensor"), scatter_dimension=0, tiled=True),
        lax.psum_scatter(vector_total[3], ("dp", "tensor"), scatter_dimension=0, tiled=True),
        lax.psum_scatter(vector_total[4], ("dp", "tensor"), scatter_dimension=0, tiled=True),
        lax.psum_scatter(vector_total[5], ("dp", "tensor"), scatter_dimension=0, tiled=True),
        lax.psum_scatter(vector_total[6], ("dp", "tensor"), scatter_dimension=0, tiled=True),
    )
    return (
        jnp.stack(results),
        jnp.stack(token_grads),
        jnp.stack(encoder_grads),
        weight_total[0],
        weight_total[1],
        weight_total[2],
        weight_total[3],
        weight_total[4],
        weight_total[5],
        weight_total[6],
        weight_total[7],
        vector_shards[6],
        vector_shards[0],
        vector_shards[1],
        vector_shards[2],
        vector_shards[3],
        vector_shards[4],
        vector_shards[5],
    )


def solution(mesh):
    in_specs = (
        P("dp", "tensor", None),
        P("dp", "tensor", None),
        P("dp", None),
        P("dp", None),
        P("dp", None, "tensor"),
        P("tensor", "dp"),
        P("dp", "tensor"),
        P("dp", None, "tensor"),
        P("tensor", "dp"),
        P(None, ("dp", "tensor")),
        P(("dp", "tensor")),
        P(("dp", "tensor"), None),
        P(("dp", "tensor")),
        P(("dp", "tensor")),
        P(("dp", "tensor")),
        P(("dp", "tensor")),
        P(("dp", "tensor")),
        P(("dp", "tensor")),
        P(("dp", "tensor")),
        P("dp", "tensor", None),
    )
    out_specs = (
        P("dp", "tensor", None),
        P("dp", "tensor", None),
        P("dp", "tensor", None),
        P("dp", None, "tensor"),
        P("tensor", "dp"),
        P("dp", "tensor"),
        P("dp", None, "tensor"),
        P("tensor", "dp"),
        P(None, ("dp", "tensor")),
        P(("dp", "tensor")),
        P(("dp", "tensor"), None),
        P(("dp", "tensor")),
        P(("dp", "tensor")),
        P(("dp", "tensor")),
        P(("dp", "tensor")),
        P(("dp", "tensor")),
        P(("dp", "tensor")),
        P(("dp", "tensor")),
    )

    def run(*arrays):
        width = arrays[0].shape[2]
        aligned = width // mesh.shape["dp"] % 16 == 0 and mesh.shape["dp"] % 4 == 0
        inner = fast_local if aligned and mesh.shape["tensor"] == 2 else plain_local
        return jax.shard_map(inner, mesh=mesh, in_specs=in_specs, out_specs=out_specs, check_vma=False)(*arrays)

    return run
```
